32 devices in a mesh: dom: 4 (over x, core), phase: 2 (over y), feat: 4 (over z).
Axes of the slice: x: 2, y: 2, z: 4, core: 2. Of those that a mesh axis runs over, the one named last changes fastest.
Arguments:
- node_in: bfloat16 [131072, 256], P(('dom', 'phase', 'feat')), may hold values from -6 to 6
- out_cot: bfloat16 [131072, 256], P(('dom', 'phase', 'feat')), may hold values from -6 to 6
- adjacency: bfloat16 [1024, 4, 128, 128], P(('dom', 'phase', 'feat')), may hold values from -0.25 to 0.25
- tile_nbrs: int32 [1024, 4], P(('dom', 'phase', 'feat')), may hold values from 0 to 47, as said below
- bound_tiles: int32 [32, 2, 8], P(('dom', 'phase', 'feat')), may hold values from 0 to 15, as said below
- live_tiles: int32 [32], P(('dom', 'phase', 'feat')), may hold values from 16 to 32, as said below
- w_self: bfloat16 [2, 256, 256], replicated, may hold values from -0.25 to 0.25
- w_nbr: bfloat16 [2, 256, 256], replicated, may hold values from -0.25 to 0.25
- pre_bias: float32 [2, 256], replicated, may hold values from -3 to 3
- w_out: bfloat16 [2, 256, 256], replicated, may hold values from -0.375 to 0.375
Outputs:
- section_out: bfloat16 [2, 131072, 256], P(None, ('dom', 'phase', 'feat'))
- section_in_grad: bfloat16 [2, 131072, 256], P(None, ('dom', 'phase', 'feat'))
- grad_self: float32 [2, 256, 256], replicated
- grad_nbr: float32 [2, 256, 256], replicated
- grad_bias: float32 [2, 256], replicated
- grad_out: float32 [2, 256, 256], replicated
The draws below stay inside these ranges and needn't reach their ends.
Inputs may be any that keep to these rules, and one draw needn't show every extreme that they name: `live_tiles`: some partition has all 32 tiles live. `bound_tiles`: for each partition the 16 entries are the tiles 0 to 15, each once. `tile_nbrs`: slot 0 of local tile i is i; every entry of a live tile names a live own tile (below 32) or an extended tile (from 32 on); each extended tile is named by some live tile; all entries of a tile that is not live are i.
All inputs are finite; a program needn't handle non-finite values.
Results may differ from the reference program's by a relative error of at most 0.008.
Values may be sent and summed in bfloat16 or wider, within the bound.
No kernel may reach another device: no remote copies, remote signals or barrier semaphores. Data moves between devices by JAX's collectives and lax.ppermute only.
A program may use at most 192 MiB of HBM per device.

```python
import jax
import jax.numpy as jnp
from jax import lax

HID = 256
TILE = 128
SLOTS = 4
TILES = 32
EDGE_TILES = 8
PARTS_SIZE = 32
NODE_TILES = 1024
NODES = 131072


def live_counts(key):
    counts = jax.random.randint(jax.random.fold_in(key, 11), (PARTS_SIZE,), TILES // 2, TILES + 1)
    full_part = jax.random.randint(jax.random.fold_in(key, 12), (), 0, PARTS_SIZE)
    small_part = jax.random.randint(jax.random.fold_in(key, 13), (), 0, PARTS_SIZE)
    positions = jnp.arange(PARTS_SIZE)
    counts = jnp.where(positions == small_part, TILES // 2, counts)
    counts = jnp.where(positions == full_part, TILES, counts)
    return counts.astype(jnp.int32)


def draw_live_tiles(key, part):
    return live_counts(key)


def draw_bound_tiles(key, part):
    half_tiles = TILES // 2
    scores = jax.random.randint(jax.random.fold_in(key, 21), (PARTS_SIZE, half_tiles), 0, 1 << 20) * half_tiles + jnp.arange(half_tiles)[None, :]
    ranked = jnp.argsort(scores, axis=1).astype(jnp.int32)
    return ranked.reshape(PARTS_SIZE, 2, EDGE_TILES)


def draw_tile_nbrs(key, part):
    counts = live_counts(key)
    raw_pick = jax.random.randint(jax.random.fold_in(key, 31), (PARTS_SIZE, TILES, SLOTS), 0, TILES + 2 * EDGE_TILES)
    local_pick = raw_pick % counts[:, None, None]
    chosen = jnp.where(raw_pick < TILES, local_pick, raw_pick)
    own_tile = jnp.broadcast_to(jnp.arange(TILES)[None, :, None], (PARTS_SIZE, TILES, SLOTS))
    slot_index = jnp.broadcast_to(jnp.arange(SLOTS)[None, None, :], (PARTS_SIZE, TILES, SLOTS))
    chosen = jnp.where(slot_index == 0, own_tile, chosen)
    chosen = jnp.where((slot_index == 1) & (own_tile < 2 * EDGE_TILES), TILES + own_tile, chosen)
    chosen = jnp.where(own_tile >= counts[:, None, None], own_tile, chosen)
    return chosen.reshape(PARTS_SIZE * TILES, SLOTS).astype(jnp.int32)


def steps_of(own_key, extent, shards, least, high):
    def one(dim, shards_of):
        steps = jax.random.uniform(jax.random.fold_in(jax.random.fold_in(own_key, 6), dim), (shards_of,), jnp.float32, least / len(shards), high / len(shards))
        return jnp.repeat(jnp.exp(steps), extent[dim] // shards_of).reshape((-1,) + (1,) * (len(extent) - dim - 1))

    gain = one(*shards[0])
    for cut in shards[1:]:
        gain = gain * one(*cut)
    return gain


def noise(own_key, shape, deviation, limit, split=(), held_as=jnp.bfloat16):
    values = jax.random.normal(own_key, shape, jnp.float32) * deviation
    if len(split) > 0:
        values = steps_of(own_key, shape, split, -0.22, 0.18) * values
    return jnp.clip(values, min=-limit, max=limit).astype(held_as)


def setup_inputs(seed: int = 0) -> dict:
    streams_of = jax.random.split(jax.random.key(seed), 11)
    return {
        "node_in": noise(streams_of[0], (NODES, HID), 1.0, 6.0, ((0, 32),)),
        "out_cot": noise(streams_of[1], (NODES, HID), 1.0, 6.0, ((0, 32),)),
        "adjacency": noise(streams_of[2], (NODE_TILES, SLOTS, TILE, TILE), (TILE * SLOTS) ** -0.5, 0.25, ((0, 32),)),
        "tile_nbrs": draw_tile_nbrs(jax.random.fold_in(streams_of[10], 71), 0),
        "bound_tiles": draw_bound_tiles(jax.random.fold_in(streams_of[10], 71), 0),
        "live_tiles": draw_live_tiles(jax.random.fold_in(streams_of[10], 71), 0),
        "w_self": noise(streams_of[6], (2, HID, HID), (2 * HID) ** -0.5, 0.25),
        "w_nbr": noise(streams_of[7], (2, HID, HID), (2 * HID) ** -0.5, 0.25),
        "pre_bias": noise(streams_of[8], (2, HID), 0.5, 3.0, (), jnp.float32),
        "w_out": noise(streams_of[9], (2, HID, HID), HID ** -0.5, 0.375),
    }


def silu_slope(pre_act):
    sigma = jax.nn.sigmoid(pre_act)
    return sigma * (1.0 + pre_act * (1.0 - sigma))


def tile_pick(node_tiles, index_rows):
    return jax.vmap(lambda block_rows, chosen: block_rows[chosen])(node_tiles, index_rows)


def extend_tiles(node_tiles, bound_tiles):
    west_send = tile_pick(node_tiles, bound_tiles[:, 0])
    east_send = tile_pick(node_tiles, bound_tiles[:, 1])
    return jnp.concatenate([node_tiles, jnp.roll(east_send, 1, axis=0), jnp.roll(west_send, -1, axis=0)], axis=1)


def aggregate(extended, neighbours, adj_tiles):
    def one_part(operands):
        ext_part, nbr_part, adj_part = operands
        picked = ext_part[nbr_part]
        return jnp.einsum("tkij,tkjc->tic", adj_part.astype(jnp.float32), picked.astype(jnp.float32))
    return lax.map(one_part, (extended, neighbours, adj_tiles))


def spread_back(delta_tiles, neighbours, adj_tiles, bound_tiles):
    def one_part(operands):
        delta_part, nbr_part, adj_part = operands
        contrib = jnp.einsum("tkij,tic->tkjc", adj_part.astype(jnp.float32), delta_part.astype(jnp.float32))
        return jax.ops.segment_sum(contrib.reshape(TILES * SLOTS, TILE, -1), nbr_part.reshape(-1), num_segments=TILES + 2 * EDGE_TILES)
    collected = lax.map(one_part, (delta_tiles, neighbours, adj_tiles))
    local_part = collected[:, :TILES]
    west_part = collected[:, TILES:TILES + EDGE_TILES]
    east_part = collected[:, TILES + EDGE_TILES:]
    add_rows = jax.vmap(lambda block_rows, chosen, values: block_rows.at[chosen].add(values))
    local_part = add_rows(local_part, bound_tiles[:, 1], jnp.roll(west_part, -1, axis=0))
    local_part = add_rows(local_part, bound_tiles[:, 0], jnp.roll(east_part, 1, axis=0))
    return local_part


def forward(features, w_self, w_nbr, pre_bias, w_out, neighbours, adj_tiles, bound_tiles, row_mask):
    node_tiles = features.reshape(PARTS_SIZE, TILES, TILE, HID)
    summed = aggregate(extend_tiles(node_tiles, bound_tiles), neighbours, adj_tiles)
    gathered = summed.reshape(NODES, HID).astype(jnp.bfloat16)
    pre_act = jnp.dot(features, w_self, preferred_element_type=jnp.float32) + jnp.dot(gathered, w_nbr, preferred_element_type=jnp.float32) + pre_bias
    hidden = jax.nn.silu(pre_act).astype(jnp.bfloat16)
    result = (row_mask * (features.astype(jnp.float32) + jnp.dot(hidden, w_out, preferred_element_type=jnp.float32))).astype(jnp.bfloat16)
    return result, (features, gathered, pre_act, hidden)


def backward(upstream, saved_state, w_self, w_nbr, w_out, neighbours, adj_tiles, bound_tiles, row_mask):
    features, gathered, pre_act, hidden = saved_state
    masked = (upstream.astype(jnp.float32) * row_mask).astype(jnp.bfloat16)
    grad_out = jnp.dot(hidden.T, masked, preferred_element_type=jnp.float32)
    grad_hidden = jnp.dot(masked, w_out.T, preferred_element_type=jnp.float32)
    grad_pre = (grad_hidden * silu_slope(pre_act)).astype(jnp.bfloat16)
    grad_self = jnp.dot(features.T, grad_pre, preferred_element_type=jnp.float32)
    grad_nbr = jnp.dot(gathered.T, grad_pre, preferred_element_type=jnp.float32)
    grad_bias = jnp.sum(grad_pre.astype(jnp.float32), axis=0)
    direct = masked.astype(jnp.float32) + jnp.dot(grad_pre, w_self.T, preferred_element_type=jnp.float32)
    grad_gathered = jnp.dot(grad_pre, w_nbr.T, preferred_element_type=jnp.float32).astype(jnp.bfloat16)
    returned = spread_back(grad_gathered.reshape(PARTS_SIZE, TILES, TILE, HID), neighbours, adj_tiles, bound_tiles)
    grad_in = (direct + returned.reshape(NODES, HID)).astype(jnp.bfloat16)
    return grad_in, (grad_self, grad_nbr, grad_bias, grad_out)


def reference(node_in, out_cot, adjacency, tile_nbrs, bound_tiles, live_tiles, w_self, w_nbr, pre_bias, w_out):
    tile_live = (jnp.arange(TILES)[None, :] < live_tiles[:, None]).astype(jnp.float32)
    row_mask = jnp.repeat(tile_live.reshape(-1), TILE)[:, None]
    neighbours = tile_nbrs.reshape(PARTS_SIZE, TILES, SLOTS)
    adj_tiles = adjacency.reshape(PARTS_SIZE, TILES, SLOTS, TILE, TILE)
    first_out, first_saved = forward(node_in, w_self[0], w_nbr[0], pre_bias[0], w_out[0], neighbours, adj_tiles, bound_tiles, row_mask)
    second_out, second_saved = forward(first_out, w_self[1], w_nbr[1], pre_bias[1], w_out[1], neighbours, adj_tiles, bound_tiles, row_mask)
    grad_mid, later_grads = backward(out_cot, second_saved, w_self[1], w_nbr[1], w_out[1], neighbours, adj_tiles, bound_tiles, row_mask)
    grad_first, early_grads = backward(grad_mid, first_saved, w_self[0], w_nbr[0], w_out[0], neighbours, adj_tiles, bound_tiles, row_mask)
    return (jnp.stack([first_out, second_out]), jnp.stack([grad_first, grad_mid]),
            jnp.stack([early_grads[0], later_grads[0]]), jnp.stack([early_grads[1], later_grads[1]]),
            jnp.stack([early_grads[2], later_grads[2]]), jnp.stack([early_grads[3], later_grads[3]]))
```

```python
import functools

import jax
import jax.numpy as jnp
from jax import lax
from jax.experimental import pallas as pl
from jax.experimental.pallas import tpu as pltpu
from jax.sharding import PartitionSpec as P

AXES = ("dom", "phase", "feat")
PLANE = ("dom", "phase")
BF16 = jnp.bfloat16
F32 = jnp.float32
UNROLL = 8
ANY = pl.BlockSpec(memory_space=pl.ANY)
SMEM = pl.BlockSpec(memory_space=pltpu.SMEM)
VMEM_BYTES = 44 * 1024 * 1024


class Sizes:
    def __init__(self, adjacency, features, bound):
        self.tiles, self.slots, self.rows, _ = adjacency.shape
        self.cols = features.shape[-1]
        self.edge = bound.shape[-1]
        self.lent = 2 * self.edge
        self.ext = self.tiles + self.lent
        self.pairs = self.tiles * self.slots
        self.group = next(g for g in (4, 2, 1) if self.edge % g == 0 and self.tiles % g == 0)
        self.steps = self.tiles // self.group
        self.lent_steps = self.lent // self.group
        self.edge_steps = self.edge // self.group

    def nodes(self, count, dtype=BF16):
        return jax.ShapeDtypeStruct((count, self.rows, self.cols), dtype)

    def block(self, index):
        return pl.BlockSpec((self.group, self.rows, self.cols), lambda s, *_: (index(s), 0, 0))


def passed_along(value, steps):
    count = lax.axis_size(AXES)
    return lax.ppermute(value, AXES, [(i, (i + steps) % count) for i in range(count)])


def dot(a, b):
    return jnp.dot(a, b, preferred_element_type=F32)


def dot_rows(a, b):
    return lax.dot_general(a, b, (((0,), (0,)), ((), ())), preferred_element_type=F32)


def whole(shape):
    return pl.BlockSpec(shape, lambda *_: (0,) * len(shape))


def layer_of(cols, layer):
    return pl.BlockSpec((None, cols, cols), lambda *_: (layer, 0, 0))


def turned(cols, layer, which):
    return pl.BlockSpec((None, None, cols, cols), lambda *_: (layer, which, 0, 0))


def call(kernel, name, grid, prefetch, in_specs, out_specs, out_shape, scratch, flops, moved, args, aliases=None):
    return pl.pallas_call(
        kernel,
        grid_spec=pltpu.PrefetchScalarGridSpec(
            num_scalar_prefetch=prefetch,
            grid=grid,
            in_specs=in_specs,
            out_specs=out_specs,
            scratch_shapes=scratch,
        ),
        out_shape=out_shape,
        input_output_aliases=aliases or {},
        compiler_params=pltpu.CompilerParams(vmem_limit_bytes=VMEM_BYTES),
        cost_estimate=pl.CostEstimate(flops=int(flops), bytes_accessed=int(moved), transcendentals=0),
        name=name,
    )(*args)


def lend(z, bound, features):
    def kernel(bound, feats, west, east, sems):
        copies = []
        for i in range(z.edge):
            for side, target in ((0, west), (1, east)):
                copy = pltpu.make_async_copy(
                    feats.at[bound[0, side, i]], target.at[i], sems.at[side * z.edge + i]
                )
                copy.start()
                copies.append(copy)
        for copy in copies:
            copy.wait()

    return pl.pallas_call(
        kernel,
        in_specs=[SMEM, ANY],
        out_specs=[ANY, ANY],
        out_shape=[z.nodes(z.edge), z.nodes(z.edge)],
        scratch_shapes=[pltpu.SemaphoreType.DMA((z.lent,))],
        name="lend",
    )(bound, features)


def arrange(z, bound, nbrs, live, features, cot, adjacency, w_self, w_nbr, w_out):
    t, s4, r, c = z.tiles, z.slots, z.rows, z.cols

    def at_position(q, bound):
        clipped = jnp.minimum(q, z.lent - 1)
        return jnp.where(q < z.lent, bound[0, clipped // z.edge, clipped % z.edge], q)

    def kernel(bound, nbrs, live, feats, cot, adj, ws, wn, wo, f_out, m_out, ap, at, wt, meta, counts, place, inverse):
        q = pl.program_id(0)

        @pl.when(q == 0)
        def _():
            for layer in range(2):
                wt[layer, 0] = ws[layer].T
                wt[layer, 1] = wn[layer].T
                wt[layer, 2] = wo[layer].T
            for i in range(z.lent):
                inverse[bound[0, i // z.edge, i % z.edge]] = i

            def kind_of(position, target):
                return jnp.where(target < t, 0, jnp.where(position < z.lent, 2, 1))

            def count(position, carry):
                own, outer, lent = carry
                tile = at_position(position, bound)
                for k in range(s4):
                    target = nbrs[tile, k]
                    moved = jnp.where(
                        target < z.lent, inverse[jnp.minimum(target, z.lent - 1)], target
                    )
                    meta[position * s4 + k] = moved
                    kind = kind_of(position, moved)
                    own = own + jnp.where(kind == 0, 1, 0)
                    outer = outer + jnp.where(kind == 1, 1, 0)
                    lent = lent + jnp.where(kind == 2, 1, 0)
                return own, outer, lent

            zero = jnp.int32(0)
            own, outer, lent = lax.fori_loop(0, t, count, (zero, zero, zero))
            counts[0] = own
            counts[1] = outer
            counts[2] = lent

            def put(position, carry):
                own, outer, lent = carry
                for k in range(s4):
                    target = meta[position * s4 + k]
                    kind = kind_of(position, target)
                    slot = jnp.where(kind == 0, own, jnp.where(kind == 1, outer, lent))
                    place[position * s4 + k] = slot
                    meta[z.pairs + slot] = position
                    meta[2 * z.pairs + slot] = target
                    own = own + jnp.where(kind == 0, 1, 0)
                    outer = outer + jnp.where(kind == 1, 1, 0)
                    lent = lent + jnp.where(kind == 2, 1, 0)
                return own, outer, lent

            lax.fori_loop(0, t, put, (zero, own, own + outer))

        tile = at_position(q, bound)
        f_out[...] = feats[...]
        m_out[...] = jnp.where(tile < live[0], cot[...], jnp.zeros_like(cot))
        ap[0] = jnp.concatenate([adj[0, k] for k in range(s4)], axis=1)
        for k in range(s4):
            at[place[q * s4 + k]] = adj[0, k].T

    nodes_in = pl.BlockSpec((1, r, c), lambda q, bound, *_: (at_position(q, bound), 0, 0))
    nodes_out = pl.BlockSpec((1, r, c), lambda q, *_: (q, 0, 0))
    return call(
        kernel,
        "arrange",
        (t,),
        3,
        [
            nodes_in,
            nodes_in,
            pl.BlockSpec((1, s4, r, r), lambda q, bound, *_: (at_position(q, bound), 0, 0, 0)),
            whole((2, c, c)),
            whole((2, c, c)),
            whole((2, c, c)),
        ],
        [
            nodes_out,
            nodes_out,
            pl.BlockSpec((1, r, s4 * r), lambda q, *_: (q, 0, 0)),
            whole((z.pairs, r, r)),
            whole((2, 3, c, c)),
            SMEM,
            SMEM,
        ],
        [
            z.nodes(t),
            z.nodes(t),
            jax.ShapeDtypeStruct((t, r, s4 * r), BF16),
            jax.ShapeDtypeStruct((z.pairs, r, r), BF16),
            jax.ShapeDtypeStruct((2, 3, c, c), BF16),
            jax.ShapeDtypeStruct((3 * z.pairs,), jnp.int32),
            jax.ShapeDtypeStruct((8,), jnp.int32),
        ],
        [pltpu.SMEM((z.pairs,), jnp.int32), pltpu.SMEM((z.lent,), jnp.int32)],
        0,
        20 * 2**20,
        (bound, nbrs, live, features, cot, adjacency, w_self, w_nbr, w_out),
    )


def load_extended(z, own, fw, fe, ext, sems):
    copies = [
        pltpu.make_async_copy(own, ext.at[pl.ds(0, z.tiles)], sems.at[0]),
        pltpu.make_async_copy(fw, ext.at[pl.ds(z.tiles, z.edge)], sems.at[1]),
        pltpu.make_async_copy(fe, ext.at[pl.ds(z.tiles + z.edge, z.edge)], sems.at[2]),
    ]
    for copy in copies:
        copy.start()
    for copy in copies:
        copy.wait()


def aggregate(z, meta, first, ap, ext, agg):
    for g in range(z.group):
        base = (first + g) * z.slots
        picked = jnp.concatenate([ext[meta[base + k]] for k in range(z.slots)], axis=0)
        agg[g] = dot(ap[g], picked).astype(BF16)


def flat(z, value):
    return value.reshape(z.group * z.rows, z.cols)


def tiled(z, value):
    return value.reshape(z.group, z.rows, z.cols)


def live_rows(z, value, first, live):
    parts = []
    for g in range(z.group):
        part = value[g * z.rows : (g + 1) * z.rows]
        parts.append(jnp.where(first + g < live, part, jnp.zeros_like(part)))
    return jnp.concatenate(parts, axis=0)


def pre_activation(z, f, agg, ws, wn, bias, layer):
    return dot(f, ws[...]) + dot(agg, wn[...]) + bias[layer : layer + 1, :]


def sigmoid(v):
    return 1.0 / (1.0 + jnp.exp(-v))


def first_lent(z, meta, f0, fw, fe, ap, w_self, w_nbr, bias, w_out):
    def kernel(meta, own, fw, fe, ap, ws, wn, bias, wo, west, east, agg, ext, sems):
        s = pl.program_id(0)

        @pl.when(s == 0)
        def _():
            load_extended(z, own, fw, fe, ext, sems)

        first = s * z.group
        aggregate(z, meta, first, ap, ext, agg)
        f = flat(z, ext[pl.ds(first, z.group)])
        pre = pre_activation(z, f, flat(z, agg[...]), ws, wn, bias, 0)
        act = (pre * sigmoid(pre)).astype(BF16)
        out = tiled(z, (f.astype(F32) + dot(act, wo[...])).astype(BF16))

        @pl.when(s < z.edge_steps)
        def _():
            west[...] = out

        @pl.when(s >= z.edge_steps)
        def _():
            east[...] = out

    c = z.cols
    return call(
        kernel,
        "first_lent",
        (z.lent_steps,),
        1,
        [ANY, ANY, ANY, pl.BlockSpec((z.group, z.rows, z.slots * z.rows), lambda s, *_: (s, 0, 0)),
         layer_of(c, 0), layer_of(c, 0), whole((2, c)), layer_of(c, 0)],
        [
            z.block(lambda s: jnp.minimum(s, z.edge_steps - 1)),
            z.block(lambda s: jnp.maximum(s - z.edge_steps, 0)),
            z.block(lambda s: s),
        ],
        [z.nodes(z.edge), z.nodes(z.edge), z.nodes(z.tiles)],
        [pltpu.VMEM((z.ext, z.rows, z.cols), BF16), pltpu.SemaphoreType.DMA((3,))],
        2e9,
        8 * 2**20,
        (meta, f0, fw, fe, ap, w_self, w_nbr, bias, w_out),
    )


def first_rest(z, meta, bound, live, f0, fw, fe, ap, w_self, w_nbr, bias, w_out, west, east, agg0):
    rest = z.tiles - z.lent

    def kernel(meta, bound, live, own, fw, fe, ap, ws, wn, bias, wo, west, east, _agg, f1, out, agg, ext, keep, sems, more):
        s = pl.program_id(0)
        copies = [
            pltpu.make_async_copy(west, f1.at[pl.ds(0, z.edge)], more.at[0]),
            pltpu.make_async_copy(east, f1.at[pl.ds(z.edge, z.edge)], more.at[1]),
        ]
        for i in range(z.edge):
            for side, source in ((0, west), (1, east)):
                copies.append(
                    pltpu.make_async_copy(
                        source.at[i], out.at[0, bound[0, side, i]], more.at[2 + side * z.edge + i]
                    )
                )

        @pl.when(s == 0)
        def _():
            load_extended(z, own, fw, fe, ext, sems)
            for copy in copies:
                copy.start()

        first = z.lent + s * z.group
        aggregate(z, meta, first, ap, ext, agg)
        f = flat(z, ext[pl.ds(first, z.group)])
        pre = pre_activation(z, f, flat(z, agg[...]), ws, wn, bias, 0)
        act = (pre * sigmoid(pre)).astype(BF16)
        res = live_rows(z, f.astype(F32) + dot(act, wo[...]), first, live[0])
        keep[pl.ds(s * z.group, z.group)] = tiled(z, res.astype(BF16))

        @pl.when(s == pl.num_programs(0) - 1)
        def _():
            last = [
                pltpu.make_async_copy(keep, f1.at[pl.ds(z.lent, rest)], more.at[2 + z.lent]),
                pltpu.make_async_copy(keep, out.at[0, pl.ds(z.lent, rest)], more.at[3 + z.lent]),
            ]
            for copy in last:
                copy.start()
            for copy in copies + last:
                copy.wait()

    c = z.cols
    return call(
        kernel,
        "first_rest",
        (z.steps - z.lent_steps,),
        3,
        [ANY, ANY, ANY,
         pl.BlockSpec((z.group, z.rows, z.slots * z.rows), lambda s, *_: (s + z.lent_steps, 0, 0)),
         layer_of(c, 0), layer_of(c, 0), whole((2, c)), layer_of(c, 0), ANY, ANY, ANY],
        [ANY, ANY, z.block(lambda s: s + z.lent_steps)],
        [
            z.nodes(z.tiles),
            jax.ShapeDtypeStruct((2, z.tiles, z.rows, z.cols), BF16),
            z.nodes(z.tiles),
        ],
        [
            pltpu.VMEM((z.ext, z.rows, z.cols), BF16),
            pltpu.VMEM((rest, z.rows, z.cols), BF16),
            pltpu.SemaphoreType.DMA((3,)),
            pltpu.SemaphoreType.DMA((4 + z.lent,)),
        ],
        2e9,
        12 * 2**20,
        (meta, bound, live, f0, fw, fe, ap, w_self, w_nbr, bias, w_out, west, east, agg0),
        {13: 2},
    )


def spread(z, meta, start, stop, at, source, acc, shift, spare):
    def body(i, carry):
        for u in range(UNROLL):
            pair = start + i * UNROLL + u
            inside = pair < stop
            pair = jnp.minimum(pair, z.pairs - 1)
            target = jnp.where(inside, meta[2 * z.pairs + pair] - shift, spare)
            acc[target] += dot(at[pair], source[meta[z.pairs + pair]])
        return carry

    lax.fori_loop(0, (stop - start + UNROLL - 1) // UNROLL, body, 0)


def second(z, meta, counts, f1, fw, fe, ap, at, m1, w_self, w_nbr, bias, wt):
    def kernel(meta, counts, own, fw, fe, ap, at_hbm, m, ws, wn, bias, wnt, wot,
               agg, act, dpre, dagg, to_west, to_east, ext, at, kept, acc, sems, at_sem):
        s = pl.program_id(0)
        at_copy = pltpu.make_async_copy(at_hbm, at, at_sem)

        @pl.when(s == 0)
        def _():
            load_extended(z, own, fw, fe, ext, sems)
            at_copy.start()

        first = s * z.group
        aggregate(z, meta, first, ap, ext, agg)
        f = flat(z, ext[pl.ds(first, z.group)])
        pre = pre_activation(z, f, flat(z, agg[...]), ws, wn, bias, 1)
        sig = sigmoid(pre)
        act[...] = tiled(z, (pre * sig).astype(BF16))
        slope = sig * (1.0 + pre * (1.0 - sig))
        grad = (dot(flat(z, m[...]), wot[...]) * slope).astype(BF16)
        dpre[...] = tiled(z, grad)
        back = tiled(z, dot(grad, wnt[...]).astype(BF16))
        dagg[...] = back
        kept[pl.ds(first, z.group)] = back

        @pl.when(s == pl.num_programs(0) - 1)
        def _():
            at_copy.wait()
            acc[...] = jnp.zeros_like(acc)
            spread(z, meta, counts[0], z.pairs, at, kept, acc, z.tiles, z.lent)
            to_west[...] = acc[pl.ds(0, z.edge)].astype(BF16)
            to_east[...] = acc[pl.ds(z.edge, z.edge)].astype(BF16)

    c = z.cols
    edge_whole = whole((z.edge, z.rows, z.cols))
    return call(
        kernel,
        "second",
        (z.steps,),
        2,
        [ANY, ANY, ANY, pl.BlockSpec((z.group, z.rows, z.slots * z.rows), lambda s, *_: (s, 0, 0)),
         ANY, z.block(lambda s: s), layer_of(c, 1), layer_of(c, 1), whole((2, c)),
         turned(c, 1, 1), turned(c, 1, 2)],
        [z.block(lambda s: s)] * 4 + [edge_whole, edge_whole],
        [z.nodes(z.tiles)] * 4 + [z.nodes(z.edge)] * 2,
        [
            pltpu.VMEM((z.ext, z.rows, z.cols), BF16),
            pltpu.VMEM((z.pairs, z.rows, z.rows), BF16),
            pltpu.VMEM((z.tiles, z.rows, z.cols), BF16),
            pltpu.VMEM((z.lent + 1, z.rows, z.cols), F32),
            pltpu.SemaphoreType.DMA((3,)),
            pltpu.SemaphoreType.DMA,
        ],
        5e9,
        20 * 2**20,
        (meta, counts, f1, fw, fe, ap, at, m1, w_self, w_nbr, bias, wt, wt),
    )


def weight_grads(z, me, pieces, f, agg, act, m, dpre, name):
    c = z.cols
    piece = -(-(3 * c + 1) // (pieces * 16)) * 16
    height = piece * pieces

    def kernel(me, f, agg, act, m, dpre, *rest):
        outs, acc = rest[:-1], rest[-1]
        s = pl.program_id(0)

        @pl.when(s == 0)
        def _():
            acc[...] = jnp.zeros_like(acc)

        grad = flat(z, dpre[...])
        acc[pl.ds(0, c), :] += dot_rows(flat(z, f[...]), grad)
        acc[pl.ds(c, c), :] += dot_rows(flat(z, agg[...]), grad)
        acc[pl.ds(2 * c, c), :] += dot_rows(flat(z, act[...]), flat(z, m[...]))
        acc[pl.ds(3 * c, 1), :] += jnp.sum(grad.astype(F32), axis=0, keepdims=True)

        @pl.when(s == pl.num_programs(0) - 1)
        def _():
            for i in range(pieces):
                owner = lax.rem(me[0] + i, pieces)
                start = pl.multiple_of(owner * piece, 16)
                outs[i][...] = acc[pl.ds(start, piece), :].astype(BF16)

    return call(
        kernel,
        name,
        (z.steps,),
        1,
        [z.block(lambda s: s)] * 5,
        [whole((piece, c))] * pieces,
        [jax.ShapeDtypeStruct((piece, c), BF16)] * pieces,
        [pltpu.VMEM((height, c), F32)],
        4e9,
        10 * 2**20,
        (me, f, agg, act, m, dpre),
    )


def plane_pass(value, steps):
    count = lax.axis_size(PLANE)
    return lax.ppermute(value, PLANE, [(i, (i + steps) % count) for i in range(count)])


def added(parts):
    total = parts[0].astype(F32)
    for part in parts[1:]:
        total = total + part.astype(F32)
    return total.astype(BF16)


def summed_over_parts(pieces):
    count = len(pieces)
    share = added([pieces[0]] + [plane_pass(pieces[i], i) for i in range(1, count)])
    lines = lax.axis_size("feat")
    if lines & (lines - 1) == 0:
        step = 1
        while step < lines:
            other = lax.ppermute(share, "feat", [(i, i ^ step) for i in range(lines)])
            share = added([share, other])
            step *= 2
    else:
        share = lax.psum(share.astype(F32), "feat").astype(BF16)
    return [share] + [plane_pass(share, i) for i in range(1, count)]


def unpack(z, me, early, late):
    c = z.cols
    count = len(early)
    piece = early[0].shape[0]

    def kernel(me, *refs):
        ins, (g_self, g_nbr, g_bias, g_out, buf) = refs[: 2 * count], refs[2 * count :]
        for layer in range(2):
            for i in range(count):
                owner = lax.rem(me[0] + count - i, count)
                start = pl.multiple_of(owner * piece, 16)
                buf[pl.ds(start, piece), :] = ins[layer * count + i][...].astype(F32)
            g_self[layer] = buf[pl.ds(0, c), :]
            g_nbr[layer] = buf[pl.ds(c, c), :]
            g_out[layer] = buf[pl.ds(2 * c, c), :]
            g_bias[layer : layer + 1, :] = buf[pl.ds(3 * c, 1), :]

    square = jax.ShapeDtypeStruct((2, c, c), F32)
    return call(
        kernel,
        "unpack",
        (1,),
        1,
        [whole((piece, c))] * (2 * count),
        [whole((2, c, c)), whole((2, c, c)), whole((2, c)), whole((2, c, c))],
        [square, square, jax.ShapeDtypeStruct((2, c), F32), square],
        [pltpu.VMEM((piece * count, c), F32)],
        0,
        3 * 2**20,
        (me, *early, *late),
    )


def second_out(z, bound, live, f1, act, w_out, out):
    def kernel(bound, live, f, act, wo, _out, out, keep, sems):
        s = pl.program_id(0)
        first = s * z.group
        res = flat(z, f[...]).astype(F32) + dot(flat(z, act[...]), wo[...])
        keep[pl.ds(first, z.group)] = tiled(z, live_rows(z, res, first, live[0]).astype(BF16))

        @pl.when(s == pl.num_programs(0) - 1)
        def _():
            rest = z.tiles - z.lent
            copies = [
                pltpu.make_async_copy(
                    keep.at[i], out.at[1, bound[0, i // z.edge, i % z.edge]], sems.at[i]
                )
                for i in range(z.lent)
            ]
            copies.append(
                pltpu.make_async_copy(
                    keep.at[pl.ds(z.lent, rest)], out.at[1, pl.ds(z.lent, rest)], sems.at[z.lent]
                )
            )
            for copy in copies:
                copy.start()
            for copy in copies:
                copy.wait()

    return call(
        kernel,
        "second_out",
        (z.steps,),
        2,
        [z.block(lambda s: s), z.block(lambda s: s), layer_of(z.cols, 1), ANY],
        ANY,
        jax.ShapeDtypeStruct(out.shape, BF16),
        [pltpu.VMEM((z.tiles, z.rows, z.cols), BF16), pltpu.SemaphoreType.DMA((z.lent + 1,))],
        5e8,
        6 * 2**20,
        (bound, live, f1, act, w_out, out),
        {5: 0},
    )


def input_grad(z, layer, meta, counts, live, m, dpre, dagg, at, wt, grads):
    rest = z.tiles - z.lent
    fresh = grads is None

    def kernel(meta, counts, live, m, dpre, dagg_hbm, at_hbm, wst, *refs):
        if not fresh:
            refs = refs[1:]
        grads, part, masked, at, dagg, acc, keep, sems = refs
        s = pl.program_id(0)

        @pl.when(s == 0)
        def _():
            copies = [
                pltpu.make_async_copy(at_hbm, at, sems.at[0]),
                pltpu.make_async_copy(dagg_hbm, dagg, sems.at[1]),
            ]
            for copy in copies:
                copy.start()
            acc[...] = jnp.zeros_like(acc)
            for copy in copies:
                copy.wait()
            spread(z, meta, 0, counts[0], at, dagg, acc, 0, z.tiles)

        first = s * z.group
        res = flat(z, m[...]).astype(F32) + dot(flat(z, dpre[...]), wst[...])
        res = res + flat(z, acc[pl.ds(first, z.group)])

        @pl.when(s < z.lent_steps)
        def _():
            part[...] = tiled(z, res)

        @pl.when(s >= z.lent_steps)
        def _():
            keep[pl.ds(first - z.lent, z.group)] = tiled(z, res.astype(BF16))
            masked[...] = tiled(z, live_rows(z, res, first, live[0]).astype(BF16))

        @pl.when(s == pl.num_programs(0) - 1)
        def _():
            copy = pltpu.make_async_copy(keep, grads.at[layer, pl.ds(z.lent, rest)], sems.at[2])
            copy.start()
            copy.wait()

    args = [meta, counts, live, m, dpre, dagg, at, wt]
    in_specs = [z.block(lambda s: s), z.block(lambda s: s), ANY, ANY, turned(z.cols, layer, 0)]
    if not fresh:
        args.append(grads)
        in_specs.append(ANY)
    return call(
        kernel,
        "input_grad%d" % layer,
        (z.steps,),
        3,
        in_specs,
        [
            ANY,
            z.block(lambda s: jnp.minimum(s, z.lent_steps - 1)),
            z.block(lambda s: jnp.maximum(s, z.lent_steps)),
        ],
        [
            jax.ShapeDtypeStruct((2, z.tiles, z.rows, z.cols), BF16),
            z.nodes(z.lent, F32),
            z.nodes(z.tiles),
        ],
        [
            pltpu.VMEM((z.pairs, z.rows, z.rows), BF16),
            pltpu.VMEM((z.tiles, z.rows, z.cols), BF16),
            pltpu.VMEM((z.tiles + 1, z.rows, z.cols), F32),
            pltpu.VMEM((rest, z.rows, z.cols), BF16),
            pltpu.SemaphoreType.DMA((3,)),
        ],
        2e9,
        18 * 2**20,
        args,
        None if fresh else {8: 0},
    )


def early_rest(z, meta, counts, f0, agg0, m0, at, w_self, w_nbr, bias, wt):
    def kernel(meta, counts, f, agg, m, at_hbm, ws, wn, bias, wnt, wot,
               act, slope_out, dpre, dagg, part, at, kept, acc, sem):
        s = pl.program_id(0)
        copy = pltpu.make_async_copy(at_hbm, at, sem)

        @pl.when(s == 0)
        def _():
            copy.start()

        pre = pre_activation(z, flat(z, f[...]), flat(z, agg[...]), ws, wn, bias, 0)
        sig = sigmoid(pre)
        act[...] = tiled(z, (pre * sig).astype(BF16))
        slope = sig * (1.0 + pre * (1.0 - sig))

        @pl.when(s < z.lent_steps)
        def _():
            slope_out[...] = tiled(z, slope)

        @pl.when(s >= z.lent_steps)
        def _():
            grad = (dot(flat(z, m[...]), wot[...]) * slope).astype(BF16)
            dpre[...] = tiled(z, grad)
            back = tiled(z, dot(grad, wnt[...]).astype(BF16))
            dagg[...] = back
            kept[pl.ds(s * z.group, z.group)] = back

        @pl.when(s == pl.num_programs(0) - 1)
        def _():
            copy.wait()
            acc[...] = jnp.zeros_like(acc)
            spread(z, meta, counts[0], counts[0] + counts[1], at, kept, acc, z.tiles, z.lent)
            part[...] = acc[pl.ds(0, z.lent)]

    c = z.cols
    late = lambda s: jnp.maximum(s, z.lent_steps)
    return call(
        kernel,
        "early_rest",
        (z.steps,),
        2,
        [z.block(lambda s: s), z.block(lambda s: s), z.block(late), ANY,
         layer_of(c, 0), layer_of(c, 0), whole((2, c)), turned(c, 0, 1), turned(c, 0, 2)],
        [
            z.block(lambda s: s),
            z.block(lambda s: jnp.minimum(s, z.lent_steps - 1)),
            z.block(late),
            z.block(late),
            whole((z.lent, z.rows, z.cols)),
        ],
        [z.nodes(z.tiles), z.nodes(z.lent, F32), z.nodes(z.tiles), z.nodes(z.tiles), z.nodes(z.lent, F32)],
        [
            pltpu.VMEM((z.pairs, z.rows, z.rows), BF16),
            pltpu.VMEM((z.tiles, z.rows, z.cols), BF16),
            pltpu.VMEM((z.lent + 1, z.rows, z.cols), F32),
            pltpu.SemaphoreType.DMA,
        ],
        4e9,
        20 * 2**20,
        (meta, counts, f0, agg0, m0, at, w_self, w_nbr, bias, wt, wt),
    )


def early_lent(z, meta, counts, bound, part, fw, fe, slope, outer, at, wt, m0, dpre0, dagg0, grads):
    def kernel(meta, counts, bound, part, fw, fe, slope, outer, at_hbm, wnt, wot, _m, _d, _a, _g,
               m, dpre, dagg, grads, to_west, to_east, at, kept, acc, keep, sem, sems):
        s = pl.program_id(0)
        at_copy = pltpu.make_async_copy(at_hbm, at, sem)

        @pl.when(s == 0)
        def _():
            at_copy.start()

        got = jnp.where(s < z.edge_steps, fw[...], fe[...])
        g = flat(z, (part[...] + got.astype(F32)).astype(BF16))
        m[...] = tiled(z, g)
        keep[pl.ds(s * z.group, z.group)] = tiled(z, g)
        grad = (dot(g, wot[...]) * flat(z, slope[...])).astype(BF16)
        dpre[...] = tiled(z, grad)
        back = tiled(z, dot(grad, wnt[...]).astype(BF16))
        dagg[...] = back
        kept[pl.ds(s * z.group, z.group)] = back

        @pl.when(s == pl.num_programs(0) - 1)
        def _():
            copies = [
                pltpu.make_async_copy(
                    keep.at[i], grads.at[1, bound[0, i // z.edge, i % z.edge]], sems.at[i]
                )
                for i in range(z.lent)
            ]
            for copy in copies:
                copy.start()
            at_copy.wait()
            acc[pl.ds(0, z.lent)] = outer[...]
            spread(z, meta, counts[0] + counts[1], z.pairs, at, kept, acc, z.tiles, z.lent)
            to_west[...] = acc[pl.ds(0, z.edge)].astype(BF16)
            to_east[...] = acc[pl.ds(z.edge, z.edge)].astype(BF16)
            for copy in copies:
                copy.wait()

    c = z.cols
    edge_whole = whole((z.edge, z.rows, z.cols))
    return call(
        kernel,
        "early_lent",
        (z.lent_steps,),
        3,
        [
            z.block(lambda s: s),
            z.block(lambda s: jnp.minimum(s, z.edge_steps - 1)),
            z.block(lambda s: jnp.maximum(s - z.edge_steps, 0)),
            z.block(lambda s: s),
            whole((z.lent, z.rows, z.cols)),
            ANY,
            turned(c, 0, 1),
            turned(c, 0, 2),
            ANY,
            ANY,
            ANY,
            ANY,
        ],
        [z.block(lambda s: s)] * 3 + [ANY, edge_whole, edge_whole],
        [z.nodes(z.tiles)] * 3 + [jax.ShapeDtypeStruct(grads.shape, BF16)] + [z.nodes(z.edge)] * 2,
        [
            pltpu.VMEM((z.pairs, z.rows, z.rows), BF16),
            pltpu.VMEM((z.lent, z.rows, z.cols), BF16),
            pltpu.VMEM((z.lent + 1, z.rows, z.cols), F32),
            pltpu.VMEM((z.lent, z.rows, z.cols), BF16),
            pltpu.SemaphoreType.DMA,
            pltpu.SemaphoreType.DMA((z.lent,)),
        ],
        2e9,
        14 * 2**20,
        (meta, counts, bound, part, fw, fe, slope, outer, at, wt, wt, m0, dpre0, dagg0, grads),
        {11: 0, 12: 1, 13: 2, 14: 3},
    )


def finish(z, bound, part, fw, fe, grads):
    def kernel(bound, part, fw, fe, _g, grads, keep, sems):
        s = pl.program_id(0)
        got = jnp.where(s < z.edge_steps, fw[...], fe[...])
        keep[pl.ds(s * z.group, z.group)] = (part[...] + got.astype(F32)).astype(BF16)

        @pl.when(s == pl.num_programs(0) - 1)
        def _():
            copies = [
                pltpu.make_async_copy(
                    keep.at[i], grads.at[0, bound[0, i // z.edge, i % z.edge]], sems.at[i]
                )
                for i in range(z.lent)
            ]
            for copy in copies:
                copy.start()
            for copy in copies:
                copy.wait()

    return call(
        kernel,
        "finish",
        (z.lent_steps,),
        1,
        [
            z.block(lambda s: s),
            z.block(lambda s: jnp.minimum(s, z.edge_steps - 1)),
            z.block(lambda s: jnp.maximum(s - z.edge_steps, 0)),
            ANY,
        ],
        ANY,
        jax.ShapeDtypeStruct(grads.shape, BF16),
        [pltpu.VMEM((z.lent, z.rows, z.cols), BF16), pltpu.SemaphoreType.DMA((z.lent,))],
        0,
        4 * 2**20,
        (bound, part, fw, fe, grads),
        {4: 0},
    )


def per_device(
    node_in, out_cot, adjacency, tile_nbrs, bound_tiles, live_tiles, w_self, w_nbr, pre_bias, w_out
):
    z = Sizes(adjacency, node_in, bound_tiles)
    t, r, c = z.tiles, z.rows, z.cols
    features = node_in.reshape(t, r, c)
    cot = out_cot.reshape(t, r, c)
    pieces = lax.axis_size(PLANE)
    me = lax.axis_index(PLANE).astype(jnp.int32).reshape(1)

    west, east = lend(z, bound_tiles, features)
    from_west = passed_along(east, 1)
    from_east = passed_along(west, -1)
    f0, m1, ap, at, wt, meta, counts = arrange(
        z, bound_tiles, tile_nbrs, live_tiles, features, cot, adjacency, w_self, w_nbr, w_out
    )

    west, east, agg0 = first_lent(z, meta, f0, from_west, from_east, ap, w_self, w_nbr, pre_bias, w_out)
    next_west = passed_along(east, 1)
    next_east = passed_along(west, -1)
    f1, section_out, agg0 = first_rest(
        z, meta, bound_tiles, live_tiles, f0, from_west, from_east, ap, w_self, w_nbr, pre_bias, w_out,
        west, east, agg0,
    )

    agg1, act1, dpre1, dagg1, to_west, to_east = second(
        z, meta, counts, f1, next_west, next_east, ap, at, m1, w_self, w_nbr, pre_bias, wt
    )
    back_west = passed_along(to_east, 1)
    back_east = passed_along(to_west, -1)
    grads, part, m0 = input_grad(z, 1, meta, counts, live_tiles, m1, dpre1, dagg1, at, wt, None)
    late = summed_over_parts(weight_grads(z, me, pieces, f1, agg1, act1, m1, dpre1, "weight_grads1"))
    act0, slope, dpre0, dagg0, outer = early_rest(
        z, meta, counts, f0, agg0, m0, at, w_self, w_nbr, pre_bias, wt
    )
    section_out = second_out(z, bound_tiles, live_tiles, f1, act1, w_out, section_out)

    m0, dpre0, dagg0, grads, to_west, to_east = early_lent(
        z, meta, counts, bound_tiles, part, back_west, back_east, slope, outer, at, wt, m0, dpre0, dagg0, grads
    )
    back_west = passed_along(to_east, 1)
    back_east = passed_along(to_west, -1)
    early = summed_over_parts(weight_grads(z, me, pieces, f0, agg0, act0, m0, dpre0, "weight_grads0"))
    grads, part, _ = input_grad(z, 0, meta, counts, live_tiles, m0, dpre0, dagg0, at, wt, grads)
    grads = finish(z, bound_tiles, part, back_west, back_east, grads)

    grad_self, grad_nbr, grad_bias, grad_out = unpack(z, me, early, late)
    return (
        section_out.reshape(2, t * r, c),
        grads.reshape(2, t * r, c),
        grad_self,
        grad_nbr,
        grad_bias,
        grad_out,
    )


def solution(mesh):
    rows = P(AXES)
    in_specs = (rows, rows, rows, rows, rows, rows, P(), P(), P(), P())
    out_specs = (P(None, AXES), P(None, AXES), P(), P(), P(), P())
    return jax.shard_map(
        per_device, mesh=mesh, in_specs=in_specs, out_specs=out_specs, check_vma=False
    )
```

```python
import jax
import jax.numpy as jnp
from jax import lax
from jax.experimental import pallas as pl
from jax.experimental.pallas import tpu as pltpu
from jax.sharding import PartitionSpec as P

AXES = ("dom", "phase", "feat")
PLANE = ("dom", "phase")
BF16 = jnp.bfloat16
F32 = jnp.float32
UNROLL = 8
ANY = pl.BlockSpec(memory_space=pl.ANY)
SMEM = pl.BlockSpec(memory_space=pltpu.SMEM)
VMEM = pl.BlockSpec(memory_space=pltpu.VMEM)
MIB = 1024 * 1024


class Sizes:
    def __init__(self, adjacency, features, bound):
        self.tiles, self.slots, self.rows, _ = adjacency.shape
        self.cols = features.shape[-1]
        self.edge = bound.shape[-1]
        self.lent = 2 * self.edge
        self.rest = self.tiles - self.lent
        self.ext = self.tiles + self.lent
        self.pairs = self.tiles * self.slots
        self.group = next(g for g in (4, 2, 1) if self.edge % g == 0 and self.rest % g == 0)
        self.parts = ((0, 0, self.lent), (1, self.lent, self.rest))

    def nodes(self, count, dtype=BF16):
        return jax.ShapeDtypeStruct((count, self.rows, self.cols), dtype)

    def held(self, count, dtype=BF16):
        return pltpu.VMEM((count, self.rows, self.cols), dtype)

    def flat(self, value):
        return value.reshape(self.group * self.rows, self.cols)

    def tiled(self, value):
        return value.reshape(self.group, self.rows, self.cols)


def group_of(z, array, part, first):
    if isinstance(array, tuple):
        base = z.lent if part else 0
        return array[part].at[pl.ds(first - base, z.group)]
    return array.at[pl.ds(first, z.group)]


def each_group(z, body, parts=(0, 1), unroll=1):
    for part, base, count in z.parts:
        if part in parts:

            @pl.loop(0, count // z.group, unroll=unroll)
            def _(s):
                body(part, base + s * z.group)


def passed_along(value, steps):
    count = lax.axis_size(AXES)
    return lax.ppermute(value, AXES, [(i, (i + steps) % count) for i in range(count)])


def dot(a, b):
    return jnp.dot(a, b, preferred_element_type=F32)


def dot_rows(a, b):
    return lax.dot_general(a, b, (((0,), (0,)), ((), ())), preferred_element_type=F32)


def call(kernel, name, in_specs, out_specs, out_shape, scratch, limit, args, aliases=None):
    return pl.pallas_call(
        kernel,
        in_specs=in_specs,
        out_specs=out_specs,
        out_shape=out_shape,
        scratch_shapes=scratch,
        input_output_aliases=aliases or {},
        compiler_params=pltpu.CompilerParams(vmem_limit_bytes=limit * MIB),
        cost_estimate=pl.CostEstimate(flops=1000, bytes_accessed=1000, transcendentals=0),
        name=name,
    )(*args)


def sigmoid(v):
    return 0.5 * jnp.tanh(0.5 * v) + 0.5


def lend(z, bound, features):
    def kernel(bound, feats, west, east, sems):
        copies = []
        for i in range(z.edge):
            for side, target in ((0, west), (1, east)):
                copy = pltpu.make_async_copy(
                    feats.at[bound[0, side, i]], target.at[i], sems.at[side * z.edge + i]
                )
                copy.start()
                copies.append(copy)
        for copy in copies:
            copy.wait()

    return call(
        kernel,
        "lend",
        [SMEM, ANY],
        [VMEM, VMEM],
        [z.nodes(z.edge), z.nodes(z.edge)],
        [pltpu.SemaphoreType.DMA((z.lent,))],
        4,
        (bound, features),
    )


def arrange(z, bound, nbrs, live, features, cot, adjacency):
    s4 = z.slots

    def kernel(bound, nbrs, live, feats, cot, adj, f_lent, f_rest, m_lent, m_rest, ap, meta, counts, inverse, sems):
        copies = []

        def start(source, target):
            copy = pltpu.make_async_copy(source, target, sems.at[len(copies)])
            copy.start()
            copies.append(copy)

        tail = pl.ds(z.lent, z.rest)
        start(adj.at[tail], ap.at[tail])
        start(feats.at[tail], f_rest)
        start(cot.at[tail], m_rest)
        for i in range(z.lent):
            tile = bound[0, i // z.edge, i % z.edge]
            inverse[tile] = i
            start(adj.at[tile], ap.at[i])
            start(feats.at[tile], f_lent.at[i])
            start(cot.at[tile], m_lent.at[i])

        def kind_of(position, target):
            return jnp.where(target < z.tiles, 0, jnp.where(position < z.lent, 2, 1))

        def step(kind, sums):
            return tuple(total + jnp.where(kind == i, 1, 0) for i, total in enumerate(sums))

        def count(position, sums):
            clipped = jnp.minimum(position, z.lent - 1)
            tile = jnp.where(position < z.lent, bound[0, clipped // z.edge, clipped % z.edge], position)
            for k in range(s4):
                target = nbrs[tile, k]
                moved = jnp.where(target < z.lent, inverse[jnp.minimum(target, z.lent - 1)], target)
                meta[position * s4 + k] = moved
                sums = step(kind_of(position, moved), sums)
            return sums

        zero = jnp.int32(0)
        own, outer, lent = lax.fori_loop(0, z.tiles, count, (zero, zero, zero))
        counts[0] = own
        counts[1] = outer
        counts[2] = lent

        def put(position, sums):
            for k in range(s4):
                target = meta[position * s4 + k]
                kind = kind_of(position, target)
                slot = jnp.where(kind == 0, sums[0], jnp.where(kind == 1, sums[1], sums[2]))
                meta[z.pairs + slot] = position * s4 + k
                meta[2 * z.pairs + slot] = target
                sums = step(kind, sums)
            return sums

        lax.fori_loop(0, z.tiles, put, (zero, own, own + outer))
        for copy in copies:
            copy.wait()

        @pl.loop(0, z.rest)
        def _(i):
            @pl.when(z.lent + i >= live[0])
            def _():
                m_rest[i] = jnp.zeros((z.rows, z.cols), BF16)

    return call(
        kernel,
        "arrange",
        [SMEM, SMEM, SMEM, ANY, ANY, ANY],
        [VMEM] * 5 + [SMEM, SMEM],
        [
            z.nodes(z.lent),
            z.nodes(z.rest),
            z.nodes(z.lent),
            z.nodes(z.rest),
            jax.ShapeDtypeStruct(adjacency.shape, BF16),
            jax.ShapeDtypeStruct((3 * z.pairs,), jnp.int32),
            jax.ShapeDtypeStruct((8,), jnp.int32),
        ],
        [pltpu.SMEM((z.lent,), jnp.int32), pltpu.SemaphoreType.DMA((3 * z.lent + 3,))],
        12,
        (bound, nbrs, live, features, cot, adjacency),
    )


def turn(z, ap, w_self, w_nbr, w_out):
    def kernel(ap, ws, wn, wo, at, wt):
        for layer in range(2):
            wt[layer, 0] = ws[layer].T
            wt[layer, 1] = wn[layer].T
            wt[layer, 2] = wo[layer].T

        @pl.loop(0, z.tiles)
        def _(q):
            for k in range(z.slots):
                at[q * z.slots + k] = ap[q, k].T

    return call(
        kernel,
        "turn",
        [VMEM] * 4,
        [VMEM, VMEM],
        [
            jax.ShapeDtypeStruct((z.pairs, z.rows, z.rows), BF16),
            jax.ShapeDtypeStruct((2, 3, z.cols, z.cols), BF16),
        ],
        [],
        12,
        (ap, w_self, w_nbr, w_out),
    )


def fill_extended(z, own, fw, fe, ext):
    ext[pl.ds(0, z.lent)] = own[0][...]
    ext[pl.ds(z.lent, z.rest)] = own[1][...]
    ext[pl.ds(z.tiles, z.edge)] = fw[...]
    ext[pl.ds(z.tiles + z.edge, z.edge)] = fe[...]


def aggregate(z, meta, first, ap, ext):
    rows = []
    for g in range(z.group):
        base = (first + g) * z.slots
        picked = jnp.concatenate([ext[meta[base + k]] for k in range(z.slots)], axis=0)
        blocks = jnp.concatenate([ap[first + g, k] for k in range(z.slots)], axis=1)
        rows.append(dot(blocks, picked).astype(BF16))
    return jnp.concatenate(rows, axis=0)


def live_rows(z, value, first, live):
    parts = []
    for g in range(z.group):
        part = value[g * z.rows : (g + 1) * z.rows]
        parts.append(jnp.where(first + g < live, part, jnp.zeros_like(part)))
    return jnp.concatenate(parts, axis=0)


def first_lent(z, meta, f0, fw, fe, ap, w_self, w_nbr, bias, w_out):
    def kernel(meta, f_lent, f_rest, fw, fe, ap, ws, wn, bias, wo, west, east, agg, ext):
        fill_extended(z, (f_lent, f_rest), fw, fe, ext)

        def work(first, target, offset):
            here = pl.ds(first, z.group)
            f = z.flat(ext[here])
            aggs = aggregate(z, meta, first, ap, ext)
            agg[here] = z.tiled(aggs)
            pre = dot(f, ws[0]) + dot(aggs, wn[0]) + bias[0:1, :]
            act = (pre * sigmoid(pre)).astype(BF16)
            target[pl.ds(offset, z.group)] = z.tiled((f.astype(F32) + dot(act, wo[0])).astype(BF16))

        @pl.loop(0, z.edge // z.group)
        def _(s):
            work(s * z.group, west, s * z.group)
            work(z.edge + s * z.group, east, s * z.group)

    return call(
        kernel,
        "first_lent",
        [SMEM] + [VMEM] * 9,
        [VMEM] * 3,
        [z.nodes(z.edge), z.nodes(z.edge), z.nodes(z.lent)],
        [z.held(z.ext)],
        12,
        (meta, *f0, fw, fe, ap, w_self, w_nbr, bias, w_out),
    )


def first_rest(z, meta, bound, live, f0, fw, fe, ap, w_self, w_nbr, bias, w_out, west, east):
    def kernel(meta, bound, live, f_lent, f_rest, fw, fe, ap, ws, wn, bias, wo, west, east,
               f1_lent, f1_rest, out, agg, ext, sems):
        copies = []
        for i in range(z.edge):
            for side, source in ((0, west), (1, east)):
                copy = pltpu.make_async_copy(
                    source.at[i], out.at[0, bound[0, side, i]], sems.at[side * z.edge + i]
                )
                copy.start()
                copies.append(copy)
        fill_extended(z, (f_lent, f_rest), fw, fe, ext)
        f1_lent[pl.ds(0, z.edge)] = west[...]
        f1_lent[pl.ds(z.edge, z.edge)] = east[...]

        def work(part, first):
            f = z.flat(ext[pl.ds(first, z.group)])
            aggs = aggregate(z, meta, first, ap, ext)
            here = pl.ds(first - z.lent, z.group)
            agg[here] = z.tiled(aggs)
            pre = dot(f, ws[0]) + dot(aggs, wn[0]) + bias[0:1, :]
            act = (pre * sigmoid(pre)).astype(BF16)
            res = live_rows(z, f.astype(F32) + dot(act, wo[0]), first, live[0])
            f1_rest[here] = z.tiled(res.astype(BF16))

        each_group(z, work, (1,))
        copy = pltpu.make_async_copy(f1_rest, out.at[0, pl.ds(z.lent, z.rest)], sems.at[z.lent])
        copy.start()
        for other in copies:
            other.wait()
        copy.wait()

    return call(
        kernel,
        "first_rest",
        [SMEM] * 3 + [VMEM] * 11,
        [VMEM, VMEM, ANY, VMEM],
        [
            z.nodes(z.lent),
            z.nodes(z.rest),
            jax.ShapeDtypeStruct((2, z.tiles, z.rows, z.cols), BF16),
            z.nodes(z.rest),
        ],
        [z.held(z.ext), pltpu.SemaphoreType.DMA((1 + z.lent,))],
        12,
        (meta, bound, live, *f0, fw, fe, ap, w_self, w_nbr, bias, w_out, west, east),
    )


def second_own(z, f1, m1, w_self, bias, wt):
    def kernel(f_lent, f_rest, m_lent, m_rest, ws, bias, wt, own, hidden):
        def work(part, first):
            f = z.flat(group_of(z, (f_lent, f_rest), part, first)[...])
            m = z.flat(group_of(z, (m_lent, m_rest), part, first)[...])
            here = pl.ds(first, z.group)
            own[here] = z.tiled(dot(f, ws[1]) + bias[1:2, :])
            hidden[here] = z.tiled(dot(m, wt[1, 2]))

        each_group(z, work)

    return call(
        kernel,
        "second_own",
        [VMEM] * 7,
        [VMEM] * 2,
        [z.nodes(z.tiles, F32)] * 2,
        [],
        12,
        (*f1, *m1, w_self, bias, wt),
    )


def saved(z, f0, agg0, w_self, w_nbr, bias):
    def kernel(f_lent, f_rest, a_lent, a_rest, ws, wn, bias, act, slope):
        def work(part, first):
            f = z.flat(group_of(z, (f_lent, f_rest), part, first)[...])
            aggs = z.flat(group_of(z, (a_lent, a_rest), part, first)[...])
            pre = dot(f, ws[0]) + dot(aggs, wn[0]) + bias[0:1, :]
            sig = sigmoid(pre)
            here = pl.ds(first, z.group)
            act[here] = z.tiled((pre * sig).astype(BF16))
            slope[here] = z.tiled(sig * (1.0 + pre * (1.0 - sig)))

        each_group(z, work)

    return call(
        kernel,
        "saved",
        [VMEM] * 7,
        [VMEM] * 2,
        [z.nodes(z.tiles), z.nodes(z.tiles, F32)],
        [],
        12,
        (*f0, *agg0, w_self, w_nbr, bias),
    )


def spread(z, meta, start, stop, at, source, acc, shift, spare):
    def body(i, carry):
        for u in range(UNROLL):
            entry = start + i * UNROLL + u
            inside = entry < stop
            entry = jnp.minimum(entry, z.pairs - 1)
            target = jnp.where(inside, meta[2 * z.pairs + entry] - shift, spare)
            pair = meta[z.pairs + entry]
            acc[target] += dot(at[pair], source(pair // z.slots))
        return carry

    lax.fori_loop(0, (stop - start + UNROLL - 1) // UNROLL, body, 0)


def second(z, meta, counts, f1, fw, fe, ap, at, own, hidden, w_nbr, wt):
    def kernel(meta, counts, f_lent, f_rest, fw, fe, ap, at, own, hidden, wn, wt,
               agg, act, dpre, dagg, to_west, to_east, ext, acc):
        fill_extended(z, (f_lent, f_rest), fw, fe, ext)
        acc[...] = jnp.zeros_like(acc)

        def work(part, first):
            here = pl.ds(first, z.group)
            aggs = aggregate(z, meta, first, ap, ext)
            agg[here] = z.tiled(aggs)
            pre = z.flat(own[here]) + dot(aggs, wn[1])
            sig = sigmoid(pre)
            act[here] = z.tiled((pre * sig).astype(BF16))
            grad = (z.flat(hidden[here]) * (sig * (1.0 + pre * (1.0 - sig)))).astype(BF16)
            dpre[here] = z.tiled(grad)
            dagg[here] = z.tiled(dot(grad, wt[1, 1]).astype(BF16))

        each_group(z, work)
        spread(z, meta, counts[0], z.pairs, at, lambda q: dagg[q], acc, z.tiles, z.lent)
        to_west[...] = acc[pl.ds(0, z.edge)].astype(BF16)
        to_east[...] = acc[pl.ds(z.edge, z.edge)].astype(BF16)

    return call(
        kernel,
        "second",
        [SMEM] * 2 + [VMEM] * 10,
        [VMEM] * 6,
        [z.nodes(z.tiles)] * 4 + [z.nodes(z.edge)] * 2,
        [z.held(z.ext), z.held(z.lent + 1, F32)],
        16,
        (meta, counts, *f1, fw, fe, ap, at, own, hidden, w_nbr, wt),
    )


def weight_grads(z, me, pieces, f, agg, act, m, dpre, name):
    c = z.cols
    piece = -(-(3 * c + 1) // (pieces * 16)) * 16
    height = piece * pieces
    arrays = (f, agg, act, m, dpre)
    flat_args = [x for a in arrays for x in (a if isinstance(a, tuple) else (a,))]

    def kernel(me, *refs):
        refs = list(refs)
        f, agg, act, m, dpre = [
            (refs.pop(0), refs.pop(0)) if isinstance(a, tuple) else refs.pop(0) for a in arrays
        ]
        outs, acc = refs[:-1], refs[-1]
        acc[...] = jnp.zeros_like(acc)

        def work(part, first):
            def rows(array):
                return z.flat(group_of(z, array, part, first)[...])

            grad = rows(dpre)
            acc[pl.ds(0, c), :] += dot_rows(rows(f), grad)
            acc[pl.ds(c, c), :] += dot_rows(rows(agg), grad)
            acc[pl.ds(2 * c, c), :] += dot_rows(rows(act), rows(m))
            acc[pl.ds(3 * c, 1), :] += jnp.sum(grad.astype(F32), axis=0, keepdims=True)

        each_group(z, work)
        for i in range(pieces):
            owner = lax.rem(me[0] + i, pieces)
            outs[i][...] = acc[pl.ds(pl.multiple_of(owner * piece, 16), piece), :]

    return call(
        kernel,
        name,
        [SMEM] + [VMEM] * len(flat_args),
        [VMEM] * pieces,
        [jax.ShapeDtypeStruct((piece, c), F32)] * pieces,
        [pltpu.VMEM((height, c), F32)],
        12,
        (me, *flat_args),
    )


def plane_pass(value, steps):
    count = lax.axis_size(PLANE)
    return lax.ppermute(value, PLANE, [(i, (i + steps) % count) for i in range(count)])


def added(parts):
    total = parts[0].astype(F32)
    for part in parts[1:]:
        total = total + part.astype(F32)
    return total.astype(BF16)


def summed_over_parts(pieces):
    count = len(pieces)
    share = added([pieces[0]] + [plane_pass(pieces[i], i) for i in range(1, count)])
    lines = lax.axis_size("feat")
    if lines & (lines - 1) == 0:
        step = 1
        while step < lines:
            other = lax.ppermute(share, "feat", [(i, i ^ step) for i in range(lines)])
            share = added([share, other])
            step *= 2
    else:
        share = lax.psum(share.astype(F32), "feat").astype(BF16)
    return lax.all_gather(share, PLANE, axis=0, tiled=True)


def unpack(z, early, late):
    c = z.cols

    def kernel(early, late, g_self, g_nbr, g_bias, g_out):
        for layer, packed in ((0, early), (1, late)):
            g_self[layer] = packed[pl.ds(0, c), :].astype(F32)
            g_nbr[layer] = packed[pl.ds(c, c), :].astype(F32)
            g_out[layer] = packed[pl.ds(2 * c, c), :].astype(F32)
            g_bias[layer : layer + 1, :] = packed[pl.ds(3 * c, 16), :].astype(F32)[0:1]

    square = jax.ShapeDtypeStruct((2, c, c), F32)
    return call(
        kernel,
        "unpack",
        [VMEM] * 2,
        [VMEM] * 4,
        [square, square, jax.ShapeDtypeStruct((2, c), F32), square],
        [],
        12,
        (early, late),
    )


def second_out(z, bound, live, f1, act, w_out, out):
    def kernel(bound, live, f_lent, f_rest, act, wo, _out, out, keep, sems):
        copies = []

        def work(part, first):
            f = z.flat(group_of(z, (f_lent, f_rest), part, first)[...])
            res = f.astype(F32) + dot(z.flat(act[pl.ds(first, z.group)]), wo[1])
            keep[pl.ds(first, z.group)] = z.tiled(live_rows(z, res, first, live[0]).astype(BF16))

        each_group(z, work, (0,))
        for i in range(z.lent):
            copy = pltpu.make_async_copy(
                keep.at[i], out.at[1, bound[0, i // z.edge, i % z.edge]], sems.at[i]
            )
            copy.start()
            copies.append(copy)
        each_group(z, work, (1,))
        tail = pl.ds(z.lent, z.rest)
        copy = pltpu.make_async_copy(keep.at[tail], out.at[1, tail], sems.at[z.lent])
        copy.start()
        copies.append(copy)
        for copy in copies:
            copy.wait()

    return call(
        kernel,
        "second_out",
        [SMEM] * 2 + [VMEM] * 4 + [ANY],
        ANY,
        jax.ShapeDtypeStruct(out.shape, BF16),
        [z.held(z.tiles), pltpu.SemaphoreType.DMA((z.lent + 1,))],
        12,
        (bound, live, *f1, act, w_out, out),
        {6: 0},
    )


def input_grad(z, layer, meta, counts, live, m, dpre, dagg, at, wt, grads):
    fresh = grads is None
    arrays = (m, dpre, dagg)
    flat_args = [x for a in arrays for x in (a if isinstance(a, tuple) else (a,))]

    def kernel(meta, counts, live, *refs):
        refs = list(refs)
        m, dpre, dagg = [
            (refs.pop(0), refs.pop(0)) if isinstance(a, tuple) else refs.pop(0) for a in arrays
        ]
        at, wt = refs[:2]
        grads, part_out, masked, acc, keep, sem = refs[2 if fresh else 3 :]

        def direct(part, first):
            mine = z.flat(group_of(z, m, part, first)[...]).astype(F32)
            res = mine + dot(z.flat(group_of(z, dpre, part, first)[...]), wt[layer, 0])
            acc[pl.ds(first, z.group)] = z.tiled(res)

        each_group(z, direct)

        def source(q):
            if not isinstance(dagg, tuple):
                return dagg[q]
            lent = dagg[0][jnp.minimum(q, z.lent - 1)]
            rest = dagg[1][jnp.maximum(q - z.lent, 0)]
            return jnp.where(q < z.lent, lent, rest)

        spread(z, meta, 0, counts[0], at, source, acc, 0, z.tiles)
        tail = pl.ds(z.lent, z.rest)
        keep[...] = acc[tail].astype(BF16)
        copy = pltpu.make_async_copy(keep, grads.at[layer, tail], sem)
        copy.start()
        part_out[...] = acc[pl.ds(0, z.lent)]

        @pl.loop(0, z.rest)
        def _(i):
            value = keep[i]
            masked[i] = jnp.where(z.lent + i < live[0], value, jnp.zeros_like(value))

        copy.wait()

    args = [meta, counts, live, *flat_args, at, wt]
    if not fresh:
        args.append(grads)
    return call(
        kernel,
        "input_grad%d" % layer,
        [SMEM] * 3 + [VMEM] * (len(flat_args) + 2) + ([] if fresh else [ANY]),
        [ANY, VMEM, VMEM],
        [
            jax.ShapeDtypeStruct((2, z.tiles, z.rows, z.cols), BF16),
            z.nodes(z.lent, F32),
            z.nodes(z.rest),
        ],
        [z.held(z.tiles + 1, F32), z.held(z.rest), pltpu.SemaphoreType.DMA],
        16,
        args,
        None if fresh else {len(args) - 1: 0},
    )


def early_rest(z, meta, counts, m0, slope, at, wt):
    def kernel(meta, counts, m, slope, at, wt, dpre, dagg, outer, acc):
        def work(part, first):
            here = pl.ds(first - z.lent, z.group)
            grad = dot(z.flat(m[here]), wt[0, 2]) * z.flat(slope[pl.ds(first, z.group)])
            grad = grad.astype(BF16)
            dpre[here] = z.tiled(grad)
            dagg[here] = z.tiled(dot(grad, wt[0, 1]).astype(BF16))

        each_group(z, work, (1,))
        acc[...] = jnp.zeros_like(acc)

        def source(q):
            return dagg[jnp.maximum(q - z.lent, 0)]

        spread(z, meta, counts[0], counts[0] + counts[1], at, source, acc, z.tiles, z.lent)
        outer[...] = acc[pl.ds(0, z.lent)]

    return call(
        kernel,
        "early_rest",
        [SMEM] * 2 + [VMEM] * 4,
        [VMEM] * 3,
        [z.nodes(z.rest), z.nodes(z.rest), z.nodes(z.lent, F32)],
        [z.held(z.lent + 1, F32)],
        12,
        (meta, counts, m0, slope, at, wt),
    )


def early_lent(z, meta, counts, bound, part, fw, fe, slope, outer, at, wt, grads):
    def kernel(meta, counts, bound, part, fw, fe, slope, outer, at, wt, _g,
               m, dpre, dagg, grads, to_west, to_east, acc, sems):
        def work(first, got):
            here = pl.ds(first, z.group)
            g = z.flat((part[here] + got.astype(F32)).astype(BF16))
            m[here] = z.tiled(g)
            grad = (dot(g, wt[0, 2]) * z.flat(slope[here])).astype(BF16)
            dpre[here] = z.tiled(grad)
            dagg[here] = z.tiled(dot(grad, wt[0, 1]).astype(BF16))

        @pl.loop(0, z.edge // z.group)
        def _(s):
            here = pl.ds(s * z.group, z.group)
            work(s * z.group, fw[here])
            work(z.edge + s * z.group, fe[here])

        copies = [
            pltpu.make_async_copy(m.at[i], grads.at[1, bound[0, i // z.edge, i % z.edge]], sems.at[i])
            for i in range(z.lent)
        ]
        for copy in copies:
            copy.start()
        acc[pl.ds(0, z.lent)] = outer[...]
        acc[z.lent] = jnp.zeros((z.rows, z.cols), F32)

        def source(q):
            return dagg[jnp.minimum(q, z.lent - 1)]

        spread(z, meta, counts[0] + counts[1], z.pairs, at, source, acc, z.tiles, z.lent)
        to_west[...] = acc[pl.ds(0, z.edge)].astype(BF16)
        to_east[...] = acc[pl.ds(z.edge, z.edge)].astype(BF16)
        for copy in copies:
            copy.wait()

    return call(
        kernel,
        "early_lent",
        [SMEM] * 3 + [VMEM] * 7 + [ANY],
        [VMEM] * 3 + [ANY] + [VMEM] * 2,
        [z.nodes(z.lent)] * 3 + [jax.ShapeDtypeStruct(grads.shape, BF16)] + [z.nodes(z.edge)] * 2,
        [z.held(z.lent + 1, F32), pltpu.SemaphoreType.DMA((z.lent,))],
        12,
        (meta, counts, bound, part, fw, fe, slope, outer, at, wt, grads),
        {10: 3},
    )


def finish(z, bound, part, fw, fe, grads):
    def kernel(bound, part, fw, fe, _g, grads, keep, sems):
        copies = []
        for i in range(z.lent):
            got = fw[i] if i < z.edge else fe[i - z.edge]
            keep[i] = (part[i] + got.astype(F32)).astype(BF16)
            copy = pltpu.make_async_copy(
                keep.at[i], grads.at[0, bound[0, i // z.edge, i % z.edge]], sems.at[i]
            )
            copy.start()
            copies.append(copy)
        for copy in copies:
            copy.wait()

    return call(
        kernel,
        "finish",
        [SMEM] + [VMEM] * 3 + [ANY],
        ANY,
        jax.ShapeDtypeStruct(grads.shape, BF16),
        [z.held(z.lent), pltpu.SemaphoreType.DMA((z.lent,))],
        12,
        (bound, part, fw, fe, grads),
        {4: 0},
    )


def per_device(
    node_in, out_cot, adjacency, tile_nbrs, bound_tiles, live_tiles, w_self, w_nbr, pre_bias, w_out
):
    z = Sizes(adjacency, node_in, bound_tiles)
    t, r, c = z.tiles, z.rows, z.cols
    features = node_in.reshape(t, r, c)
    cot = out_cot.reshape(t, r, c)
    pieces = lax.axis_size(PLANE)
    me = lax.axis_index(PLANE).astype(jnp.int32).reshape(1)

    west, east = lend(z, bound_tiles, features)
    from_west = passed_along(east, 1)
    from_east = passed_along(west, -1)
    *nodes, ap, meta, counts = arrange(z, bound_tiles, tile_nbrs, live_tiles, features, cot, adjacency)
    f0, m1 = tuple(nodes[:2]), tuple(nodes[2:])
    at, wt = turn(z, ap, w_self, w_nbr, w_out)

    west, east, agg_lent = first_lent(z, meta, f0, from_west, from_east, ap, w_self, w_nbr, pre_bias, w_out)
    next_west = passed_along(east, 1)
    next_east = passed_along(west, -1)
    f1_lent, f1_rest, section_out, agg_rest = first_rest(
        z, meta, bound_tiles, live_tiles, f0, from_west, from_east, ap, w_self, w_nbr, pre_bias, w_out,
        west, east,
    )
    f1, agg0 = (f1_lent, f1_rest), (agg_lent, agg_rest)
    own, hidden = second_own(z, f1, m1, w_self, pre_bias, wt)
    act0, slope = saved(z, f0, agg0, w_self, w_nbr, pre_bias)

    agg1, act1, dpre1, dagg1, to_west, to_east = second(
        z, meta, counts, f1, next_west, next_east, ap, at, own, hidden, w_nbr, wt
    )
    back_west = passed_along(to_east, 1)
    back_east = passed_along(to_west, -1)
    grads, part, m0_rest = input_grad(z, 1, meta, counts, live_tiles, m1, dpre1, dagg1, at, wt, None)
    dpre_rest, dagg_rest, outer = early_rest(z, meta, counts, m0_rest, slope, at, wt)
    late = summed_over_parts(weight_grads(z, me, pieces, f1, agg1, act1, m1, dpre1, "weight_grads1"))
    section_out = second_out(z, bound_tiles, live_tiles, f1, act1, w_out, section_out)

    m0_lent, dpre_lent, dagg_lent, grads, to_west, to_east = early_lent(
        z, meta, counts, bound_tiles, part, back_west, back_east, slope, outer, at, wt, grads
    )
    back_west = passed_along(to_east, 1)
    back_east = passed_along(to_west, -1)
    m0, dpre0, dagg0 = (m0_lent, m0_rest), (dpre_lent, dpre_rest), (dagg_lent, dagg_rest)
    early = summed_over_parts(weight_grads(z, me, pieces, f0, agg0, act0, m0, dpre0, "weight_grads0"))
    grads, part, _ = input_grad(z, 0, meta, counts, live_tiles, m0, dpre0, dagg0, at, wt, grads)
    grads = finish(z, bound_tiles, part, back_west, back_east, grads)

    grad_self, grad_nbr, grad_bias, grad_out = unpack(z, early, late)
    return (
        section_out.reshape(2, t * r, c),
        grads.reshape(2, t * r, c),
        grad_self,
        grad_nbr,
        grad_bias,
        grad_out,
    )


def solution(mesh):
    rows = P(AXES)
    in_specs = (rows, rows, rows, rows, rows, rows, P(), P(), P(), P())
    out_specs = (P(None, AXES), P(None, AXES), P(), P(), P(), P())
    return jax.shard_map(
        per_device, mesh=mesh, in_specs=in_specs, out_specs=out_specs, check_vma=False
    )
```

```python
import jax
import jax.numpy as jnp
from jax import lax
from jax.experimental import pallas as pl
from jax.experimental.pallas import tpu as pltpu
from jax.sharding import PartitionSpec as P

AXES = ("dom", "phase", "feat")
PLANE = ("dom", "phase")
BF16 = jnp.bfloat16
F32 = jnp.float32
UNROLL = 8
ANY = pl.BlockSpec(memory_space=pltpu.HBM)
SMEM = pl.BlockSpec(memory_space=pltpu.SMEM)
VMEM = pl.BlockSpec(memory_space=pltpu.VMEM)
MIB = 1024 * 1024


class Sizes:
    def __init__(self, adjacency, features, bound):
        self.tiles, self.slots, self.rows, _ = adjacency.shape
        self.cols = features.shape[-1]
        self.edge = bound.shape[-1]
        self.lent = 2 * self.edge
        self.rest = self.tiles - self.lent
        self.ext = self.tiles + self.lent
        self.pairs = self.tiles * self.slots
        self.group = next(g for g in (4, 2, 1) if self.edge % g == 0 and self.rest % g == 0)
        self.parts = ((0, 0, self.lent), (1, self.lent, self.rest))

    def nodes(self, count, dtype=BF16):
        return jax.ShapeDtypeStruct((count, self.rows, self.cols), dtype)

    def held(self, count, dtype=BF16):
        return pltpu.VMEM((count, self.rows, self.cols), dtype)

    def flat(self, value):
        return value.reshape(self.group * self.rows, self.cols)

    def tiled(self, value):
        return value.reshape(self.group, self.rows, self.cols)


def group_of(z, array, part, first):
    if isinstance(array, tuple):
        base = z.lent if part else 0
        return array[part].at[pl.ds(first - base, z.group)]
    return array.at[pl.ds(first, z.group)]


def each_group(z, body, parts=(0, 1), unroll=1):
    for part, base, count in z.parts:
        if part in parts:

            @pl.loop(0, count // z.group, unroll=unroll)
            def _(s):
                body(part, base + s * z.group)


def passed_along(value, steps):
    count = lax.axis_size(AXES)
    return lax.ppermute(value, AXES, [(i, (i + steps) % count) for i in range(count)])


def dot(a, b):
    return jnp.dot(a, b, preferred_element_type=F32)


def dot_rows(a, b):
    return lax.dot_general(a, b, (((0,), (0,)), ((), ())), preferred_element_type=F32)


def call(kernel, name, in_specs, out_specs, out_shape, scratch, limit, args, aliases=None):
    return pl.pallas_call(
        kernel,
        in_specs=in_specs,
        out_specs=out_specs,
        out_shape=out_shape,
        scratch_shapes=scratch,
        input_output_aliases=aliases or {},
        compiler_params=pltpu.CompilerParams(vmem_limit_bytes=limit * MIB),
        cost_estimate=pl.CostEstimate(flops=1000, bytes_accessed=1000, transcendentals=0),
        name=name,
    )(*args)


def sigmoid(v):
    return 0.5 * jnp.tanh(0.5 * v) + 0.5


def lend(z, bound, features):
    def kernel(bound, feats, west, east, sems):
        copies = []
        for i in range(z.edge):
            for side, target in ((0, west), (1, east)):
                copy = pltpu.make_async_copy(
                    feats.at[bound[0, side, i]], target.at[i], sems.at[side * z.edge + i]
                )
                copy.start()
                copies.append(copy)
        for copy in copies:
            copy.wait()

    return call(
        kernel,
        "lend",
        [SMEM, ANY],
        [VMEM, VMEM],
        [z.nodes(z.edge), z.nodes(z.edge)],
        [pltpu.SemaphoreType.DMA((z.lent,))],
        2,
        (bound, features),
    )


def arrange(z, bound, nbrs, live, features, cot, adjacency):
    s4 = z.slots

    def kernel(bound, nbrs, live, feats, cot, adj, f_lent, f_rest, m_lent, m_rest, ap, meta, counts, inverse, sems):
        copies = []

        def start(source, target):
            copy = pltpu.make_async_copy(source, target, sems.at[len(copies)])
            copy.start()
            copies.append(copy)

        tail = pl.ds(z.lent, z.rest)
        start(adj.at[tail], ap.at[tail])
        start(feats.at[tail], f_rest)
        start(cot.at[tail], m_rest)
        for i in range(z.lent):
            tile = bound[0, i // z.edge, i % z.edge]
            inverse[tile] = i
            start(adj.at[tile], ap.at[i])
            start(feats.at[tile], f_lent.at[i])
            start(cot.at[tile], m_lent.at[i])

        def kind_of(position, target):
            return jnp.where(target < z.tiles, 0, jnp.where(position < z.lent, 2, 1))

        def step(kind, sums):
            return tuple(total + jnp.where(kind == i, 1, 0) for i, total in enumerate(sums))

        def count(position, sums):
            clipped = jnp.minimum(position, z.lent - 1)
            tile = jnp.where(position < z.lent, bound[0, clipped // z.edge, clipped % z.edge], position)
            for k in range(s4):
                target = nbrs[tile, k]
                moved = jnp.where(target < z.lent, inverse[jnp.minimum(target, z.lent - 1)], target)
                meta[position * s4 + k] = moved
                sums = step(kind_of(position, moved), sums)
            return sums

        zero = jnp.int32(0)
        own, outer, lent = lax.fori_loop(0, z.tiles, count, (zero, zero, zero))
        counts[0] = own
        counts[1] = outer
        counts[2] = lent

        def put(position, sums):
            for k in range(s4):
                target = meta[position * s4 + k]
                kind = kind_of(position, target)
                slot = jnp.where(kind == 0, sums[0], jnp.where(kind == 1, sums[1], sums[2]))
                meta[z.pairs + slot] = position * s4 + k
                meta[2 * z.pairs + slot] = target
                sums = step(kind, sums)
            return sums

        lax.fori_loop(0, z.tiles, put, (zero, own, own + outer))
        for copy in copies:
            copy.wait()

        @pl.loop(0, z.rest)
        def _(i):
            @pl.when(z.lent + i >= live[0])
            def _():
                m_rest[i] = jnp.zeros((z.rows, z.cols), BF16)

    return call(
        kernel,
        "arrange",
        [SMEM, SMEM, SMEM, ANY, ANY, ANY],
        [VMEM] * 5 + [SMEM, SMEM],
        [
            z.nodes(z.lent),
            z.nodes(z.rest),
            z.nodes(z.lent),
            z.nodes(z.rest),
            jax.ShapeDtypeStruct(adjacency.shape, BF16),
            jax.ShapeDtypeStruct((3 * z.pairs,), jnp.int32),
            jax.ShapeDtypeStruct((8,), jnp.int32),
        ],
        [pltpu.SMEM((z.lent,), jnp.int32), pltpu.SemaphoreType.DMA((3 * z.lent + 3,))],
        6,
        (bound, nbrs, live, features, cot, adjacency),
    )


def turn(z, ap, w_self, w_nbr, w_out):
    def kernel(ap, ws, wn, wo, at, wt):
        for layer in range(2):
            wt[layer, 0] = ws[layer].T
            wt[layer, 1] = wn[layer].T
            wt[layer, 2] = wo[layer].T

        @pl.loop(0, z.tiles)
        def _(q):
            for k in range(z.slots):
                at[q * z.slots + k] = ap[q, k].T

    return call(
        kernel,
        "turn",
        [VMEM] * 4,
        [VMEM, VMEM],
        [
            jax.ShapeDtypeStruct((z.pairs, z.rows, z.rows), BF16),
            jax.ShapeDtypeStruct((2, 3, z.cols, z.cols), BF16),
        ],
        [],
        6,
        (ap, w_self, w_nbr, w_out),
    )


def fill_extended(z, own, fw, fe, ext):
    ext[pl.ds(0, z.lent)] = own[0][...]
    ext[pl.ds(z.lent, z.rest)] = own[1][...]
    ext[pl.ds(z.tiles, z.edge)] = fw[...]
    ext[pl.ds(z.tiles + z.edge, z.edge)] = fe[...]


def aggregate(z, meta, first, ap, ext):
    rows = []
    for g in range(z.group):
        base = (first + g) * z.slots
        picked = jnp.concatenate([ext[meta[base + k]] for k in range(z.slots)], axis=0)
        blocks = jnp.concatenate([ap[first + g, k] for k in range(z.slots)], axis=1)
        rows.append(dot(blocks, picked).astype(BF16))
    return jnp.concatenate(rows, axis=0)


def live_rows(z, value, first, live):
    parts = []
    for g in range(z.group):
        part = value[g * z.rows : (g + 1) * z.rows]
        parts.append(jnp.where(first + g < live, part, jnp.zeros_like(part)))
    return jnp.concatenate(parts, axis=0)


def first_lent(z, meta, f0, fw, fe, ap, w_self, w_nbr, bias, w_out):
    def kernel(meta, f_lent, f_rest, fw, fe, ap, ws, wn, bias, wo, west, east, agg, ext):
        fill_extended(z, (f_lent, f_rest), fw, fe, ext)

        def work(first, target, offset):
            here = pl.ds(first, z.group)
            f = z.flat(ext[here])
            aggs = aggregate(z, meta, first, ap, ext)
            agg[here] = z.tiled(aggs)
            pre = dot(f, ws[0]) + dot(aggs, wn[0]) + bias[0:1, :]
            act = (pre * sigmoid(pre)).astype(BF16)
            target[pl.ds(offset, z.group)] = z.tiled((f.astype(F32) + dot(act, wo[0])).astype(BF16))

        @pl.loop(0, z.edge // z.group)
        def _(s):
            work(s * z.group, west, s * z.group)
            work(z.edge + s * z.group, east, s * z.group)

    return call(
        kernel,
        "first_lent",
        [SMEM] + [VMEM] * 9,
        [VMEM] * 3,
        [z.nodes(z.edge), z.nodes(z.edge), z.nodes(z.lent)],
        [z.held(z.ext)],
        6,
        (meta, *f0, fw, fe, ap, w_self, w_nbr, bias, w_out),
    )


def first_rest(z, meta, bound, live, f0, fw, fe, ap, w_self, w_nbr, bias, w_out, west, east):
    def kernel(meta, bound, live, f_lent, f_rest, fw, fe, ap, ws, wn, bias, wo, west, east,
               f1_lent, f1_rest, out, agg, ext, sems):
        copies = []
        for i in range(z.edge):
            for side, source in ((0, west), (1, east)):
                copy = pltpu.make_async_copy(
                    source.at[i], out.at[0, bound[0, side, i]], sems.at[side * z.edge + i]
                )
                copy.start()
                copies.append(copy)
        fill_extended(z, (f_lent, f_rest), fw, fe, ext)
        f1_lent[pl.ds(0, z.edge)] = west[...]
        f1_lent[pl.ds(z.edge, z.edge)] = east[...]

        def work(part, first):
            f = z.flat(ext[pl.ds(first, z.group)])
            aggs = aggregate(z, meta, first, ap, ext)
            here = pl.ds(first - z.lent, z.group)
            agg[here] = z.tiled(aggs)
            pre = dot(f, ws[0]) + dot(aggs, wn[0]) + bias[0:1, :]
            act = (pre * sigmoid(pre)).astype(BF16)
            res = live_rows(z, f.astype(F32) + dot(act, wo[0]), first, live[0])
            f1_rest[here] = z.tiled(res.astype(BF16))

        each_group(z, work, (1,))
        copy = pltpu.make_async_copy(f1_rest, out.at[0, pl.ds(z.lent, z.rest)], sems.at[z.lent])
        copy.start()
        for other in copies:
            other.wait()
        copy.wait()

    return call(
        kernel,
        "first_rest",
        [SMEM] * 3 + [VMEM] * 11,
        [VMEM, VMEM, ANY, VMEM],
        [
            z.nodes(z.lent),
            z.nodes(z.rest),
            jax.ShapeDtypeStruct((2, z.tiles, z.rows, z.cols), BF16),
            z.nodes(z.rest),
        ],
        [z.held(z.ext), pltpu.SemaphoreType.DMA((1 + z.lent,))],
        6,
        (meta, bound, live, *f0, fw, fe, ap, w_self, w_nbr, bias, w_out, west, east),
    )


def second_own(z, f1, m1, w_self, bias, wt):
    def kernel(f_lent, f_rest, m_lent, m_rest, ws, bias, wt, own, hidden):
        def work(part, first):
            f = z.flat(group_of(z, (f_lent, f_rest), part, first)[...])
            m = z.flat(group_of(z, (m_lent, m_rest), part, first)[...])
            here = pl.ds(first, z.group)
            own[here] = z.tiled(dot(f, ws[1]) + bias[1:2, :])
            hidden[here] = z.tiled(dot(m, wt[1, 2]))

        each_group(z, work)

    return call(
        kernel,
        "second_own",
        [VMEM] * 7,
        [VMEM] * 2,
        [z.nodes(z.tiles, F32)] * 2,
        [],
        6,
        (*f1, *m1, w_self, bias, wt),
    )


def saved(z, f0, agg0, w_self, w_nbr, bias):
    def kernel(f_lent, f_rest, a_lent, a_rest, ws, wn, bias, act, slope):
        def work(part, first):
            f = z.flat(group_of(z, (f_lent, f_rest), part, first)[...])
            aggs = z.flat(group_of(z, (a_lent, a_rest), part, first)[...])
            pre = dot(f, ws[0]) + dot(aggs, wn[0]) + bias[0:1, :]
            sig = sigmoid(pre)
            here = pl.ds(first, z.group)
            act[here] = z.tiled((pre * sig).astype(BF16))
            slope[here] = z.tiled(sig * (1.0 + pre * (1.0 - sig)))

        each_group(z, work)

    return call(
        kernel,
        "saved",
        [VMEM] * 7,
        [VMEM] * 2,
        [z.nodes(z.tiles), z.nodes(z.tiles, F32)],
        [],
        6,
        (*f0, *agg0, w_self, w_nbr, bias),
    )


def spread(z, meta, start, stop, at, source, acc, shift, spare):
    def body(i, carry):
        for u in range(UNROLL):
            entry = start + i * UNROLL + u
            inside = entry < stop
            entry = jnp.minimum(entry, z.pairs - 1)
            target = jnp.where(inside, meta[2 * z.pairs + entry] - shift, spare)
            pair = meta[z.pairs + entry]
            acc[target] += dot(at[pair], source(pair // z.slots))
        return carry

    lax.fori_loop(0, (stop - start + UNROLL - 1) // UNROLL, body, 0)


def second(z, meta, counts, f1, fw, fe, ap, at, own, hidden, w_nbr, wt):
    def kernel(meta, counts, f_lent, f_rest, fw, fe, ap, at, own, hidden, wn, wt,
               agg, act, dpre, dagg, to_west, to_east, ext, acc):
        fill_extended(z, (f_lent, f_rest), fw, fe, ext)
        acc[...] = jnp.zeros_like(acc)

        def work(part, first):
            here = pl.ds(first, z.group)
            aggs = aggregate(z, meta, first, ap, ext)
            agg[here] = z.tiled(aggs)
            pre = z.flat(own[here]) + dot(aggs, wn[1])
            sig = sigmoid(pre)
            act[here] = z.tiled((pre * sig).astype(BF16))
            grad = (z.flat(hidden[here]) * (sig * (1.0 + pre * (1.0 - sig)))).astype(BF16)
            dpre[here] = z.tiled(grad)
            dagg[here] = z.tiled(dot(grad, wt[1, 1]).astype(BF16))

        each_group(z, work, unroll=2)
        spread(z, meta, counts[0], z.pairs, at, lambda q: dagg[q], acc, z.tiles, z.lent)
        to_west[...] = acc[pl.ds(0, z.edge)].astype(BF16)
        to_east[...] = acc[pl.ds(z.edge, z.edge)].astype(BF16)

    return call(
        kernel,
        "second",
        [SMEM] * 2 + [VMEM] * 10,
        [VMEM] * 6,
        [z.nodes(z.tiles)] * 4 + [z.nodes(z.edge)] * 2,
        [z.held(z.ext), z.held(z.lent + 1, F32)],
        8,
        (meta, counts, *f1, fw, fe, ap, at, own, hidden, w_nbr, wt),
    )


def weight_grads(z, pieces, f, agg, act, m, dpre, name):
    c = z.cols
    piece = -(-(3 * c + 1) // (pieces * 16)) * 16
    height = piece * pieces
    arrays = (f, agg, act, m, dpre)
    flat_args = [x for a in arrays for x in (a if isinstance(a, tuple) else (a,))]

    def kernel(*refs):
        refs = list(refs)
        f, agg, act, m, dpre = [
            (refs.pop(0), refs.pop(0)) if isinstance(a, tuple) else refs.pop(0) for a in arrays
        ]
        out, acc = refs
        acc[...] = jnp.zeros_like(acc)

        def work(part, first):
            def rows(array):
                return z.flat(group_of(z, array, part, first)[...])

            grad = rows(dpre)
            acc[pl.ds(0, c), :] += dot_rows(rows(f), grad)
            acc[pl.ds(c, c), :] += dot_rows(rows(agg), grad)
            acc[pl.ds(2 * c, c), :] += dot_rows(rows(act), rows(m))
            acc[pl.ds(3 * c, 1), :] += jnp.sum(grad.astype(F32), axis=0, keepdims=True)

        each_group(z, work)
        for i in range(pieces):
            out[i] = acc[pl.ds(i * piece, piece), :].astype(BF16)

    return call(
        kernel,
        name,
        [VMEM] * len(flat_args),
        VMEM,
        jax.ShapeDtypeStruct((pieces, piece, c), BF16),
        [pltpu.VMEM((height, c), F32)],
        6,
        flat_args,
    )


def exchanged(value, axes):
    return lax.all_to_all(value, axes, 0, 0, tiled=True)


def to_all(value, axes):
    return exchanged(jnp.broadcast_to(value, (lax.axis_size(axes),) + value.shape), axes)


def added(values):
    return jnp.sum(values.astype(F32), axis=0).astype(BF16)


def plane_share(pieces):
    return added(exchanged(pieces, PLANE))


def summed_over_parts(shares):
    shares = added(to_all(jnp.stack(shares), "feat"))
    return to_all(shares, PLANE)


def unpack(z, packed):
    c = z.cols
    pieces, _, piece, _ = packed.shape

    def kernel(packed, g_self, g_nbr, g_bias, g_out, buf):
        for layer in range(2):
            for i in range(pieces):
                buf[pl.ds(i * piece, piece), :] = packed[i, layer].astype(F32)
            g_self[layer] = buf[pl.ds(0, c), :]
            g_nbr[layer] = buf[pl.ds(c, c), :]
            g_out[layer] = buf[pl.ds(2 * c, c), :]
            g_bias[layer : layer + 1, :] = buf[pl.ds(3 * c, 1), :]

    square = jax.ShapeDtypeStruct((2, c, c), F32)
    return call(
        kernel,
        "unpack",
        [VMEM],
        [VMEM] * 4,
        [square, square, jax.ShapeDtypeStruct((2, c), F32), square],
        [pltpu.VMEM((pieces * piece, c), F32)],
        6,
        (packed,),
    )


def second_out(z, bound, live, f1, act, w_out, out):
    def kernel(bound, live, f_lent, f_rest, act, wo, _out, out, keep, sems):
        copies = []

        def work(part, first):
            f = z.flat(group_of(z, (f_lent, f_rest), part, first)[...])
            res = f.astype(F32) + dot(z.flat(act[pl.ds(first, z.group)]), wo[1])
            keep[pl.ds(first, z.group)] = z.tiled(live_rows(z, res, first, live[0]).astype(BF16))

        each_group(z, work, (0,))
        for i in range(z.lent):
            copy = pltpu.make_async_copy(
                keep.at[i], out.at[1, bound[0, i // z.edge, i % z.edge]], sems.at[i]
            )
            copy.start()
            copies.append(copy)
        each_group(z, work, (1,))
        tail = pl.ds(z.lent, z.rest)
        copy = pltpu.make_async_copy(keep.at[tail], out.at[1, tail], sems.at[z.lent])
        copy.start()
        copies.append(copy)
        for copy in copies:
            copy.wait()

    return call(
        kernel,
        "second_out",
        [SMEM] * 2 + [VMEM] * 4 + [ANY],
        ANY,
        jax.ShapeDtypeStruct(out.shape, BF16),
        [z.held(z.tiles), pltpu.SemaphoreType.DMA((z.lent + 1,))],
        6,
        (bound, live, *f1, act, w_out, out),
        {6: 0},
    )


def input_grad(z, layer, meta, counts, live, m, dpre, dagg, at, wt, grads):
    fresh = grads is None
    arrays = (m, dpre, dagg)
    flat_args = [x for a in arrays for x in (a if isinstance(a, tuple) else (a,))]

    def kernel(meta, counts, live, *refs):
        refs = list(refs)
        m, dpre, dagg = [
            (refs.pop(0), refs.pop(0)) if isinstance(a, tuple) else refs.pop(0) for a in arrays
        ]
        at, wt = refs[:2]
        grads, part_out, masked, acc, keep, sem = refs[2 if fresh else 3 :]

        def direct(part, first):
            mine = z.flat(group_of(z, m, part, first)[...]).astype(F32)
            res = mine + dot(z.flat(group_of(z, dpre, part, first)[...]), wt[layer, 0])
            acc[pl.ds(first, z.group)] = z.tiled(res)

        each_group(z, direct)

        def source(q):
            if not isinstance(dagg, tuple):
                return dagg[q]
            lent = dagg[0][jnp.minimum(q, z.lent - 1)]
            rest = dagg[1][jnp.maximum(q - z.lent, 0)]
            return jnp.where(q < z.lent, lent, rest)

        spread(z, meta, 0, counts[0], at, source, acc, 0, z.tiles)
        tail = pl.ds(z.lent, z.rest)
        keep[...] = acc[tail].astype(BF16)
        copy = pltpu.make_async_copy(keep, grads.at[layer, tail], sem)
        copy.start()
        part_out[...] = acc[pl.ds(0, z.lent)]

        @pl.loop(0, z.rest)
        def _(i):
            value = keep[i]
            masked[i] = jnp.where(z.lent + i < live[0], value, jnp.zeros_like(value))

        copy.wait()

    args = [meta, counts, live, *flat_args, at, wt]
    if not fresh:
        args.append(grads)
    return call(
        kernel,
        "input_grad%d" % layer,
        [SMEM] * 3 + [VMEM] * (len(flat_args) + 2) + ([] if fresh else [ANY]),
        [ANY, VMEM, VMEM],
        [
            jax.ShapeDtypeStruct((2, z.tiles, z.rows, z.cols), BF16),
            z.nodes(z.lent, F32),
            z.nodes(z.rest),
        ],
        [z.held(z.tiles + 1, F32), z.held(z.rest), pltpu.SemaphoreType.DMA],
        10,
        args,
        None if fresh else {len(args) - 1: 0},
    )


def early_rest(z, meta, counts, m0, slope, at, wt):
    def kernel(meta, counts, m, slope, at, wt, dpre, dagg, outer, acc):
        def work(part, first):
            here = pl.ds(first - z.lent, z.group)
            grad = dot(z.flat(m[here]), wt[0, 2]) * z.flat(slope[pl.ds(first, z.group)])
            grad = grad.astype(BF16)
            dpre[here] = z.tiled(grad)
            dagg[here] = z.tiled(dot(grad, wt[0, 1]).astype(BF16))

        each_group(z, work, (1,))
        acc[...] = jnp.zeros_like(acc)

        def source(q):
            return dagg[jnp.maximum(q - z.lent, 0)]

        spread(z, meta, counts[0], counts[0] + counts[1], at, source, acc, z.tiles, z.lent)
        outer[...] = acc[pl.ds(0, z.lent)]

    return call(
        kernel,
        "early_rest",
        [SMEM] * 2 + [VMEM] * 4,
        [VMEM] * 3,
        [z.nodes(z.rest), z.nodes(z.rest), z.nodes(z.lent, F32)],
        [z.held(z.lent + 1, F32)],
        6,
        (meta, counts, m0, slope, at, wt),
    )


def early_lent(z, meta, counts, bound, part, fw, fe, slope, outer, at, wt, grads):
    def kernel(meta, counts, bound, part, fw, fe, slope, outer, at, wt, _g,
               m, dpre, dagg, grads, to_west, to_east, acc, sems):
        def work(first, got):
            here = pl.ds(first, z.group)
            g = z.flat((part[here] + got.astype(F32)).astype(BF16))
            m[here] = z.tiled(g)
            grad = (dot(g, wt[0, 2]) * z.flat(slope[here])).astype(BF16)
            dpre[here] = z.tiled(grad)
            dagg[here] = z.tiled(dot(grad, wt[0, 1]).astype(BF16))

        @pl.loop(0, z.edge // z.group)
        def _(s):
            here = pl.ds(s * z.group, z.group)
            work(s * z.group, fw[here])
            work(z.edge + s * z.group, fe[here])

        copies = [
            pltpu.make_async_copy(m.at[i], grads.at[1, bound[0, i // z.edge, i % z.edge]], sems.at[i])
            for i in range(z.lent)
        ]
        for copy in copies:
            copy.start()
        acc[pl.ds(0, z.lent)] = outer[...]
        acc[z.lent] = jnp.zeros((z.rows, z.cols), F32)

        def source(q):
            return dagg[jnp.minimum(q, z.lent - 1)]

        spread(z, meta, counts[0] + counts[1], z.pairs, at, source, acc, z.tiles, z.lent)
        to_west[...] = acc[pl.ds(0, z.edge)].astype(BF16)
        to_east[...] = acc[pl.ds(z.edge, z.edge)].astype(BF16)
        for copy in copies:
            copy.wait()

    return call(
        kernel,
        "early_lent",
        [SMEM] * 3 + [VMEM] * 7 + [ANY],
        [VMEM] * 3 + [ANY] + [VMEM] * 2,
        [z.nodes(z.lent)] * 3 + [jax.ShapeDtypeStruct(grads.shape, BF16)] + [z.nodes(z.edge)] * 2,
        [z.held(z.lent + 1, F32), pltpu.SemaphoreType.DMA((z.lent,))],
        6,
        (meta, counts, bound, part, fw, fe, slope, outer, at, wt, grads),
        {10: 3},
    )


def finish(z, bound, part, fw, fe, grads):
    def kernel(bound, part, fw, fe, _g, grads, keep, sems):
        copies = []
        for i in range(z.lent):
            got = fw[i] if i < z.edge else fe[i - z.edge]
            keep[i] = (part[i] + got.astype(F32)).astype(BF16)
            copy = pltpu.make_async_copy(
                keep.at[i], grads.at[0, bound[0, i // z.edge, i % z.edge]], sems.at[i]
            )
            copy.start()
            copies.append(copy)
        for copy in copies:
            copy.wait()

    return call(
        kernel,
        "finish",
        [SMEM] + [VMEM] * 3 + [ANY],
        ANY,
        jax.ShapeDtypeStruct(grads.shape, BF16),
        [z.held(z.lent), pltpu.SemaphoreType.DMA((z.lent,))],
        4,
        (bound, part, fw, fe, grads),
        {4: 0},
    )


def per_device(
    node_in, out_cot, adjacency, tile_nbrs, bound_tiles, live_tiles, w_self, w_nbr, pre_bias, w_out
):
    z = Sizes(adjacency, node_in, bound_tiles)
    t, r, c = z.tiles, z.rows, z.cols
    features = node_in.reshape(t, r, c)
    cot = out_cot.reshape(t, r, c)
    pieces = lax.axis_size(PLANE)

    west, east = lend(z, bound_tiles, features)
    from_west = passed_along(east, 1)
    from_east = passed_along(west, -1)
    *nodes, ap, meta, counts = arrange(z, bound_tiles, tile_nbrs, live_tiles, features, cot, adjacency)
    f0, m1 = tuple(nodes[:2]), tuple(nodes[2:])
    at, wt = turn(z, ap, w_self, w_nbr, w_out)

    west, east, agg_lent = first_lent(z, meta, f0, from_west, from_east, ap, w_self, w_nbr, pre_bias, w_out)
    next_west = passed_along(east, 1)
    next_east = passed_along(west, -1)
    f1_lent, f1_rest, section_out, agg_rest = first_rest(
        z, meta, bound_tiles, live_tiles, f0, from_west, from_east, ap, w_self, w_nbr, pre_bias, w_out,
        west, east,
    )
    f1, agg0 = (f1_lent, f1_rest), (agg_lent, agg_rest)
    own, hidden = second_own(z, f1, m1, w_self, pre_bias, wt)
    act0, slope = saved(z, f0, agg0, w_self, w_nbr, pre_bias)

    agg1, act1, dpre1, dagg1, to_west, to_east = second(
        z, meta, counts, f1, next_west, next_east, ap, at, own, hidden, w_nbr, wt
    )
    back_west = passed_along(to_east, 1)
    back_east = passed_along(to_west, -1)
    grads, part, m0_rest = input_grad(z, 1, meta, counts, live_tiles, m1, dpre1, dagg1, at, wt, None)
    dpre_rest, dagg_rest, outer = early_rest(z, meta, counts, m0_rest, slope, at, wt)
    late = plane_share(weight_grads(z, pieces, f1, agg1, act1, m1, dpre1, "weight_grads1"))
    section_out = second_out(z, bound_tiles, live_tiles, f1, act1, w_out, section_out)

    m0_lent, dpre_lent, dagg_lent, grads, to_west, to_east = early_lent(
        z, meta, counts, bound_tiles, part, back_west, back_east, slope, outer, at, wt, grads
    )
    back_west = passed_along(to_east, 1)
    back_east = passed_along(to_west, -1)
    m0, dpre0, dagg0 = (m0_lent, m0_rest), (dpre_lent, dpre_rest), (dagg_lent, dagg_rest)
    early = plane_share(weight_grads(z, pieces, f0, agg0, act0, m0, dpre0, "weight_grads0"))
    grads, part, _ = input_grad(z, 0, meta, counts, live_tiles, m0, dpre0, dagg0, at, wt, grads)
    grads = finish(z, bound_tiles, part, back_west, back_east, grads)

    grad_self, grad_nbr, grad_bias, grad_out = unpack(z, summed_over_parts([early, late]))
    return (
        section_out.reshape(2, t * r, c),
        grads.reshape(2, t * r, c),
        grad_self,
        grad_nbr,
        grad_bias,
        grad_out,
    )


def solution(mesh):
    rows = P(AXES)
    in_specs = (rows, rows, rows, rows, rows, rows, P(), P(), P(), P())
    out_specs = (P(None, AXES), P(None, AXES), P(), P(), P(), P())
    return jax.shard_map(
        per_device, mesh=mesh, in_specs=in_specs, out_specs=out_specs, check_vma=False
    )
```

```python
import jax
import jax.numpy as jnp
from jax import lax
from jax.experimental import pallas as pl
from jax.experimental.pallas import tpu as pltpu
from jax.sharding import PartitionSpec as P

AXES = ("dom", "phase", "feat")
PLANE = ("dom", "phase")
BF16 = jnp.bfloat16
F32 = jnp.float32
UNROLL = 8
ANY = pl.BlockSpec(memory_space=pl.ANY)
SMEM = pl.BlockSpec(memory_space=pltpu.SMEM)
VMEM = pl.BlockSpec(memory_space=pltpu.VMEM)
MIB = 1024 * 1024
TOKEN = jax.ShapeDtypeStruct((8, 128), F32)


class Sizes:
    def __init__(self, adjacency, features, bound):
        self.tiles, self.slots, self.rows, _ = adjacency.shape
        self.cols = features.shape[-1]
        self.edge = bound.shape[-1]
        self.lent = 2 * self.edge
        self.rest = self.tiles - self.lent
        self.ext = self.tiles + self.lent
        self.pairs = self.tiles * self.slots
        self.group = next(g for g in (4, 2, 1) if self.edge % g == 0 and self.rest % g == 0)
        self.parts = ((0, 0, self.lent), (1, self.lent, self.rest))

    def nodes(self, count, dtype=BF16):
        return jax.ShapeDtypeStruct((count, self.rows, self.cols), dtype)

    def held(self, count, dtype=BF16):
        return pltpu.VMEM((count, self.rows, self.cols), dtype)

    def flat(self, value):
        return value.reshape(self.group * self.rows, self.cols)

    def tiled(self, value):
        return value.reshape(self.group, self.rows, self.cols)


def group_of(z, array, part, first):
    if isinstance(array, tuple):
        base = z.lent if part else 0
        return array[part].at[pl.ds(first - base, z.group)]
    return array.at[pl.ds(first, z.group)]


def each_group(z, body, parts=(0, 1), unroll=1):
    for part, base, count in z.parts:
        if part in parts:

            @pl.loop(0, count // z.group, unroll=unroll)
            def _(s):
                body(part, base + s * z.group)


def passed_along(value, steps):
    count = lax.axis_size(AXES)
    return lax.ppermute(value, AXES, [(i, (i + steps) % count) for i in range(count)])


def dot(a, b):
    return jnp.dot(a, b, preferred_element_type=F32)


def dot_rows(a, b):
    return lax.dot_general(a, b, (((0,), (0,)), ((), ())), preferred_element_type=F32)


def call(kernel, name, in_specs, out_specs, out_shape, scratch, limit, args, aliases=None):
    return pl.pallas_call(
        kernel,
        in_specs=in_specs,
        out_specs=out_specs,
        out_shape=out_shape,
        scratch_shapes=scratch,
        input_output_aliases=aliases or {},
        compiler_params=pltpu.CompilerParams(vmem_limit_bytes=limit * MIB),
        cost_estimate=pl.CostEstimate(flops=1000, bytes_accessed=1000, transcendentals=0),
        name=name,
    )(*args)


def sigmoid(v):
    return 0.5 * jnp.tanh(0.5 * v) + 0.5


def lend(z, bound, features):
    def kernel(bound, feats, west, east, sems):
        copies = []
        for i in range(z.edge):
            for side, target in ((0, west), (1, east)):
                copy = pltpu.make_async_copy(
                    feats.at[bound[0, side, i]], target.at[i], sems.at[side * z.edge + i]
                )
                copy.start()
                copies.append(copy)
        for copy in copies:
            copy.wait()

    return call(
        kernel,
        "lend",
        [SMEM, ANY],
        [VMEM, VMEM],
        [z.nodes(z.edge), z.nodes(z.edge)],
        [pltpu.SemaphoreType.DMA((z.lent,))],
        2,
        (bound, features),
    )


def arrange(z, bound, nbrs, live, features, cot, adjacency):
    s4 = z.slots

    def kernel(bound, nbrs, live, feats, cot, adj, f_lent, f_rest, m_lent, m_rest, ap, meta, counts, inverse, sems):
        copies = []

        def start(source, target):
            copy = pltpu.make_async_copy(source, target, sems.at[len(copies)])
            copy.start()
            copies.append(copy)

        tail = pl.ds(z.lent, z.rest)
        start(adj.at[tail], ap.at[tail])
        start(feats.at[tail], f_rest)
        start(cot.at[tail], m_rest)
        for i in range(z.lent):
            tile = bound[0, i // z.edge, i % z.edge]
            inverse[tile] = i
            start(adj.at[tile], ap.at[i])
            start(feats.at[tile], f_lent.at[i])
            start(cot.at[tile], m_lent.at[i])

        def kind_of(position, target):
            return jnp.where(target < z.tiles, 0, jnp.where(position < z.lent, 2, 1))

        def step(kind, sums):
            return tuple(total + jnp.where(kind == i, 1, 0) for i, total in enumerate(sums))

        def count(position, sums):
            clipped = jnp.minimum(position, z.lent - 1)
            tile = jnp.where(position < z.lent, bound[0, clipped // z.edge, clipped % z.edge], position)
            for k in range(s4):
                target = nbrs[tile, k]
                moved = jnp.where(target < z.lent, inverse[jnp.minimum(target, z.lent - 1)], target)
                meta[position * s4 + k] = moved
                sums = step(kind_of(position, moved), sums)
            return sums

        zero = jnp.int32(0)
        own, outer, lent = lax.fori_loop(0, z.tiles, count, (zero, zero, zero))
        counts[0] = own
        counts[1] = outer
        counts[2] = lent

        def put(position, sums):
            for k in range(s4):
                target = meta[position * s4 + k]
                kind = kind_of(position, target)
                slot = jnp.where(kind == 0, sums[0], jnp.where(kind == 1, sums[1], sums[2]))
                meta[z.pairs + slot] = position * s4 + k
                meta[2 * z.pairs + slot] = target
                sums = step(kind, sums)
            return sums

        lax.fori_loop(0, z.tiles, put, (zero, own, own + outer))
        for copy in copies:
            copy.wait()

        @pl.loop(0, z.rest)
        def _(i):
            @pl.when(z.lent + i >= live[0])
            def _():
                m_rest[i] = jnp.zeros((z.rows, z.cols), BF16)

    return call(
        kernel,
        "arrange",
        [SMEM, SMEM, SMEM, ANY, ANY, ANY],
        [VMEM] * 5 + [SMEM, SMEM],
        [
            z.nodes(z.lent),
            z.nodes(z.rest),
            z.nodes(z.lent),
            z.nodes(z.rest),
            jax.ShapeDtypeStruct(adjacency.shape, BF16),
            jax.ShapeDtypeStruct((3 * z.pairs,), jnp.int32),
            jax.ShapeDtypeStruct((8,), jnp.int32),
        ],
        [pltpu.SMEM((z.lent,), jnp.int32), pltpu.SemaphoreType.DMA((3 * z.lent + 3,))],
        6,
        (bound, nbrs, live, features, cot, adjacency),
    )


def turn(z, ap, w_self, w_nbr, w_out):
    def kernel(ap, ws, wn, wo, at, wt):
        for layer in range(2):
            wt[layer, 0] = ws[layer].T
            wt[layer, 1] = wn[layer].T
            wt[layer, 2] = wo[layer].T

        @pl.loop(0, z.tiles)
        def _(q):
            for k in range(z.slots):
                at[q * z.slots + k] = ap[q, k].T

    return call(
        kernel,
        "turn",
        [VMEM] * 4,
        [VMEM, VMEM],
        [
            jax.ShapeDtypeStruct((z.pairs, z.rows, z.rows), BF16),
            jax.ShapeDtypeStruct((2, 3, z.cols, z.cols), BF16),
        ],
        [],
        6,
        (ap, w_self, w_nbr, w_out),
    )


def fill_extended(z, own, fw, fe, ext):
    ext[pl.ds(0, z.lent)] = own[0][...]
    ext[pl.ds(z.lent, z.rest)] = own[1][...]
    ext[pl.ds(z.tiles, z.edge)] = fw[...]
    ext[pl.ds(z.tiles + z.edge, z.edge)] = fe[...]


def aggregate(z, meta, first, ap, ext):
    rows = []
    for g in range(z.group):
        base = (first + g) * z.slots
        picked = jnp.concatenate([ext[meta[base + k]] for k in range(z.slots)], axis=0)
        blocks = jnp.concatenate([ap[first + g, k] for k in range(z.slots)], axis=1)
        rows.append(dot(blocks, picked).astype(BF16))
    return jnp.concatenate(rows, axis=0)


def live_rows(z, value, first, live):
    parts = []
    for g in range(z.group):
        part = value[g * z.rows : (g + 1) * z.rows]
        parts.append(jnp.where(first + g < live, part, jnp.zeros_like(part)))
    return jnp.concatenate(parts, axis=0)


def first_lent(z, meta, f0, fw, fe, ap, w_self, w_nbr, bias, w_out):
    def kernel(meta, f_lent, f_rest, fw, fe, ap, ws, wn, bias, wo, west, east, agg, ext):
        fill_extended(z, (f_lent, f_rest), fw, fe, ext)

        def work(first, target, offset):
            here = pl.ds(first, z.group)
            f = z.flat(ext[here])
            aggs = aggregate(z, meta, first, ap, ext)
            agg[here] = z.tiled(aggs)
            pre = dot(f, ws[0]) + dot(aggs, wn[0]) + bias[0:1, :]
            act = (pre * sigmoid(pre)).astype(BF16)
            target[pl.ds(offset, z.group)] = z.tiled((f.astype(F32) + dot(act, wo[0])).astype(BF16))

        @pl.loop(0, z.edge // z.group)
        def _(s):
            work(s * z.group, west, s * z.group)
            work(z.edge + s * z.group, east, s * z.group)

    return call(
        kernel,
        "first_lent",
        [SMEM] + [VMEM] * 9,
        [VMEM] * 3,
        [z.nodes(z.edge), z.nodes(z.edge), z.nodes(z.lent)],
        [z.held(z.ext)],
        8,
        (meta, *f0, fw, fe, ap, w_self, w_nbr, bias, w_out),
    )


def first_rest(z, meta, bound, live, f0, fw, fe, ap, w_self, w_nbr, bias, w_out, west, east):
    def kernel(meta, bound, live, f_lent, f_rest, fw, fe, ap, ws, wn, bias, wo, west, east,
               f1_lent, f1_rest, out, agg, ext, sems):
        copies = []
        for i in range(z.edge):
            for side, source in ((0, west), (1, east)):
                copy = pltpu.make_async_copy(
                    source.at[i], out.at[0, bound[0, side, i]], sems.at[side * z.edge + i]
                )
                copy.start()
                copies.append(copy)
        fill_extended(z, (f_lent, f_rest), fw, fe, ext)
        f1_lent[pl.ds(0, z.edge)] = west[...]
        f1_lent[pl.ds(z.edge, z.edge)] = east[...]

        def work(part, first):
            f = z.flat(ext[pl.ds(first, z.group)])
            aggs = aggregate(z, meta, first, ap, ext)
            here = pl.ds(first - z.lent, z.group)
            agg[here] = z.tiled(aggs)
            pre = dot(f, ws[0]) + dot(aggs, wn[0]) + bias[0:1, :]
            act = (pre * sigmoid(pre)).astype(BF16)
            res = live_rows(z, f.astype(F32) + dot(act, wo[0]), first, live[0])
            f1_rest[here] = z.tiled(res.astype(BF16))

        each_group(z, work, (1,))
        copy = pltpu.make_async_copy(f1_rest, out.at[0, pl.ds(z.lent, z.rest)], sems.at[z.lent])
        copy.start()
        for other in copies:
            other.wait()
        copy.wait()

    return call(
        kernel,
        "first_rest",
        [SMEM] * 3 + [VMEM] * 11,
        [VMEM, VMEM, ANY, VMEM],
        [
            z.nodes(z.lent),
            z.nodes(z.rest),
            jax.ShapeDtypeStruct((2, z.tiles, z.rows, z.cols), BF16),
            z.nodes(z.rest),
        ],
        [z.held(z.ext), pltpu.SemaphoreType.DMA((1 + z.lent,))],
        10,
        (meta, bound, live, *f0, fw, fe, ap, w_self, w_nbr, bias, w_out, west, east),
    )


def second_own(z, m1, wt):
    def kernel(m_lent, m_rest, wt, hidden):
        def work(part, first):
            m = z.flat(group_of(z, (m_lent, m_rest), part, first)[...])
            hidden[pl.ds(first, z.group)] = z.tiled(dot(m, wt[1, 2]))

        each_group(z, work)

    return call(
        kernel,
        "second_own",
        [VMEM] * 3,
        VMEM,
        z.nodes(z.tiles, F32),
        [],
        8,
        (*m1, wt),
    )


def saved(z, f0, agg0, w_self, w_nbr, bias):
    def kernel(f_lent, f_rest, a_lent, a_rest, ws, wn, bias, act, slope, token):
        token[...] = jnp.zeros_like(token)

        def work(part, first):
            f = z.flat(group_of(z, (f_lent, f_rest), part, first)[...])
            aggs = z.flat(group_of(z, (a_lent, a_rest), part, first)[...])
            pre = dot(f, ws[0]) + dot(aggs, wn[0]) + bias[0:1, :]
            sig = sigmoid(pre)
            here = pl.ds(first, z.group)
            act[here] = z.tiled((pre * sig).astype(BF16))
            slope[here] = z.tiled(sig * (1.0 + pre * (1.0 - sig)))

        each_group(z, work)

    return call(
        kernel,
        "saved",
        [VMEM] * 7,
        [VMEM] * 3,
        [z.nodes(z.tiles), z.nodes(z.tiles, F32), TOKEN],
        [],
        10,
        (*f0, *agg0, w_self, w_nbr, bias),
    )


def spread(z, meta, start, stop, at, source, acc, shift, spare):
    def body(i, carry):
        for u in range(UNROLL):
            entry = start + i * UNROLL + u
            inside = entry < stop
            entry = jnp.minimum(entry, z.pairs - 1)
            target = jnp.where(inside, meta[2 * z.pairs + entry] - shift, spare)
            pair = meta[z.pairs + entry]
            acc[target] += dot(at[pair], source(pair // z.slots))
        return carry

    lax.fori_loop(0, (stop - start + UNROLL - 1) // UNROLL, body, 0)


def second(z, meta, counts, f1, fw, fe, ap, at, hidden, w_self, w_nbr, bias, wt, after):
    def kernel(meta, counts, f_lent, f_rest, fw, fe, ap, at, hidden, ws, wn, bias, wt, _after,
               agg, act, dpre, dagg, to_west, to_east, ext, acc):
        fill_extended(z, (f_lent, f_rest), fw, fe, ext)
        acc[...] = jnp.zeros_like(acc)

        def work(part, first):
            here = pl.ds(first, z.group)
            aggs = aggregate(z, meta, first, ap, ext)
            agg[here] = z.tiled(aggs)
            pre = dot(z.flat(ext[here]), ws[1]) + dot(aggs, wn[1]) + bias[1:2, :]
            sig = sigmoid(pre)
            act[here] = z.tiled((pre * sig).astype(BF16))
            grad = (z.flat(hidden[here]) * (sig * (1.0 + pre * (1.0 - sig)))).astype(BF16)
            dpre[here] = z.tiled(grad)
            dagg[here] = z.tiled(dot(grad, wt[1, 1]).astype(BF16))

        each_group(z, work, unroll=2)
        spread(z, meta, counts[0], z.pairs, at, lambda q: dagg[q], acc, z.tiles, z.lent)
        to_west[...] = acc[pl.ds(0, z.edge)].astype(BF16)
        to_east[...] = acc[pl.ds(z.edge, z.edge)].astype(BF16)

    return call(
        kernel,
        "second",
        [SMEM] * 2 + [VMEM] * 12,
        [VMEM] * 6,
        [z.nodes(z.tiles)] * 4 + [z.nodes(z.edge)] * 2,
        [z.held(z.ext), z.held(z.lent + 1, F32)],
        12,
        (meta, counts, *f1, fw, fe, ap, at, hidden, w_self, w_nbr, bias, wt, after),
    )


class Plane:
    def __init__(self):
        dom, phase = lax.axis_size("dom"), lax.axis_size("phase")
        self.pair = 2 if dom % 2 == 0 else 1
        self.phase = phase
        self.groups = dom // self.pair * phase
        self.count = dom * phase
        place = lax.axis_index("dom")
        half = lax.rem(place, self.pair)
        group = place // self.pair * phase + lax.axis_index("phase")
        self.me = jnp.stack([half, group]).astype(jnp.int32)

    def index(self, half, group):
        return (group // self.phase * self.pair + half) * self.phase + group % self.phase

    def across(self, value):
        pairs = [
            (self.index(h, g), self.index((h + 1) % self.pair, g))
            for h in range(self.pair)
            for g in range(self.groups)
        ]
        return lax.ppermute(value, PLANE, pairs)

    def along(self, value, steps):
        pairs = [
            (self.index(h, g), self.index(h, (g + steps) % self.groups))
            for h in range(self.pair)
            for g in range(self.groups)
        ]
        return lax.ppermute(value, PLANE, pairs)


def weight_grads(z, plane, f, agg, act, m, dpre, name):
    c = z.cols
    piece = -(-(3 * c + 1) // (plane.count * 16)) * 16
    arrays = (f, agg, act, m, dpre)
    flat_args = [x for a in arrays for x in (a if isinstance(a, tuple) else (a,))]

    def kernel(me, *refs):
        refs = list(refs)
        f, agg, act, m, dpre = [
            (refs.pop(0), refs.pop(0)) if isinstance(a, tuple) else refs.pop(0) for a in arrays
        ]
        outs, acc = refs[:-1], refs[-1]
        acc[...] = jnp.zeros_like(acc)

        def work(part, first):
            def rows(array):
                return z.flat(group_of(z, array, part, first)[...])

            grad = rows(dpre)
            acc[pl.ds(0, c), :] += dot_rows(rows(f), grad)
            acc[pl.ds(c, c), :] += dot_rows(rows(agg), grad)
            acc[pl.ds(2 * c, c), :] += dot_rows(rows(act), rows(m))
            acc[pl.ds(3 * c, 1), :] += jnp.sum(grad.astype(F32), axis=0, keepdims=True)

        each_group(z, work)
        for h, out in enumerate(outs):
            half = lax.rem(me[0] + h, plane.pair)
            for g in range(plane.groups):
                owner = half * plane.groups + lax.rem(me[1] + g, plane.groups)
                out[g] = acc[pl.ds(pl.multiple_of(owner * piece, 16), piece), :].astype(BF16)

    return call(
        kernel,
        name,
        [SMEM] + [VMEM] * len(flat_args),
        [VMEM] * plane.pair,
        [jax.ShapeDtypeStruct((plane.groups, piece, c), BF16)] * plane.pair,
        [pltpu.VMEM((piece * plane.count, c), F32)],
        14,
        (plane.me, *flat_args),
    )


def added(*values):
    total = values[0].astype(F32)
    for value in values[1:]:
        total = total + value.astype(F32)
    return total.astype(BF16)


def pair_sums(plane, halves):
    if plane.pair == 1:
        return halves[0]
    return added(halves[0], plane.across(halves[1]))


def share_totals(plane, late, halves):
    both = jnp.stack([pair_sums(plane, halves), late], axis=1)
    share = added(both[0], *[plane.along(both[g], g) for g in range(1, plane.groups)])
    lines = lax.axis_size("feat")
    if lines & (lines - 1) == 0:
        step = 1
        while step < lines:
            share = added(share, lax.ppermute(share, "feat", [(i, i ^ step) for i in range(lines)]))
            step *= 2
    else:
        share = lax.psum(share.astype(F32), "feat").astype(BF16)
    gathered = jnp.stack([share] + [plane.along(share, g) for g in range(1, plane.groups)])
    if plane.pair == 1:
        return gathered[None]
    return jnp.stack([gathered, plane.across(gathered)])


def second_out(z, bound, live, f1, act, w_out, out):
    def kernel(bound, live, f_lent, f_rest, act, wo, _out, out, token, keep, sems):
        copies = []
        token[...] = jnp.zeros_like(token)

        def work(part, first):
            f = z.flat(group_of(z, (f_lent, f_rest), part, first)[...])
            res = f.astype(F32) + dot(z.flat(act[pl.ds(first, z.group)]), wo[1])
            keep[pl.ds(first, z.group)] = z.tiled(live_rows(z, res, first, live[0]).astype(BF16))

        each_group(z, work, (0,))
        for i in range(z.lent):
            copy = pltpu.make_async_copy(
                keep.at[i], out.at[1, bound[0, i // z.edge, i % z.edge]], sems.at[i]
            )
            copy.start()
            copies.append(copy)
        each_group(z, work, (1,))
        tail = pl.ds(z.lent, z.rest)
        copy = pltpu.make_async_copy(keep.at[tail], out.at[1, tail], sems.at[z.lent])
        copy.start()
        copies.append(copy)
        for copy in copies:
            copy.wait()

    return call(
        kernel,
        "second_out",
        [SMEM] * 2 + [VMEM] * 4 + [ANY],
        [ANY, VMEM],
        [jax.ShapeDtypeStruct(out.shape, BF16), TOKEN],
        [z.held(z.tiles), pltpu.SemaphoreType.DMA((z.lent + 1,))],
        12,
        (bound, live, *f1, act, w_out, out),
        {6: 0},
    )


def input_grad(z, layer, meta, counts, m, dpre, dagg, at, wt):
    arrays = (m, dpre, dagg)
    flat_args = [x for a in arrays for x in (a if isinstance(a, tuple) else (a,))]

    def kernel(meta, counts, *refs):
        refs = list(refs)
        m, dpre, dagg = [
            (refs.pop(0), refs.pop(0)) if isinstance(a, tuple) else refs.pop(0) for a in arrays
        ]
        at, wt, part_out, rest_out, acc = refs

        def direct(part, first):
            mine = z.flat(group_of(z, m, part, first)[...]).astype(F32)
            res = mine + dot(z.flat(group_of(z, dpre, part, first)[...]), wt[layer, 0])
            acc[pl.ds(first, z.group)] = z.tiled(res)

        each_group(z, direct)

        def source(q):
            if not isinstance(dagg, tuple):
                return dagg[q]
            lent = dagg[0][jnp.minimum(q, z.lent - 1)]
            rest = dagg[1][jnp.maximum(q - z.lent, 0)]
            return jnp.where(q < z.lent, lent, rest)

        spread(z, meta, 0, counts[0], at, source, acc, 0, z.tiles)
        part_out[...] = acc[pl.ds(0, z.lent)]
        rest_out[...] = acc[pl.ds(z.lent, z.rest)].astype(BF16)

    return call(
        kernel,
        "input_grad%d" % layer,
        [SMEM] * 2 + [VMEM] * (len(flat_args) + 2),
        [VMEM, VMEM],
        [z.nodes(z.lent, F32), z.nodes(z.rest)],
        [z.held(z.tiles + 1, F32)],
        28,
        [meta, counts, *flat_args, at, wt],
    )


def early_rest(z, meta, counts, live, upstream, slope, at, wt):
    def kernel(meta, counts, live, g, slope, at, wt, grads, m, dpre, dagg, outer, acc, sem):
        copy = pltpu.make_async_copy(g, grads.at[1, pl.ds(z.lent, z.rest)], sem)
        copy.start()

        def work(part, first):
            here = pl.ds(first - z.lent, z.group)
            masked = live_rows(z, z.flat(g[here]), first, live[0])
            m[here] = z.tiled(masked)
            grad = dot(masked, wt[0, 2]) * z.flat(slope[pl.ds(first, z.group)])
            grad = grad.astype(BF16)
            dpre[here] = z.tiled(grad)
            dagg[here] = z.tiled(dot(grad, wt[0, 1]).astype(BF16))

        each_group(z, work, (1,))
        acc[...] = jnp.zeros_like(acc)

        def source(q):
            return dagg[jnp.maximum(q - z.lent, 0)]

        spread(z, meta, counts[0], counts[0] + counts[1], at, source, acc, z.tiles, z.lent)
        outer[...] = acc[pl.ds(0, z.lent)]
        copy.wait()

    return call(
        kernel,
        "early_rest",
        [SMEM] * 3 + [VMEM] * 4,
        [ANY] + [VMEM] * 4,
        [jax.ShapeDtypeStruct((2, z.tiles, z.rows, z.cols), BF16)]
        + [z.nodes(z.rest)] * 3
        + [z.nodes(z.lent, F32)],
        [z.held(z.lent + 1, F32), pltpu.SemaphoreType.DMA],
        14,
        (meta, counts, live, upstream, slope, at, wt),
    )


def early_lent(z, meta, counts, bound, part, fw, fe, slope, outer, at, wt, grads, after):
    def kernel(meta, counts, bound, part, fw, fe, slope, outer, at, wt, _g, _ready, _late,
               m, dpre, dagg, grads, to_west, to_east, acc, sems):
        def work(first, got):
            here = pl.ds(first, z.group)
            g = z.flat((part[here] + got.astype(F32)).astype(BF16))
            m[here] = z.tiled(g)
            grad = (dot(g, wt[0, 2]) * z.flat(slope[here])).astype(BF16)
            dpre[here] = z.tiled(grad)
            dagg[here] = z.tiled(dot(grad, wt[0, 1]).astype(BF16))

        @pl.loop(0, z.edge // z.group)
        def _(s):
            here = pl.ds(s * z.group, z.group)
            work(s * z.group, fw[here])
            work(z.edge + s * z.group, fe[here])

        copies = [
            pltpu.make_async_copy(m.at[i], grads.at[1, bound[0, i // z.edge, i % z.edge]], sems.at[i])
            for i in range(z.lent)
        ]
        for copy in copies:
            copy.start()
        acc[pl.ds(0, z.lent)] = outer[...]
        acc[z.lent] = jnp.zeros((z.rows, z.cols), F32)

        def source(q):
            return dagg[jnp.minimum(q, z.lent - 1)]

        spread(z, meta, counts[0] + counts[1], z.pairs, at, source, acc, z.tiles, z.lent)
        to_west[...] = acc[pl.ds(0, z.edge)].astype(BF16)
        to_east[...] = acc[pl.ds(z.edge, z.edge)].astype(BF16)
        for copy in copies:
            copy.wait()

    return call(
        kernel,
        "early_lent",
        [SMEM] * 3 + [VMEM] * 7 + [ANY, VMEM, VMEM],
        [VMEM] * 3 + [ANY] + [VMEM] * 2,
        [z.nodes(z.lent)] * 3 + [jax.ShapeDtypeStruct(grads.shape, BF16)] + [z.nodes(z.edge)] * 2,
        [z.held(z.lent + 1, F32), pltpu.SemaphoreType.DMA((z.lent,))],
        16,
        (meta, counts, bound, part, fw, fe, slope, outer, at, wt, grads, *after),
        {10: 3},
    )


def finish(z, plane, bound, part, rest, fw, fe, totals, grads):
    c = z.cols
    piece = totals.shape[3]

    def kernel(me, bound, part, rest, fw, fe, totals, _g, grads, g_self, g_nbr, g_bias, g_out, keep, buf, sems):
        copies = [pltpu.make_async_copy(rest, grads.at[0, pl.ds(z.lent, z.rest)], sems.at[z.lent])]
        copies[0].start()
        for i in range(z.lent):
            got = fw[i] if i < z.edge else fe[i - z.edge]
            keep[i] = (part[i] + got.astype(F32)).astype(BF16)
            copy = pltpu.make_async_copy(
                keep.at[i], grads.at[0, bound[0, i // z.edge, i % z.edge]], sems.at[i]
            )
            copy.start()
            copies.append(copy)
        for layer in range(2):
            for h in range(plane.pair):
                half = lax.rem(me[0] + h, plane.pair)
                for g in range(plane.groups):
                    owner = half * plane.groups + lax.rem(me[1] + plane.groups - g, plane.groups)
                    start = pl.multiple_of(owner * piece, 16)
                    buf[pl.ds(start, piece), :] = totals[h, g, layer].astype(F32)
            g_self[layer] = buf[pl.ds(0, c), :]
            g_nbr[layer] = buf[pl.ds(c, c), :]
            g_out[layer] = buf[pl.ds(2 * c, c), :]
            g_bias[layer : layer + 1, :] = buf[pl.ds(3 * c, 1), :]
        for copy in copies:
            copy.wait()

    square = jax.ShapeDtypeStruct((2, c, c), F32)
    return call(
        kernel,
        "finish",
        [SMEM] * 2 + [VMEM] * 5 + [ANY],
        [ANY] + [VMEM] * 4,
        [jax.ShapeDtypeStruct(grads.shape, BF16), square, square, jax.ShapeDtypeStruct((2, c), F32), square],
        [
            z.held(z.lent),
            pltpu.VMEM((piece * plane.count, c), F32),
            pltpu.SemaphoreType.DMA((z.lent + 1,)),
        ],
        14,
        (plane.me, bound, part, rest, fw, fe, totals, grads),
        {7: 0},
    )


def per_device(
    node_in, out_cot, adjacency, tile_nbrs, bound_tiles, live_tiles, w_self, w_nbr, pre_bias, w_out
):
    z = Sizes(adjacency, node_in, bound_tiles)
    t, r, c = z.tiles, z.rows, z.cols
    features = node_in.reshape(t, r, c)
    cot = out_cot.reshape(t, r, c)
    plane = Plane()

    west, east = lend(z, bound_tiles, features)
    from_west = passed_along(east, 1)
    from_east = passed_along(west, -1)
    *nodes, ap, meta, counts = arrange(z, bound_tiles, tile_nbrs, live_tiles, features, cot, adjacency)
    f0, m1 = tuple(nodes[:2]), tuple(nodes[2:])
    at, wt = turn(z, ap, w_self, w_nbr, w_out)

    west, east, agg_lent = first_lent(z, meta, f0, from_west, from_east, ap, w_self, w_nbr, pre_bias, w_out)
    next_west = passed_along(east, 1)
    next_east = passed_along(west, -1)
    f1_lent, f1_rest, section_out, agg_rest = first_rest(
        z, meta, bound_tiles, live_tiles, f0, from_west, from_east, ap, w_self, w_nbr, pre_bias, w_out,
        west, east,
    )
    f1, agg0 = (f1_lent, f1_rest), (agg_lent, agg_rest)
    hidden = second_own(z, m1, wt)
    act0, slope, ready = saved(z, f0, agg0, w_self, w_nbr, pre_bias)

    agg1, act1, dpre1, dagg1, to_west, to_east = second(
        z, meta, counts, f1, next_west, next_east, ap, at, hidden, w_self, w_nbr, pre_bias, wt, ready
    )
    back_west = passed_along(to_east, 1)
    back_east = passed_along(to_west, -1)
    part, upstream = input_grad(z, 1, meta, counts, m1, dpre1, dagg1, at, wt)
    grads, m0_rest, dpre_rest, dagg_rest, outer = early_rest(
        z, meta, counts, live_tiles, upstream, slope, at, wt
    )
    late = pair_sums(plane, weight_grads(z, plane, f1, agg1, act1, m1, dpre1, "weight_grads1"))
    section_out, ready = second_out(z, bound_tiles, live_tiles, f1, act1, w_out, section_out)

    m0_lent, dpre_lent, dagg_lent, grads, to_west, to_east = early_lent(
        z, meta, counts, bound_tiles, part, back_west, back_east, slope, outer, at, wt, grads,
        (ready, late),
    )
    back_west = passed_along(to_east, 1)
    back_east = passed_along(to_west, -1)
    m0, dpre0, dagg0 = (m0_lent, m0_rest), (dpre_lent, dpre_rest), (dagg_lent, dagg_rest)
    halves = weight_grads(z, plane, f0, agg0, act0, m0, dpre0, "weight_grads0")

    def last(late, halves, m0, dpre0, dagg0, meta, counts, at, wt):
        sums = share_totals(plane, late, halves)
        return (sums, *input_grad(z, 0, meta, counts, m0, dpre0, dagg0, at, wt))

    args = (late, halves, m0, dpre0, dagg0, meta, counts, at, wt)
    shapes = jax.eval_shape(last, *args)
    totals, part, rest = lax.cond(
        live_tiles[0] > 0, last, lambda *_: tuple(jnp.zeros(a.shape, a.dtype) for a in shapes), *args
    )
    grads, grad_self, grad_nbr, grad_bias, grad_out = finish(
        z, plane, bound_tiles, part, rest, back_west, back_east, totals, grads
    )
    return (
        section_out.reshape(2, t * r, c),
        grads.reshape(2, t * r, c),
        grad_self,
        grad_nbr,
        grad_bias,
        grad_out,
    )


def solution(mesh):
    rows = P(AXES)
    in_specs = (rows, rows, rows, rows, rows, rows, P(), P(), P(), P())
    out_specs = (P(None, AXES), P(None, AXES), P(), P(), P(), P())
    return jax.shard_map(
        per_device, mesh=mesh, in_specs=in_specs, out_specs=out_specs, check_vma=False
    )
```

```python
import jax
import jax.numpy as jnp
from jax import lax
from jax.experimental import pallas as pl
from jax.experimental.pallas import tpu as pltpu
from jax.sharding import PartitionSpec as P

AXES = ("dom", "phase", "feat")
PLANE = ("dom", "phase")
BF16 = jnp.bfloat16
F32 = jnp.float32
UNROLL = 8
ANY = pl.BlockSpec(memory_space=pl.ANY)
SMEM = pl.BlockSpec(memory_space=pltpu.SMEM)
VMEM = pl.BlockSpec(memory_space=pltpu.VMEM)
MIB = 1024 * 1024
TOKEN = jax.ShapeDtypeStruct((8, 128), F32)


class Sizes:
    def __init__(self, adjacency, features, bound):
        self.tiles, self.slots, self.rows, _ = adjacency.shape
        self.cols = features.shape[-1]
        self.edge = bound.shape[-1]
        self.lent = 2 * self.edge
        self.rest = self.tiles - self.lent
        self.ext = self.tiles + self.lent
        self.pairs = self.tiles * self.slots
        self.group = next(g for g in (4, 2, 1) if self.edge % g == 0 and self.rest % g == 0)
        self.parts = ((0, 0, self.lent), (1, self.lent, self.rest))

    def nodes(self, count, dtype=BF16):
        return jax.ShapeDtypeStruct((count, self.rows, self.cols), dtype)

    def held(self, count, dtype=BF16):
        return pltpu.VMEM((count, self.rows, self.cols), dtype)

    def flat(self, value):
        return value.reshape(self.group * self.rows, self.cols)

    def tiled(self, value):
        return value.reshape(self.group, self.rows, self.cols)


def group_of(z, array, part, first):
    if isinstance(array, tuple):
        base = z.lent if part else 0
        return array[part].at[pl.ds(first - base, z.group)]
    return array.at[pl.ds(first, z.group)]


def each_group(z, body, parts=(0, 1), unroll=1):
    for part, base, count in z.parts:
        if part in parts:

            @pl.loop(0, count // z.group, unroll=unroll)
            def _(s):
                body(part, base + s * z.group)


def passed_along(value, steps):
    count = lax.axis_size(AXES)
    return lax.ppermute(value, AXES, [(i, (i + steps) % count) for i in range(count)])


def dot(a, b):
    return jnp.dot(a, b, preferred_element_type=F32)


def dot_rows(a, b):
    return lax.dot_general(a, b, (((0,), (0,)), ((), ())), preferred_element_type=F32)


def call(kernel, name, in_specs, out_specs, out_shape, scratch, limit, args, aliases=None):
    return pl.pallas_call(
        kernel,
        in_specs=in_specs,
        out_specs=out_specs,
        out_shape=out_shape,
        scratch_shapes=scratch,
        input_output_aliases=aliases or {},
        compiler_params=pltpu.CompilerParams(vmem_limit_bytes=limit * MIB),
        cost_estimate=pl.CostEstimate(flops=1000, bytes_accessed=1000, transcendentals=0),
        name=name,
    )(*args)


def sigmoid(v):
    return 0.5 * jnp.tanh(0.5 * v) + 0.5


def lend(z, bound, features):
    def kernel(bound, feats, west, east, sems):
        copies = []
        for i in range(z.edge):
            for side, target in ((0, west), (1, east)):
                copy = pltpu.make_async_copy(
                    feats.at[bound[0, side, i]], target.at[i], sems.at[side * z.edge + i]
                )
                copy.start()
                copies.append(copy)
        for copy in copies:
            copy.wait()

    return call(
        kernel,
        "lend",
        [SMEM, ANY],
        [VMEM, VMEM],
        [z.nodes(z.edge), z.nodes(z.edge)],
        [pltpu.SemaphoreType.DMA((z.lent,))],
        56,
        (bound, features),
    )


def arrange(z, bound, nbrs, live, features, cot, adjacency):
    s4 = z.slots

    def kernel(bound, nbrs, live, feats, cot, adj, f_lent, f_rest, m_lent, m_rest, ap, meta, counts, inverse, sems):
        copies = []

        def start(source, target):
            copy = pltpu.make_async_copy(source, target, sems.at[len(copies)])
            copy.start()
            copies.append(copy)

        tail = pl.ds(z.lent, z.rest)
        start(adj.at[tail], ap.at[tail])
        start(feats.at[tail], f_rest)
        start(cot.at[tail], m_rest)
        for i in range(z.lent):
            tile = bound[0, i // z.edge, i % z.edge]
            inverse[tile] = i
            start(adj.at[tile], ap.at[i])
            start(feats.at[tile], f_lent.at[i])
            start(cot.at[tile], m_lent.at[i])

        def kind_of(position, target):
            return jnp.where(target < z.tiles, 0, jnp.where(position < z.lent, 2, 1))

        def step(kind, sums):
            return tuple(total + jnp.where(kind == i, 1, 0) for i, total in enumerate(sums))

        def count(position, sums):
            clipped = jnp.minimum(position, z.lent - 1)
            tile = jnp.where(position < z.lent, bound[0, clipped // z.edge, clipped % z.edge], position)
            for k in range(s4):
                target = nbrs[tile, k]
                moved = jnp.where(target < z.lent, inverse[jnp.minimum(target, z.lent - 1)], target)
                meta[position * s4 + k] = moved
                sums = step(kind_of(position, moved), sums)
            return sums

        zero = jnp.int32(0)
        own, outer, lent = lax.fori_loop(0, z.tiles, count, (zero, zero, zero))
        counts[0] = own
        counts[1] = outer
        counts[2] = lent

        def put(position, sums):
            for k in range(s4):
                target = meta[position * s4 + k]
                kind = kind_of(position, target)
                slot = jnp.where(kind == 0, sums[0], jnp.where(kind == 1, sums[1], sums[2]))
                meta[z.pairs + slot] = position * s4 + k
                meta[2 * z.pairs + slot] = target
                sums = step(kind, sums)
            return sums

        lax.fori_loop(0, z.tiles, put, (zero, own, own + outer))
        for copy in copies:
            copy.wait()

        @pl.loop(0, z.rest)
        def _(i):
            @pl.when(z.lent + i >= live[0])
            def _():
                m_rest[i] = jnp.zeros((z.rows, z.cols), BF16)

    return call(
        kernel,
        "arrange",
        [SMEM, SMEM, SMEM, ANY, ANY, ANY],
        [VMEM] * 5 + [SMEM, SMEM],
        [
            z.nodes(z.lent),
            z.nodes(z.rest),
            z.nodes(z.lent),
            z.nodes(z.rest),
            jax.ShapeDtypeStruct(adjacency.shape, BF16),
            jax.ShapeDtypeStruct((3 * z.pairs,), jnp.int32),
            jax.ShapeDtypeStruct((8,), jnp.int32),
        ],
        [pltpu.SMEM((z.lent,), jnp.int32), pltpu.SemaphoreType.DMA((3 * z.lent + 3,))],
        6,
        (bound, nbrs, live, features, cot, adjacency),
    )


def turn(z, ap, w_self, w_nbr, w_out):
    def kernel(ap, ws, wn, wo, at, wt):
        for layer in range(2):
            wt[layer, 0] = ws[layer].T
            wt[layer, 1] = wn[layer].T
            wt[layer, 2] = wo[layer].T

        @pl.loop(0, z.tiles)
        def _(q):
            for k in range(z.slots):
                at[q * z.slots + k] = ap[q, k].T

    return call(
        kernel,
        "turn",
        [VMEM] * 4,
        [VMEM, VMEM],
        [
            jax.ShapeDtypeStruct((z.pairs, z.rows, z.rows), BF16),
            jax.ShapeDtypeStruct((2, 3, z.cols, z.cols), BF16),
        ],
        [],
        6,
        (ap, w_self, w_nbr, w_out),
    )


def fill_extended(z, own, fw, fe, ext):
    ext[pl.ds(0, z.lent)] = own[0][...]
    ext[pl.ds(z.lent, z.rest)] = own[1][...]
    ext[pl.ds(z.tiles, z.edge)] = fw[...]
    ext[pl.ds(z.tiles + z.edge, z.edge)] = fe[...]


def aggregate(z, meta, first, ap, ext):
    rows = []
    for g in range(z.group):
        base = (first + g) * z.slots
        picked = jnp.concatenate([ext[meta[base + k]] for k in range(z.slots)], axis=0)
        blocks = jnp.concatenate([ap[first + g, k] for k in range(z.slots)], axis=1)
        rows.append(dot(blocks, picked).astype(BF16))
    return jnp.concatenate(rows, axis=0)


def live_rows(z, value, first, live):
    parts = []
    for g in range(z.group):
        part = value[g * z.rows : (g + 1) * z.rows]
        parts.append(jnp.where(first + g < live, part, jnp.zeros_like(part)))
    return jnp.concatenate(parts, axis=0)


def first_lent(z, meta, f0, fw, fe, ap, w_self, w_nbr, bias, w_out):
    def kernel(meta, f_lent, f_rest, fw, fe, ap, ws, wn, bias, wo, west, east, agg, ext):
        fill_extended(z, (f_lent, f_rest), fw, fe, ext)

        def work(first, target, offset):
            here = pl.ds(first, z.group)
            f = z.flat(ext[here])
            aggs = aggregate(z, meta, first, ap, ext)
            agg[here] = z.tiled(aggs)
            pre = dot(f, ws[0]) + dot(aggs, wn[0]) + bias[0:1, :]
            act = (pre * sigmoid(pre)).astype(BF16)
            target[pl.ds(offset, z.group)] = z.tiled((f.astype(F32) + dot(act, wo[0])).astype(BF16))

        @pl.loop(0, z.edge // z.group)
        def _(s):
            work(s * z.group, west, s * z.group)
            work(z.edge + s * z.group, east, s * z.group)

    return call(
        kernel,
        "first_lent",
        [SMEM] + [VMEM] * 9,
        [VMEM] * 3,
        [z.nodes(z.edge), z.nodes(z.edge), z.nodes(z.lent)],
        [z.held(z.ext)],
        8,
        (meta, *f0, fw, fe, ap, w_self, w_nbr, bias, w_out),
    )


def first_rest(z, meta, bound, live, f0, fw, fe, ap, w_self, w_nbr, bias, w_out, west, east):
    def kernel(meta, bound, live, f_lent, f_rest, fw, fe, ap, ws, wn, bias, wo, west, east,
               f1_lent, f1_rest, out, agg, ext, sems):
        copies = []
        for i in range(z.edge):
            for side, source in ((0, west), (1, east)):
                copy = pltpu.make_async_copy(
                    source.at[i], out.at[0, bound[0, side, i]], sems.at[side * z.edge + i]
                )
                copy.start()
                copies.append(copy)
        fill_extended(z, (f_lent, f_rest), fw, fe, ext)
        f1_lent[pl.ds(0, z.edge)] = west[...]
        f1_lent[pl.ds(z.edge, z.edge)] = east[...]

        def work(part, first):
            f = z.flat(ext[pl.ds(first, z.group)])
            aggs = aggregate(z, meta, first, ap, ext)
            here = pl.ds(first - z.lent, z.group)
            agg[here] = z.tiled(aggs)
            pre = dot(f, ws[0]) + dot(aggs, wn[0]) + bias[0:1, :]
            act = (pre * sigmoid(pre)).astype(BF16)
            res = live_rows(z, f.astype(F32) + dot(act, wo[0]), first, live[0])
            f1_rest[here] = z.tiled(res.astype(BF16))

        each_group(z, work, (1,))
        copy = pltpu.make_async_copy(f1_rest, out.at[0, pl.ds(z.lent, z.rest)], sems.at[z.lent])
        copy.start()
        for other in copies:
            other.wait()
        copy.wait()

    return call(
        kernel,
        "first_rest",
        [SMEM] * 3 + [VMEM] * 11,
        [VMEM, VMEM, ANY, VMEM],
        [
            z.nodes(z.lent),
            z.nodes(z.rest),
            jax.ShapeDtypeStruct((2, z.tiles, z.rows, z.cols), BF16),
            z.nodes(z.rest),
        ],
        [z.held(z.ext), pltpu.SemaphoreType.DMA((1 + z.lent,))],
        10,
        (meta, bound, live, *f0, fw, fe, ap, w_self, w_nbr, bias, w_out, west, east),
    )


def second_own(z, m1, wt):
    def kernel(m_lent, m_rest, wt, hidden):
        def work(part, first):
            m = z.flat(group_of(z, (m_lent, m_rest), part, first)[...])
            hidden[pl.ds(first, z.group)] = z.tiled(dot(m, wt[1, 2]))

        each_group(z, work)

    return call(
        kernel,
        "second_own",
        [VMEM] * 3,
        VMEM,
        z.nodes(z.tiles, F32),
        [],
        8,
        (*m1, wt),
    )


def saved(z, f0, agg0, w_self, w_nbr, bias):
    def kernel(f_lent, f_rest, a_lent, a_rest, ws, wn, bias, act, slope, token):
        token[...] = jnp.zeros_like(token)

        def work(part, first):
            f = z.flat(group_of(z, (f_lent, f_rest), part, first)[...])
            aggs = z.flat(group_of(z, (a_lent, a_rest), part, first)[...])
            pre = dot(f, ws[0]) + dot(aggs, wn[0]) + bias[0:1, :]
            sig = sigmoid(pre)
            here = pl.ds(first, z.group)
            act[here] = z.tiled((pre * sig).astype(BF16))
            slope[here] = z.tiled(sig * (1.0 + pre * (1.0 - sig)))

        each_group(z, work)

    return call(
        kernel,
        "saved",
        [VMEM] * 7,
        [VMEM] * 3,
        [z.nodes(z.tiles), z.nodes(z.tiles, F32), TOKEN],
        [],
        10,
        (*f0, *agg0, w_self, w_nbr, bias),
    )


def spread(z, meta, start, stop, at, source, acc, shift, spare):
    def body(i, carry):
        for u in range(UNROLL):
            entry = start + i * UNROLL + u
            inside = entry < stop
            entry = jnp.minimum(entry, z.pairs - 1)
            target = jnp.where(inside, meta[2 * z.pairs + entry] - shift, spare)
            pair = meta[z.pairs + entry]
            acc[target] += dot(at[pair], source(pair // z.slots))
        return carry

    lax.fori_loop(0, (stop - start + UNROLL - 1) // UNROLL, body, 0)


def second(z, meta, counts, f1, fw, fe, ap, at, hidden, w_self, w_nbr, bias, wt, after):
    def kernel(meta, counts, f_lent, f_rest, fw, fe, ap, at, hidden, ws, wn, bias, wt, _after,
               agg, act, dpre, dagg, to_west, to_east, ext, acc):
        fill_extended(z, (f_lent, f_rest), fw, fe, ext)
        acc[...] = jnp.zeros_like(acc)

        def work(part, first):
            here = pl.ds(first, z.group)
            aggs = aggregate(z, meta, first, ap, ext)
            agg[here] = z.tiled(aggs)
            pre = dot(z.flat(ext[here]), ws[1]) + dot(aggs, wn[1]) + bias[1:2, :]
            sig = sigmoid(pre)
            act[here] = z.tiled((pre * sig).astype(BF16))
            grad = (z.flat(hidden[here]) * (sig * (1.0 + pre * (1.0 - sig)))).astype(BF16)
            dpre[here] = z.tiled(grad)
            dagg[here] = z.tiled(dot(grad, wt[1, 1]).astype(BF16))

        each_group(z, work, unroll=2)
        spread(z, meta, counts[0], z.pairs, at, lambda q: dagg[q], acc, z.tiles, z.lent)
        to_west[...] = acc[pl.ds(0, z.edge)].astype(BF16)
        to_east[...] = acc[pl.ds(z.edge, z.edge)].astype(BF16)

    return call(
        kernel,
        "second",
        [SMEM] * 2 + [VMEM] * 12,
        [VMEM] * 6,
        [z.nodes(z.tiles)] * 4 + [z.nodes(z.edge)] * 2,
        [z.held(z.ext), z.held(z.lent + 1, F32)],
        12,
        (meta, counts, *f1, fw, fe, ap, at, hidden, w_self, w_nbr, bias, wt, after),
    )


class Plane:
    def __init__(self):
        dom, phase = lax.axis_size("dom"), lax.axis_size("phase")
        core = 2 if dom % 2 == 0 else 1
        self.sizes = (core, dom // core, phase)
        self.count = dom * phase
        place = lax.axis_index("dom")
        self.me = jnp.stack([lax.rem(place, core), place // core, lax.axis_index("phase")]).astype(jnp.int32)

    def piece_of(self, me, steps):
        at = [lax.rem(me[i] + (steps[i] + n) % n, n) for i, n in enumerate(self.sizes)]
        return (at[0] * self.sizes[1] + at[1]) * self.sizes[2] + at[2]

    def passed(self, value, dim, steps):
        pairs = []
        for c in range(self.sizes[0]):
            for d in range(self.sizes[1]):
                for p in range(self.sizes[2]):
                    to = [c, d, p]
                    to[dim] = (to[dim] + steps) % self.sizes[dim]
                    source = (d * self.sizes[0] + c) * self.sizes[2] + p
                    target = (to[1] * self.sizes[0] + to[0]) * self.sizes[2] + to[2]
                    pairs.append((source, target))
        return lax.ppermute(value, PLANE, pairs)

    def received(self, parts, dim):
        return [parts[0]] + [self.passed(parts[i], dim, i) for i in range(1, self.sizes[dim])]


def weight_grads(z, plane, f, agg, act, m, dpre, name):
    c = z.cols
    piece = -(-(3 * c + 1) // (plane.count * 16)) * 16
    core, ahead, side = plane.sizes
    arrays = (f, agg, act, m, dpre)
    flat_args = [x for a in arrays for x in (a if isinstance(a, tuple) else (a,))]

    def kernel(me, *refs):
        refs = list(refs)
        f, agg, act, m, dpre = [
            (refs.pop(0), refs.pop(0)) if isinstance(a, tuple) else refs.pop(0) for a in arrays
        ]
        outs, acc = refs[:-1], refs[-1]
        acc[...] = jnp.zeros_like(acc)

        def work(part, first):
            def rows(array):
                return z.flat(group_of(z, array, part, first)[...])

            grad = rows(dpre)
            acc[pl.ds(0, c), :] += dot_rows(rows(f), grad)
            acc[pl.ds(c, c), :] += dot_rows(rows(agg), grad)
            acc[pl.ds(2 * c, c), :] += dot_rows(rows(act), rows(m))
            acc[pl.ds(3 * c, 1), :] += jnp.sum(grad.astype(F32), axis=0, keepdims=True)

        each_group(z, work)
        for i, out in enumerate(outs):
            for j in range(ahead):
                for k in range(side):
                    owner = pl.multiple_of(plane.piece_of(me, (i, j, k)) * piece, 16)
                    out[j, k] = acc[pl.ds(owner, piece), :].astype(BF16)

    return call(
        kernel,
        name,
        [SMEM] + [VMEM] * len(flat_args),
        [VMEM] * core,
        [jax.ShapeDtypeStruct((ahead, side, piece, c), BF16)] * core,
        [pltpu.VMEM((piece * plane.count, c), F32)],
        14,
        (plane.me, *flat_args),
    )


def added(values, split=False, after=None):
    shape = values[0].shape
    count = shape[0] if split else 1

    def kernel(*refs):
        outs = refs[-count:]
        for i, out in enumerate(outs):
            parts = [ref[i] if split else ref[...] for ref in refs[: len(values)]]
            total = parts[0].astype(F32)
            for part in parts[1:]:
                total = total + part.astype(F32)
            out[...] = total.astype(BF16)

    args = list(values) if after is None else [*values, after]
    outs = call(
        kernel,
        "added",
        [VMEM] * len(args),
        [VMEM] * count,
        [jax.ShapeDtypeStruct(shape[1:] if split else shape, BF16)] * count,
        [],
        8,
        args,
    )
    return outs if split else outs[0]


def plane_share(plane, pieces, after=None):
    parts = added(plane.received(pieces, 0), split=True)
    parts = added(plane.received(parts, 1), split=True)
    return added(plane.received(parts, 2), after=after)


def share_totals(plane, share):
    lines = lax.axis_size("feat")
    if lines & (lines - 1) == 0:
        step = 1
        while step < lines:
            other = lax.ppermute(share, "feat", [(i, i ^ step) for i in range(lines)])
            share = added([share, other])
            step *= 2
    else:
        share = lax.psum(share.astype(F32), "feat").astype(BF16)
    for dim in (2, 1):
        size = plane.sizes[dim]
        share = jnp.stack([share] + [plane.passed(share, dim, i) for i in range(1, size)])
    return [share] + [plane.passed(share, 0, i) for i in range(1, plane.sizes[0])]


def second_out(z, bound, live, f1, act, w_out, out):
    def kernel(bound, live, f_lent, f_rest, act, wo, _out, out, token, keep, sems):
        copies = []
        token[...] = jnp.zeros_like(token)

        def work(part, first):
            f = z.flat(group_of(z, (f_lent, f_rest), part, first)[...])
            res = f.astype(F32) + dot(z.flat(act[pl.ds(first, z.group)]), wo[1])
            keep[pl.ds(first, z.group)] = z.tiled(live_rows(z, res, first, live[0]).astype(BF16))

        each_group(z, work, (0,))
        for i in range(z.lent):
            copy = pltpu.make_async_copy(
                keep.at[i], out.at[1, bound[0, i // z.edge, i % z.edge]], sems.at[i]
            )
            copy.start()
            copies.append(copy)
        each_group(z, work, (1,))
        tail = pl.ds(z.lent, z.rest)
        copy = pltpu.make_async_copy(keep.at[tail], out.at[1, tail], sems.at[z.lent])
        copy.start()
        copies.append(copy)
        for copy in copies:
            copy.wait()

    return call(
        kernel,
        "second_out",
        [SMEM] * 2 + [VMEM] * 4 + [ANY],
        [ANY, VMEM],
        [jax.ShapeDtypeStruct(out.shape, BF16), TOKEN],
        [z.held(z.tiles), pltpu.SemaphoreType.DMA((z.lent + 1,))],
        12,
        (bound, live, *f1, act, w_out, out),
        {6: 0},
    )


def input_grad(z, layer, meta, counts, m, dpre, dagg, at, wt):
    arrays = (m, dpre, dagg)
    flat_args = [x for a in arrays for x in (a if isinstance(a, tuple) else (a,))]

    def kernel(meta, counts, *refs):
        refs = list(refs)
        m, dpre, dagg = [
            (refs.pop(0), refs.pop(0)) if isinstance(a, tuple) else refs.pop(0) for a in arrays
        ]
        at, wt, part_out, rest_out, token, acc = refs
        token[...] = jnp.zeros_like(token)

        def direct(part, first):
            mine = z.flat(group_of(z, m, part, first)[...]).astype(F32)
            res = mine + dot(z.flat(group_of(z, dpre, part, first)[...]), wt[layer, 0])
            acc[pl.ds(first, z.group)] = z.tiled(res)

        each_group(z, direct)

        def source(q):
            if not isinstance(dagg, tuple):
                return dagg[q]
            lent = dagg[0][jnp.minimum(q, z.lent - 1)]
            rest = dagg[1][jnp.maximum(q - z.lent, 0)]
            return jnp.where(q < z.lent, lent, rest)

        spread(z, meta, 0, counts[0], at, source, acc, 0, z.tiles)
        part_out[...] = acc[pl.ds(0, z.lent)]
        rest_out[...] = acc[pl.ds(z.lent, z.rest)].astype(BF16)

    return call(
        kernel,
        "input_grad%d" % layer,
        [SMEM] * 2 + [VMEM] * (len(flat_args) + 2),
        [VMEM] * 3,
        [z.nodes(z.lent, F32), z.nodes(z.rest), TOKEN],
        [z.held(z.tiles + 1, F32)],
        28,
        [meta, counts, *flat_args, at, wt],
    )


def early_rest(z, meta, counts, live, upstream, slope, at, wt):
    def kernel(meta, counts, live, g, slope, at, wt, grads, m, dpre, dagg, outer, acc, sem):
        copy = pltpu.make_async_copy(g, grads.at[1, pl.ds(z.lent, z.rest)], sem)
        copy.start()

        def work(part, first):
            here = pl.ds(first - z.lent, z.group)
            masked = live_rows(z, z.flat(g[here]), first, live[0])
            m[here] = z.tiled(masked)
            grad = dot(masked, wt[0, 2]) * z.flat(slope[pl.ds(first, z.group)])
            grad = grad.astype(BF16)
            dpre[here] = z.tiled(grad)
            dagg[here] = z.tiled(dot(grad, wt[0, 1]).astype(BF16))

        each_group(z, work, (1,))
        acc[...] = jnp.zeros_like(acc)

        def source(q):
            return dagg[jnp.maximum(q - z.lent, 0)]

        spread(z, meta, counts[0], counts[0] + counts[1], at, source, acc, z.tiles, z.lent)
        outer[...] = acc[pl.ds(0, z.lent)]
        copy.wait()

    return call(
        kernel,
        "early_rest",
        [SMEM] * 3 + [VMEM] * 4,
        [ANY] + [VMEM] * 4,
        [jax.ShapeDtypeStruct((2, z.tiles, z.rows, z.cols), BF16)]
        + [z.nodes(z.rest)] * 3
        + [z.nodes(z.lent, F32)],
        [z.held(z.lent + 1, F32), pltpu.SemaphoreType.DMA],
        14,
        (meta, counts, live, upstream, slope, at, wt),
    )


def early_lent(z, meta, counts, bound, part, fw, fe, slope, outer, at, wt, grads, after):
    def kernel(meta, counts, bound, part, fw, fe, slope, outer, at, wt, _g, _ready, _late,
               m, dpre, dagg, grads, to_west, to_east, acc, sems):
        def work(first, got):
            here = pl.ds(first, z.group)
            g = z.flat((part[here] + got.astype(F32)).astype(BF16))
            m[here] = z.tiled(g)
            grad = (dot(g, wt[0, 2]) * z.flat(slope[here])).astype(BF16)
            dpre[here] = z.tiled(grad)
            dagg[here] = z.tiled(dot(grad, wt[0, 1]).astype(BF16))

        @pl.loop(0, z.edge // z.group)
        def _(s):
            here = pl.ds(s * z.group, z.group)
            work(s * z.group, fw[here])
            work(z.edge + s * z.group, fe[here])

        copies = [
            pltpu.make_async_copy(m.at[i], grads.at[1, bound[0, i // z.edge, i % z.edge]], sems.at[i])
            for i in range(z.lent)
        ]
        for copy in copies:
            copy.start()
        acc[pl.ds(0, z.lent)] = outer[...]
        acc[z.lent] = jnp.zeros((z.rows, z.cols), F32)

        def source(q):
            return dagg[jnp.minimum(q, z.lent - 1)]

        spread(z, meta, counts[0] + counts[1], z.pairs, at, source, acc, z.tiles, z.lent)
        to_west[...] = acc[pl.ds(0, z.edge)].astype(BF16)
        to_east[...] = acc[pl.ds(z.edge, z.edge)].astype(BF16)
        for copy in copies:
            copy.wait()

    return call(
        kernel,
        "early_lent",
        [SMEM] * 3 + [VMEM] * 7 + [ANY, VMEM, VMEM],
        [VMEM] * 3 + [ANY] + [VMEM] * 2,
        [z.nodes(z.lent)] * 3 + [jax.ShapeDtypeStruct(grads.shape, BF16)] + [z.nodes(z.edge)] * 2,
        [z.held(z.lent + 1, F32), pltpu.SemaphoreType.DMA((z.lent,))],
        16,
        (meta, counts, bound, part, fw, fe, slope, outer, at, wt, grads, *after),
        {10: 3},
    )


def finish(z, plane, bound, part, rest, fw, fe, early, late, grads):
    c = z.cols
    piece = early[0].shape[2]
    core, ahead, side = plane.sizes

    def kernel(me, bound, part, rest, fw, fe, *refs):
        totals = refs[: 2 * core]
        _g, grads, g_self, g_nbr, g_bias, g_out, keep, buf, sems = refs[2 * core :]
        copies = [pltpu.make_async_copy(rest, grads.at[0, pl.ds(z.lent, z.rest)], sems.at[z.lent])]
        copies[0].start()
        for i in range(z.lent):
            got = fw[i] if i < z.edge else fe[i - z.edge]
            keep[i] = (part[i] + got.astype(F32)).astype(BF16)
            copy = pltpu.make_async_copy(
                keep.at[i], grads.at[0, bound[0, i // z.edge, i % z.edge]], sems.at[i]
            )
            copy.start()
            copies.append(copy)
        for layer in range(2):
            for i in range(core):
                for j in range(ahead):
                    for k in range(side):
                        start = pl.multiple_of(plane.piece_of(me, (-i, -j, -k)) * piece, 16)
                        buf[pl.ds(start, piece), :] = totals[layer * core + i][j, k].astype(F32)
            g_self[layer] = buf[pl.ds(0, c), :]
            g_nbr[layer] = buf[pl.ds(c, c), :]
            g_out[layer] = buf[pl.ds(2 * c, c), :]
            g_bias[layer : layer + 1, :] = buf[pl.ds(3 * c, 1), :]
        for copy in copies:
            copy.wait()

    square = jax.ShapeDtypeStruct((2, c, c), F32)
    return call(
        kernel,
        "finish",
        [SMEM] * 2 + [VMEM] * (4 + 2 * core) + [ANY],
        [ANY] + [VMEM] * 4,
        [jax.ShapeDtypeStruct(grads.shape, BF16), square, square, jax.ShapeDtypeStruct((2, c), F32), square],
        [
            z.held(z.lent),
            pltpu.VMEM((piece * plane.count, c), F32),
            pltpu.SemaphoreType.DMA((z.lent + 1,)),
        ],
        14,
        (plane.me, bound, part, rest, fw, fe, *early, *late, grads),
        {6 + 2 * core: 0},
    )


def per_device(
    node_in, out_cot, adjacency, tile_nbrs, bound_tiles, live_tiles, w_self, w_nbr, pre_bias, w_out
):
    z = Sizes(adjacency, node_in, bound_tiles)
    t, r, c = z.tiles, z.rows, z.cols
    features = node_in.reshape(t, r, c)
    cot = out_cot.reshape(t, r, c)
    plane = Plane()

    west, east = lend(z, bound_tiles, features)
    from_west = passed_along(east, 1)
    from_east = passed_along(west, -1)
    *nodes, ap, meta, counts = arrange(z, bound_tiles, tile_nbrs, live_tiles, features, cot, adjacency)
    f0, m1 = tuple(nodes[:2]), tuple(nodes[2:])
    at, wt = turn(z, ap, w_self, w_nbr, w_out)

    west, east, agg_lent = first_lent(z, meta, f0, from_west, from_east, ap, w_self, w_nbr, pre_bias, w_out)
    next_west = passed_along(east, 1)
    next_east = passed_along(west, -1)
    f1_lent, f1_rest, section_out, agg_rest = first_rest(
        z, meta, bound_tiles, live_tiles, f0, from_west, from_east, ap, w_self, w_nbr, pre_bias, w_out,
        west, east,
    )
    f1, agg0 = (f1_lent, f1_rest), (agg_lent, agg_rest)
    hidden = second_own(z, m1, wt)
    act0, slope, ready = saved(z, f0, agg0, w_self, w_nbr, pre_bias)

    agg1, act1, dpre1, dagg1, to_west, to_east = second(
        z, meta, counts, f1, next_west, next_east, ap, at, hidden, w_self, w_nbr, pre_bias, wt, ready
    )
    back_west = passed_along(to_east, 1)
    back_east = passed_along(to_west, -1)
    part, upstream, _ = input_grad(z, 1, meta, counts, m1, dpre1, dagg1, at, wt)
    grads, m0_rest, dpre_rest, dagg_rest, outer = early_rest(
        z, meta, counts, live_tiles, upstream, slope, at, wt
    )
    late = plane_share(plane, weight_grads(z, plane, f1, agg1, act1, m1, dpre1, "weight_grads1"))
    section_out, ready = second_out(z, bound_tiles, live_tiles, f1, act1, w_out, section_out)

    m0_lent, dpre_lent, dagg_lent, grads, to_west, to_east = early_lent(
        z, meta, counts, bound_tiles, part, back_west, back_east, slope, outer, at, wt, grads,
        (ready, late),
    )
    back_west = passed_along(to_east, 1)
    back_east = passed_along(to_west, -1)
    m0, dpre0, dagg0 = (m0_lent, m0_rest), (dpre_lent, dpre_rest), (dagg_lent, dagg_rest)
    halves = weight_grads(z, plane, f0, agg0, act0, m0, dpre0, "weight_grads0")

    def last(late, halves, m0, dpre0, dagg0, meta, counts, at, wt):
        part, rest, done = input_grad(z, 0, meta, counts, m0, dpre0, dagg0, at, wt)
        early = plane_share(plane, halves, done)
        return share_totals(plane, early), share_totals(plane, late), part, rest

    args = (late, halves, m0, dpre0, dagg0, meta, counts, at, wt)
    shapes = jax.eval_shape(last, *args)
    early, late, part, rest = lax.cond(
        live_tiles[0] > 0,
        last,
        lambda *_: jax.tree.map(lambda a: jnp.zeros(a.shape, a.dtype), shapes),
        *args,
    )
    grads, grad_self, grad_nbr, grad_bias, grad_out = finish(
        z, plane, bound_tiles, part, rest, back_west, back_east, early, late, grads
    )
    return (
        section_out.reshape(2, t * r, c),
        grads.reshape(2, t * r, c),
        grad_self,
        grad_nbr,
        grad_bias,
        grad_out,
    )


def solution(mesh):
    rows = P(AXES)
    in_specs = (rows, rows, rows, rows, rows, rows, P(), P(), P(), P())
    out_specs = (P(None, AXES), P(None, AXES), P(), P(), P(), P())
    return jax.shard_map(
        per_device, mesh=mesh, in_specs=in_specs, out_specs=out_specs, check_vma=False
    )
```

```python
import jax
import jax.numpy as jnp
from jax import lax
from jax.experimental import pallas as pl
from jax.experimental.pallas import tpu as pltpu
from jax.sharding import PartitionSpec as P

AXES = ("dom", "phase", "feat")
PLANE = ("dom", "phase")
BF16 = jnp.bfloat16
F32 = jnp.float32
ANY = pl.BlockSpec(memory_space=pl.ANY)
SMEM = pl.BlockSpec(memory_space=pltpu.SMEM)
VMEM = pl.BlockSpec(memory_space=pltpu.VMEM)
MIB = 1024 * 1024
TOKEN = jax.ShapeDtypeStruct((8, 128), F32)


class Sizes:
    def __init__(self, adjacency, features, bound):
        self.tiles, self.slots, self.rows, _ = adjacency.shape
        self.cols = features.shape[-1]
        self.edge = bound.shape[-1]
        self.lent = 2 * self.edge
        self.rest = self.tiles - self.lent
        self.ext = self.tiles + self.lent
        self.pairs = self.tiles * self.slots
        self.group = next(g for g in (4, 2, 1) if self.edge % g == 0 and self.rest % g == 0)
        self.parts = ((0, 0, self.lent), (1, self.lent, self.rest))
        self.index = Index(self)

    def nodes(self, count, dtype=BF16):
        return jax.ShapeDtypeStruct((count, self.rows, self.cols), dtype)

    def held(self, count, dtype=BF16):
        return pltpu.VMEM((count, self.rows, self.cols), dtype)

    def flat(self, value):
        return value.reshape(self.group * self.rows, self.cols)

    def tiled(self, value):
        return value.reshape(self.group, self.rows, self.cols)


def group_of(z, array, part, first):
    if isinstance(array, tuple):
        base = z.lent if part else 0
        return array[part].at[pl.ds(first - base, z.group)]
    return array.at[pl.ds(first, z.group)]


def each_group(z, body, parts=(0, 1), unroll=1):
    for part, base, count in z.parts:
        if part in parts:

            @pl.loop(0, count // z.group, unroll=unroll)
            def _(s):
                body(part, base + s * z.group)


def passed_along(value, steps):
    count = lax.axis_size(AXES)
    return lax.ppermute(value, AXES, [(i, (i + steps) % count) for i in range(count)])


def dot(a, b):
    return jnp.dot(a, b, preferred_element_type=F32)


def dot_rows(a, b):
    return lax.dot_general(a, b, (((0,), (0,)), ((), ())), preferred_element_type=F32)


def call(kernel, name, in_specs, out_specs, out_shape, scratch, limit, args, aliases=None):
    return pl.pallas_call(
        kernel,
        in_specs=in_specs,
        out_specs=out_specs,
        out_shape=out_shape,
        scratch_shapes=scratch,
        input_output_aliases=aliases or {},
        compiler_params=pltpu.CompilerParams(vmem_limit_bytes=limit * MIB),
        cost_estimate=pl.CostEstimate(flops=1000, bytes_accessed=1000, transcendentals=0),
        name=name,
    )(*args)


def sigmoid(v):
    return 0.5 * jnp.tanh(0.5 * v) + 0.5


def lend(z, bound, features):
    def kernel(bound, feats, west, east, sems):
        copies = []
        for i in range(z.edge):
            for side, target in ((0, west), (1, east)):
                copy = pltpu.make_async_copy(
                    feats.at[bound[0, side, i]], target.at[i], sems.at[side * z.edge + i]
                )
                copy.start()
                copies.append(copy)
        for copy in copies:
            copy.wait()

    return call(
        kernel,
        "lend",
        [SMEM, ANY],
        [VMEM, VMEM],
        [z.nodes(z.edge), z.nodes(z.edge)],
        [pltpu.SemaphoreType.DMA((z.lent,))],
        56,
        (bound, features),
    )


class Index:
    QUAD = 4

    def __init__(self, z):
        self.first = (0, z.tiles, z.tiles + z.lent, z.tiles + 2 * z.lent, z.tiles + 3 * z.lent)
        self.targets = z.tiles + 3 * z.lent + 1
        self.more = tuple(self.QUAD * self.targets + i * z.pairs for i in range(5))
        self.size = self.QUAD * self.targets + 5 * z.pairs
        self.size = -(-self.size // 8) * 8


def arrange(z, bound, nbrs, live, place, features, cot, adjacency):
    s4 = z.slots
    x = z.index

    def kernel(bound, nbrs, live, place, feats, cot, adj, f_lent, f_rest, m_lent, m_rest, adj_out,
               tiles, reads, blocks, sources, targets, counts, me, inverse, used, sems):
        copies = []
        for i in range(8):
            me[i] = place[i]

        def start(source, target):
            copy = pltpu.make_async_copy(source, target, sems.at[len(copies)])
            copy.start()
            copies.append(copy)

        tail = pl.ds(z.lent, z.rest)
        start(feats.at[tail], f_rest)
        start(cot.at[tail], m_rest)
        start(adj, adj_out)
        for i in range(z.lent):
            tile = bound[0, i // z.edge, i % z.edge]
            inverse[tile] = i
            start(feats.at[tile], f_lent.at[i])
            start(cot.at[tile], m_lent.at[i])

        @pl.loop(0, x.targets)
        def _(i):
            used[i] = 0
            for k in range(x.QUAD):
                blocks[i * x.QUAD + k] = -1
                sources[i * x.QUAD + k] = 0

        for i in range(8):
            counts[i] = 0

        def put(table, target, block, position):
            place = used[target]
            used[target] = place + 1
            fits = place < x.QUAD
            listed = counts[table]
            counts[table] = listed + jnp.where(fits, 0, 1)
            at = jnp.where(fits, target * x.QUAD + place, x.more[0] + table * z.pairs + listed)
            blocks[at] = block
            sources[at] = position
            return at

        @pl.loop(0, z.tiles)
        def _(position):
            clipped = jnp.minimum(position, z.lent - 1)
            tile = jnp.where(position < z.lent, bound[0, clipped // z.edge, clipped % z.edge], position)
            tiles[position] = tile
            for k in range(s4):
                target = nbrs[tile, k]
                moved = jnp.where(target < z.lent, inverse[jnp.minimum(target, z.lent - 1)], target)
                reads[position * s4 + k] = moved
                block = tile * s4 + k
                own = moved < z.tiles
                at = put(jnp.where(own, 0, 1), moved, block, position)
                targets[at] = jnp.where(own, moved, moved - z.tiles)
                lent = position < z.lent
                table = jnp.where(own, 4, jnp.where(lent, 2, 3))
                shift = jnp.where(lent, z.lent, 2 * z.lent)
                at = put(table, jnp.where(own, x.first[4], moved + shift), block, position)
                targets[at] = moved - z.tiles

        for copy in copies:
            copy.wait()

        @pl.loop(0, z.rest)
        def _(i):
            @pl.when(z.lent + i >= live[0])
            def _():
                m_rest[i] = jnp.zeros((z.rows, z.cols), BF16)

    return call(
        kernel,
        "arrange",
        [SMEM] * 4 + [ANY] * 3,
        [VMEM] * 5 + [SMEM] * 7,
        [z.nodes(z.lent), z.nodes(z.rest), z.nodes(z.lent), z.nodes(z.rest)]
        + [jax.ShapeDtypeStruct(adjacency.shape, BF16)]
        + [jax.ShapeDtypeStruct((n,), jnp.int32) for n in (z.tiles, z.pairs, x.size, x.size, x.size, 8, 8)],
        [
            pltpu.SMEM((z.lent,), jnp.int32),
            pltpu.SMEM((x.targets,), jnp.int32),
            pltpu.SemaphoreType.DMA((2 * z.lent + 3,)),
        ],
        12,
        (bound, nbrs, live, place, features, cot, adjacency),
    )


def turn(z, w_self, w_nbr, w_out):
    def kernel(ws, wn, wo, wt):
        for layer in range(2):
            wt[layer, 0] = ws[layer].T
            wt[layer, 1] = wn[layer].T
            wt[layer, 2] = wo[layer].T

    return call(
        kernel,
        "turn",
        [VMEM] * 3,
        VMEM,
        jax.ShapeDtypeStruct((2, 3, z.cols, z.cols), BF16),
        [],
        6,
        (w_self, w_nbr, w_out),
    )


def fill_extended(z, own, fw, fe, ext):
    ext[pl.ds(0, z.lent)] = own[0][...]
    ext[pl.ds(z.lent, z.rest)] = own[1][...]
    ext[pl.ds(z.tiles, z.edge)] = fw[...]
    ext[pl.ds(z.tiles + z.edge, z.edge)] = fe[...]


def aggregate(z, tiles, reads, first, adj, ext):
    rows = []
    for g in range(z.group):
        base = (first + g) * z.slots
        block = tiles[first + g] * z.slots
        picked = jnp.concatenate([ext[reads[base + k]] for k in range(z.slots)], axis=0)
        blocks = jnp.concatenate([adj[block + k] for k in range(z.slots)], axis=1)
        rows.append(dot(blocks, picked).astype(BF16))
    return jnp.concatenate(rows, axis=0)


def live_rows(z, value, first, live):
    parts = []
    for g in range(z.group):
        part = value[g * z.rows : (g + 1) * z.rows]
        parts.append(jnp.where(first + g < live, part, jnp.zeros_like(part)))
    return jnp.concatenate(parts, axis=0)


def first_lent(z, tiles, reads, f0, fw, fe, adj, w_self, w_nbr, bias, w_out):
    def kernel(tiles, reads, f_lent, f_rest, fw, fe, adj, ws, wn, bias, wo, west, east, agg, ext):
        fill_extended(z, (f_lent, f_rest), fw, fe, ext)

        def work(first, target, offset):
            here = pl.ds(first, z.group)
            f = z.flat(ext[here])
            aggs = aggregate(z, tiles, reads, first, adj, ext)
            agg[here] = z.tiled(aggs)
            pre = dot(f, ws[0]) + dot(aggs, wn[0]) + bias[0:1, :]
            act = (pre * sigmoid(pre)).astype(BF16)
            target[pl.ds(offset, z.group)] = z.tiled((f.astype(F32) + dot(act, wo[0])).astype(BF16))

        @pl.loop(0, z.edge // z.group)
        def _(s):
            work(s * z.group, west, s * z.group)
            work(z.edge + s * z.group, east, s * z.group)

    return call(
        kernel,
        "first_lent",
        [SMEM] * 2 + [VMEM] * 9,
        [VMEM] * 3,
        [z.nodes(z.edge), z.nodes(z.edge), z.nodes(z.lent)],
        [z.held(z.ext)],
        12,
        (tiles, reads, *f0, fw, fe, adj, w_self, w_nbr, bias, w_out),
    )


def first_rest(z, tiles, reads, bound, live, f0, fw, fe, adj, w_self, w_nbr, bias, w_out, west, east):
    def kernel(tiles, reads, bound, live, f_lent, f_rest, fw, fe, adj, ws, wn, bias, wo, west, east,
               f1_lent, f1_rest, out, agg, ext, sems):
        copies = []
        for i in range(z.edge):
            for side, source in ((0, west), (1, east)):
                copy = pltpu.make_async_copy(
                    source.at[i], out.at[0, bound[0, side, i]], sems.at[side * z.edge + i]
                )
                copy.start()
                copies.append(copy)
        fill_extended(z, (f_lent, f_rest), fw, fe, ext)
        f1_lent[pl.ds(0, z.edge)] = west[...]
        f1_lent[pl.ds(z.edge, z.edge)] = east[...]

        def work(part, first):
            f = z.flat(ext[pl.ds(first, z.group)])
            aggs = aggregate(z, tiles, reads, first, adj, ext)
            here = pl.ds(first - z.lent, z.group)
            agg[here] = z.tiled(aggs)
            pre = dot(f, ws[0]) + dot(aggs, wn[0]) + bias[0:1, :]
            act = (pre * sigmoid(pre)).astype(BF16)
            res = live_rows(z, f.astype(F32) + dot(act, wo[0]), first, live[0])
            f1_rest[here] = z.tiled(res.astype(BF16))

        each_group(z, work, (1,))
        copy = pltpu.make_async_copy(f1_rest, out.at[0, pl.ds(z.lent, z.rest)], sems.at[z.lent])
        copy.start()
        for other in copies:
            other.wait()
        copy.wait()

    return call(
        kernel,
        "first_rest",
        [SMEM] * 4 + [VMEM] * 11,
        [VMEM, VMEM, ANY, VMEM],
        [
            z.nodes(z.lent),
            z.nodes(z.rest),
            jax.ShapeDtypeStruct((2, z.tiles, z.rows, z.cols), BF16),
            z.nodes(z.rest),
        ],
        [z.held(z.ext), pltpu.SemaphoreType.DMA((1 + z.lent,))],
        10,
        (tiles, reads, bound, live, *f0, fw, fe, adj, w_self, w_nbr, bias, w_out, west, east),
    )


def second_own(z, m1, wt):
    def kernel(m_lent, m_rest, wt, hidden):
        def work(part, first):
            m = z.flat(group_of(z, (m_lent, m_rest), part, first)[...])
            hidden[pl.ds(first, z.group)] = z.tiled(dot(m, wt[1, 2]))

        each_group(z, work)

    return call(
        kernel,
        "second_own",
        [VMEM] * 3,
        VMEM,
        z.nodes(z.tiles, F32),
        [],
        8,
        (*m1, wt),
    )


def saved(z, f0, agg0, w_self, w_nbr, bias):
    def kernel(f_lent, f_rest, a_lent, a_rest, ws, wn, bias, act, slope):
        def work(part, first):
            f = z.flat(group_of(z, (f_lent, f_rest), part, first)[...])
            aggs = z.flat(group_of(z, (a_lent, a_rest), part, first)[...])
            pre = dot(f, ws[0]) + dot(aggs, wn[0]) + bias[0:1, :]
            sig = sigmoid(pre)
            here = pl.ds(first, z.group)
            act[here] = z.tiled((pre * sig).astype(BF16))
            slope[here] = z.tiled(sig * (1.0 + pre * (1.0 - sig)))

        each_group(z, work)

    return call(
        kernel,
        "saved",
        [VMEM] * 7,
        [VMEM] * 2,
        [z.nodes(z.tiles), z.nodes(z.tiles, F32)],
        [],
        10,
        (*f0, *agg0, w_self, w_nbr, bias),
    )


def spread(z, tables, table, count, adj, source, acc, add):
    blocks, sources, targets, counts = tables
    x = z.index

    @pl.loop(0, count, unroll=4)
    def _(target):
        base = (x.first[table] + target) * x.QUAD
        lefts, rights = [], []
        for k in range(x.QUAD):
            block = blocks[base + k]
            left = adj[jnp.maximum(block, 0)]
            lefts.append(jnp.where(block >= 0, left, jnp.zeros_like(left)).T)
            rights.append(source(sources[base + k]))
        value = dot(jnp.concatenate(lefts, axis=1), jnp.concatenate(rights, axis=0))
        if add:
            acc[target] += value
        else:
            acc[target] = value

    @pl.loop(0, counts[table])
    def _(i):
        at = x.more[table] + i
        acc[targets[at]] += dot(adj[blocks[at]].T, source(sources[at]))


def second(z, tiles, reads, tables, f1, fw, fe, adj, hidden, w_self, w_nbr, bias, wt):
    def kernel(tiles, reads, blocks, sources, targets, counts, f_lent, f_rest, fw, fe, adj, hidden, ws, wn, bias, wt,
               agg, act, dpre, dagg, to_west, to_east, ext, acc):
        fill_extended(z, (f_lent, f_rest), fw, fe, ext)

        def work(part, first):
            here = pl.ds(first, z.group)
            aggs = aggregate(z, tiles, reads, first, adj, ext)
            agg[here] = z.tiled(aggs)
            pre = dot(z.flat(ext[here]), ws[1]) + dot(aggs, wn[1]) + bias[1:2, :]
            sig = sigmoid(pre)
            act[here] = z.tiled((pre * sig).astype(BF16))
            grad = (z.flat(hidden[here]) * (sig * (1.0 + pre * (1.0 - sig)))).astype(BF16)
            dpre[here] = z.tiled(grad)
            dagg[here] = z.tiled(dot(grad, wt[1, 1]).astype(BF16))

        each_group(z, work, unroll=2)
        spread(z, (blocks, sources, targets, counts), 1, z.lent, adj, lambda q: dagg[q], acc, False)
        to_west[...] = acc[pl.ds(0, z.edge)].astype(BF16)
        to_east[...] = acc[pl.ds(z.edge, z.edge)].astype(BF16)

    return call(
        kernel,
        "second",
        [SMEM] * 6 + [VMEM] * 10,
        [VMEM] * 6,
        [z.nodes(z.tiles)] * 4 + [z.nodes(z.edge)] * 2,
        [z.held(z.ext), z.held(z.lent, F32)],
        12,
        (tiles, reads, *tables, *f1, fw, fe, adj, hidden, w_self, w_nbr, bias, wt),
    )


class Plane:
    def __init__(self):
        dom, phase = lax.axis_size("dom"), lax.axis_size("phase")
        core = 2 if dom % 2 == 0 else 1
        self.sizes = (core, dom // core, phase)
        self.count = dom * phase
        place = lax.axis_index("dom")
        place = [lax.rem(place, core), place // core, lax.axis_index("phase")]
        self.place = jnp.stack(place + [jnp.zeros_like(place[0])] * 5).astype(jnp.int32)
        self.me = None

    def piece_of(self, me, steps):
        at = [lax.rem(me[i] + (steps[i] + n) % n, n) for i, n in enumerate(self.sizes)]
        return (at[0] * self.sizes[1] + at[1]) * self.sizes[2] + at[2]

    def passed(self, value, dim, steps):
        return self.passed_by(value, [steps if i == dim else 0 for i in range(3)])

    def passed_by(self, value, steps):
        pairs = []
        for c in range(self.sizes[0]):
            for d in range(self.sizes[1]):
                for p in range(self.sizes[2]):
                    to = [(at + by) % n for at, by, n in zip((c, d, p), steps, self.sizes)]
                    source = (d * self.sizes[0] + c) * self.sizes[2] + p
                    target = (to[1] * self.sizes[0] + to[0]) * self.sizes[2] + to[2]
                    pairs.append((source, target))
        return lax.ppermute(value, PLANE, pairs)

    def received(self, parts, dim):
        return [parts[0]] + [self.passed(parts[i], dim, i) for i in range(1, self.sizes[dim])]


def weight_grads(z, plane, f, agg, act, m, dpre, name):
    c = z.cols
    piece = -(-(3 * c + 1) // (plane.count * 16)) * 16
    core, ahead, side = plane.sizes
    arrays = (f, agg, act, m, dpre)
    flat_args = [x for a in arrays for x in (a if isinstance(a, tuple) else (a,))]

    def kernel(me, *refs):
        refs = list(refs)
        f, agg, act, m, dpre = [
            (refs.pop(0), refs.pop(0)) if isinstance(a, tuple) else refs.pop(0) for a in arrays
        ]
        outs, acc = refs[:-1], refs[-1]
        acc[...] = jnp.zeros_like(acc)

        def work(part, first):
            def rows(array):
                return z.flat(group_of(z, array, part, first)[...])

            grad = rows(dpre)
            acc[pl.ds(0, c), :] += dot_rows(rows(f), grad)
            acc[pl.ds(c, c), :] += dot_rows(rows(agg), grad)
            acc[pl.ds(2 * c, c), :] += dot_rows(rows(act), rows(m))
            acc[pl.ds(3 * c, 1), :] += jnp.sum(grad.astype(F32), axis=0, keepdims=True)

        each_group(z, work)
        for i, out in enumerate(outs):
            for j in range(ahead):
                for k in range(side):
                    owner = pl.multiple_of(plane.piece_of(me, (i, j, k)) * piece, 16)
                    out[j, k] = acc[pl.ds(owner, piece), :].astype(BF16)

    return call(
        kernel,
        name,
        [SMEM] + [VMEM] * len(flat_args),
        [VMEM] * core,
        [jax.ShapeDtypeStruct((ahead, side, piece, c), BF16)] * core,
        [pltpu.VMEM((piece * plane.count, c), F32)],
        14,
        (plane.me, *flat_args),
    )


def added(values, split=False, after=(), pairs=False):
    shape = values[0].shape
    count = shape[0] if split else 1

    def kernel(*refs):
        outs = refs[-count:]
        for i, out in enumerate(outs):
            parts = [ref[i] if split else ref[...] for ref in refs[: len(values)]]
            parts = [part.astype(F32) for part in parts]
            if pairs:
                parts = [parts[0] + parts[1], parts[2] + parts[3]]
            total = parts[0]
            for part in parts[1:]:
                total = total + part
            out[...] = total.astype(BF16)

    args = [*values, *after]
    outs = call(
        kernel,
        "added",
        [VMEM] * len(values) + [ANY] * len(after),
        [VMEM] * count,
        [jax.ShapeDtypeStruct(shape[1:] if split else shape, BF16)] * count,
        [],
        8,
        args,
    )
    return outs if split else outs[0]


def plane_parts(plane, pieces):
    parts = added(plane.received(pieces, 0), split=True)
    parts = added(plane.received(parts, 1), split=True)
    return plane.received(parts, 2)


def line_sum(share):
    lines = lax.axis_size("feat")
    if lines & (lines - 1) != 0:
        return lax.psum(share.astype(F32), "feat").astype(BF16)
    step = 1
    while step < lines:
        other = lax.ppermute(share, "feat", [(i, i ^ step) for i in range(lines)])
        share = added([share, other])
        step *= 2
    return share


def line_sum_at_once(share):
    lines = lax.axis_size("feat")
    if lines != 4:
        return line_sum(share)
    others = [lax.ppermute(share, "feat", [(i, i ^ s) for i in range(lines)]) for s in (1, 2, 3)]
    return added([share, *others], pairs=True)


def stacked(values):
    def kernel(*refs):
        for i, ref in enumerate(refs[:-1]):
            refs[-1][i] = ref[...]

    shape = (len(values),) + values[0].shape
    out = jax.ShapeDtypeStruct(shape, values[0].dtype)
    return call(kernel, "stacked", [VMEM] * len(values), VMEM, out, [], 4, values)


def plane_gathered(plane, share):
    for dim in (2, 1):
        size = plane.sizes[dim]
        share = stacked([share] + [plane.passed(share, dim, i) for i in range(1, size)])
    return [share] + [plane.passed(share, 0, i) for i in range(1, plane.sizes[0])]


def plane_gathered_at_once(plane, share):
    core, ahead, side = plane.sizes
    steps = [(i, j, k) for i in range(core) for j in range(ahead) for k in range(side)]
    return [share] + [plane.passed_by(share, by) for by in steps[1:]]


def second_out(z, bound, live, f1, act, w_out, out):
    def kernel(bound, live, f_lent, f_rest, act, wo, _out, out, token, keep, sems):
        copies = []
        token[...] = jnp.zeros_like(token)

        def work(part, first):
            f = z.flat(group_of(z, (f_lent, f_rest), part, first)[...])
            res = f.astype(F32) + dot(z.flat(act[pl.ds(first, z.group)]), wo[1])
            keep[pl.ds(first, z.group)] = z.tiled(live_rows(z, res, first, live[0]).astype(BF16))

        each_group(z, work, (0,))
        for i in range(z.lent):
            copy = pltpu.make_async_copy(
                keep.at[i], out.at[1, bound[0, i // z.edge, i % z.edge]], sems.at[i]
            )
            copy.start()
            copies.append(copy)
        each_group(z, work, (1,))
        tail = pl.ds(z.lent, z.rest)
        copy = pltpu.make_async_copy(keep.at[tail], out.at[1, tail], sems.at[z.lent])
        copy.start()
        copies.append(copy)
        for copy in copies:
            copy.wait()

    return call(
        kernel,
        "second_out",
        [SMEM] * 2 + [VMEM] * 4 + [ANY],
        [ANY, VMEM],
        [jax.ShapeDtypeStruct(out.shape, BF16), TOKEN],
        [z.held(z.tiles), pltpu.SemaphoreType.DMA((z.lent + 1,))],
        12,
        (bound, live, *f1, act, w_out, out),
        {6: 0},
    )


def input_grad(z, layer, tables, m, dpre, dagg, adj, wt):
    arrays = (m, dpre, dagg)
    flat_args = [x for a in arrays for x in (a if isinstance(a, tuple) else (a,))]

    def kernel(blocks, sources, targets, counts, *refs):
        refs = list(refs)
        m, dpre, dagg = [
            (refs.pop(0), refs.pop(0)) if isinstance(a, tuple) else refs.pop(0) for a in arrays
        ]
        adj, wt, part_out, rest_out, token, acc = refs
        token[...] = jnp.zeros_like(token)

        def direct(part, first):
            mine = z.flat(group_of(z, m, part, first)[...]).astype(F32)
            res = mine + dot(z.flat(group_of(z, dpre, part, first)[...]), wt[layer, 0])
            acc[pl.ds(first, z.group)] = z.tiled(res)

        each_group(z, direct)

        def source(q):
            if not isinstance(dagg, tuple):
                return dagg[q]
            lent = dagg[0][jnp.minimum(q, z.lent - 1)]
            rest = dagg[1][jnp.maximum(q - z.lent, 0)]
            return jnp.where(q < z.lent, lent, rest)

        spread(z, (blocks, sources, targets, counts), 0, z.tiles, adj, source, acc, True)
        part_out[...] = acc[pl.ds(0, z.lent)]
        rest_out[...] = acc[pl.ds(z.lent, z.rest)].astype(BF16)

    return call(
        kernel,
        "input_grad%d" % layer,
        [SMEM] * 4 + [VMEM] * (len(flat_args) + 2),
        [VMEM] * 3,
        [z.nodes(z.lent, F32), z.nodes(z.rest), TOKEN],
        [z.held(z.tiles, F32)],
        20,
        [*tables, *flat_args, adj, wt],
    )


def early_rest(z, tables, live, upstream, slope, adj, wt):
    def kernel(blocks, sources, targets, counts, live, g, slope, adj, wt, grads, m, dpre, dagg, outer, sem):
        copy = pltpu.make_async_copy(g, grads.at[1, pl.ds(z.lent, z.rest)], sem)
        copy.start()

        def work(part, first):
            here = pl.ds(first - z.lent, z.group)
            masked = live_rows(z, z.flat(g[here]), first, live[0])
            m[here] = z.tiled(masked)
            grad = dot(masked, wt[0, 2]) * z.flat(slope[pl.ds(first, z.group)])
            grad = grad.astype(BF16)
            dpre[here] = z.tiled(grad)
            dagg[here] = z.tiled(dot(grad, wt[0, 1]).astype(BF16))

        each_group(z, work, (1,))

        def source(q):
            return dagg[jnp.maximum(q - z.lent, 0)]

        spread(z, (blocks, sources, targets, counts), 3, z.lent, adj, source, outer, False)
        copy.wait()

    return call(
        kernel,
        "early_rest",
        [SMEM] * 5 + [VMEM] * 4,
        [ANY] + [VMEM] * 4,
        [jax.ShapeDtypeStruct((2, z.tiles, z.rows, z.cols), BF16)]
        + [z.nodes(z.rest)] * 3
        + [z.nodes(z.lent, F32)],
        [pltpu.SemaphoreType.DMA],
        14,
        (*tables, live, upstream, slope, adj, wt),
    )


def early_lent(z, tables, bound, part, fw, fe, slope, outer, adj, wt, grads, after):
    def kernel(blocks, sources, targets, counts, bound, part, fw, fe, slope, outer, adj, wt, _g, _ready, _late,
               m, dpre, dagg, grads, to_west, to_east, acc, sems):
        def work(first, got):
            here = pl.ds(first, z.group)
            g = z.flat((part[here] + got.astype(F32)).astype(BF16))
            m[here] = z.tiled(g)
            grad = (dot(g, wt[0, 2]) * z.flat(slope[here])).astype(BF16)
            dpre[here] = z.tiled(grad)
            dagg[here] = z.tiled(dot(grad, wt[0, 1]).astype(BF16))

        @pl.loop(0, z.edge // z.group)
        def _(s):
            here = pl.ds(s * z.group, z.group)
            work(s * z.group, fw[here])
            work(z.edge + s * z.group, fe[here])

        copies = [
            pltpu.make_async_copy(m.at[i], grads.at[1, bound[0, i // z.edge, i % z.edge]], sems.at[i])
            for i in range(z.lent)
        ]
        for copy in copies:
            copy.start()
        acc[...] = outer[...]

        def source(q):
            return dagg[jnp.minimum(q, z.lent - 1)]

        spread(z, (blocks, sources, targets, counts), 2, z.lent, adj, source, acc, True)
        to_west[...] = acc[pl.ds(0, z.edge)].astype(BF16)
        to_east[...] = acc[pl.ds(z.edge, z.edge)].astype(BF16)
        for copy in copies:
            copy.wait()

    return call(
        kernel,
        "early_lent",
        [SMEM] * 5 + [VMEM] * 7 + [ANY, VMEM, VMEM],
        [VMEM] * 3 + [ANY] + [VMEM] * 2,
        [z.nodes(z.lent)] * 3 + [jax.ShapeDtypeStruct(grads.shape, BF16)] + [z.nodes(z.edge)] * 2,
        [z.held(z.lent, F32), pltpu.SemaphoreType.DMA((z.lent,))],
        16,
        (*tables, bound, part, fw, fe, slope, outer, adj, wt, grads, *after),
        {12: 3},
    )


def finish(z, bound, part, rest, fw, fe, grads):
    def kernel(bound, part, rest, fw, fe, _g, grads, keep, sems):
        copies = [pltpu.make_async_copy(rest, grads.at[0, pl.ds(z.lent, z.rest)], sems.at[z.lent])]
        copies[0].start()
        for i in range(z.lent):
            got = fw[i] if i < z.edge else fe[i - z.edge]
            keep[i] = (part[i] + got.astype(F32)).astype(BF16)
            copy = pltpu.make_async_copy(
                keep.at[i], grads.at[0, bound[0, i // z.edge, i % z.edge]], sems.at[i]
            )
            copy.start()
            copies.append(copy)
        for copy in copies:
            copy.wait()

    return call(
        kernel,
        "finish",
        [SMEM] + [VMEM] * 4 + [ANY],
        ANY,
        jax.ShapeDtypeStruct(grads.shape, BF16),
        [z.held(z.lent), pltpu.SemaphoreType.DMA((z.lent + 1,))],
        14,
        (bound, part, rest, fw, fe, grads),
        {5: 0},
    )


def unpack(z, plane, early, late):
    c = z.cols
    piece = early[0].shape[0]
    core, ahead, side = plane.sizes

    def kernel(me, *refs):
        refs = list(refs)
        early, late = refs[: plane.count], refs[plane.count : plane.count + core]
        g_self, g_nbr, g_bias, g_out, buf = refs[plane.count + core :]
        for layer in range(2):
            for i in range(core):
                for j in range(ahead):
                    for k in range(side):
                        start = pl.multiple_of(plane.piece_of(me, (-i, -j, -k)) * piece, 16)
                        if layer == 0:
                            got = early[(i * ahead + j) * side + k][...]
                        else:
                            got = late[i][j, k]
                        buf[pl.ds(start, piece), :] = got.astype(F32)
            g_self[layer] = buf[pl.ds(0, c), :]
            g_nbr[layer] = buf[pl.ds(c, c), :]
            g_out[layer] = buf[pl.ds(2 * c, c), :]
            g_bias[layer : layer + 1, :] = buf[pl.ds(3 * c, 1), :]

    square = jax.ShapeDtypeStruct((2, c, c), F32)
    return call(
        kernel,
        "unpack",
        [SMEM] + [VMEM] * (plane.count + core),
        [VMEM] * 4,
        [square, square, jax.ShapeDtypeStruct((2, c), F32), square],
        [pltpu.VMEM((piece * plane.count, c), F32)],
        10,
        (plane.me, *early, *late),
    )


def per_device(
    node_in, out_cot, adjacency, tile_nbrs, bound_tiles, live_tiles, w_self, w_nbr, pre_bias, w_out
):
    z = Sizes(adjacency, node_in, bound_tiles)
    t, r, c = z.tiles, z.rows, z.cols
    features = node_in.reshape(t, r, c)
    cot = out_cot.reshape(t, r, c)
    plane = Plane()

    west, east = lend(z, bound_tiles, features)
    from_west = passed_along(east, 1)
    from_east = passed_along(west, -1)
    *nodes, adj, tiles, reads, blocks, sources, targets, counts, plane.me = arrange(
        z, bound_tiles, tile_nbrs, live_tiles, plane.place, features, cot, adjacency.reshape(z.pairs, r, r)
    )
    f0, m1 = tuple(nodes[:2]), tuple(nodes[2:])
    tables = (blocks, sources, targets, counts)
    wt = turn(z, w_self, w_nbr, w_out)

    west, east, agg_lent = first_lent(
        z, tiles, reads, f0, from_west, from_east, adj, w_self, w_nbr, pre_bias, w_out
    )
    next_west = passed_along(east, 1)
    next_east = passed_along(west, -1)
    f1_lent, f1_rest, section_out, agg_rest = first_rest(
        z, tiles, reads, bound_tiles, live_tiles, f0, from_west, from_east, adj, w_self, w_nbr, pre_bias, w_out,
        west, east,
    )
    f1, agg0 = (f1_lent, f1_rest), (agg_lent, agg_rest)
    hidden = second_own(z, m1, wt)

    agg1, act1, dpre1, dagg1, to_west, to_east = second(
        z, tiles, reads, tables, f1, next_west, next_east, adj, hidden, w_self, w_nbr, pre_bias, wt
    )
    back_west = passed_along(to_east, 1)
    back_east = passed_along(to_west, -1)
    late = weight_grads(z, plane, f1, agg1, act1, m1, dpre1, "weight_grads1")
    late = added(plane_parts(plane, late))
    part, upstream, _ = input_grad(z, 1, tables, m1, dpre1, dagg1, adj, wt)
    section_out, ready = second_out(z, bound_tiles, live_tiles, f1, act1, w_out, section_out)
    act0, slope = saved(z, f0, agg0, w_self, w_nbr, pre_bias)
    grads, m0_rest, dpre_rest, dagg_rest, outer = early_rest(
        z, tables, live_tiles, upstream, slope, adj, wt
    )

    m0_lent, dpre_lent, dagg_lent, grads, to_west, to_east = early_lent(
        z, tables, bound_tiles, part, back_west, back_east, slope, outer, adj, wt, grads, (ready, late)
    )
    back_west = passed_along(to_east, 1)
    back_east = passed_along(to_west, -1)
    m0, dpre0, dagg0 = (m0_lent, m0_rest), (dpre_lent, dpre_rest), (dagg_lent, dagg_rest)
    early = weight_grads(z, plane, f0, agg0, act0, m0, dpre0, "weight_grads0")

    def meanwhile(early, late, tables, m0, dpre0, dagg0, adj, wt):
        part, rest, _ = input_grad(z, 0, tables, m0, dpre0, dagg0, adj, wt)
        return plane_parts(plane, early), plane_gathered(plane, line_sum(late)), part, rest

    args = (early, late, tables, m0, dpre0, dagg0, adj, wt)
    shapes = jax.eval_shape(meanwhile, *args)
    early, late, part, rest = lax.cond(
        live_tiles[0] > 0,
        meanwhile,
        lambda *_: jax.tree.map(lambda a: jnp.zeros(a.shape, a.dtype), shapes),
        *args,
    )
    early = line_sum_at_once(added(early, after=(back_west, back_east)))
    early = plane_gathered_at_once(plane, early)
    grads = finish(z, bound_tiles, part, rest, back_west, back_east, grads)
    grad_self, grad_nbr, grad_bias, grad_out = unpack(z, plane, early, late)
    return (
        section_out.reshape(2, t * r, c),
        grads.reshape(2, t * r, c),
        grad_self,
        grad_nbr,
        grad_bias,
        grad_out,
    )


def solution(mesh):
    rows = P(AXES)
    in_specs = (rows, rows, rows, rows, rows, rows, P(), P(), P(), P())
    out_specs = (P(None, AXES), P(None, AXES), P(), P(), P(), P())
    return jax.shard_map(
        per_device, mesh=mesh, in_specs=in_specs, out_specs=out_specs, check_vma=False
    )
```

```python
import jax
import jax.numpy as jnp
from jax import lax
from jax.experimental import pallas as pl
from jax.experimental.pallas import tpu as pltpu
from jax.sharding import PartitionSpec as P

AXES = ("dom", "phase", "feat")
PLANE = ("dom", "phase")
BF16 = jnp.bfloat16
F32 = jnp.float32
ANY = pl.BlockSpec(memory_space=pl.ANY)
SMEM = pl.BlockSpec(memory_space=pltpu.SMEM)
VMEM = pl.BlockSpec(memory_space=pltpu.VMEM)
MIB = 1024 * 1024
TOKEN = jax.ShapeDtypeStruct((8, 128), F32)


class Sizes:
    def __init__(self, adjacency, features, bound):
        self.tiles, self.slots, self.rows, _ = adjacency.shape
        self.cols = features.shape[-1]
        self.edge = bound.shape[-1]
        self.lent = 2 * self.edge
        self.rest = self.tiles - self.lent
        self.ext = self.tiles + self.lent
        self.pairs = self.tiles * self.slots
        self.group = next(g for g in (4, 2, 1) if self.edge % g == 0 and self.rest % g == 0)
        self.parts = ((0, 0, self.lent), (1, self.lent, self.rest))
        self.index = Index(self)

    def nodes(self, count, dtype=BF16):
        return jax.ShapeDtypeStruct((count, self.rows, self.cols), dtype)

    def held(self, count, dtype=BF16):
        return pltpu.VMEM((count, self.rows, self.cols), dtype)

    def flat(self, value):
        return value.reshape(self.group * self.rows, self.cols)

    def tiled(self, value):
        return value.reshape(self.group, self.rows, self.cols)


def group_of(z, array, part, first):
    if isinstance(array, tuple):
        base = z.lent if part else 0
        return array[part].at[pl.ds(first - base, z.group)]
    return array.at[pl.ds(first, z.group)]


def each_group(z, body, parts=(0, 1), unroll=1):
    for part, base, count in z.parts:
        if part in parts:

            @pl.loop(0, count // z.group, unroll=unroll)
            def _(s):
                body(part, base + s * z.group)


def passed_along(value, steps):
    count = lax.axis_size(AXES)
    return lax.ppermute(value, AXES, [(i, (i + steps) % count) for i in range(count)])


def dot(a, b):
    return jnp.dot(a, b, preferred_element_type=F32)


def dot_rows(a, b):
    return lax.dot_general(a, b, (((0,), (0,)), ((), ())), preferred_element_type=F32)


def call(kernel, name, in_specs, out_specs, out_shape, scratch, limit, args, aliases=None):
    return pl.pallas_call(
        kernel,
        in_specs=in_specs,
        out_specs=out_specs,
        out_shape=out_shape,
        scratch_shapes=scratch,
        input_output_aliases=aliases or {},
        compiler_params=pltpu.CompilerParams(vmem_limit_bytes=limit * MIB),
        cost_estimate=pl.CostEstimate(flops=1000, bytes_accessed=1000, transcendentals=0),
        name=name,
    )(*args)


def sigmoid(v):
    return 0.5 * jnp.tanh(0.5 * v) + 0.5


def lend(z, bound, features):
    def kernel(bound, feats, west, east, sems):
        copies = []
        for i in range(z.edge):
            for side, target in ((0, west), (1, east)):
                copy = pltpu.make_async_copy(
                    feats.at[bound[0, side, i]], target.at[i], sems.at[side * z.edge + i]
                )
                copy.start()
                copies.append(copy)
        for copy in copies:
            copy.wait()

    return call(
        kernel,
        "lend",
        [SMEM, ANY],
        [VMEM, VMEM],
        [z.nodes(z.edge), z.nodes(z.edge)],
        [pltpu.SemaphoreType.DMA((z.lent,))],
        56,
        (bound, features),
    )


class Index:
    QUAD = 4

    def __init__(self, z):
        self.first = (0, z.tiles, z.tiles + z.lent, z.tiles + 2 * z.lent, z.tiles + 3 * z.lent)
        self.targets = z.tiles + 3 * z.lent + 1
        self.more = tuple(self.QUAD * self.targets + i * z.pairs for i in range(5))
        self.size = self.QUAD * self.targets + 5 * z.pairs
        self.size = -(-self.size // 8) * 8


def arrange(z, bound, nbrs, live, place, features, cot, adjacency):
    s4 = z.slots
    x = z.index

    def kernel(bound, nbrs, live, place, feats, cot, adj, f_lent, f_rest, m_lent, m_rest, adj_out,
               tiles, reads, blocks, sources, targets, counts, me, inverse, used, sems):
        copies = []
        for i in range(8):
            me[i] = place[i]

        def start(source, target):
            copy = pltpu.make_async_copy(source, target, sems.at[len(copies)])
            copy.start()
            copies.append(copy)

        tail = pl.ds(z.lent, z.rest)
        start(feats.at[tail], f_rest)
        start(cot.at[tail], m_rest)
        start(adj, adj_out)
        for i in range(z.lent):
            tile = bound[0, i // z.edge, i % z.edge]
            inverse[tile] = i
            start(feats.at[tile], f_lent.at[i])
            start(cot.at[tile], m_lent.at[i])

        @pl.loop(0, x.targets)
        def _(i):
            used[i] = 0
            for k in range(x.QUAD):
                blocks[i * x.QUAD + k] = -1
                sources[i * x.QUAD + k] = 0

        for i in range(8):
            counts[i] = 0

        def put(table, target, block, position):
            place = used[target]
            used[target] = place + 1
            fits = place < x.QUAD
            listed = counts[table]
            counts[table] = listed + jnp.where(fits, 0, 1)
            at = jnp.where(fits, target * x.QUAD + place, x.more[0] + table * z.pairs + listed)
            blocks[at] = block
            sources[at] = position
            return at

        @pl.loop(0, z.tiles)
        def _(position):
            clipped = jnp.minimum(position, z.lent - 1)
            tile = jnp.where(position < z.lent, bound[0, clipped // z.edge, clipped % z.edge], position)
            tiles[position] = tile
            for k in range(s4):
                target = nbrs[tile, k]
                moved = jnp.where(target < z.lent, inverse[jnp.minimum(target, z.lent - 1)], target)
                reads[position * s4 + k] = moved
                block = tile * s4 + k
                own = moved < z.tiles
                at = put(jnp.where(own, 0, 1), moved, block, position)
                targets[at] = jnp.where(own, moved, moved - z.tiles)
                lent = position < z.lent
                table = jnp.where(own, 4, jnp.where(lent, 2, 3))
                shift = jnp.where(lent, z.lent, 2 * z.lent)
                at = put(table, jnp.where(own, x.first[4], moved + shift), block, position)
                targets[at] = moved - z.tiles

        for copy in copies:
            copy.wait()

        @pl.loop(0, z.rest)
        def _(i):
            @pl.when(z.lent + i >= live[0])
            def _():
                m_rest[i] = jnp.zeros((z.rows, z.cols), BF16)

    return call(
        kernel,
        "arrange",
        [SMEM] * 4 + [ANY] * 3,
        [VMEM] * 5 + [SMEM] * 7,
        [z.nodes(z.lent), z.nodes(z.rest), z.nodes(z.lent), z.nodes(z.rest)]
        + [jax.ShapeDtypeStruct(adjacency.shape, BF16)]
        + [jax.ShapeDtypeStruct((n,), jnp.int32) for n in (z.tiles, z.pairs, x.size, x.size, x.size, 8, 8)],
        [
            pltpu.SMEM((z.lent,), jnp.int32),
            pltpu.SMEM((x.targets,), jnp.int32),
            pltpu.SemaphoreType.DMA((2 * z.lent + 3,)),
        ],
        12,
        (bound, nbrs, live, place, features, cot, adjacency),
    )


def turn(z, adj, w_self, w_nbr, w_out):
    def kernel(adj, ws, wn, wo, at, wt):
        for layer in range(2):
            wt[layer, 0] = ws[layer].T
            wt[layer, 1] = wn[layer].T
            wt[layer, 2] = wo[layer].T

        @pl.loop(0, z.pairs, unroll=4)
        def _(i):
            at[i] = adj[i].T

    return call(
        kernel,
        "turn",
        [VMEM] * 4,
        [VMEM, VMEM],
        [jax.ShapeDtypeStruct(adj.shape, BF16), jax.ShapeDtypeStruct((2, 3, z.cols, z.cols), BF16)],
        [],
        12,
        (adj, w_self, w_nbr, w_out),
    )


def fill_extended(z, own, fw, fe, ext):
    ext[pl.ds(0, z.lent)] = own[0][...]
    ext[pl.ds(z.lent, z.rest)] = own[1][...]
    ext[pl.ds(z.tiles, z.edge)] = fw[...]
    ext[pl.ds(z.tiles + z.edge, z.edge)] = fe[...]


def aggregate(z, tiles, reads, first, adj, ext):
    rows = []
    for g in range(z.group):
        base = (first + g) * z.slots
        block = tiles[first + g] * z.slots
        picked = jnp.concatenate([ext[reads[base + k]] for k in range(z.slots)], axis=0)
        blocks = jnp.concatenate([adj[block + k] for k in range(z.slots)], axis=1)
        rows.append(dot(blocks, picked).astype(BF16))
    return jnp.concatenate(rows, axis=0)


def live_rows(z, value, first, live):
    parts = []
    for g in range(z.group):
        part = value[g * z.rows : (g + 1) * z.rows]
        parts.append(jnp.where(first + g < live, part, jnp.zeros_like(part)))
    return jnp.concatenate(parts, axis=0)


def first_lent(z, tiles, reads, f0, fw, fe, adj, w_self, w_nbr, bias, w_out):
    def kernel(tiles, reads, f_lent, f_rest, fw, fe, adj, ws, wn, bias, wo, west, east, agg, ext):
        fill_extended(z, (f_lent, f_rest), fw, fe, ext)

        def work(first, target, offset):
            here = pl.ds(first, z.group)
            f = z.flat(ext[here])
            aggs = aggregate(z, tiles, reads, first, adj, ext)
            agg[here] = z.tiled(aggs)
            pre = dot(f, ws[0]) + dot(aggs, wn[0]) + bias[0:1, :]
            act = (pre * sigmoid(pre)).astype(BF16)
            target[pl.ds(offset, z.group)] = z.tiled((f.astype(F32) + dot(act, wo[0])).astype(BF16))

        @pl.loop(0, z.edge // z.group)
        def _(s):
            work(s * z.group, west, s * z.group)
            work(z.edge + s * z.group, east, s * z.group)

    return call(
        kernel,
        "first_lent",
        [SMEM] * 2 + [VMEM] * 9,
        [VMEM] * 3,
        [z.nodes(z.edge), z.nodes(z.edge), z.nodes(z.lent)],
        [z.held(z.ext)],
        12,
        (tiles, reads, *f0, fw, fe, adj, w_self, w_nbr, bias, w_out),
    )


def first_rest(z, tiles, reads, bound, live, f0, fw, fe, adj, w_self, w_nbr, bias, w_out, west, east):
    def kernel(tiles, reads, bound, live, f_lent, f_rest, fw, fe, adj, ws, wn, bias, wo, west, east,
               f1_lent, f1_rest, out, agg, ext, sems):
        copies = []
        for i in range(z.edge):
            for side, source in ((0, west), (1, east)):
                copy = pltpu.make_async_copy(
                    source.at[i], out.at[0, bound[0, side, i]], sems.at[side * z.edge + i]
                )
                copy.start()
                copies.append(copy)
        fill_extended(z, (f_lent, f_rest), fw, fe, ext)
        f1_lent[pl.ds(0, z.edge)] = west[...]
        f1_lent[pl.ds(z.edge, z.edge)] = east[...]

        def work(part, first):
            f = z.flat(ext[pl.ds(first, z.group)])
            aggs = aggregate(z, tiles, reads, first, adj, ext)
            here = pl.ds(first - z.lent, z.group)
            agg[here] = z.tiled(aggs)
            pre = dot(f, ws[0]) + dot(aggs, wn[0]) + bias[0:1, :]
            act = (pre * sigmoid(pre)).astype(BF16)
            res = live_rows(z, f.astype(F32) + dot(act, wo[0]), first, live[0])
            f1_rest[here] = z.tiled(res.astype(BF16))

        each_group(z, work, (1,))
        copy = pltpu.make_async_copy(f1_rest, out.at[0, pl.ds(z.lent, z.rest)], sems.at[z.lent])
        copy.start()
        for other in copies:
            other.wait()
        copy.wait()

    return call(
        kernel,
        "first_rest",
        [SMEM] * 4 + [VMEM] * 11,
        [VMEM, VMEM, ANY, VMEM],
        [
            z.nodes(z.lent),
            z.nodes(z.rest),
            jax.ShapeDtypeStruct((2, z.tiles, z.rows, z.cols), BF16),
            z.nodes(z.rest),
        ],
        [z.held(z.ext), pltpu.SemaphoreType.DMA((1 + z.lent,))],
        10,
        (tiles, reads, bound, live, *f0, fw, fe, adj, w_self, w_nbr, bias, w_out, west, east),
    )


def second_own(z, m1, wt):
    def kernel(m_lent, m_rest, wt, hidden):
        def work(part, first):
            m = z.flat(group_of(z, (m_lent, m_rest), part, first)[...])
            hidden[pl.ds(first, z.group)] = z.tiled(dot(m, wt[1, 2]))

        each_group(z, work)

    return call(
        kernel,
        "second_own",
        [VMEM] * 3,
        VMEM,
        z.nodes(z.tiles, F32),
        [],
        8,
        (*m1, wt),
    )


def saved(z, f0, agg0, w_self, w_nbr, bias):
    def kernel(f_lent, f_rest, a_lent, a_rest, ws, wn, bias, act, slope, token):
        token[...] = jnp.zeros_like(token)

        def work(part, first):
            f = z.flat(group_of(z, (f_lent, f_rest), part, first)[...])
            aggs = z.flat(group_of(z, (a_lent, a_rest), part, first)[...])
            pre = dot(f, ws[0]) + dot(aggs, wn[0]) + bias[0:1, :]
            sig = sigmoid(pre)
            here = pl.ds(first, z.group)
            act[here] = z.tiled((pre * sig).astype(BF16))
            slope[here] = z.tiled(sig * (1.0 + pre * (1.0 - sig)))

        each_group(z, work)

    return call(
        kernel,
        "saved",
        [VMEM] * 7,
        [VMEM] * 3,
        [z.nodes(z.tiles), z.nodes(z.tiles, F32), TOKEN],
        [],
        10,
        (*f0, *agg0, w_self, w_nbr, bias),
    )


def spread(z, tables, table, count, at, source, acc, add):
    blocks, sources, targets, counts = tables
    x = z.index

    @pl.loop(0, count, unroll=4)
    def _(target):
        base = (x.first[table] + target) * x.QUAD
        lefts, rights = [], []
        for k in range(x.QUAD):
            block = blocks[base + k]
            left = at[jnp.maximum(block, 0)]
            lefts.append(jnp.where(block >= 0, left, jnp.zeros_like(left)))
            rights.append(source(sources[base + k]))
        value = dot(jnp.concatenate(lefts, axis=1), jnp.concatenate(rights, axis=0))
        if add:
            acc[target] += value
        else:
            acc[target] = value

    @pl.loop(0, counts[table])
    def _(i):
        place = x.more[table] + i
        acc[targets[place]] += dot(at[blocks[place]], source(sources[place]))


def second(z, tiles, reads, tables, f1, fw, fe, adj, at, hidden, w_self, w_nbr, bias, wt, after):
    def kernel(tiles, reads, blocks, sources, targets, counts, f_lent, f_rest, fw, fe, adj, at, hidden, ws, wn,
               bias, wt, _after,
               agg, act, dpre, dagg, to_west, to_east, ext, acc):
        fill_extended(z, (f_lent, f_rest), fw, fe, ext)

        def work(part, first):
            here = pl.ds(first, z.group)
            aggs = aggregate(z, tiles, reads, first, adj, ext)
            agg[here] = z.tiled(aggs)
            pre = dot(z.flat(ext[here]), ws[1]) + dot(aggs, wn[1]) + bias[1:2, :]
            sig = sigmoid(pre)
            act[here] = z.tiled((pre * sig).astype(BF16))
            grad = (z.flat(hidden[here]) * (sig * (1.0 + pre * (1.0 - sig)))).astype(BF16)
            dpre[here] = z.tiled(grad)
            dagg[here] = z.tiled(dot(grad, wt[1, 1]).astype(BF16))

        each_group(z, work, unroll=2)
        spread(z, (blocks, sources, targets, counts), 1, z.lent, at, lambda q: dagg[q], acc, False)
        to_west[...] = acc[pl.ds(0, z.edge)].astype(BF16)
        to_east[...] = acc[pl.ds(z.edge, z.edge)].astype(BF16)

    return call(
        kernel,
        "second",
        [SMEM] * 6 + [VMEM] * 12,
        [VMEM] * 6,
        [z.nodes(z.tiles)] * 4 + [z.nodes(z.edge)] * 2,
        [z.held(z.ext), z.held(z.lent, F32)],
        12,
        (tiles, reads, *tables, *f1, fw, fe, adj, at, hidden, w_self, w_nbr, bias, wt, after),
    )


class Plane:
    def __init__(self):
        dom, phase = lax.axis_size("dom"), lax.axis_size("phase")
        core = 2 if dom % 2 == 0 else 1
        self.sizes = (core, dom // core, phase)
        self.count = dom * phase
        place = lax.axis_index("dom")
        place = [lax.rem(place, core), place // core, lax.axis_index("phase")]
        self.place = jnp.stack(place + [jnp.zeros_like(place[0])] * 5).astype(jnp.int32)
        self.me = None

    def piece_of(self, me, steps):
        at = [lax.rem(me[i] + (steps[i] + n) % n, n) for i, n in enumerate(self.sizes)]
        return (at[0] * self.sizes[1] + at[1]) * self.sizes[2] + at[2]

    def passed(self, value, dim, steps):
        return self.passed_by(value, [steps if i == dim else 0 for i in range(3)])

    def passed_by(self, value, steps):
        pairs = []
        for c in range(self.sizes[0]):
            for d in range(self.sizes[1]):
                for p in range(self.sizes[2]):
                    to = [(at + by) % n for at, by, n in zip((c, d, p), steps, self.sizes)]
                    source = (d * self.sizes[0] + c) * self.sizes[2] + p
                    target = (to[1] * self.sizes[0] + to[0]) * self.sizes[2] + to[2]
                    pairs.append((source, target))
        return lax.ppermute(value, PLANE, pairs)

    def received(self, parts, dim):
        return [parts[0]] + [self.passed(parts[i], dim, i) for i in range(1, self.sizes[dim])]


def weight_grads(z, plane, f, agg, act, m, dpre, name):
    c = z.cols
    piece = -(-(3 * c + 1) // (plane.count * 16)) * 16
    core, ahead, side = plane.sizes
    arrays = (f, agg, act, m, dpre)
    flat_args = [x for a in arrays for x in (a if isinstance(a, tuple) else (a,))]

    def kernel(me, *refs):
        refs = list(refs)
        f, agg, act, m, dpre = [
            (refs.pop(0), refs.pop(0)) if isinstance(a, tuple) else refs.pop(0) for a in arrays
        ]
        outs, acc = refs[:-1], refs[-1]
        acc[...] = jnp.zeros_like(acc)

        def work(part, first):
            def rows(array):
                return z.flat(group_of(z, array, part, first)[...])

            grad = rows(dpre)
            acc[pl.ds(0, c), :] += dot_rows(rows(f), grad)
            acc[pl.ds(c, c), :] += dot_rows(rows(agg), grad)
            acc[pl.ds(2 * c, c), :] += dot_rows(rows(act), rows(m))
            acc[pl.ds(3 * c, 1), :] += jnp.sum(grad.astype(F32), axis=0, keepdims=True)

        each_group(z, work)
        for i, out in enumerate(outs):
            for j in range(ahead):
                for k in range(side):
                    owner = pl.multiple_of(plane.piece_of(me, (i, j, k)) * piece, 16)
                    out[j, k] = acc[pl.ds(owner, piece), :].astype(BF16)

    return call(
        kernel,
        name,
        [SMEM] + [VMEM] * len(flat_args),
        [VMEM] * core,
        [jax.ShapeDtypeStruct((ahead, side, piece, c), BF16)] * core,
        [pltpu.VMEM((piece * plane.count, c), F32)],
        14,
        (plane.me, *flat_args),
    )


def added(values, split=False, after=()):
    shape = values[0].shape
    count = shape[0] if split else 1

    def kernel(*refs):
        outs = refs[-count:]
        for i, out in enumerate(outs):
            parts = [ref[i] if split else ref[...] for ref in refs[: len(values)]]
            parts = [part.astype(F32) for part in parts]
            total = parts[0]
            for part in parts[1:]:
                total = total + part
            out[...] = total.astype(BF16)

    args = [*values, *after]
    outs = call(
        kernel,
        "added",
        [VMEM] * len(values) + [ANY] * len(after),
        [VMEM] * count,
        [jax.ShapeDtypeStruct(shape[1:] if split else shape, BF16)] * count,
        [],
        8,
        args,
    )
    return outs if split else outs[0]


def plane_parts(plane, pieces, after=((), ())):
    parts = added(plane.received(pieces, 0), split=True, after=after[0])
    parts = added(plane.received(parts, 1), split=True, after=after[1])
    return plane.received(parts, 2)


def joined(parts, other, after):
    def kernel(*refs):
        total = refs[0][...].astype(F32)
        for ref in refs[1 : len(parts)]:
            total = total + ref[...].astype(F32)
        refs[-1][0] = total.astype(BF16)
        refs[-1][1] = refs[len(parts)][...]

    return call(
        kernel,
        "joined",
        [VMEM] * (len(parts) + 1) + [ANY] * len(after),
        VMEM,
        jax.ShapeDtypeStruct((2,) + other.shape, BF16),
        [],
        8,
        (*parts, other, *after),
    )


def line_sum(share):
    lines = lax.axis_size("feat")
    if lines & (lines - 1) != 0:
        return lax.psum(share.astype(F32), "feat").astype(BF16)
    step = 1
    while step < lines:
        other = lax.ppermute(share, "feat", [(i, i ^ step) for i in range(lines)])
        share = added([share, other])
        step *= 2
    return share


def stacked(values):
    def kernel(*refs):
        for i, ref in enumerate(refs[:-1]):
            refs[-1][i] = ref[...]

    shape = (len(values),) + values[0].shape
    out = jax.ShapeDtypeStruct(shape, values[0].dtype)
    return call(kernel, "stacked", [VMEM] * len(values), VMEM, out, [], 4, values)


def plane_gathered(plane, share):
    core, ahead, side = plane.sizes
    steps = [(0, j, k) for j in range(ahead) for k in range(side)]
    share = stacked([share] + [plane.passed_by(share, by) for by in steps[1:]])
    share = share.reshape(ahead, side, *share.shape[-3:])
    return [share] + [plane.passed(share, 0, i) for i in range(1, core)]


def second_out(z, bound, live, f1, act, w_out, out):
    def kernel(bound, live, f_lent, f_rest, act, wo, _out, out, token, keep, sems):
        copies = []
        token[...] = jnp.zeros_like(token)

        def work(part, first):
            f = z.flat(group_of(z, (f_lent, f_rest), part, first)[...])
            res = f.astype(F32) + dot(z.flat(act[pl.ds(first, z.group)]), wo[1])
            keep[pl.ds(first, z.group)] = z.tiled(live_rows(z, res, first, live[0]).astype(BF16))

        each_group(z, work, (0,))
        for i in range(z.lent):
            copy = pltpu.make_async_copy(
                keep.at[i], out.at[1, bound[0, i // z.edge, i % z.edge]], sems.at[i]
            )
            copy.start()
            copies.append(copy)
        each_group(z, work, (1,))
        tail = pl.ds(z.lent, z.rest)
        copy = pltpu.make_async_copy(keep.at[tail], out.at[1, tail], sems.at[z.lent])
        copy.start()
        copies.append(copy)
        for copy in copies:
            copy.wait()

    return call(
        kernel,
        "second_out",
        [SMEM] * 2 + [VMEM] * 4 + [ANY],
        [ANY, VMEM],
        [jax.ShapeDtypeStruct(out.shape, BF16), TOKEN],
        [z.held(z.tiles), pltpu.SemaphoreType.DMA((z.lent + 1,))],
        12,
        (bound, live, *f1, act, w_out, out),
        {6: 0},
    )


def input_grad(z, layer, tables, m, dpre, dagg, at, wt):
    arrays = (m, dpre, dagg)
    flat_args = [x for a in arrays for x in (a if isinstance(a, tuple) else (a,))]

    def kernel(blocks, sources, targets, counts, *refs):
        refs = list(refs)
        m, dpre, dagg = [
            (refs.pop(0), refs.pop(0)) if isinstance(a, tuple) else refs.pop(0) for a in arrays
        ]
        at, wt, part_out, rest_out, token, acc = refs
        token[...] = jnp.zeros_like(token)

        def direct(part, first):
            mine = z.flat(group_of(z, m, part, first)[...]).astype(F32)
            res = mine + dot(z.flat(group_of(z, dpre, part, first)[...]), wt[layer, 0])
            acc[pl.ds(first, z.group)] = z.tiled(res)

        each_group(z, direct)

        def source(q):
            if not isinstance(dagg, tuple):
                return dagg[q]
            lent = dagg[0][jnp.minimum(q, z.lent - 1)]
            rest = dagg[1][jnp.maximum(q - z.lent, 0)]
            return jnp.where(q < z.lent, lent, rest)

        spread(z, (blocks, sources, targets, counts), 0, z.tiles, at, source, acc, True)
        part_out[...] = acc[pl.ds(0, z.lent)]
        rest_out[...] = acc[pl.ds(z.lent, z.rest)].astype(BF16)

    return call(
        kernel,
        "input_grad%d" % layer,
        [SMEM] * 4 + [VMEM] * (len(flat_args) + 2),
        [VMEM] * 3,
        [z.nodes(z.lent, F32), z.nodes(z.rest), TOKEN],
        [z.held(z.tiles, F32)],
        20,
        [*tables, *flat_args, at, wt],
    )


def early_rest(z, tables, live, upstream, slope, at, wt):
    def kernel(blocks, sources, targets, counts, live, g, slope, at, wt, grads, m, dpre, dagg, outer, sem):
        copy = pltpu.make_async_copy(g, grads.at[1, pl.ds(z.lent, z.rest)], sem)
        copy.start()

        def work(part, first):
            here = pl.ds(first - z.lent, z.group)
            masked = live_rows(z, z.flat(g[here]), first, live[0])
            m[here] = z.tiled(masked)
            grad = dot(masked, wt[0, 2]) * z.flat(slope[pl.ds(first, z.group)])
            grad = grad.astype(BF16)
            dpre[here] = z.tiled(grad)
            dagg[here] = z.tiled(dot(grad, wt[0, 1]).astype(BF16))

        each_group(z, work, (1,))

        def source(q):
            return dagg[jnp.maximum(q - z.lent, 0)]

        spread(z, (blocks, sources, targets, counts), 3, z.lent, at, source, outer, False)
        copy.wait()

    return call(
        kernel,
        "early_rest",
        [SMEM] * 5 + [VMEM] * 4,
        [ANY] + [VMEM] * 4,
        [jax.ShapeDtypeStruct((2, z.tiles, z.rows, z.cols), BF16)]
        + [z.nodes(z.rest)] * 3
        + [z.nodes(z.lent, F32)],
        [pltpu.SemaphoreType.DMA],
        14,
        (*tables, live, upstream, slope, at, wt),
    )


def early_lent(z, tables, bound, part, fw, fe, slope, outer, at, wt, grads, after):
    def kernel(blocks, sources, targets, counts, bound, part, fw, fe, slope, outer, at, wt, _g, _ready, _late,
               m, dpre, dagg, grads, to_west, to_east, acc, sems):
        def work(first, got):
            here = pl.ds(first, z.group)
            g = z.flat((part[here] + got.astype(F32)).astype(BF16))
            m[here] = z.tiled(g)
            grad = (dot(g, wt[0, 2]) * z.flat(slope[here])).astype(BF16)
            dpre[here] = z.tiled(grad)
            dagg[here] = z.tiled(dot(grad, wt[0, 1]).astype(BF16))

        @pl.loop(0, z.edge // z.group)
        def _(s):
            here = pl.ds(s * z.group, z.group)
            work(s * z.group, fw[here])
            work(z.edge + s * z.group, fe[here])

        copies = [
            pltpu.make_async_copy(m.at[i], grads.at[1, bound[0, i // z.edge, i % z.edge]], sems.at[i])
            for i in range(z.lent)
        ]
        for copy in copies:
            copy.start()
        acc[...] = outer[...]

        def source(q):
            return dagg[jnp.minimum(q, z.lent - 1)]

        spread(z, (blocks, sources, targets, counts), 2, z.lent, at, source, acc, True)
        to_west[...] = acc[pl.ds(0, z.edge)].astype(BF16)
        to_east[...] = acc[pl.ds(z.edge, z.edge)].astype(BF16)
        for copy in copies:
            copy.wait()

    return call(
        kernel,
        "early_lent",
        [SMEM] * 5 + [VMEM] * 7 + [ANY, VMEM, VMEM],
        [VMEM] * 3 + [ANY] + [VMEM] * 2,
        [z.nodes(z.lent)] * 3 + [jax.ShapeDtypeStruct(grads.shape, BF16)] + [z.nodes(z.edge)] * 2,
        [z.held(z.lent, F32), pltpu.SemaphoreType.DMA((z.lent,))],
        16,
        (*tables, bound, part, fw, fe, slope, outer, at, wt, grads, *after),
        {12: 3},
    )


def finish(z, bound, part, rest, fw, fe, grads):
    def kernel(bound, part, rest, fw, fe, _g, grads, keep, sems):
        copies = [pltpu.make_async_copy(rest, grads.at[0, pl.ds(z.lent, z.rest)], sems.at[z.lent])]
        copies[0].start()
        for i in range(z.lent):
            got = fw[i] if i < z.edge else fe[i - z.edge]
            keep[i] = (part[i] + got.astype(F32)).astype(BF16)
            copy = pltpu.make_async_copy(
                keep.at[i], grads.at[0, bound[0, i // z.edge, i % z.edge]], sems.at[i]
            )
            copy.start()
            copies.append(copy)
        for copy in copies:
            copy.wait()

    return call(
        kernel,
        "finish",
        [SMEM] + [VMEM] * 4 + [ANY],
        ANY,
        jax.ShapeDtypeStruct(grads.shape, BF16),
        [z.held(z.lent), pltpu.SemaphoreType.DMA((z.lent + 1,))],
        14,
        (bound, part, rest, fw, fe, grads),
        {5: 0},
    )


def unpack(z, plane, pieces):
    c = z.cols
    piece = pieces[0].shape[3]
    core, ahead, side = plane.sizes

    def kernel(me, *refs):
        pieces = refs[:core]
        *outs, bias, buf, sems = refs[core:]
        copies = []
        for layer in range(2):
            for i in range(core):
                for j in range(ahead):
                    for k in range(side):
                        start = pl.multiple_of(plane.piece_of(me, (-i, -j, -k)) * piece, 16)
                        buf[layer, pl.ds(start, piece), :] = pieces[i][j, k, layer].astype(F32)
            for i, out in enumerate(outs):
                copy = pltpu.make_async_copy(
                    buf.at[layer, pl.ds(i * c, c)], out.at[layer], sems.at[3 * layer + i]
                )
                copy.start()
                copies.append(copy)
            bias[layer : layer + 1, :] = buf[layer, pl.ds(3 * c, 1), :]
        for copy in copies:
            copy.wait()

    square = jax.ShapeDtypeStruct((2, c, c), F32)
    return call(
        kernel,
        "unpack",
        [SMEM] + [VMEM] * core,
        [ANY] * 3 + [VMEM],
        [square, square, square, jax.ShapeDtypeStruct((2, c), F32)],
        [pltpu.VMEM((2, piece * plane.count, c), F32), pltpu.SemaphoreType.DMA((6,))],
        10,
        (plane.me, *pieces),
    )


def per_device(
    node_in, out_cot, adjacency, tile_nbrs, bound_tiles, live_tiles, w_self, w_nbr, pre_bias, w_out
):
    z = Sizes(adjacency, node_in, bound_tiles)
    t, r, c = z.tiles, z.rows, z.cols
    features = node_in.reshape(t, r, c)
    cot = out_cot.reshape(t, r, c)
    plane = Plane()

    west, east = lend(z, bound_tiles, features)
    from_west = passed_along(east, 1)
    from_east = passed_along(west, -1)
    *nodes, adj, tiles, reads, blocks, sources, targets, counts, plane.me = arrange(
        z, bound_tiles, tile_nbrs, live_tiles, plane.place, features, cot, adjacency.reshape(z.pairs, r, r)
    )
    f0, m1 = tuple(nodes[:2]), tuple(nodes[2:])
    tables = (blocks, sources, targets, counts)
    at, wt = turn(z, adj, w_self, w_nbr, w_out)

    west, east, agg_lent = first_lent(
        z, tiles, reads, f0, from_west, from_east, adj, w_self, w_nbr, pre_bias, w_out
    )
    next_west = passed_along(east, 1)
    next_east = passed_along(west, -1)
    f1_lent, f1_rest, section_out, agg_rest = first_rest(
        z, tiles, reads, bound_tiles, live_tiles, f0, from_west, from_east, adj, w_self, w_nbr, pre_bias, w_out,
        west, east,
    )
    f1, agg0 = (f1_lent, f1_rest), (agg_lent, agg_rest)
    hidden = second_own(z, m1, wt)
    act0, slope, ready = saved(z, f0, agg0, w_self, w_nbr, pre_bias)

    agg1, act1, dpre1, dagg1, to_west, to_east = second(
        z, tiles, reads, tables, f1, next_west, next_east, adj, at, hidden, w_self, w_nbr, pre_bias, wt, ready
    )
    back_west = passed_along(to_east, 1)
    back_east = passed_along(to_west, -1)
    late = weight_grads(z, plane, f1, agg1, act1, m1, dpre1, "weight_grads1")
    section_out, ready = second_out(z, bound_tiles, live_tiles, f1, act1, w_out, section_out)
    part, upstream, done = input_grad(z, 1, tables, m1, dpre1, dagg1, at, wt)
    late = plane_parts(plane, late, ((ready,), (done,)))
    grads, m0_rest, dpre_rest, dagg_rest, outer = early_rest(
        z, tables, live_tiles, upstream, slope, at, wt
    )
    late = added(late, after=(outer,))

    m0_lent, dpre_lent, dagg_lent, grads, to_west, to_east = early_lent(
        z, tables, bound_tiles, part, back_west, back_east, slope, outer, at, wt, grads, (ready, late)
    )
    back_west = passed_along(to_east, 1)
    back_east = passed_along(to_west, -1)
    m0, dpre0, dagg0 = (m0_lent, m0_rest), (dpre_lent, dpre_rest), (dagg_lent, dagg_rest)
    early = weight_grads(z, plane, f0, agg0, act0, m0, dpre0, "weight_grads0")


    def meanwhile(early, tables, m0, dpre0, dagg0, at, wt):
        part, rest, _ = input_grad(z, 0, tables, m0, dpre0, dagg0, at, wt)
        return plane_parts(plane, early), part, rest

    args = (early, tables, m0, dpre0, dagg0, at, wt)
    shapes = jax.eval_shape(meanwhile, *args)
    early, part, rest = lax.cond(
        live_tiles[0] > 0,
        meanwhile,
        lambda *_: jax.tree.map(lambda a: jnp.zeros(a.shape, a.dtype), shapes),
        *args,
    )
    shares = line_sum(joined(early, late, (back_west, back_east)))
    pieces = plane_gathered(plane, shares)
    grads = finish(z, bound_tiles, part, rest, back_west, back_east, grads)
    grad_self, grad_nbr, grad_out, grad_bias = unpack(z, plane, pieces)
    return (
        section_out.reshape(2, t * r, c),
        grads.reshape(2, t * r, c),
        grad_self,
        grad_nbr,
        grad_bias,
        grad_out,
    )


def solution(mesh):
    rows = P(AXES)
    in_specs = (rows, rows, rows, rows, rows, rows, P(), P(), P(), P())
    out_specs = (P(None, AXES), P(None, AXES), P(), P(), P(), P())
    return jax.shard_map(
        per_device, mesh=mesh, in_specs=in_specs, out_specs=out_specs, check_vma=False
    )
```

```python
import jax
import jax.numpy as jnp
from jax import lax
from jax.experimental import pallas as pl
from jax.experimental.pallas import tpu as pltpu
from jax.sharding import PartitionSpec as P

AXES = ("dom", "phase", "feat")
PLANE = ("dom", "phase")
BF16 = jnp.bfloat16
F32 = jnp.float32
ANY = pl.BlockSpec(memory_space=pl.ANY)
SMEM = pl.BlockSpec(memory_space=pltpu.SMEM)
VMEM = pl.BlockSpec(memory_space=pltpu.VMEM)
MIB = 1024 * 1024
TOKEN = jax.ShapeDtypeStruct((8, 128), F32)


class Sizes:
    def __init__(self, adjacency, features, bound):
        self.tiles, self.slots, self.rows, _ = adjacency.shape
        self.cols = features.shape[-1]
        self.edge = bound.shape[-1]
        self.lent = 2 * self.edge
        self.rest = self.tiles - self.lent
        self.ext = self.tiles + self.lent
        self.pairs = self.tiles * self.slots
        self.group = next(g for g in (4, 2, 1) if self.edge % g == 0 and self.rest % g == 0)
        self.parts = ((0, 0, self.lent), (1, self.lent, self.rest))
        self.index = Index(self)

    def nodes(self, count, dtype=BF16):
        return jax.ShapeDtypeStruct((count, self.rows, self.cols), dtype)

    def held(self, count, dtype=BF16):
        return pltpu.VMEM((count, self.rows, self.cols), dtype)

    def flat(self, value):
        return value.reshape(self.group * self.rows, self.cols)

    def tiled(self, value):
        return value.reshape(self.group, self.rows, self.cols)


def group_of(z, array, part, first):
    if isinstance(array, tuple):
        base = z.lent if part else 0
        return array[part].at[pl.ds(first - base, z.group)]
    return array.at[pl.ds(first, z.group)]


def each_group(z, body, parts=(0, 1), unroll=1):
    for part, base, count in z.parts:
        if part in parts:

            @pl.loop(0, count // z.group, unroll=unroll)
            def _(s):
                body(part, base + s * z.group)


def passed_along(value, steps):
    count = lax.axis_size(AXES)
    return lax.ppermute(value, AXES, [(i, (i + steps) % count) for i in range(count)])


def dot(a, b):
    return jnp.dot(a, b, preferred_element_type=F32)


def dot_rows(a, b):
    return lax.dot_general(a, b, (((0,), (0,)), ((), ())), preferred_element_type=F32)


def call(kernel, name, in_specs, out_specs, out_shape, scratch, limit, args, aliases=None):
    return pl.pallas_call(
        kernel,
        in_specs=in_specs,
        out_specs=out_specs,
        out_shape=out_shape,
        scratch_shapes=scratch,
        input_output_aliases=aliases or {},
        compiler_params=pltpu.CompilerParams(vmem_limit_bytes=limit * MIB),
        cost_estimate=pl.CostEstimate(flops=1000, bytes_accessed=1000, transcendentals=0),
        name=name,
    )(*args)


def sigmoid(v):
    return 0.5 * jnp.tanh(0.5 * v) + 0.5


def lend(z, bound, features):
    def kernel(bound, feats, west, east, sems):
        copies = []
        for i in range(z.edge):
            for side, target in ((0, west), (1, east)):
                copy = pltpu.make_async_copy(
                    feats.at[bound[0, side, i]], target.at[i], sems.at[side * z.edge + i]
                )
                copy.start()
                copies.append(copy)
        for copy in copies:
            copy.wait()

    return call(
        kernel,
        "lend",
        [SMEM, ANY],
        [VMEM, VMEM],
        [z.nodes(z.edge), z.nodes(z.edge)],
        [pltpu.SemaphoreType.DMA((z.lent,))],
        56,
        (bound, features),
    )


class Index:
    QUAD = 4

    def __init__(self, z):
        self.first = (0, z.tiles, z.tiles + z.lent, z.tiles + 2 * z.lent, z.tiles + 3 * z.lent)
        self.targets = z.tiles + 3 * z.lent + 1
        self.more = tuple(self.QUAD * self.targets + i * z.pairs for i in range(5))
        self.size = self.QUAD * self.targets + 5 * z.pairs
        self.size = -(-self.size // 8) * 8


def arrange(z, bound, nbrs, live, place, features, cot, adjacency):
    s4 = z.slots
    x = z.index

    def kernel(bound, nbrs, live, place, feats, cot, adj, f_lent, f_rest, m_lent, m_rest, adj_out,
               tiles, reads, blocks, sources, targets, counts, me, inverse, used, sems):
        copies = []
        for i in range(8):
            me[i] = place[i]

        def start(source, target):
            copy = pltpu.make_async_copy(source, target, sems.at[len(copies)])
            copy.start()
            copies.append(copy)

        tail = pl.ds(z.lent, z.rest)
        start(feats.at[tail], f_rest)
        start(cot.at[tail], m_rest)
        start(adj, adj_out)
        for i in range(z.lent):
            tile = bound[0, i // z.edge, i % z.edge]
            inverse[tile] = i
            start(feats.at[tile], f_lent.at[i])
            start(cot.at[tile], m_lent.at[i])

        @pl.loop(0, x.targets)
        def _(i):
            used[i] = 0
            for k in range(x.QUAD):
                blocks[i * x.QUAD + k] = -1
                sources[i * x.QUAD + k] = 0

        for i in range(8):
            counts[i] = 0

        def put(table, target, block, position):
            place = used[target]
            used[target] = place + 1
            fits = place < x.QUAD
            listed = counts[table]
            counts[table] = listed + jnp.where(fits, 0, 1)
            at = jnp.where(fits, target * x.QUAD + place, x.more[0] + table * z.pairs + listed)
            blocks[at] = block
            sources[at] = position
            return at

        @pl.loop(0, z.tiles)
        def _(position):
            clipped = jnp.minimum(position, z.lent - 1)
            tile = jnp.where(position < z.lent, bound[0, clipped // z.edge, clipped % z.edge], position)
            tiles[position] = tile
            for k in range(s4):
                target = nbrs[tile, k]
                moved = jnp.where(target < z.lent, inverse[jnp.minimum(target, z.lent - 1)], target)
                reads[position * s4 + k] = moved
                block = tile * s4 + k
                own = moved < z.tiles
                at = put(jnp.where(own, 0, 1), moved, block, position)
                targets[at] = jnp.where(own, moved, moved - z.tiles)
                lent = position < z.lent
                table = jnp.where(own, 4, jnp.where(lent, 2, 3))
                shift = jnp.where(lent, z.lent, 2 * z.lent)
                at = put(table, jnp.where(own, x.first[4], moved + shift), block, position)
                targets[at] = moved - z.tiles

        for copy in copies:
            copy.wait()

        @pl.loop(0, z.rest)
        def _(i):
            @pl.when(z.lent + i >= live[0])
            def _():
                m_rest[i] = jnp.zeros((z.rows, z.cols), BF16)

    return call(
        kernel,
        "arrange",
        [SMEM] * 4 + [ANY] * 3,
        [VMEM] * 5 + [SMEM] * 7,
        [z.nodes(z.lent), z.nodes(z.rest), z.nodes(z.lent), z.nodes(z.rest)]
        + [jax.ShapeDtypeStruct(adjacency.shape, BF16)]
        + [jax.ShapeDtypeStruct((n,), jnp.int32) for n in (z.tiles, z.pairs, x.size, x.size, x.size, 8, 8)],
        [
            pltpu.SMEM((z.lent,), jnp.int32),
            pltpu.SMEM((x.targets,), jnp.int32),
            pltpu.SemaphoreType.DMA((2 * z.lent + 3,)),
        ],
        12,
        (bound, nbrs, live, place, features, cot, adjacency),
    )


def turn(z, adj, w_self, w_nbr, w_out):
    def kernel(adj, ws, wn, wo, at, wt):
        for layer in range(2):
            wt[layer, 0] = ws[layer].T
            wt[layer, 1] = wn[layer].T
            wt[layer, 2] = wo[layer].T

        @pl.loop(0, z.pairs, unroll=4)
        def _(i):
            at[i] = adj[i].T

    return call(
        kernel,
        "turn",
        [VMEM] * 4,
        [VMEM, VMEM],
        [jax.ShapeDtypeStruct(adj.shape, BF16), jax.ShapeDtypeStruct((2, 3, z.cols, z.cols), BF16)],
        [],
        12,
        (adj, w_self, w_nbr, w_out),
    )


def fill_extended(z, own, fw, fe, ext):
    ext[pl.ds(0, z.lent)] = own[0][...]
    ext[pl.ds(z.lent, z.rest)] = own[1][...]
    ext[pl.ds(z.tiles, z.edge)] = fw[...]
    ext[pl.ds(z.tiles + z.edge, z.edge)] = fe[...]


def aggregate(z, tiles, reads, first, adj, ext):
    rows = []
    for g in range(z.group):
        base = (first + g) * z.slots
        block = tiles[first + g] * z.slots
        picked = jnp.concatenate([ext[reads[base + k]] for k in range(z.slots)], axis=0)
        blocks = jnp.concatenate([adj[block + k] for k in range(z.slots)], axis=1)
        rows.append(dot(blocks, picked).astype(BF16))
    return jnp.concatenate(rows, axis=0)


def live_rows(z, value, first, live):
    parts = []
    for g in range(z.group):
        part = value[g * z.rows : (g + 1) * z.rows]
        parts.append(jnp.where(first + g < live, part, jnp.zeros_like(part)))
    return jnp.concatenate(parts, axis=0)


def first_lent(z, tiles, reads, f0, fw, fe, adj, w_self, w_nbr, bias, w_out):
    def kernel(tiles, reads, f_lent, f_rest, fw, fe, adj, ws, wn, bias, wo, west, east, agg, ext):
        fill_extended(z, (f_lent, f_rest), fw, fe, ext)

        def work(first, target, offset):
            here = pl.ds(first, z.group)
            f = z.flat(ext[here])
            aggs = aggregate(z, tiles, reads, first, adj, ext)
            agg[here] = z.tiled(aggs)
            pre = dot(f, ws[0]) + dot(aggs, wn[0]) + bias[0:1, :]
            act = (pre * sigmoid(pre)).astype(BF16)
            target[pl.ds(offset, z.group)] = z.tiled((f.astype(F32) + dot(act, wo[0])).astype(BF16))

        @pl.loop(0, z.edge // z.group)
        def _(s):
            work(s * z.group, west, s * z.group)
            work(z.edge + s * z.group, east, s * z.group)

    return call(
        kernel,
        "first_lent",
        [SMEM] * 2 + [VMEM] * 9,
        [VMEM] * 3,
        [z.nodes(z.edge), z.nodes(z.edge), z.nodes(z.lent)],
        [z.held(z.ext)],
        12,
        (tiles, reads, *f0, fw, fe, adj, w_self, w_nbr, bias, w_out),
    )


def first_rest(z, tiles, reads, bound, live, f0, fw, fe, adj, w_self, w_nbr, bias, w_out, west, east):
    def kernel(tiles, reads, bound, live, f_lent, f_rest, fw, fe, adj, ws, wn, bias, wo, west, east,
               f1_lent, f1_rest, out, agg, ext, sems):
        copies = []
        for i in range(z.edge):
            for side, source in ((0, west), (1, east)):
                copy = pltpu.make_async_copy(
                    source.at[i], out.at[0, bound[0, side, i]], sems.at[side * z.edge + i]
                )
                copy.start()
                copies.append(copy)
        fill_extended(z, (f_lent, f_rest), fw, fe, ext)
        f1_lent[pl.ds(0, z.edge)] = west[...]
        f1_lent[pl.ds(z.edge, z.edge)] = east[...]

        def work(part, first):
            f = z.flat(ext[pl.ds(first, z.group)])
            aggs = aggregate(z, tiles, reads, first, adj, ext)
            here = pl.ds(first - z.lent, z.group)
            agg[here] = z.tiled(aggs)
            pre = dot(f, ws[0]) + dot(aggs, wn[0]) + bias[0:1, :]
            act = (pre * sigmoid(pre)).astype(BF16)
            res = live_rows(z, f.astype(F32) + dot(act, wo[0]), first, live[0])
            f1_rest[here] = z.tiled(res.astype(BF16))

        each_group(z, work, (1,))
        copy = pltpu.make_async_copy(f1_rest, out.at[0, pl.ds(z.lent, z.rest)], sems.at[z.lent])
        copy.start()
        for other in copies:
            other.wait()
        copy.wait()

    return call(
        kernel,
        "first_rest",
        [SMEM] * 4 + [VMEM] * 11,
        [VMEM, VMEM, ANY, VMEM],
        [
            z.nodes(z.lent),
            z.nodes(z.rest),
            jax.ShapeDtypeStruct((2, z.tiles, z.rows, z.cols), BF16),
            z.nodes(z.rest),
        ],
        [z.held(z.ext), pltpu.SemaphoreType.DMA((1 + z.lent,))],
        10,
        (tiles, reads, bound, live, *f0, fw, fe, adj, w_self, w_nbr, bias, w_out, west, east),
    )


def second_own(z, f1, m1, w_self, bias, wt):
    def kernel(f_lent, f_rest, m_lent, m_rest, ws, bias, wt, own, hidden):
        def work(part, first):
            f = z.flat(group_of(z, (f_lent, f_rest), part, first)[...])
            m = z.flat(group_of(z, (m_lent, m_rest), part, first)[...])
            here = pl.ds(first, z.group)
            own[here] = z.tiled(dot(f, ws[1]) + bias[1:2, :])
            hidden[here] = z.tiled(dot(m, wt[1, 2]))

        each_group(z, work)

    return call(
        kernel,
        "second_own",
        [VMEM] * 7,
        [VMEM] * 2,
        [z.nodes(z.tiles, F32)] * 2,
        [],
        12,
        (*f1, *m1, w_self, bias, wt),
    )


def saved(z, f0, agg0, w_self, w_nbr, bias):
    def kernel(f_lent, f_rest, a_lent, a_rest, ws, wn, bias, act, slope, token):
        token[...] = jnp.zeros_like(token)

        def work(part, first):
            f = z.flat(group_of(z, (f_lent, f_rest), part, first)[...])
            aggs = z.flat(group_of(z, (a_lent, a_rest), part, first)[...])
            pre = dot(f, ws[0]) + dot(aggs, wn[0]) + bias[0:1, :]
            sig = sigmoid(pre)
            here = pl.ds(first, z.group)
            act[here] = z.tiled((pre * sig).astype(BF16))
            slope[here] = z.tiled(sig * (1.0 + pre * (1.0 - sig)))

        each_group(z, work)

    return call(
        kernel,
        "saved",
        [VMEM] * 7,
        [VMEM] * 3,
        [z.nodes(z.tiles), z.nodes(z.tiles, F32), TOKEN],
        [],
        10,
        (*f0, *agg0, w_self, w_nbr, bias),
    )


def spread(z, tables, table, count, at, source, acc, add):
    blocks, sources, targets, counts = tables
    x = z.index

    @pl.loop(0, count, unroll=4)
    def _(target):
        base = (x.first[table] + target) * x.QUAD
        lefts, rights = [], []
        for k in range(x.QUAD):
            block = blocks[base + k]
            left = at[jnp.maximum(block, 0)]
            lefts.append(jnp.where(block >= 0, left, jnp.zeros_like(left)))
            rights.append(source(sources[base + k]))
        value = dot(jnp.concatenate(lefts, axis=1), jnp.concatenate(rights, axis=0))
        if add:
            acc[target] += value
        else:
            acc[target] = value

    @pl.loop(0, counts[table])
    def _(i):
        place = x.more[table] + i
        acc[targets[place]] += dot(at[blocks[place]], source(sources[place]))


def second(z, tiles, reads, tables, f1, fw, fe, adj, at, own, hidden, w_nbr, wt, after):
    groups = z.tiles // z.group

    def kernel(tiles, reads, blocks, sources, targets, counts, f_lent, f_rest, fw, fe, adj, at, own, hidden, wn,
               wt, _after, agg, act, dpre, dagg, to_west, to_east, ext, acc):
        fill_extended(z, (f_lent, f_rest), fw, fe, ext)

        def gather(s):
            agg[pl.ds(s * z.group, z.group)] = z.tiled(aggregate(z, tiles, reads, s * z.group, adj, ext))

        def middle(s):
            here = pl.ds(s * z.group, z.group)
            pre = z.flat(own[here]) + dot(z.flat(agg[here]), wn[1])
            sig = sigmoid(pre)
            act[here] = z.tiled((pre * sig).astype(BF16))
            slope = sig * (1.0 + pre * (1.0 - sig))
            dpre[here] = z.tiled((z.flat(hidden[here]) * slope).astype(BF16))

        def last(s):
            here = pl.ds(s * z.group, z.group)
            dagg[here] = z.tiled(dot(z.flat(dpre[here]), wt[1, 1]).astype(BF16))

        for s in range(groups + 2):
            if s < groups:
                gather(s)
            if 0 <= s - 1 < groups:
                middle(s - 1)
            if s >= 2:
                last(s - 2)

        spread(z, (blocks, sources, targets, counts), 1, z.lent, at, lambda q: dagg[q], acc, False)
        to_west[...] = acc[pl.ds(0, z.edge)].astype(BF16)
        to_east[...] = acc[pl.ds(z.edge, z.edge)].astype(BF16)

    return call(
        kernel,
        "second",
        [SMEM] * 6 + [VMEM] * 11,
        [VMEM] * 6,
        [z.nodes(z.tiles)] * 4 + [z.nodes(z.edge)] * 2,
        [z.held(z.ext), z.held(z.lent, F32)],
        12,
        (tiles, reads, *tables, *f1, fw, fe, adj, at, own, hidden, w_nbr, wt, after),
    )


class Plane:
    def __init__(self):
        dom, phase = lax.axis_size("dom"), lax.axis_size("phase")
        core = 2 if dom % 2 == 0 else 1
        self.sizes = (core, dom // core, phase)
        self.count = dom * phase
        place = lax.axis_index("dom")
        place = [lax.rem(place, core), place // core, lax.axis_index("phase")]
        self.place = jnp.stack(place + [jnp.zeros_like(place[0])] * 5).astype(jnp.int32)
        self.me = None

    def piece_of(self, me, steps):
        at = [lax.rem(me[i] + (steps[i] + n) % n, n) for i, n in enumerate(self.sizes)]
        return (at[0] * self.sizes[1] + at[1]) * self.sizes[2] + at[2]

    def passed(self, value, dim, steps):
        return self.passed_by(value, [steps if i == dim else 0 for i in range(3)])

    def passed_by(self, value, steps):
        pairs = []
        for c in range(self.sizes[0]):
            for d in range(self.sizes[1]):
                for p in range(self.sizes[2]):
                    to = [(at + by) % n for at, by, n in zip((c, d, p), steps, self.sizes)]
                    source = (d * self.sizes[0] + c) * self.sizes[2] + p
                    target = (to[1] * self.sizes[0] + to[0]) * self.sizes[2] + to[2]
                    pairs.append((source, target))
        return lax.ppermute(value, PLANE, pairs)

    def received(self, parts, dim):
        return [parts[0]] + [self.passed(parts[i], dim, i) for i in range(1, self.sizes[dim])]


def weight_grads(z, plane, f, agg, act, m, dpre, name):
    c = z.cols
    piece = -(-(3 * c + 1) // (plane.count * 16)) * 16
    core, ahead, side = plane.sizes
    arrays = (f, agg, act, m, dpre)
    flat_args = [x for a in arrays for x in (a if isinstance(a, tuple) else (a,))]

    def kernel(me, *refs):
        refs = list(refs)
        f, agg, act, m, dpre = [
            (refs.pop(0), refs.pop(0)) if isinstance(a, tuple) else refs.pop(0) for a in arrays
        ]
        *outs, acc, sums = refs
        acc[...] = jnp.zeros_like(acc)
        sums[...] = jnp.zeros_like(sums)

        def work(part, first):
            def rows(array):
                return z.flat(group_of(z, array, part, first)[...])

            grad = rows(dpre)
            turned = grad.T
            sums[0] += dot(turned, rows(f))
            sums[1] += dot(turned, rows(agg))
            sums[2] += dot(rows(m).T, rows(act))
            acc[pl.ds(3 * c, 1), :] += jnp.sum(grad.astype(F32), axis=0, keepdims=True)

        each_group(z, work)
        for i in range(3):
            acc[pl.ds(i * c, c), :] = sums[i].T
        for i, out in enumerate(outs):
            for j in range(ahead):
                for k in range(side):
                    owner = pl.multiple_of(plane.piece_of(me, (i, j, k)) * piece, 16)
                    out[j, k] = acc[pl.ds(owner, piece), :].astype(BF16)

    return call(
        kernel,
        name,
        [SMEM] + [VMEM] * len(flat_args),
        [VMEM] * core,
        [jax.ShapeDtypeStruct((ahead, side, piece, c), BF16)] * core,
        [pltpu.VMEM((piece * plane.count, c), F32), pltpu.VMEM((3, c, c), F32)],
        14,
        (plane.me, *flat_args),
    )


def added(values, split=False, after=()):
    shape = values[0].shape
    count = shape[0] if split else 1

    def kernel(*refs):
        outs = refs[-count:]
        for i, out in enumerate(outs):
            parts = [ref[i] if split else ref[...] for ref in refs[: len(values)]]
            parts = [part.astype(F32) for part in parts]
            total = parts[0]
            for part in parts[1:]:
                total = total + part
            out[...] = total.astype(BF16)

    args = [*values, *after]
    outs = call(
        kernel,
        "added",
        [VMEM] * len(values) + [ANY] * len(after),
        [VMEM] * count,
        [jax.ShapeDtypeStruct(shape[1:] if split else shape, BF16)] * count,
        [],
        8,
        args,
    )
    return outs if split else outs[0]


def plane_parts(plane, pieces, after=((), ())):
    parts = added(plane.received(pieces, 0), split=True, after=after[0])
    parts = added(plane.received(parts, 1), split=True, after=after[1])
    return plane.received(parts, 2)


def joined(parts, other):
    def kernel(*refs):
        total = refs[0][...].astype(F32)
        for ref in refs[1 : len(parts)]:
            total = total + ref[...].astype(F32)
        refs[-1][0] = total.astype(BF16)
        refs[-1][1] = refs[len(parts)][...]

    return call(
        kernel,
        "joined",
        [VMEM] * (len(parts) + 1),
        VMEM,
        jax.ShapeDtypeStruct((2,) + other.shape, BF16),
        [],
        8,
        (*parts, other),
    )


def line_sum(share, after):
    lines = lax.axis_size("feat")
    if lines & (lines - 1) != 0:
        return lax.psum(share.astype(F32), "feat").astype(BF16)
    step = 1
    while step < lines:
        other = lax.ppermute(share, "feat", [(i, i ^ step) for i in range(lines)])
        share = added([share, other], after=after if step == 1 else ())
        step *= 2
    return share


def stacked(values):
    def kernel(*refs):
        for i, ref in enumerate(refs[:-1]):
            refs[-1][i] = ref[...]

    shape = (len(values),) + values[0].shape
    out = jax.ShapeDtypeStruct(shape, values[0].dtype)
    return call(kernel, "stacked", [VMEM] * len(values), VMEM, out, [], 4, values)


def plane_gathered(plane, share):
    core, ahead, side = plane.sizes
    steps = [(0, j, k) for j in range(ahead) for k in range(side)]
    share = stacked([share] + [plane.passed_by(share, by) for by in steps[1:]])
    share = share.reshape(ahead, side, *share.shape[-3:])
    return [share] + [plane.passed(share, 0, i) for i in range(1, core)]


def second_out(z, bound, live, f1, act, w_out, out):
    def kernel(bound, live, f_lent, f_rest, act, wo, _out, out, token, keep, sems):
        copies = []
        token[...] = jnp.zeros_like(token)

        def work(part, first):
            f = z.flat(group_of(z, (f_lent, f_rest), part, first)[...])
            res = f.astype(F32) + dot(z.flat(act[pl.ds(first, z.group)]), wo[1])
            keep[pl.ds(first, z.group)] = z.tiled(live_rows(z, res, first, live[0]).astype(BF16))

        each_group(z, work, (0,))
        for i in range(z.lent):
            copy = pltpu.make_async_copy(
                keep.at[i], out.at[1, bound[0, i // z.edge, i % z.edge]], sems.at[i]
            )
            copy.start()
            copies.append(copy)
        each_group(z, work, (1,))
        tail = pl.ds(z.lent, z.rest)
        copy = pltpu.make_async_copy(keep.at[tail], out.at[1, tail], sems.at[z.lent])
        copy.start()
        copies.append(copy)
        for copy in copies:
            copy.wait()

    return call(
        kernel,
        "second_out",
        [SMEM] * 2 + [VMEM] * 4 + [ANY],
        [ANY, VMEM],
        [jax.ShapeDtypeStruct(out.shape, BF16), TOKEN],
        [z.held(z.tiles), pltpu.SemaphoreType.DMA((z.lent + 1,))],
        12,
        (bound, live, *f1, act, w_out, out),
        {6: 0},
    )


def input_grad(z, layer, tables, m, dpre, dagg, at, wt):
    arrays = (m, dpre, dagg)
    flat_args = [x for a in arrays for x in (a if isinstance(a, tuple) else (a,))]

    def kernel(blocks, sources, targets, counts, *refs):
        refs = list(refs)
        m, dpre, dagg = [
            (refs.pop(0), refs.pop(0)) if isinstance(a, tuple) else refs.pop(0) for a in arrays
        ]
        at, wt, part_out, rest_out, token, acc = refs
        token[...] = jnp.zeros_like(token)
        x = z.index

        def source(q):
            if not isinstance(dagg, tuple):
                return dagg[q]
            lent = dagg[0][jnp.minimum(q, z.lent - 1)]
            rest = dagg[1][jnp.maximum(q - z.lent, 0)]
            return jnp.where(q < z.lent, lent, rest)

        def tile_of(array, part, base, i):
            return array[part][i] if isinstance(array, tuple) else array[base + i]

        for part, base, count in z.parts:

            @pl.loop(0, count, unroll=4)
            def _(i):
                lefts, rights = [tile_of(dpre, part, base, i)], [wt[layer, 0]]
                for k in range(x.QUAD):
                    block = blocks[(base + i) * x.QUAD + k]
                    left = at[jnp.maximum(block, 0)]
                    lefts.append(jnp.where(block >= 0, left, jnp.zeros_like(left)))
                    rights.append(source(sources[(base + i) * x.QUAD + k]))
                value = dot(jnp.concatenate(lefts, axis=1), jnp.concatenate(rights, axis=0))
                acc[base + i] = value + tile_of(m, part, base, i).astype(F32)

        @pl.loop(0, counts[0])
        def _(i):
            place = x.more[0] + i
            acc[targets[place]] += dot(at[blocks[place]], source(sources[place]))

        part_out[...] = acc[pl.ds(0, z.lent)]
        rest_out[...] = acc[pl.ds(z.lent, z.rest)].astype(BF16)

    return call(
        kernel,
        "input_grad%d" % layer,
        [SMEM] * 4 + [VMEM] * (len(flat_args) + 2),
        [VMEM] * 3,
        [z.nodes(z.lent, F32), z.nodes(z.rest), TOKEN],
        [z.held(z.tiles, F32)],
        20,
        [*tables, *flat_args, at, wt],
    )


def early_rest(z, tables, live, upstream, slope, at, wt):
    def kernel(blocks, sources, targets, counts, live, g, slope, at, wt, grads, m, dpre, dagg, outer, sem):
        copy = pltpu.make_async_copy(g, grads.at[1, pl.ds(z.lent, z.rest)], sem)
        copy.start()

        def work(part, first):
            here = pl.ds(first - z.lent, z.group)
            masked = live_rows(z, z.flat(g[here]), first, live[0])
            m[here] = z.tiled(masked)
            grad = dot(masked, wt[0, 2]) * z.flat(slope[pl.ds(first, z.group)])
            grad = grad.astype(BF16)
            dpre[here] = z.tiled(grad)
            dagg[here] = z.tiled(dot(grad, wt[0, 1]).astype(BF16))

        each_group(z, work, (1,))

        def source(q):
            return dagg[jnp.maximum(q - z.lent, 0)]

        spread(z, (blocks, sources, targets, counts), 3, z.lent, at, source, outer, False)
        copy.wait()

    return call(
        kernel,
        "early_rest",
        [SMEM] * 5 + [VMEM] * 4,
        [ANY] + [VMEM] * 4,
        [jax.ShapeDtypeStruct((2, z.tiles, z.rows, z.cols), BF16)]
        + [z.nodes(z.rest)] * 3
        + [z.nodes(z.lent, F32)],
        [pltpu.SemaphoreType.DMA],
        14,
        (*tables, live, upstream, slope, at, wt),
    )


def early_lent(z, tables, bound, part, fw, fe, slope, outer, at, wt, grads, after):
    def kernel(blocks, sources, targets, counts, bound, part, fw, fe, slope, outer, at, wt, _g, _ready, _late,
               m, dpre, dagg, grads, to_west, to_east, acc, sems):
        def work(first, got):
            here = pl.ds(first, z.group)
            g = z.flat((part[here] + got.astype(F32)).astype(BF16))
            m[here] = z.tiled(g)
            grad = (dot(g, wt[0, 2]) * z.flat(slope[here])).astype(BF16)
            dpre[here] = z.tiled(grad)
            dagg[here] = z.tiled(dot(grad, wt[0, 1]).astype(BF16))

        @pl.loop(0, z.edge // z.group)
        def _(s):
            here = pl.ds(s * z.group, z.group)
            work(s * z.group, fw[here])
            work(z.edge + s * z.group, fe[here])

        copies = [
            pltpu.make_async_copy(m.at[i], grads.at[1, bound[0, i // z.edge, i % z.edge]], sems.at[i])
            for i in range(z.lent)
        ]
        for copy in copies:
            copy.start()
        acc[...] = outer[...]

        def source(q):
            return dagg[jnp.minimum(q, z.lent - 1)]

        spread(z, (blocks, sources, targets, counts), 2, z.lent, at, source, acc, True)
        to_west[...] = acc[pl.ds(0, z.edge)].astype(BF16)
        to_east[...] = acc[pl.ds(z.edge, z.edge)].astype(BF16)
        for copy in copies:
            copy.wait()

    return call(
        kernel,
        "early_lent",
        [SMEM] * 5 + [VMEM] * 7 + [ANY, VMEM, VMEM],
        [VMEM] * 3 + [ANY] + [VMEM] * 2,
        [z.nodes(z.lent)] * 3 + [jax.ShapeDtypeStruct(grads.shape, BF16)] + [z.nodes(z.edge)] * 2,
        [z.held(z.lent, F32), pltpu.SemaphoreType.DMA((z.lent,))],
        16,
        (*tables, bound, part, fw, fe, slope, outer, at, wt, grads, *after),
        {12: 3},
    )


def finish(z, bound, part, rest, fw, fe, grads):
    def kernel(bound, part, rest, fw, fe, _g, grads, keep, sems):
        copies = [pltpu.make_async_copy(rest, grads.at[0, pl.ds(z.lent, z.rest)], sems.at[z.lent])]
        copies[0].start()
        for i in range(z.lent):
            got = fw[i] if i < z.edge else fe[i - z.edge]
            keep[i] = (part[i] + got.astype(F32)).astype(BF16)
            copy = pltpu.make_async_copy(
                keep.at[i], grads.at[0, bound[0, i // z.edge, i % z.edge]], sems.at[i]
            )
            copy.start()
            copies.append(copy)
        for copy in copies:
            copy.wait()

    return call(
        kernel,
        "finish",
        [SMEM] + [VMEM] * 4 + [ANY],
        ANY,
        jax.ShapeDtypeStruct(grads.shape, BF16),
        [z.held(z.lent), pltpu.SemaphoreType.DMA((z.lent + 1,))],
        14,
        (bound, part, rest, fw, fe, grads),
        {5: 0},
    )


def unpack(z, plane, pieces):
    c = z.cols
    piece = pieces[0].shape[3]
    core, ahead, side = plane.sizes

    def kernel(me, *refs):
        pieces = refs[:core]
        *outs, bias, buf, sems = refs[core:]
        copies = []
        for layer in range(2):
            for i in range(core):
                for j in range(ahead):
                    for k in range(side):
                        start = pl.multiple_of(plane.piece_of(me, (-i, -j, -k)) * piece, 16)
                        buf[layer, pl.ds(start, piece), :] = pieces[i][j, k, layer].astype(F32)
            for i, out in enumerate(outs):
                copy = pltpu.make_async_copy(
                    buf.at[layer, pl.ds(i * c, c)], out.at[layer], sems.at[3 * layer + i]
                )
                copy.start()
                copies.append(copy)
            bias[layer : layer + 1, :] = buf[layer, pl.ds(3 * c, 1), :]
        for copy in copies:
            copy.wait()

    square = jax.ShapeDtypeStruct((2, c, c), F32)
    return call(
        kernel,
        "unpack",
        [SMEM] + [VMEM] * core,
        [ANY] * 3 + [VMEM],
        [square, square, square, jax.ShapeDtypeStruct((2, c), F32)],
        [pltpu.VMEM((2, piece * plane.count, c), F32), pltpu.SemaphoreType.DMA((6,))],
        10,
        (plane.me, *pieces),
    )


def per_device(
    node_in, out_cot, adjacency, tile_nbrs, bound_tiles, live_tiles, w_self, w_nbr, pre_bias, w_out
):
    z = Sizes(adjacency, node_in, bound_tiles)
    t, r, c = z.tiles, z.rows, z.cols
    features = node_in.reshape(t, r, c)
    cot = out_cot.reshape(t, r, c)
    plane = Plane()

    west, east = lend(z, bound_tiles, features)
    from_west = passed_along(east, 1)
    from_east = passed_along(west, -1)
    *nodes, adj, tiles, reads, blocks, sources, targets, counts, plane.me = arrange(
        z, bound_tiles, tile_nbrs, live_tiles, plane.place, features, cot, adjacency.reshape(z.pairs, r, r)
    )
    f0, m1 = tuple(nodes[:2]), tuple(nodes[2:])
    tables = (blocks, sources, targets, counts)
    at, wt = turn(z, adj, w_self, w_nbr, w_out)

    west, east, agg_lent = first_lent(
        z, tiles, reads, f0, from_west, from_east, adj, w_self, w_nbr, pre_bias, w_out
    )
    next_west = passed_along(east, 1)
    next_east = passed_along(west, -1)
    f1_lent, f1_rest, section_out, agg_rest = first_rest(
        z, tiles, reads, bound_tiles, live_tiles, f0, from_west, from_east, adj, w_self, w_nbr, pre_bias, w_out,
        west, east,
    )
    f1, agg0 = (f1_lent, f1_rest), (agg_lent, agg_rest)
    own, hidden = second_own(z, f1, m1, w_self, pre_bias, wt)
    act0, slope, ready = saved(z, f0, agg0, w_self, w_nbr, pre_bias)

    agg1, act1, dpre1, dagg1, to_west, to_east = second(
        z, tiles, reads, tables, f1, next_west, next_east, adj, at, own, hidden, w_nbr, wt, ready
    )
    back_west = passed_along(to_east, 1)
    back_east = passed_along(to_west, -1)
    late = weight_grads(z, plane, f1, agg1, act1, m1, dpre1, "weight_grads1")
    section_out, ready = second_out(z, bound_tiles, live_tiles, f1, act1, w_out, section_out)
    part, upstream, done = input_grad(z, 1, tables, m1, dpre1, dagg1, at, wt)
    late = plane_parts(plane, late, ((ready,), (done,)))
    grads, m0_rest, dpre_rest, dagg_rest, outer = early_rest(
        z, tables, live_tiles, upstream, slope, at, wt
    )
    late = added(late, after=(outer,))

    m0_lent, dpre_lent, dagg_lent, grads, to_west, to_east = early_lent(
        z, tables, bound_tiles, part, back_west, back_east, slope, outer, at, wt, grads, (ready, late)
    )
    back_west = passed_along(to_east, 1)
    back_east = passed_along(to_west, -1)
    m0, dpre0, dagg0 = (m0_lent, m0_rest), (dpre_lent, dpre_rest), (dagg_lent, dagg_rest)
    early = weight_grads(z, plane, f0, agg0, act0, m0, dpre0, "weight_grads0")


    def meanwhile(early, tables, m0, dpre0, dagg0, at, wt):
        part, rest, _ = input_grad(z, 0, tables, m0, dpre0, dagg0, at, wt)
        return plane_parts(plane, early), part, rest

    args = (early, tables, m0, dpre0, dagg0, at, wt)
    shapes = jax.eval_shape(meanwhile, *args)
    early, part, rest = lax.cond(
        live_tiles[0] > 0,
        meanwhile,
        lambda *_: jax.tree.map(lambda a: jnp.zeros(a.shape, a.dtype), shapes),
        *args,
    )
    shares = line_sum(joined(early, late), (back_west, back_east))
    pieces = plane_gathered(plane, shares)
    grads = finish(z, bound_tiles, part, rest, back_west, back_east, grads)
    grad_self, grad_nbr, grad_out, grad_bias = unpack(z, plane, pieces)
    return (
        section_out.reshape(2, t * r, c),
        grads.reshape(2, t * r, c),
        grad_self,
        grad_nbr,
        grad_bias,
        grad_out,
    )


def solution(mesh):
    rows = P(AXES)
    in_specs = (rows, rows, rows, rows, rows, rows, P(), P(), P(), P())
    out_specs = (P(None, AXES), P(None, AXES), P(), P(), P(), P())
    return jax.shard_map(
        per_device, mesh=mesh, in_specs=in_specs, out_specs=out_specs, check_vma=False
    )
```

```python
import jax
import jax.numpy as jnp
from jax import lax
from jax.experimental import pallas as pl
from jax.experimental.pallas import tpu as pltpu
from jax.sharding import PartitionSpec as P

AXES = ("dom", "phase", "feat")
PLANE = ("dom", "phase")
BF16 = jnp.bfloat16
F32 = jnp.float32
ANY = pl.BlockSpec(memory_space=pl.ANY)
SMEM = pl.BlockSpec(memory_space=pltpu.SMEM)
VMEM = pl.BlockSpec(memory_space=pltpu.VMEM)
MIB = 1024 * 1024
TOKEN = jax.ShapeDtypeStruct((8, 128), F32)


class Sizes:
    def __init__(self, adjacency, features, bound):
        self.tiles, self.slots, self.rows, _ = adjacency.shape
        self.cols = features.shape[-1]
        self.edge = bound.shape[-1]
        self.lent = 2 * self.edge
        self.rest = self.tiles - self.lent
        self.ext = self.tiles + self.lent
        self.pairs = self.tiles * self.slots
        self.group = next(g for g in (4, 2, 1) if self.edge % g == 0 and self.rest % g == 0)
        self.parts = ((0, 0, self.lent), (1, self.lent, self.rest))
        self.index = Index(self)

    def nodes(self, count, dtype=BF16):
        return jax.ShapeDtypeStruct((count, self.rows, self.cols), dtype)

    def held(self, count, dtype=BF16):
        return pltpu.VMEM((count, self.rows, self.cols), dtype)

    def flat(self, value):
        return value.reshape(self.group * self.rows, self.cols)

    def tiled(self, value):
        return value.reshape(self.group, self.rows, self.cols)


def group_of(z, array, part, first):
    if isinstance(array, tuple):
        base = z.lent if part else 0
        return array[part].at[pl.ds(first - base, z.group)]
    return array.at[pl.ds(first, z.group)]


def each_group(z, body, parts=(0, 1), unroll=1):
    for part, base, count in z.parts:
        if part in parts:

            @pl.loop(0, count // z.group, unroll=unroll)
            def _(s):
                body(part, base + s * z.group)


def staged(count, *stages):
    for s in range(count + len(stages) - 1):
        for i, stage in enumerate(stages):
            if 0 <= s - i < count:
                stage(s - i)


def passed_along(value, steps):
    count = lax.axis_size(AXES)
    return lax.ppermute(value, AXES, [(i, (i + steps) % count) for i in range(count)])


def dot(a, b):
    return jnp.dot(a, b, preferred_element_type=F32)


def dot_rows(a, b):
    return lax.dot_general(a, b, (((0,), (0,)), ((), ())), preferred_element_type=F32)


def call(kernel, name, in_specs, out_specs, out_shape, scratch, limit, args, aliases=None):
    return pl.pallas_call(
        kernel,
        in_specs=in_specs,
        out_specs=out_specs,
        out_shape=out_shape,
        scratch_shapes=scratch,
        input_output_aliases=aliases or {},
        compiler_params=pltpu.CompilerParams(vmem_limit_bytes=limit * MIB),
        cost_estimate=pl.CostEstimate(flops=1000, bytes_accessed=1000, transcendentals=0),
        name=name,
    )(*args)


def sigmoid(v):
    return 0.5 * jnp.tanh(0.5 * v) + 0.5


def lend(z, bound, features):
    def kernel(bound, feats, west, east, buf, sem):
        copy = pltpu.make_async_copy(feats.at[pl.ds(0, z.lent)], buf, sem)
        copy.start()
        copy.wait()
        for i in range(z.edge):
            west[i] = buf[bound[0, 0, i]]
            east[i] = buf[bound[0, 1, i]]

    return call(
        kernel,
        "lend",
        [SMEM, ANY],
        [VMEM, VMEM],
        [z.nodes(z.edge), z.nodes(z.edge)],
        [z.held(z.lent), pltpu.SemaphoreType.DMA],
        56,
        (bound, features),
    )


class Index:
    QUAD = 4

    def __init__(self, z):
        self.first = (0, z.tiles, z.tiles + z.lent, z.tiles + 2 * z.lent, z.tiles + 3 * z.lent)
        self.targets = z.tiles + 3 * z.lent + 1
        self.more = tuple(self.QUAD * self.targets + i * z.pairs for i in range(5))
        self.size = self.QUAD * self.targets + 5 * z.pairs
        self.size = -(-self.size // 8) * 8


def arrange(z, bound, nbrs, live, place, features, cot, adjacency):
    s4 = z.slots
    x = z.index

    def kernel(bound, nbrs, live, place, feats, cot, adj, f_lent, f_rest, m_lent, m_rest, adj_out,
               tiles, reads, blocks, sources, targets, counts, me, inverse, used, sems):
        copies = []
        for i in range(8):
            me[i] = place[i]

        def start(source, target):
            copy = pltpu.make_async_copy(source, target, sems.at[len(copies)])
            copy.start()
            copies.append(copy)

        tail = pl.ds(z.lent, z.rest)
        start(feats.at[tail], f_rest)
        start(cot.at[tail], m_rest)
        start(adj, adj_out)
        for i in range(z.lent):
            tile = bound[0, i // z.edge, i % z.edge]
            inverse[tile] = i
            start(feats.at[tile], f_lent.at[i])
            start(cot.at[tile], m_lent.at[i])

        @pl.loop(0, x.targets)
        def _(i):
            used[i] = 0
            for k in range(x.QUAD):
                blocks[i * x.QUAD + k] = -1
                sources[i * x.QUAD + k] = 0

        for i in range(8):
            counts[i] = 0

        def put(table, target, block, position):
            place = used[target]
            used[target] = place + 1
            fits = place < x.QUAD
            listed = counts[table]
            counts[table] = listed + jnp.where(fits, 0, 1)
            at = jnp.where(fits, target * x.QUAD + place, x.more[0] + table * z.pairs + listed)
            blocks[at] = block
            sources[at] = position
            return at

        @pl.loop(0, z.tiles)
        def _(position):
            clipped = jnp.minimum(position, z.lent - 1)
            tile = jnp.where(position < z.lent, bound[0, clipped // z.edge, clipped % z.edge], position)
            tiles[position] = tile
            for k in range(s4):
                target = nbrs[tile, k]
                moved = jnp.where(target < z.lent, inverse[jnp.minimum(target, z.lent - 1)], target)
                reads[position * s4 + k] = moved
                block = tile * s4 + k
                own = moved < z.tiles
                at = put(jnp.where(own, 0, 1), moved, block, position)
                targets[at] = jnp.where(own, moved, moved - z.tiles)
                lent = position < z.lent
                table = jnp.where(own, 4, jnp.where(lent, 2, 3))
                shift = jnp.where(lent, z.lent, 2 * z.lent)
                at = put(table, jnp.where(own, x.first[4], moved + shift), block, position)
                targets[at] = moved - z.tiles

        for copy in copies:
            copy.wait()

        @pl.loop(0, z.rest)
        def _(i):
            @pl.when(z.lent + i >= live[0])
            def _():
                m_rest[i] = jnp.zeros((z.rows, z.cols), BF16)

    return call(
        kernel,
        "arrange",
        [SMEM] * 4 + [ANY] * 3,
        [VMEM] * 5 + [SMEM] * 7,
        [z.nodes(z.lent), z.nodes(z.rest), z.nodes(z.lent), z.nodes(z.rest)]
        + [jax.ShapeDtypeStruct(adjacency.shape, BF16)]
        + [jax.ShapeDtypeStruct((n,), jnp.int32) for n in (z.tiles, z.pairs, x.size, x.size, x.size, 8, 8)],
        [
            pltpu.SMEM((z.lent,), jnp.int32),
            pltpu.SMEM((x.targets,), jnp.int32),
            pltpu.SemaphoreType.DMA((2 * z.lent + 3,)),
        ],
        12,
        (bound, nbrs, live, place, features, cot, adjacency),
    )


def turn(z, adj, w_self, w_nbr, w_out):
    def kernel(adj, ws, wn, wo, at, wt):
        for layer in range(2):
            wt[layer, 0] = ws[layer].T
            wt[layer, 1] = wn[layer].T
            wt[layer, 2] = wo[layer].T

        @pl.loop(0, z.pairs, unroll=4)
        def _(i):
            at[i] = adj[i].T

    return call(
        kernel,
        "turn",
        [VMEM] * 4,
        [VMEM, VMEM],
        [jax.ShapeDtypeStruct(adj.shape, BF16), jax.ShapeDtypeStruct((2, 3, z.cols, z.cols), BF16)],
        [],
        12,
        (adj, w_self, w_nbr, w_out),
    )


def fill_extended(z, own, fw, fe, ext):
    ext[pl.ds(0, z.lent)] = own[0][...]
    ext[pl.ds(z.lent, z.rest)] = own[1][...]
    ext[pl.ds(z.tiles, z.edge)] = fw[...]
    ext[pl.ds(z.tiles + z.edge, z.edge)] = fe[...]


def aggregate(z, tiles, reads, first, adj, ext):
    rows = []
    for g in range(z.group):
        base = (first + g) * z.slots
        block = tiles[first + g] * z.slots
        picked = jnp.concatenate([ext[reads[base + k]] for k in range(z.slots)], axis=0)
        blocks = jnp.concatenate([adj[block + k] for k in range(z.slots)], axis=1)
        rows.append(dot(blocks, picked).astype(BF16))
    return jnp.concatenate(rows, axis=0)


def live_rows(z, value, first, live):
    parts = []
    for g in range(z.group):
        part = value[g * z.rows : (g + 1) * z.rows]
        parts.append(jnp.where(first + g < live, part, jnp.zeros_like(part)))
    return jnp.concatenate(parts, axis=0)


def first_lent(z, tiles, reads, f0, fw, fe, adj, w_self, w_nbr, bias, w_out):
    def kernel(tiles, reads, f_lent, f_rest, fw, fe, adj, ws, wn, bias, wo, west, east, agg, ext, acts):
        fill_extended(z, (f_lent, f_rest), fw, fe, ext)

        def gather(s):
            agg[pl.ds(s * z.group, z.group)] = z.tiled(aggregate(z, tiles, reads, s * z.group, adj, ext))

        def middle(s):
            here = pl.ds(s * z.group, z.group)
            f = z.flat(ext[here])
            pre = dot(f, ws[0]) + dot(z.flat(agg[here]), wn[0]) + bias[0:1, :]
            acts[here] = z.tiled((pre * sigmoid(pre)).astype(BF16))

        def last(s):
            here = pl.ds(s * z.group, z.group)
            out = z.flat(ext[here]).astype(F32) + dot(z.flat(acts[here]), wo[0])
            half = z.edge // z.group
            target = west if s < half else east
            target[pl.ds(s % half * z.group, z.group)] = z.tiled(out.astype(BF16))

        staged(z.lent // z.group, gather, middle, last)

    return call(
        kernel,
        "first_lent",
        [SMEM] * 2 + [VMEM] * 9,
        [VMEM] * 3,
        [z.nodes(z.edge), z.nodes(z.edge), z.nodes(z.lent)],
        [z.held(z.ext), z.held(z.lent)],
        12,
        (tiles, reads, *f0, fw, fe, adj, w_self, w_nbr, bias, w_out),
    )


def first_rest(z, tiles, reads, bound, live, f0, fw, fe, adj, w_self, w_nbr, bias, w_out, west, east):
    def kernel(tiles, reads, bound, live, f_lent, f_rest, fw, fe, adj, ws, wn, bias, wo, west, east,
               f1_lent, f1_rest, out, agg, ext, sems):
        copies = []
        for i in range(z.edge):
            for side, source in ((0, west), (1, east)):
                copy = pltpu.make_async_copy(
                    source.at[i], out.at[0, bound[0, side, i]], sems.at[side * z.edge + i]
                )
                copy.start()
                copies.append(copy)
        fill_extended(z, (f_lent, f_rest), fw, fe, ext)
        f1_lent[pl.ds(0, z.edge)] = west[...]
        f1_lent[pl.ds(z.edge, z.edge)] = east[...]

        def work(part, first):
            f = z.flat(ext[pl.ds(first, z.group)])
            aggs = aggregate(z, tiles, reads, first, adj, ext)
            here = pl.ds(first - z.lent, z.group)
            agg[here] = z.tiled(aggs)
            pre = dot(f, ws[0]) + dot(aggs, wn[0]) + bias[0:1, :]
            act = (pre * sigmoid(pre)).astype(BF16)
            res = live_rows(z, f.astype(F32) + dot(act, wo[0]), first, live[0])
            f1_rest[here] = z.tiled(res.astype(BF16))

        each_group(z, work, (1,))
        copy = pltpu.make_async_copy(f1_rest, out.at[0, pl.ds(z.lent, z.rest)], sems.at[z.lent])
        copy.start()
        for other in copies:
            other.wait()
        copy.wait()

    return call(
        kernel,
        "first_rest",
        [SMEM] * 4 + [VMEM] * 11,
        [VMEM, VMEM, ANY, VMEM],
        [
            z.nodes(z.lent),
            z.nodes(z.rest),
            jax.ShapeDtypeStruct((2, z.tiles, z.rows, z.cols), BF16),
            z.nodes(z.rest),
        ],
        [z.held(z.ext), pltpu.SemaphoreType.DMA((1 + z.lent,))],
        10,
        (tiles, reads, bound, live, *f0, fw, fe, adj, w_self, w_nbr, bias, w_out, west, east),
    )


def second_own(z, f1, m1, w_self, bias, wt):
    def kernel(f_lent, f_rest, m_lent, m_rest, ws, bias, wt, own, hidden):
        def work(part, first):
            f = z.flat(group_of(z, (f_lent, f_rest), part, first)[...])
            m = z.flat(group_of(z, (m_lent, m_rest), part, first)[...])
            here = pl.ds(first, z.group)
            own[here] = z.tiled(dot(f, ws[1]) + bias[1:2, :])
            hidden[here] = z.tiled(dot(m, wt[1, 2]))

        each_group(z, work)

    return call(
        kernel,
        "second_own",
        [VMEM] * 7,
        [VMEM] * 2,
        [z.nodes(z.tiles, F32)] * 2,
        [],
        12,
        (*f1, *m1, w_self, bias, wt),
    )


def saved(z, f0, agg0, w_self, w_nbr, bias):
    def kernel(f_lent, f_rest, a_lent, a_rest, ws, wn, bias, act, slope, token):
        token[...] = jnp.zeros_like(token)

        def work(part, first):
            f = z.flat(group_of(z, (f_lent, f_rest), part, first)[...])
            aggs = z.flat(group_of(z, (a_lent, a_rest), part, first)[...])
            pre = dot(f, ws[0]) + dot(aggs, wn[0]) + bias[0:1, :]
            sig = sigmoid(pre)
            here = pl.ds(first, z.group)
            act[here] = z.tiled((pre * sig).astype(BF16))
            slope[here] = z.tiled(sig * (1.0 + pre * (1.0 - sig)))

        each_group(z, work)

    return call(
        kernel,
        "saved",
        [VMEM] * 7,
        [VMEM] * 3,
        [z.nodes(z.tiles), z.nodes(z.tiles, F32), TOKEN],
        [],
        10,
        (*f0, *agg0, w_self, w_nbr, bias),
    )


def spread(z, tables, table, count, at, source, acc, add):
    blocks, sources, targets, counts = tables
    x = z.index

    @pl.loop(0, count, unroll=4)
    def _(target):
        base = (x.first[table] + target) * x.QUAD
        lefts, rights = [], []
        for k in range(x.QUAD):
            block = blocks[base + k]
            left = at[jnp.maximum(block, 0)]
            lefts.append(jnp.where(block >= 0, left, jnp.zeros_like(left)))
            rights.append(source(sources[base + k]))
        value = dot(jnp.concatenate(lefts, axis=1), jnp.concatenate(rights, axis=0))
        if add:
            acc[target] += value
        else:
            acc[target] = value

    @pl.loop(0, counts[table])
    def _(i):
        place = x.more[table] + i
        acc[targets[place]] += dot(at[blocks[place]], source(sources[place]))


def second(z, tiles, reads, tables, f1, fw, fe, adj, at, own, hidden, w_nbr, wt, after):
    groups = z.tiles // z.group

    def kernel(tiles, reads, blocks, sources, targets, counts, f_lent, f_rest, fw, fe, adj, at, own, hidden, wn,
               wt, _after, agg, act, dpre, dagg, to_west, to_east, ext, acc):
        fill_extended(z, (f_lent, f_rest), fw, fe, ext)

        def gather(s):
            agg[pl.ds(s * z.group, z.group)] = z.tiled(aggregate(z, tiles, reads, s * z.group, adj, ext))

        def middle(s):
            here = pl.ds(s * z.group, z.group)
            pre = z.flat(own[here]) + dot(z.flat(agg[here]), wn[1])
            sig = sigmoid(pre)
            act[here] = z.tiled((pre * sig).astype(BF16))
            slope = sig * (1.0 + pre * (1.0 - sig))
            dpre[here] = z.tiled((z.flat(hidden[here]) * slope).astype(BF16))

        def last(s):
            here = pl.ds(s * z.group, z.group)
            dagg[here] = z.tiled(dot(z.flat(dpre[here]), wt[1, 1]).astype(BF16))

        staged(groups, gather, middle, last)
        spread(z, (blocks, sources, targets, counts), 1, z.lent, at, lambda q: dagg[q], acc, False)
        to_west[...] = acc[pl.ds(0, z.edge)].astype(BF16)
        to_east[...] = acc[pl.ds(z.edge, z.edge)].astype(BF16)

    return call(
        kernel,
        "second",
        [SMEM] * 6 + [VMEM] * 11,
        [VMEM] * 6,
        [z.nodes(z.tiles)] * 4 + [z.nodes(z.edge)] * 2,
        [z.held(z.ext), z.held(z.lent, F32)],
        12,
        (tiles, reads, *tables, *f1, fw, fe, adj, at, own, hidden, w_nbr, wt, after),
    )


class Plane:
    def __init__(self):
        dom, phase = lax.axis_size("dom"), lax.axis_size("phase")
        core = 2 if dom % 2 == 0 else 1
        self.sizes = (core, dom // core, phase)
        self.count = dom * phase
        place = lax.axis_index("dom")
        place = [lax.rem(place, core), place // core, lax.axis_index("phase")]
        self.place = jnp.stack(place + [jnp.zeros_like(place[0])] * 5).astype(jnp.int32)
        self.me = None

    def piece_of(self, me, steps):
        at = [lax.rem(me[i] + (steps[i] + n) % n, n) for i, n in enumerate(self.sizes)]
        return (at[0] * self.sizes[1] + at[1]) * self.sizes[2] + at[2]

    def passed(self, value, dim, steps):
        return self.passed_by(value, [steps if i == dim else 0 for i in range(3)])

    def passed_by(self, value, steps):
        pairs = []
        for c in range(self.sizes[0]):
            for d in range(self.sizes[1]):
                for p in range(self.sizes[2]):
                    to = [(at + by) % n for at, by, n in zip((c, d, p), steps, self.sizes)]
                    source = (d * self.sizes[0] + c) * self.sizes[2] + p
                    target = (to[1] * self.sizes[0] + to[0]) * self.sizes[2] + to[2]
                    pairs.append((source, target))
        return lax.ppermute(value, PLANE, pairs)

    def received(self, parts, dim):
        return [parts[0]] + [self.passed(parts[i], dim, i) for i in range(1, self.sizes[dim])]


def weight_grads(z, plane, f, agg, act, m, dpre, name):
    c = z.cols
    piece = -(-(3 * c + 1) // (plane.count * 16)) * 16
    core, ahead, side = plane.sizes
    arrays = (f, agg, act, m, dpre)
    flat_args = [x for a in arrays for x in (a if isinstance(a, tuple) else (a,))]

    def kernel(me, *refs):
        refs = list(refs)
        f, agg, act, m, dpre = [
            (refs.pop(0), refs.pop(0)) if isinstance(a, tuple) else refs.pop(0) for a in arrays
        ]
        *outs, acc, sums = refs
        acc[...] = jnp.zeros_like(acc)
        sums[...] = jnp.zeros_like(sums)

        def work(part, first):
            def rows(array):
                return z.flat(group_of(z, array, part, first)[...])

            grad = rows(dpre)
            turned = grad.T
            sums[0] += dot(turned, rows(f))
            sums[1] += dot(turned, rows(agg))
            sums[2] += dot(rows(m).T, rows(act))
            acc[pl.ds(3 * c, 1), :] += jnp.sum(grad.astype(F32), axis=0, keepdims=True)

        each_group(z, work)
        for i in range(3):
            acc[pl.ds(i * c, c), :] = sums[i].T
        for i, out in enumerate(outs):
            for j in range(ahead):
                for k in range(side):
                    owner = pl.multiple_of(plane.piece_of(me, (i, j, k)) * piece, 16)
                    out[j, k] = acc[pl.ds(owner, piece), :].astype(BF16)

    return call(
        kernel,
        name,
        [SMEM] + [VMEM] * len(flat_args),
        [VMEM] * core,
        [jax.ShapeDtypeStruct((ahead, side, piece, c), BF16)] * core,
        [pltpu.VMEM((piece * plane.count, c), F32), pltpu.VMEM((3, c, c), F32)],
        14,
        (plane.me, *flat_args),
    )


def added(values, split=False, after=(), pairs=False):
    shape = values[0].shape
    count = shape[0] if split else 1

    def kernel(*refs):
        outs = refs[-count:]
        for i, out in enumerate(outs):
            parts = [(ref[i] if split else ref[...]).astype(F32) for ref in refs[: len(values)]]
            if pairs:
                parts = [parts[0] + parts[1], parts[2] + parts[3]]
            total = parts[0]
            for part in parts[1:]:
                total = total + part
            out[...] = total.astype(BF16)

    args = [*values, *after]
    outs = call(
        kernel,
        "added",
        [VMEM] * len(values) + [ANY] * len(after),
        [VMEM] * count,
        [jax.ShapeDtypeStruct(shape[1:] if split else shape, BF16)] * count,
        [],
        8,
        args,
    )
    return outs if split else outs[0]


def plane_parts(plane, pieces, after=((), ())):
    parts = added(plane.received(pieces, 0), split=True, after=after[0])
    parts = added(plane.received(parts, 1), split=True, after=after[1])
    return plane.received(parts, 2)


def joined(parts, other):
    def kernel(*refs):
        total = refs[0][...].astype(F32)
        for ref in refs[1 : len(parts)]:
            total = total + ref[...].astype(F32)
        refs[-1][0] = total.astype(BF16)
        refs[-1][1] = refs[len(parts)][...]

    return call(
        kernel,
        "joined",
        [VMEM] * (len(parts) + 1),
        VMEM,
        jax.ShapeDtypeStruct((2,) + other.shape, BF16),
        [],
        8,
        (*parts, other),
    )


def line_sum(share, after):
    lines = lax.axis_size("feat")
    if lines & (lines - 1) != 0:
        return lax.psum(share.astype(F32), "feat").astype(BF16)

    def from_line(value, step):
        return lax.ppermute(value, "feat", [(i, i ^ step) for i in range(lines)])

    if lines == 4:
        others = [from_line(share, step) for step in (1, 2, 3)]
        return added([share, *others], after=after, pairs=True)
    step = 1
    while step < lines:
        share = added([share, from_line(share, step)], after=after if step == 1 else ())
        step *= 2
    return share


def stacked(values):
    def kernel(*refs):
        for i, ref in enumerate(refs[:-1]):
            refs[-1][i] = ref[...]

    shape = (len(values),) + values[0].shape
    out = jax.ShapeDtypeStruct(shape, values[0].dtype)
    return call(kernel, "stacked", [VMEM] * len(values), VMEM, out, [], 4, values)


def plane_gathered(plane, share):
    core, ahead, side = plane.sizes
    steps = [(0, j, k) for j in range(ahead) for k in range(side)]
    share = stacked([share] + [plane.passed_by(share, by) for by in steps[1:]])
    share = share.reshape(ahead, side, *share.shape[-3:])
    return [share] + [plane.passed(share, 0, i) for i in range(1, core)]


def second_out(z, bound, live, f1, act, w_out, out):
    def kernel(bound, live, f_lent, f_rest, act, wo, _out, out, token, keep, sems):
        copies = []
        token[...] = jnp.zeros_like(token)

        def work(part, first):
            f = z.flat(group_of(z, (f_lent, f_rest), part, first)[...])
            res = f.astype(F32) + dot(z.flat(act[pl.ds(first, z.group)]), wo[1])
            keep[pl.ds(first, z.group)] = z.tiled(live_rows(z, res, first, live[0]).astype(BF16))

        each_group(z, work, (0,))
        for i in range(z.lent):
            copy = pltpu.make_async_copy(
                keep.at[i], out.at[1, bound[0, i // z.edge, i % z.edge]], sems.at[i]
            )
            copy.start()
            copies.append(copy)
        each_group(z, work, (1,))
        tail = pl.ds(z.lent, z.rest)
        copy = pltpu.make_async_copy(keep.at[tail], out.at[1, tail], sems.at[z.lent])
        copy.start()
        copies.append(copy)
        for copy in copies:
            copy.wait()

    return call(
        kernel,
        "second_out",
        [SMEM] * 2 + [VMEM] * 4 + [ANY],
        [ANY, VMEM],
        [jax.ShapeDtypeStruct(out.shape, BF16), TOKEN],
        [z.held(z.tiles), pltpu.SemaphoreType.DMA((z.lent + 1,))],
        12,
        (bound, live, *f1, act, w_out, out),
        {6: 0},
    )


def input_grad(z, layer, tables, m, dpre, dagg, at, wt):
    arrays = (m, dpre, dagg)
    flat_args = [x for a in arrays for x in (a if isinstance(a, tuple) else (a,))]

    def kernel(blocks, sources, targets, counts, *refs):
        refs = list(refs)
        m, dpre, dagg = [
            (refs.pop(0), refs.pop(0)) if isinstance(a, tuple) else refs.pop(0) for a in arrays
        ]
        at, wt, part_out, rest_out, token, acc = refs
        token[...] = jnp.zeros_like(token)
        x = z.index

        def source(q):
            if not isinstance(dagg, tuple):
                return dagg[q]
            lent = dagg[0][jnp.minimum(q, z.lent - 1)]
            rest = dagg[1][jnp.maximum(q - z.lent, 0)]
            return jnp.where(q < z.lent, lent, rest)

        def tile_of(array, part, base, i):
            return array[part][i] if isinstance(array, tuple) else array[base + i]

        for part, base, count in z.parts:

            @pl.loop(0, count, unroll=4)
            def _(i):
                lefts, rights = [tile_of(dpre, part, base, i)], [wt[layer, 0]]
                for k in range(x.QUAD):
                    block = blocks[(base + i) * x.QUAD + k]
                    left = at[jnp.maximum(block, 0)]
                    lefts.append(jnp.where(block >= 0, left, jnp.zeros_like(left)))
                    rights.append(source(sources[(base + i) * x.QUAD + k]))
                value = dot(jnp.concatenate(lefts, axis=1), jnp.concatenate(rights, axis=0))
                acc[base + i] = value + tile_of(m, part, base, i).astype(F32)

        @pl.loop(0, counts[0])
        def _(i):
            place = x.more[0] + i
            acc[targets[place]] += dot(at[blocks[place]], source(sources[place]))

        part_out[...] = acc[pl.ds(0, z.lent)]
        rest_out[...] = acc[pl.ds(z.lent, z.rest)].astype(BF16)

    return call(
        kernel,
        "input_grad%d" % layer,
        [SMEM] * 4 + [VMEM] * (len(flat_args) + 2),
        [VMEM] * 3,
        [z.nodes(z.lent, F32), z.nodes(z.rest), TOKEN],
        [z.held(z.tiles, F32)],
        20,
        [*tables, *flat_args, at, wt],
    )


def early_rest(z, tables, live, upstream, slope, at, wt):
    def kernel(blocks, sources, targets, counts, live, g, slope, at, wt, grads, m, dpre, dagg, outer, sem):
        copy = pltpu.make_async_copy(g, grads.at[1, pl.ds(z.lent, z.rest)], sem)
        copy.start()

        def work(part, first):
            here = pl.ds(first - z.lent, z.group)
            masked = live_rows(z, z.flat(g[here]), first, live[0])
            m[here] = z.tiled(masked)
            grad = dot(masked, wt[0, 2]) * z.flat(slope[pl.ds(first, z.group)])
            grad = grad.astype(BF16)
            dpre[here] = z.tiled(grad)
            dagg[here] = z.tiled(dot(grad, wt[0, 1]).astype(BF16))

        each_group(z, work, (1,))

        def source(q):
            return dagg[jnp.maximum(q - z.lent, 0)]

        spread(z, (blocks, sources, targets, counts), 3, z.lent, at, source, outer, False)
        copy.wait()

    return call(
        kernel,
        "early_rest",
        [SMEM] * 5 + [VMEM] * 4,
        [ANY] + [VMEM] * 4,
        [jax.ShapeDtypeStruct((2, z.tiles, z.rows, z.cols), BF16)]
        + [z.nodes(z.rest)] * 3
        + [z.nodes(z.lent, F32)],
        [pltpu.SemaphoreType.DMA],
        14,
        (*tables, live, upstream, slope, at, wt),
    )


def early_lent(z, tables, bound, part, fw, fe, slope, outer, at, wt, grads, after):
    def kernel(blocks, sources, targets, counts, bound, part, fw, fe, slope, outer, at, wt, _g, _ready, _late,
               m, dpre, dagg, grads, to_west, to_east, acc, sems):
        half = z.edge // z.group

        def collect(s):
            here = pl.ds(s * z.group, z.group)
            got = (fw if s < half else fe)[pl.ds(s % half * z.group, z.group)]
            m[here] = (part[here] + got.astype(F32)).astype(BF16)

        def middle(s):
            here = pl.ds(s * z.group, z.group)
            grad = dot(z.flat(m[here]), wt[0, 2]) * z.flat(slope[here])
            dpre[here] = z.tiled(grad.astype(BF16))

        def last(s):
            here = pl.ds(s * z.group, z.group)
            dagg[here] = z.tiled(dot(z.flat(dpre[here]), wt[0, 1]).astype(BF16))

        staged(2 * half, collect, middle, last)
        copies = [
            pltpu.make_async_copy(m.at[i], grads.at[1, bound[0, i // z.edge, i % z.edge]], sems.at[i])
            for i in range(z.lent)
        ]
        for copy in copies:
            copy.start()
        acc[...] = outer[...]

        def source(q):
            return dagg[jnp.minimum(q, z.lent - 1)]

        spread(z, (blocks, sources, targets, counts), 2, z.lent, at, source, acc, True)
        to_west[...] = acc[pl.ds(0, z.edge)].astype(BF16)
        to_east[...] = acc[pl.ds(z.edge, z.edge)].astype(BF16)
        for copy in copies:
            copy.wait()

    return call(
        kernel,
        "early_lent",
        [SMEM] * 5 + [VMEM] * 7 + [ANY, VMEM, VMEM],
        [VMEM] * 3 + [ANY] + [VMEM] * 2,
        [z.nodes(z.lent)] * 3 + [jax.ShapeDtypeStruct(grads.shape, BF16)] + [z.nodes(z.edge)] * 2,
        [z.held(z.lent, F32), pltpu.SemaphoreType.DMA((z.lent,))],
        16,
        (*tables, bound, part, fw, fe, slope, outer, at, wt, grads, *after),
        {12: 3},
    )


def finish(z, bound, part, rest, fw, fe, grads):
    def kernel(bound, part, rest, fw, fe, _g, grads, keep, sems):
        copies = [pltpu.make_async_copy(rest, grads.at[0, pl.ds(z.lent, z.rest)], sems.at[z.lent])]
        copies[0].start()
        for i in range(z.lent):
            got = fw[i] if i < z.edge else fe[i - z.edge]
            keep[i] = (part[i] + got.astype(F32)).astype(BF16)
            copy = pltpu.make_async_copy(
                keep.at[i], grads.at[0, bound[0, i // z.edge, i % z.edge]], sems.at[i]
            )
            copy.start()
            copies.append(copy)
        for copy in copies:
            copy.wait()

    return call(
        kernel,
        "finish",
        [SMEM] + [VMEM] * 4 + [ANY],
        ANY,
        jax.ShapeDtypeStruct(grads.shape, BF16),
        [z.held(z.lent), pltpu.SemaphoreType.DMA((z.lent + 1,))],
        14,
        (bound, part, rest, fw, fe, grads),
        {5: 0},
    )


def unpack(z, plane, pieces):
    c = z.cols
    piece = pieces[0].shape[3]
    core, ahead, side = plane.sizes

    def kernel(me, *refs):
        pieces = refs[:core]
        *outs, bias, buf, sems = refs[core:]
        copies = []
        for layer in range(2):
            for i in range(core):
                for j in range(ahead):
                    for k in range(side):
                        start = pl.multiple_of(plane.piece_of(me, (-i, -j, -k)) * piece, 16)
                        buf[layer, pl.ds(start, piece), :] = pieces[i][j, k, layer].astype(F32)
            for i, out in enumerate(outs):
                copy = pltpu.make_async_copy(
                    buf.at[layer, pl.ds(i * c, c)], out.at[layer], sems.at[3 * layer + i]
                )
                copy.start()
                copies.append(copy)
            bias[layer : layer + 1, :] = buf[layer, pl.ds(3 * c, 1), :]
        for copy in copies:
            copy.wait()

    square = jax.ShapeDtypeStruct((2, c, c), F32)
    return call(
        kernel,
        "unpack",
        [SMEM] + [VMEM] * core,
        [ANY] * 3 + [VMEM],
        [square, square, square, jax.ShapeDtypeStruct((2, c), F32)],
        [pltpu.VMEM((2, piece * plane.count, c), F32), pltpu.SemaphoreType.DMA((6,))],
        10,
        (plane.me, *pieces),
    )


def per_device(
    node_in, out_cot, adjacency, tile_nbrs, bound_tiles, live_tiles, w_self, w_nbr, pre_bias, w_out
):
    z = Sizes(adjacency, node_in, bound_tiles)
    t, r, c = z.tiles, z.rows, z.cols
    features = node_in.reshape(t, r, c)
    cot = out_cot.reshape(t, r, c)
    plane = Plane()

    west, east = lend(z, bound_tiles, features)
    from_west = passed_along(east, 1)
    from_east = passed_along(west, -1)
    *nodes, adj, tiles, reads, blocks, sources, targets, counts, plane.me = arrange(
        z, bound_tiles, tile_nbrs, live_tiles, plane.place, features, cot, adjacency.reshape(z.pairs, r, r)
    )
    f0, m1 = tuple(nodes[:2]), tuple(nodes[2:])
    tables = (blocks, sources, targets, counts)
    at, wt = turn(z, adj, w_self, w_nbr, w_out)

    west, east, agg_lent = first_lent(
        z, tiles, reads, f0, from_west, from_east, adj, w_self, w_nbr, pre_bias, w_out
    )
    next_west = passed_along(east, 1)
    next_east = passed_along(west, -1)
    f1_lent, f1_rest, section_out, agg_rest = first_rest(
        z, tiles, reads, bound_tiles, live_tiles, f0, from_west, from_east, adj, w_self, w_nbr, pre_bias, w_out,
        west, east,
    )
    f1, agg0 = (f1_lent, f1_rest), (agg_lent, agg_rest)
    own, hidden = second_own(z, f1, m1, w_self, pre_bias, wt)
    act0, slope, ready = saved(z, f0, agg0, w_self, w_nbr, pre_bias)

    agg1, act1, dpre1, dagg1, to_west, to_east = second(
        z, tiles, reads, tables, f1, next_west, next_east, adj, at, own, hidden, w_nbr, wt, ready
    )
    back_west = passed_along(to_east, 1)
    back_east = passed_along(to_west, -1)
    late = weight_grads(z, plane, f1, agg1, act1, m1, dpre1, "weight_grads1")
    section_out, ready = second_out(z, bound_tiles, live_tiles, f1, act1, w_out, section_out)
    part, upstream, done = input_grad(z, 1, tables, m1, dpre1, dagg1, at, wt)
    late = plane_parts(plane, late, ((ready,), (done,)))
    grads, m0_rest, dpre_rest, dagg_rest, outer = early_rest(
        z, tables, live_tiles, upstream, slope, at, wt
    )
    late = added(late, after=(outer,))

    m0_lent, dpre_lent, dagg_lent, grads, to_west, to_east = early_lent(
        z, tables, bound_tiles, part, back_west, back_east, slope, outer, at, wt, grads, (ready, late)
    )
    back_west = passed_along(to_east, 1)
    back_east = passed_along(to_west, -1)
    m0, dpre0, dagg0 = (m0_lent, m0_rest), (dpre_lent, dpre_rest), (dagg_lent, dagg_rest)
    early = weight_grads(z, plane, f0, agg0, act0, m0, dpre0, "weight_grads0")


    def meanwhile(early, tables, m0, dpre0, dagg0, at, wt):
        part, rest, _ = input_grad(z, 0, tables, m0, dpre0, dagg0, at, wt)
        return plane_parts(plane, early), part, rest

    args = (early, tables, m0, dpre0, dagg0, at, wt)
    shapes = jax.eval_shape(meanwhile, *args)
    early, part, rest = lax.cond(
        live_tiles[0] > 0,
        meanwhile,
        lambda *_: jax.tree.map(lambda a: jnp.zeros(a.shape, a.dtype), shapes),
        *args,
    )
    shares = line_sum(joined(early, late), (back_west, back_east))
    pieces = plane_gathered(plane, shares)
    grads = finish(z, bound_tiles, part, rest, back_west, back_east, grads)
    grad_self, grad_nbr, grad_out, grad_bias = unpack(z, plane, pieces)
    return (
        section_out.reshape(2, t * r, c),
        grads.reshape(2, t * r, c),
        grad_self,
        grad_nbr,
        grad_bias,
        grad_out,
    )


def solution(mesh):
    rows = P(AXES)
    in_specs = (rows, rows, rows, rows, rows, rows, P(), P(), P(), P())
    out_specs = (P(None, AXES), P(None, AXES), P(), P(), P(), P())
    return jax.shard_map(
        per_device, mesh=mesh, in_specs=in_specs, out_specs=out_specs, check_vma=False
    )
```

```python
import jax
import jax.numpy as jnp
from jax import lax
from jax.experimental import pallas as pl
from jax.experimental.pallas import tpu as pltpu
from jax.sharding import PartitionSpec as P

AXES = ("dom", "phase", "feat")
PLANE = ("dom", "phase")
BF16 = jnp.bfloat16
F32 = jnp.float32
ANY = pl.BlockSpec(memory_space=pl.ANY)
SMEM = pl.BlockSpec(memory_space=pltpu.SMEM)
VMEM = pl.BlockSpec(memory_space=pltpu.VMEM)
MIB = 1024 * 1024
TOKEN = jax.ShapeDtypeStruct((8, 128), F32)


class Sizes:
    def __init__(self, adjacency, features, bound):
        self.tiles, self.slots, self.rows, _ = adjacency.shape
        self.cols = features.shape[-1]
        self.edge = bound.shape[-1]
        self.lent = 2 * self.edge
        self.rest = self.tiles - self.lent
        self.ext = self.tiles + self.lent
        self.pairs = self.tiles * self.slots
        self.group = next(g for g in (4, 2, 1) if self.edge % g == 0 and self.rest % g == 0)
        self.parts = ((0, 0, self.lent), (1, self.lent, self.rest))
        self.index = Index(self)

    def nodes(self, count, dtype=BF16):
        return jax.ShapeDtypeStruct((count, self.rows, self.cols), dtype)

    def held(self, count, dtype=BF16):
        return pltpu.VMEM((count, self.rows, self.cols), dtype)

    def flat(self, value):
        return value.reshape(self.group * self.rows, self.cols)

    def tiled(self, value):
        return value.reshape(self.group, self.rows, self.cols)


def group_of(z, array, part, first):
    if isinstance(array, tuple):
        base = z.lent if part else 0
        return array[part].at[pl.ds(first - base, z.group)]
    return array.at[pl.ds(first, z.group)]


def each_group(z, body, parts=(0, 1), unroll=1):
    for part, base, count in z.parts:
        if part in parts:

            @pl.loop(0, count // z.group, unroll=unroll)
            def _(s):
                body(part, base + s * z.group)


def staged(count, *stages):
    for s in range(count + len(stages) - 1):
        for i, stage in enumerate(stages):
            if 0 <= s - i < count:
                stage(s - i)


def passed_along(value, steps):
    count = lax.axis_size(AXES)
    return lax.ppermute(value, AXES, [(i, (i + steps) % count) for i in range(count)])


def dot(a, b):
    return jnp.dot(a, b, preferred_element_type=F32)


def dot_rows(a, b):
    return lax.dot_general(a, b, (((0,), (0,)), ((), ())), preferred_element_type=F32)


def call(kernel, name, in_specs, out_specs, out_shape, scratch, limit, args, aliases=None):
    return pl.pallas_call(
        kernel,
        in_specs=in_specs,
        out_specs=out_specs,
        out_shape=out_shape,
        scratch_shapes=scratch,
        input_output_aliases=aliases or {},
        compiler_params=pltpu.CompilerParams(vmem_limit_bytes=limit * MIB),
        cost_estimate=pl.CostEstimate(flops=1000, bytes_accessed=1000, transcendentals=0),
        name=name,
    )(*args)


def sigmoid(v):
    return 0.5 * jnp.tanh(0.5 * v) + 0.5


def lend(z, bound, features):
    def kernel(bound, feats, west, east, buf, index, sems):
        copies = [
            pltpu.make_async_copy(feats.at[pl.ds(0, z.lent)], buf, sems.at[0]),
            pltpu.make_async_copy(bound, index, sems.at[1]),
        ]
        for copy in copies:
            copy.start()
        for copy in copies:
            copy.wait()
        for i in range(z.edge):
            west[i] = buf[index[0, 0, i]]
            east[i] = buf[index[0, 1, i]]

    return call(
        kernel,
        "lend",
        [ANY, ANY],
        [VMEM, VMEM],
        [z.nodes(z.edge), z.nodes(z.edge)],
        [z.held(z.lent), pltpu.SMEM(bound.shape, jnp.int32), pltpu.SemaphoreType.DMA((2,))],
        56,
        (bound, features),
    )


class Index:
    QUAD = 4

    def __init__(self, z):
        self.first = (0, z.tiles, z.tiles + z.lent, z.tiles + 2 * z.lent, z.tiles + 3 * z.lent)
        self.targets = z.tiles + 3 * z.lent + 1
        self.more = tuple(self.QUAD * self.targets + i * z.pairs for i in range(5))
        self.size = self.QUAD * self.targets + 5 * z.pairs
        self.size = -(-self.size // 8) * 8


def arrange(z, bound, nbrs, live, place, features, cot, adjacency):
    s4 = z.slots
    x = z.index

    def kernel(bound, nbrs, live, place, feats, cot, adj, f_lent, f_rest, m_lent, m_rest, adj_out,
               tiles, reads, blocks, sources, targets, counts, me, inverse, used, sems):
        copies = []
        for i in range(8):
            me[i] = place[i]

        def start(source, target):
            copy = pltpu.make_async_copy(source, target, sems.at[len(copies)])
            copy.start()
            copies.append(copy)

        tail = pl.ds(z.lent, z.rest)
        start(feats.at[tail], f_rest)
        start(cot.at[tail], m_rest)
        start(adj, adj_out)
        for i in range(z.lent):
            tile = bound[0, i // z.edge, i % z.edge]
            inverse[tile] = i
            start(feats.at[tile], f_lent.at[i])
            start(cot.at[tile], m_lent.at[i])

        @pl.loop(0, x.targets)
        def _(i):
            used[i] = 0
            for k in range(x.QUAD):
                blocks[i * x.QUAD + k] = -1
                sources[i * x.QUAD + k] = 0

        for i in range(8):
            counts[i] = 0

        def put(table, target, block, position):
            place = used[target]
            used[target] = place + 1
            fits = place < x.QUAD
            listed = counts[table]
            counts[table] = listed + jnp.where(fits, 0, 1)
            at = jnp.where(fits, target * x.QUAD + place, x.more[0] + table * z.pairs + listed)
            blocks[at] = block
            sources[at] = position
            return at

        @pl.loop(0, z.tiles)
        def _(position):
            clipped = jnp.minimum(position, z.lent - 1)
            tile = jnp.where(position < z.lent, bound[0, clipped // z.edge, clipped % z.edge], position)
            tiles[position] = tile
            for k in range(s4):
                target = nbrs[tile, k]
                moved = jnp.where(target < z.lent, inverse[jnp.minimum(target, z.lent - 1)], target)
                reads[position * s4 + k] = moved
                block = tile * s4 + k
                own = moved < z.tiles
                at = put(jnp.where(own, 0, 1), moved, block, position)
                targets[at] = jnp.where(own, moved, moved - z.tiles)
                lent = position < z.lent
                table = jnp.where(own, 4, jnp.where(lent, 2, 3))
                shift = jnp.where(lent, z.lent, 2 * z.lent)
                at = put(table, jnp.where(own, x.first[4], moved + shift), block, position)
                targets[at] = moved - z.tiles

        for copy in copies:
            copy.wait()

        @pl.loop(0, z.rest)
        def _(i):
            @pl.when(z.lent + i >= live[0])
            def _():
                m_rest[i] = jnp.zeros((z.rows, z.cols), BF16)

    return call(
        kernel,
        "arrange",
        [SMEM] * 4 + [ANY] * 3,
        [VMEM] * 5 + [SMEM] * 7,
        [z.nodes(z.lent), z.nodes(z.rest), z.nodes(z.lent), z.nodes(z.rest)]
        + [jax.ShapeDtypeStruct(adjacency.shape, BF16)]
        + [jax.ShapeDtypeStruct((n,), jnp.int32) for n in (z.tiles, z.pairs, x.size, x.size, x.size, 8, 8)],
        [
            pltpu.SMEM((z.lent,), jnp.int32),
            pltpu.SMEM((x.targets,), jnp.int32),
            pltpu.SemaphoreType.DMA((2 * z.lent + 3,)),
        ],
        12,
        (bound, nbrs, live, place, features, cot, adjacency),
    )


def turn(z, adj, w_self, w_nbr, w_out):
    def kernel(adj, ws, wn, wo, at, wt):
        for layer in range(2):
            wt[layer, 0] = ws[layer].T
            wt[layer, 1] = wn[layer].T
            wt[layer, 2] = wo[layer].T

        @pl.loop(0, z.pairs, unroll=4)
        def _(i):
            at[i] = adj[i].T

    return call(
        kernel,
        "turn",
        [VMEM] * 4,
        [VMEM, VMEM],
        [jax.ShapeDtypeStruct(adj.shape, BF16), jax.ShapeDtypeStruct((2, 3, z.cols, z.cols), BF16)],
        [],
        12,
        (adj, w_self, w_nbr, w_out),
    )


def fill_extended(z, own, fw, fe, ext):
    ext[pl.ds(0, z.lent)] = own[0][...]
    ext[pl.ds(z.lent, z.rest)] = own[1][...]
    ext[pl.ds(z.tiles, z.edge)] = fw[...]
    ext[pl.ds(z.tiles + z.edge, z.edge)] = fe[...]


def aggregate(z, tiles, reads, first, adj, ext):
    rows = []
    for g in range(z.group):
        base = (first + g) * z.slots
        block = tiles[first + g] * z.slots
        picked = jnp.concatenate([ext[reads[base + k]] for k in range(z.slots)], axis=0)
        blocks = jnp.concatenate([adj[block + k] for k in range(z.slots)], axis=1)
        rows.append(dot(blocks, picked).astype(BF16))
    return jnp.concatenate(rows, axis=0)


def live_rows(z, value, first, live):
    parts = []
    for g in range(z.group):
        part = value[g * z.rows : (g + 1) * z.rows]
        parts.append(jnp.where(first + g < live, part, jnp.zeros_like(part)))
    return jnp.concatenate(parts, axis=0)


def first_lent(z, tiles, reads, f0, fw, fe, adj, w_self, w_nbr, bias, w_out):
    def kernel(tiles, reads, f_lent, f_rest, fw, fe, adj, ws, wn, bias, wo, west, east, agg, ext, acts):
        fill_extended(z, (f_lent, f_rest), fw, fe, ext)

        def gather(s):
            agg[pl.ds(s * z.group, z.group)] = z.tiled(aggregate(z, tiles, reads, s * z.group, adj, ext))

        def middle(s):
            here = pl.ds(s * z.group, z.group)
            f = z.flat(ext[here])
            pre = dot(f, ws[0]) + dot(z.flat(agg[here]), wn[0]) + bias[0:1, :]
            acts[here] = z.tiled((pre * sigmoid(pre)).astype(BF16))

        def last(s):
            here = pl.ds(s * z.group, z.group)
            out = z.flat(ext[here]).astype(F32) + dot(z.flat(acts[here]), wo[0])
            half = z.edge // z.group
            target = west if s < half else east
            target[pl.ds(s % half * z.group, z.group)] = z.tiled(out.astype(BF16))

        staged(z.lent // z.group, gather, middle, last)

    return call(
        kernel,
        "first_lent",
        [SMEM] * 2 + [VMEM] * 9,
        [VMEM] * 3,
        [z.nodes(z.edge), z.nodes(z.edge), z.nodes(z.lent)],
        [z.held(z.ext), z.held(z.lent)],
        12,
        (tiles, reads, *f0, fw, fe, adj, w_self, w_nbr, bias, w_out),
    )


def first_rest(z, tiles, reads, bound, live, f0, fw, fe, adj, w_self, w_nbr, bias, w_out, west, east):
    def kernel(tiles, reads, bound, live, f_lent, f_rest, fw, fe, adj, ws, wn, bias, wo, west, east,
               f1_lent, f1_rest, out, agg, ext, sems):
        copies = []
        for i in range(z.edge):
            for side, source in ((0, west), (1, east)):
                copy = pltpu.make_async_copy(
                    source.at[i], out.at[0, bound[0, side, i]], sems.at[side * z.edge + i]
                )
                copy.start()
                copies.append(copy)
        fill_extended(z, (f_lent, f_rest), fw, fe, ext)
        f1_lent[pl.ds(0, z.edge)] = west[...]
        f1_lent[pl.ds(z.edge, z.edge)] = east[...]

        def work(part, first):
            f = z.flat(ext[pl.ds(first, z.group)])
            aggs = aggregate(z, tiles, reads, first, adj, ext)
            here = pl.ds(first - z.lent, z.group)
            agg[here] = z.tiled(aggs)
            pre = dot(f, ws[0]) + dot(aggs, wn[0]) + bias[0:1, :]
            act = (pre * sigmoid(pre)).astype(BF16)
            res = live_rows(z, f.astype(F32) + dot(act, wo[0]), first, live[0])
            f1_rest[here] = z.tiled(res.astype(BF16))

        each_group(z, work, (1,))
        copy = pltpu.make_async_copy(f1_rest, out.at[0, pl.ds(z.lent, z.rest)], sems.at[z.lent])
        copy.start()
        for other in copies:
            other.wait()
        copy.wait()

    return call(
        kernel,
        "first_rest",
        [SMEM] * 4 + [VMEM] * 11,
        [VMEM, VMEM, ANY, VMEM],
        [
            z.nodes(z.lent),
            z.nodes(z.rest),
            jax.ShapeDtypeStruct((2, z.tiles, z.rows, z.cols), BF16),
            z.nodes(z.rest),
        ],
        [z.held(z.ext), pltpu.SemaphoreType.DMA((1 + z.lent,))],
        10,
        (tiles, reads, bound, live, *f0, fw, fe, adj, w_self, w_nbr, bias, w_out, west, east),
    )


def second_own(z, f1, m1, w_self, bias, wt):
    def kernel(f_lent, f_rest, m_lent, m_rest, ws, bias, wt, own, hidden):
        def work(part, first):
            f = z.flat(group_of(z, (f_lent, f_rest), part, first)[...])
            m = z.flat(group_of(z, (m_lent, m_rest), part, first)[...])
            here = pl.ds(first, z.group)
            own[here] = z.tiled(dot(f, ws[1]) + bias[1:2, :])
            hidden[here] = z.tiled(dot(m, wt[1, 2]))

        each_group(z, work)

    return call(
        kernel,
        "second_own",
        [VMEM] * 7,
        [VMEM] * 2,
        [z.nodes(z.tiles, F32)] * 2,
        [],
        12,
        (*f1, *m1, w_self, bias, wt),
    )


def saved(z, f0, agg0, w_self, w_nbr, bias):
    def kernel(f_lent, f_rest, a_lent, a_rest, ws, wn, bias, act, slope, token):
        token[...] = jnp.zeros_like(token)

        def work(part, first):
            f = z.flat(group_of(z, (f_lent, f_rest), part, first)[...])
            aggs = z.flat(group_of(z, (a_lent, a_rest), part, first)[...])
            pre = dot(f, ws[0]) + dot(aggs, wn[0]) + bias[0:1, :]
            sig = sigmoid(pre)
            here = pl.ds(first, z.group)
            act[here] = z.tiled((pre * sig).astype(BF16))
            slope[here] = z.tiled(sig * (1.0 + pre * (1.0 - sig)))

        each_group(z, work)

    return call(
        kernel,
        "saved",
        [VMEM] * 7,
        [VMEM] * 3,
        [z.nodes(z.tiles), z.nodes(z.tiles, F32), TOKEN],
        [],
        10,
        (*f0, *agg0, w_self, w_nbr, bias),
    )


def spread(z, tables, table, count, at, source, acc, add):
    blocks, sources, targets, counts = tables
    x = z.index

    @pl.loop(0, count, unroll=4)
    def _(target):
        base = (x.first[table] + target) * x.QUAD
        lefts, rights = [], []
        for k in range(x.QUAD):
            block = blocks[base + k]
            left = at[jnp.maximum(block, 0)]
            lefts.append(jnp.where(block >= 0, left, jnp.zeros_like(left)))
            rights.append(source(sources[base + k]))
        value = dot(jnp.concatenate(lefts, axis=1), jnp.concatenate(rights, axis=0))
        if add:
            acc[target] += value
        else:
            acc[target] = value

    @pl.loop(0, counts[table])
    def _(i):
        place = x.more[table] + i
        acc[targets[place]] += dot(at[blocks[place]], source(sources[place]))


def second(z, tiles, reads, tables, f1, fw, fe, adj, at, own, hidden, w_nbr, wt, after):
    groups = z.tiles // z.group

    def kernel(tiles, reads, blocks, sources, targets, counts, f_lent, f_rest, fw, fe, adj, at, own, hidden, wn,
               wt, _after, agg, act, dpre, dagg, to_west, to_east, ext, acc):
        fill_extended(z, (f_lent, f_rest), fw, fe, ext)

        def gather(s):
            agg[pl.ds(s * z.group, z.group)] = z.tiled(aggregate(z, tiles, reads, s * z.group, adj, ext))

        def middle(s):
            here = pl.ds(s * z.group, z.group)
            pre = z.flat(own[here]) + dot(z.flat(agg[here]), wn[1])
            sig = sigmoid(pre)
            act[here] = z.tiled((pre * sig).astype(BF16))
            slope = sig * (1.0 + pre * (1.0 - sig))
            dpre[here] = z.tiled((z.flat(hidden[here]) * slope).astype(BF16))

        def last(s):
            here = pl.ds(s * z.group, z.group)
            dagg[here] = z.tiled(dot(z.flat(dpre[here]), wt[1, 1]).astype(BF16))

        staged(groups, gather, middle, last)
        spread(z, (blocks, sources, targets, counts), 1, z.lent, at, lambda q: dagg[q], acc, False)
        to_west[...] = acc[pl.ds(0, z.edge)].astype(BF16)
        to_east[...] = acc[pl.ds(z.edge, z.edge)].astype(BF16)

    return call(
        kernel,
        "second",
        [SMEM] * 6 + [VMEM] * 11,
        [VMEM] * 6,
        [z.nodes(z.tiles)] * 4 + [z.nodes(z.edge)] * 2,
        [z.held(z.ext), z.held(z.lent, F32)],
        12,
        (tiles, reads, *tables, *f1, fw, fe, adj, at, own, hidden, w_nbr, wt, after),
    )


class Plane:
    def __init__(self):
        dom, phase = lax.axis_size("dom"), lax.axis_size("phase")
        core = 2 if dom % 2 == 0 else 1
        self.sizes = (core, dom // core, phase)
        self.count = dom * phase
        place = lax.axis_index("dom")
        place = [lax.rem(place, core), place // core, lax.axis_index("phase")]
        self.place = jnp.stack(place + [jnp.zeros_like(place[0])] * 5).astype(jnp.int32)
        self.me = None

    def piece_of(self, me, steps):
        at = [lax.rem(me[i] + (steps[i] + n) % n, n) for i, n in enumerate(self.sizes)]
        return (at[0] * self.sizes[1] + at[1]) * self.sizes[2] + at[2]

    def passed(self, value, dim, steps):
        return self.passed_by(value, [steps if i == dim else 0 for i in range(3)])

    def passed_by(self, value, steps):
        pairs = []
        for c in range(self.sizes[0]):
            for d in range(self.sizes[1]):
                for p in range(self.sizes[2]):
                    to = [(at + by) % n for at, by, n in zip((c, d, p), steps, self.sizes)]
                    source = (d * self.sizes[0] + c) * self.sizes[2] + p
                    target = (to[1] * self.sizes[0] + to[0]) * self.sizes[2] + to[2]
                    pairs.append((source, target))
        return lax.ppermute(value, PLANE, pairs)

    def received(self, parts, dim):
        return [parts[0]] + [self.passed(parts[i], dim, i) for i in range(1, self.sizes[dim])]


def weight_grads(z, plane, f, agg, act, m, dpre, name, after=()):
    c = z.cols
    piece = -(-(3 * c + 1) // (plane.count * 16)) * 16
    core, ahead, side = plane.sizes
    arrays = (f, agg, act, m, dpre)
    flat_args = [x for a in arrays for x in (a if isinstance(a, tuple) else (a,))]

    def kernel(me, *refs):
        refs = list(refs)
        f, agg, act, m, dpre = [
            (refs.pop(0), refs.pop(0)) if isinstance(a, tuple) else refs.pop(0) for a in arrays
        ]
        *outs, acc, sums = refs[len(after) :]
        acc[...] = jnp.zeros_like(acc)
        sums[...] = jnp.zeros_like(sums)

        def work(part, first):
            def rows(array):
                return z.flat(group_of(z, array, part, first)[...])

            grad = rows(dpre)
            turned = grad.T
            sums[0] += dot(turned, rows(f))
            sums[1] += dot(turned, rows(agg))
            sums[2] += dot(rows(m).T, rows(act))
            acc[pl.ds(3 * c, 1), :] += jnp.sum(grad.astype(F32), axis=0, keepdims=True)

        each_group(z, work)
        for i in range(3):
            acc[pl.ds(i * c, c), :] = sums[i].T
        for i, out in enumerate(outs):
            for j in range(ahead):
                for k in range(side):
                    owner = pl.multiple_of(plane.piece_of(me, (i, j, k)) * piece, 16)
                    out[j, k] = acc[pl.ds(owner, piece), :].astype(BF16)

    return call(
        kernel,
        name,
        [SMEM] + [VMEM] * (len(flat_args) + len(after)),
        [VMEM] * core,
        [jax.ShapeDtypeStruct((ahead, side, piece, c), BF16)] * core,
        [pltpu.VMEM((piece * plane.count, c), F32), pltpu.VMEM((3, c, c), F32)],
        14,
        (plane.me, *flat_args, *after),
    )


def added(values, split=False, after=()):
    shape = values[0].shape
    count = shape[0] if split else 1

    def kernel(*refs):
        outs = refs[-count:]
        for i, out in enumerate(outs):
            parts = [(ref[i] if split else ref[...]).astype(F32) for ref in refs[: len(values)]]
            total = parts[0]
            for part in parts[1:]:
                total = total + part
            out[...] = total.astype(BF16)

    args = [*values, *after]
    outs = call(
        kernel,
        "added",
        [VMEM] * len(values) + [ANY] * len(after),
        [VMEM] * count,
        [jax.ShapeDtypeStruct(shape[1:] if split else shape, BF16)] * count,
        [],
        8,
        args,
    )
    return outs if split else outs[0]


def plane_parts(plane, pieces, after=((), ())):
    parts = added(plane.received(pieces, 0), split=True, after=after[0])
    parts = added(plane.received(parts, 1), split=True, after=after[1])
    return plane.received(parts, 2)


def from_line(value, step):
    lines = lax.axis_size("feat")
    return lax.ppermute(value, "feat", [(i, i ^ step) for i in range(lines)])


def joined(early, late):
    def kernel(early, late, out):
        out[0] = early[...]
        out[1] = late[...]

    out = jax.ShapeDtypeStruct((2,) + late.shape, BF16)
    return call(kernel, "joined", [VMEM] * 2, VMEM, out, [], 4, (early, late))


def line_sum_of_four(both, near, early, late, after):
    def kernel(both, near, early0, early1, late0, late1, *rest):
        out = rest[-1]
        for layer, (first, second) in enumerate(((early0, early1), (late0, late1))):
            pair = both[layer].astype(F32) + near[layer].astype(F32)
            out[layer] = (pair + (first[...].astype(F32) + second[...].astype(F32))).astype(BF16)

    return call(
        kernel,
        "line_sum",
        [VMEM] * 6 + [ANY] * len(after),
        VMEM,
        jax.ShapeDtypeStruct(both.shape, BF16),
        [],
        6,
        (both, near, *early, *late, *after),
    )


def line_sum(share):
    lines = lax.axis_size("feat")
    if lines & (lines - 1) != 0:
        return lax.psum(share.astype(F32), "feat").astype(BF16)
    step = 1
    while step < lines:
        share = added([share, from_line(share, step)])
        step *= 2
    return share


def stacked(values):
    def kernel(*refs):
        for i, ref in enumerate(refs[:-1]):
            refs[-1][i] = ref[...]

    shape = (len(values),) + values[0].shape
    out = jax.ShapeDtypeStruct(shape, values[0].dtype)
    return call(kernel, "stacked", [VMEM] * len(values), VMEM, out, [], 4, values)


def plane_gathered(plane, share):
    core, ahead, side = plane.sizes
    steps = [(0, j, k) for j in range(ahead) for k in range(side)]
    share = stacked([share] + [plane.passed_by(share, by) for by in steps[1:]])
    share = share.reshape(ahead, side, *share.shape[-3:])
    return [share] + [plane.passed(share, 0, i) for i in range(1, core)]


def second_out(z, bound, live, f1, act, w_out, out):
    def kernel(bound, live, f_lent, f_rest, act, wo, _out, out, token, keep, sems):
        copies = []
        token[...] = jnp.zeros_like(token)

        def work(part, first):
            f = z.flat(group_of(z, (f_lent, f_rest), part, first)[...])
            res = f.astype(F32) + dot(z.flat(act[pl.ds(first, z.group)]), wo[1])
            keep[pl.ds(first, z.group)] = z.tiled(live_rows(z, res, first, live[0]).astype(BF16))

        each_group(z, work, (0,))
        for i in range(z.lent):
            copy = pltpu.make_async_copy(
                keep.at[i], out.at[1, bound[0, i // z.edge, i % z.edge]], sems.at[i]
            )
            copy.start()
            copies.append(copy)
        each_group(z, work, (1,))
        tail = pl.ds(z.lent, z.rest)
        copy = pltpu.make_async_copy(keep.at[tail], out.at[1, tail], sems.at[z.lent])
        copy.start()
        copies.append(copy)
        for copy in copies:
            copy.wait()

    return call(
        kernel,
        "second_out",
        [SMEM] * 2 + [VMEM] * 4 + [ANY],
        [ANY, VMEM],
        [jax.ShapeDtypeStruct(out.shape, BF16), TOKEN],
        [z.held(z.tiles), pltpu.SemaphoreType.DMA((z.lent + 1,))],
        12,
        (bound, live, *f1, act, w_out, out),
        {6: 0},
    )


def input_grad(z, layer, tables, m, dpre, dagg, at, wt):
    arrays = (m, dpre, dagg)
    flat_args = [x for a in arrays for x in (a if isinstance(a, tuple) else (a,))]

    def kernel(blocks, sources, targets, counts, *refs):
        refs = list(refs)
        m, dpre, dagg = [
            (refs.pop(0), refs.pop(0)) if isinstance(a, tuple) else refs.pop(0) for a in arrays
        ]
        at, wt, part_out, rest_out, token, acc = refs
        token[...] = jnp.zeros_like(token)
        x = z.index

        def source(q):
            if not isinstance(dagg, tuple):
                return dagg[q]
            lent = dagg[0][jnp.minimum(q, z.lent - 1)]
            rest = dagg[1][jnp.maximum(q - z.lent, 0)]
            return jnp.where(q < z.lent, lent, rest)

        def tile_of(array, part, base, i):
            return array[part][i] if isinstance(array, tuple) else array[base + i]

        for part, base, count in z.parts:

            @pl.loop(0, count, unroll=4)
            def _(i):
                lefts, rights = [tile_of(dpre, part, base, i)], [wt[layer, 0]]
                for k in range(x.QUAD):
                    block = blocks[(base + i) * x.QUAD + k]
                    left = at[jnp.maximum(block, 0)]
                    lefts.append(jnp.where(block >= 0, left, jnp.zeros_like(left)))
                    rights.append(source(sources[(base + i) * x.QUAD + k]))
                value = dot(jnp.concatenate(lefts, axis=1), jnp.concatenate(rights, axis=0))
                acc[base + i] = value + tile_of(m, part, base, i).astype(F32)

        @pl.loop(0, counts[0])
        def _(i):
            place = x.more[0] + i
            acc[targets[place]] += dot(at[blocks[place]], source(sources[place]))

        part_out[...] = acc[pl.ds(0, z.lent)]
        rest_out[...] = acc[pl.ds(z.lent, z.rest)].astype(BF16)

    return call(
        kernel,
        "input_grad%d" % layer,
        [SMEM] * 4 + [VMEM] * (len(flat_args) + 2),
        [VMEM] * 3,
        [z.nodes(z.lent, F32), z.nodes(z.rest), TOKEN],
        [z.held(z.tiles, F32)],
        20,
        [*tables, *flat_args, at, wt],
    )


def early_rest(z, tables, live, upstream, slope, at, wt):
    def kernel(blocks, sources, targets, counts, live, g, slope, at, wt, grads, m, dpre, dagg, outer, sem):
        copy = pltpu.make_async_copy(g, grads.at[1, pl.ds(z.lent, z.rest)], sem)
        copy.start()

        def work(part, first):
            here = pl.ds(first - z.lent, z.group)
            masked = live_rows(z, z.flat(g[here]), first, live[0])
            m[here] = z.tiled(masked)
            grad = dot(masked, wt[0, 2]) * z.flat(slope[pl.ds(first, z.group)])
            grad = grad.astype(BF16)
            dpre[here] = z.tiled(grad)
            dagg[here] = z.tiled(dot(grad, wt[0, 1]).astype(BF16))

        each_group(z, work, (1,))

        def source(q):
            return dagg[jnp.maximum(q - z.lent, 0)]

        spread(z, (blocks, sources, targets, counts), 3, z.lent, at, source, outer, False)
        copy.wait()

    return call(
        kernel,
        "early_rest",
        [SMEM] * 5 + [VMEM] * 4,
        [ANY] + [VMEM] * 4,
        [jax.ShapeDtypeStruct((2, z.tiles, z.rows, z.cols), BF16)]
        + [z.nodes(z.rest)] * 3
        + [z.nodes(z.lent, F32)],
        [pltpu.SemaphoreType.DMA],
        14,
        (*tables, live, upstream, slope, at, wt),
    )


def early_lent(z, tables, part, fw, fe, slope, outer, at, wt, after):
    def kernel(blocks, sources, targets, counts, part, fw, fe, slope, outer, at, wt, _ready, _late,
               m, dpre, dagg, to_west, to_east, acc):
        half = z.edge // z.group

        def collect(s):
            here = pl.ds(s * z.group, z.group)
            got = (fw if s < half else fe)[pl.ds(s % half * z.group, z.group)]
            m[here] = (part[here] + got.astype(F32)).astype(BF16)

        def middle(s):
            here = pl.ds(s * z.group, z.group)
            grad = dot(z.flat(m[here]), wt[0, 2]) * z.flat(slope[here])
            dpre[here] = z.tiled(grad.astype(BF16))

        def last(s):
            here = pl.ds(s * z.group, z.group)
            dagg[here] = z.tiled(dot(z.flat(dpre[here]), wt[0, 1]).astype(BF16))

        staged(2 * half, collect, middle, last)
        acc[...] = outer[...]

        def source(q):
            return dagg[jnp.minimum(q, z.lent - 1)]

        spread(z, (blocks, sources, targets, counts), 2, z.lent, at, source, acc, True)
        to_west[...] = acc[pl.ds(0, z.edge)].astype(BF16)
        to_east[...] = acc[pl.ds(z.edge, z.edge)].astype(BF16)

    return call(
        kernel,
        "early_lent",
        [SMEM] * 4 + [VMEM] * 9,
        [VMEM] * 5,
        [z.nodes(z.lent)] * 3 + [z.nodes(z.edge)] * 2,
        [z.held(z.lent, F32)],
        16,
        (*tables, part, fw, fe, slope, outer, at, wt, *after),
    )


def place_lent(z, bound, m, grads):
    def kernel(bound, m, _g, grads, token, sems):
        token[...] = jnp.zeros_like(token)
        copies = [
            pltpu.make_async_copy(m.at[i], grads.at[1, bound[0, i // z.edge, i % z.edge]], sems.at[i])
            for i in range(z.lent)
        ]
        for copy in copies:
            copy.start()
        for copy in copies:
            copy.wait()

    return call(
        kernel,
        "place_lent",
        [SMEM, VMEM, ANY],
        [ANY, VMEM],
        [jax.ShapeDtypeStruct(grads.shape, BF16), TOKEN],
        [pltpu.SemaphoreType.DMA((z.lent,))],
        6,
        (bound, m, grads),
        {2: 0},
    )


def finish(z, bound, part, rest, fw, fe, grads):
    def kernel(bound, part, rest, fw, fe, _g, grads, keep, sems):
        copies = [pltpu.make_async_copy(rest, grads.at[0, pl.ds(z.lent, z.rest)], sems.at[z.lent])]
        copies[0].start()
        for i in range(z.lent):
            got = fw[i] if i < z.edge else fe[i - z.edge]
            keep[i] = (part[i] + got.astype(F32)).astype(BF16)
            copy = pltpu.make_async_copy(
                keep.at[i], grads.at[0, bound[0, i // z.edge, i % z.edge]], sems.at[i]
            )
            copy.start()
            copies.append(copy)
        for copy in copies:
            copy.wait()

    return call(
        kernel,
        "finish",
        [SMEM] + [VMEM] * 4 + [ANY],
        ANY,
        jax.ShapeDtypeStruct(grads.shape, BF16),
        [z.held(z.lent), pltpu.SemaphoreType.DMA((z.lent + 1,))],
        14,
        (bound, part, rest, fw, fe, grads),
        {5: 0},
    )


def unpack(z, plane, pieces):
    c = z.cols
    piece = pieces[0].shape[3]
    core, ahead, side = plane.sizes

    def kernel(me, *refs):
        pieces = refs[:core]
        *outs, bias, buf, sems = refs[core:]
        copies = []
        for layer in range(2):
            for i in range(core):
                for j in range(ahead):
                    for k in range(side):
                        start = pl.multiple_of(plane.piece_of(me, (-i, -j, -k)) * piece, 16)
                        buf[layer, pl.ds(start, piece), :] = pieces[i][j, k, layer].astype(F32)
            for i, out in enumerate(outs):
                copy = pltpu.make_async_copy(
                    buf.at[layer, pl.ds(i * c, c)], out.at[layer], sems.at[3 * layer + i]
                )
                copy.start()
                copies.append(copy)
            bias[layer : layer + 1, :] = buf[layer, pl.ds(3 * c, 1), :]
        for copy in copies:
            copy.wait()

    square = jax.ShapeDtypeStruct((2, c, c), F32)
    return call(
        kernel,
        "unpack",
        [SMEM] + [VMEM] * core,
        [ANY] * 3 + [VMEM],
        [square, square, square, jax.ShapeDtypeStruct((2, c), F32)],
        [pltpu.VMEM((2, piece * plane.count, c), F32), pltpu.SemaphoreType.DMA((6,))],
        10,
        (plane.me, *pieces),
    )


def per_device(
    node_in, out_cot, adjacency, tile_nbrs, bound_tiles, live_tiles, w_self, w_nbr, pre_bias, w_out
):
    z = Sizes(adjacency, node_in, bound_tiles)
    t, r, c = z.tiles, z.rows, z.cols
    features = node_in.reshape(t, r, c)
    cot = out_cot.reshape(t, r, c)
    plane = Plane()

    west, east = lend(z, bound_tiles, features)
    from_west = passed_along(east, 1)
    from_east = passed_along(west, -1)
    *nodes, adj, tiles, reads, blocks, sources, targets, counts, plane.me = arrange(
        z, bound_tiles, tile_nbrs, live_tiles, plane.place, features, cot, adjacency.reshape(z.pairs, r, r)
    )
    f0, m1 = tuple(nodes[:2]), tuple(nodes[2:])
    tables = (blocks, sources, targets, counts)
    at, wt = turn(z, adj, w_self, w_nbr, w_out)

    west, east, agg_lent = first_lent(
        z, tiles, reads, f0, from_west, from_east, adj, w_self, w_nbr, pre_bias, w_out
    )
    next_west = passed_along(east, 1)
    next_east = passed_along(west, -1)
    f1_lent, f1_rest, section_out, agg_rest = first_rest(
        z, tiles, reads, bound_tiles, live_tiles, f0, from_west, from_east, adj, w_self, w_nbr, pre_bias, w_out,
        west, east,
    )
    f1, agg0 = (f1_lent, f1_rest), (agg_lent, agg_rest)
    own, hidden = second_own(z, f1, m1, w_self, pre_bias, wt)
    act0, slope, ready = saved(z, f0, agg0, w_self, w_nbr, pre_bias)

    agg1, act1, dpre1, dagg1, to_west, to_east = second(
        z, tiles, reads, tables, f1, next_west, next_east, adj, at, own, hidden, w_nbr, wt, ready
    )
    back_west = passed_along(to_east, 1)
    back_east = passed_along(to_west, -1)
    late = weight_grads(z, plane, f1, agg1, act1, m1, dpre1, "weight_grads1")
    section_out, ready = second_out(z, bound_tiles, live_tiles, f1, act1, w_out, section_out)
    part, upstream, done = input_grad(z, 1, tables, m1, dpre1, dagg1, at, wt)
    late = plane_parts(plane, late, ((ready,), (done,)))
    grads, m0_rest, dpre_rest, dagg_rest, outer = early_rest(
        z, tables, live_tiles, upstream, slope, at, wt
    )
    late = added(late, after=(outer,))

    m0_lent, dpre_lent, dagg_lent, to_west, to_east = early_lent(
        z, tables, part, back_west, back_east, slope, outer, at, wt, (ready, late)
    )
    back_west = passed_along(to_east, 1)
    back_east = passed_along(to_west, -1)
    m0, dpre0, dagg0 = (m0_lent, m0_rest), (dpre_lent, dpre_rest), (dagg_lent, dagg_rest)
    grads, ready = place_lent(z, bound_tiles, m0_lent, grads)
    early = weight_grads(z, plane, f0, agg0, act0, m0, dpre0, "weight_grads0", (ready,))


    late_far = [from_line(late, step) for step in (2, 3)] if lax.axis_size("feat") == 4 else []

    def meanwhile(early, tables, m0, dpre0, dagg0, at, wt):
        part, rest, _ = input_grad(z, 0, tables, m0, dpre0, dagg0, at, wt)
        return added(plane_parts(plane, early)), part, rest

    args = (early, tables, m0, dpre0, dagg0, at, wt)
    shapes = jax.eval_shape(meanwhile, *args)
    early, part, rest = lax.cond(
        live_tiles[0] > 0,
        meanwhile,
        lambda *_: jax.tree.map(lambda a: jnp.zeros(a.shape, a.dtype), shapes),
        *args,
    )
    both = joined(early, late)
    if lax.axis_size("feat") == 4:
        near = from_line(both, 1)
        far = [from_line(early, step) for step in (2, 3)]
        shares = line_sum_of_four(both, near, far, late_far, (back_west, back_east))
    else:
        shares = line_sum(both)
    pieces = plane_gathered(plane, shares)
    grads = finish(z, bound_tiles, part, rest, back_west, back_east, grads)
    grad_self, grad_nbr, grad_out, grad_bias = unpack(z, plane, pieces)
    return (
        section_out.reshape(2, t * r, c),
        grads.reshape(2, t * r, c),
        grad_self,
        grad_nbr,
        grad_bias,
        grad_out,
    )


def solution(mesh):
    rows = P(AXES)
    in_specs = (rows, rows, rows, rows, rows, rows, P(), P(), P(), P())
    out_specs = (P(None, AXES), P(None, AXES), P(), P(), P(), P())
    return jax.shard_map(
        per_device, mesh=mesh, in_specs=in_specs, out_specs=out_specs, check_vma=False
    )
```

```python
import jax
import jax.numpy as jnp
from jax import lax
from jax.experimental import pallas as pl
from jax.experimental.pallas import tpu as pltpu
from jax.sharding import PartitionSpec as P

AXES = ("dom", "phase", "feat")
PLANE = ("dom", "phase")
BF16 = jnp.bfloat16
F32 = jnp.float32
ANY = pl.BlockSpec(memory_space=pl.ANY)
SMEM = pl.BlockSpec(memory_space=pltpu.SMEM)
VMEM = pl.BlockSpec(memory_space=pltpu.VMEM)
MIB = 1024 * 1024
TOKEN = jax.ShapeDtypeStruct((8, 128), F32)


class Sizes:
    def __init__(self, adjacency, features, bound):
        self.tiles, self.slots, self.rows, _ = adjacency.shape
        self.cols = features.shape[-1]
        self.edge = bound.shape[-1]
        self.lent = 2 * self.edge
        self.rest = self.tiles - self.lent
        self.ext = self.tiles + self.lent
        self.pairs = self.tiles * self.slots
        self.group = next(g for g in (4, 2, 1) if self.edge % g == 0 and self.rest % g == 0)
        self.parts = ((0, 0, self.lent), (1, self.lent, self.rest))
        self.index = Index(self)

    def nodes(self, count, dtype=BF16):
        return jax.ShapeDtypeStruct((count, self.rows, self.cols), dtype)

    def held(self, count, dtype=BF16):
        return pltpu.VMEM((count, self.rows, self.cols), dtype)

    def flat(self, value):
        return value.reshape(self.group * self.rows, self.cols)

    def tiled(self, value):
        return value.reshape(self.group, self.rows, self.cols)


def group_of(z, array, part, first):
    if isinstance(array, tuple):
        base = z.lent if part else 0
        return array[part].at[pl.ds(first - base, z.group)]
    return array.at[pl.ds(first, z.group)]


def each_group(z, body, parts=(0, 1), unroll=1):
    for part, base, count in z.parts:
        if part in parts:

            @pl.loop(0, count // z.group, unroll=unroll)
            def _(s):
                body(part, base + s * z.group)


def staged(count, *stages):
    for s in range(count + len(stages) - 1):
        for i, stage in enumerate(stages):
            if 0 <= s - i < count:
                stage(s - i)


def passed_along(value, steps):
    count = lax.axis_size(AXES)
    return lax.ppermute(value, AXES, [(i, (i + steps) % count) for i in range(count)])


def dot(a, b):
    return jnp.dot(a, b, preferred_element_type=F32)


def dot_rows(a, b):
    return lax.dot_general(a, b, (((0,), (0,)), ((), ())), preferred_element_type=F32)


def call(kernel, name, in_specs, out_specs, out_shape, scratch, limit, args, aliases=None):
    return pl.pallas_call(
        kernel,
        in_specs=in_specs,
        out_specs=out_specs,
        out_shape=out_shape,
        scratch_shapes=scratch,
        input_output_aliases=aliases or {},
        compiler_params=pltpu.CompilerParams(vmem_limit_bytes=limit * MIB),
        cost_estimate=pl.CostEstimate(flops=1000, bytes_accessed=1000, transcendentals=0),
        name=name,
    )(*args)


def sigmoid(v):
    return 0.5 * jnp.tanh(0.5 * v) + 0.5


def lend(z, bound, features):
    def kernel(bound, feats, west, east, buf, index, sems):
        copies = [
            pltpu.make_async_copy(feats.at[pl.ds(0, z.lent)], buf, sems.at[0]),
            pltpu.make_async_copy(bound, index, sems.at[1]),
        ]
        for copy in copies:
            copy.start()
        for copy in copies:
            copy.wait()
        for i in range(z.edge):
            west[i] = buf[index[0, 0, i]]
            east[i] = buf[index[0, 1, i]]

    return call(
        kernel,
        "lend",
        [ANY, ANY],
        [VMEM, VMEM],
        [z.nodes(z.edge), z.nodes(z.edge)],
        [z.held(z.lent), pltpu.SMEM(bound.shape, jnp.int32), pltpu.SemaphoreType.DMA((2,))],
        56,
        (bound, features),
    )


class Index:
    QUAD = 4

    def __init__(self, z):
        self.first = (0, z.tiles, z.tiles + z.lent, z.tiles + 2 * z.lent, z.tiles + 3 * z.lent)
        self.targets = z.tiles + 3 * z.lent + 1
        self.more = tuple(self.QUAD * self.targets + i * z.pairs for i in range(5))
        self.size = self.QUAD * self.targets + 5 * z.pairs
        self.size = -(-self.size // 8) * 8


def arrange(z, bound, nbrs, live, place, features, cot, adjacency):
    s4 = z.slots
    x = z.index

    def kernel(bound, nbrs, live, place, feats, cot, adj, f_lent, f_rest, m_lent, m_rest, adj_out, ext,
               tiles, reads, blocks, sources, targets, counts, me, inverse, used, sems):
        copies = []
        for i in range(8):
            me[i] = place[i]

        def start(source, target):
            copy = pltpu.make_async_copy(source, target, sems.at[len(copies)])
            copy.start()
            copies.append(copy)

        tail = pl.ds(z.lent, z.rest)
        start(feats.at[tail], f_rest)
        start(feats.at[tail], ext.at[tail])
        start(cot.at[tail], m_rest)
        start(adj, adj_out)
        for i in range(z.lent):
            tile = bound[0, i // z.edge, i % z.edge]
            inverse[tile] = i
            start(feats.at[tile], f_lent.at[i])
            start(feats.at[tile], ext.at[i])
            start(cot.at[tile], m_lent.at[i])

        @pl.loop(0, x.targets)
        def _(i):
            used[i] = 0
            for k in range(x.QUAD):
                blocks[i * x.QUAD + k] = -1
                sources[i * x.QUAD + k] = 0

        for i in range(8):
            counts[i] = 0

        def put(table, target, block, position):
            place = used[target]
            used[target] = place + 1
            fits = place < x.QUAD
            listed = counts[table]
            counts[table] = listed + jnp.where(fits, 0, 1)
            at = jnp.where(fits, target * x.QUAD + place, x.more[0] + table * z.pairs + listed)
            blocks[at] = block
            sources[at] = position
            return at

        @pl.loop(0, z.tiles)
        def _(position):
            clipped = jnp.minimum(position, z.lent - 1)
            tile = jnp.where(position < z.lent, bound[0, clipped // z.edge, clipped % z.edge], position)
            tiles[position] = tile
            for k in range(s4):
                target = nbrs[tile, k]
                moved = jnp.where(target < z.lent, inverse[jnp.minimum(target, z.lent - 1)], target)
                reads[position * s4 + k] = moved
                block = tile * s4 + k
                own = moved < z.tiles
                at = put(jnp.where(own, 0, 1), moved, block, position)
                targets[at] = jnp.where(own, moved, moved - z.tiles)
                lent = position < z.lent
                table = jnp.where(own, 4, jnp.where(lent, 2, 3))
                shift = jnp.where(lent, z.lent, 2 * z.lent)
                at = put(table, jnp.where(own, x.first[4], moved + shift), block, position)
                targets[at] = moved - z.tiles

        for copy in copies:
            copy.wait()

        @pl.loop(0, z.rest)
        def _(i):
            @pl.when(z.lent + i >= live[0])
            def _():
                m_rest[i] = jnp.zeros((z.rows, z.cols), BF16)

    return call(
        kernel,
        "arrange",
        [SMEM] * 4 + [ANY] * 3,
        [VMEM] * 6 + [SMEM] * 7,
        [z.nodes(z.lent), z.nodes(z.rest), z.nodes(z.lent), z.nodes(z.rest)]
        + [jax.ShapeDtypeStruct(adjacency.shape, BF16), z.nodes(z.ext)]
        + [jax.ShapeDtypeStruct((n,), jnp.int32) for n in (z.tiles, z.pairs, x.size, x.size, x.size, 8, 8)],
        [
            pltpu.SMEM((z.lent,), jnp.int32),
            pltpu.SMEM((x.targets,), jnp.int32),
            pltpu.SemaphoreType.DMA((3 * z.lent + 4,)),
        ],
        14,
        (bound, nbrs, live, place, features, cot, adjacency),
    )


def turn(z, adj, w_self, w_nbr, w_out):
    def kernel(adj, ws, wn, wo, at, wt):
        for layer in range(2):
            wt[layer, 0] = ws[layer].T
            wt[layer, 1] = wn[layer].T
            wt[layer, 2] = wo[layer].T

        @pl.loop(0, z.pairs, unroll=4)
        def _(i):
            at[i] = adj[i].T

    return call(
        kernel,
        "turn",
        [VMEM] * 4,
        [VMEM, VMEM],
        [jax.ShapeDtypeStruct(adj.shape, BF16), jax.ShapeDtypeStruct((2, 3, z.cols, z.cols), BF16)],
        [],
        12,
        (adj, w_self, w_nbr, w_out),
    )


def fill_borrowed(z, fw, fe, ext):
    ext[pl.ds(z.tiles, z.edge)] = fw[...]
    ext[pl.ds(z.tiles + z.edge, z.edge)] = fe[...]


def fill_extended(z, own, fw, fe, ext):
    ext[pl.ds(0, z.lent)] = own[0][...]
    ext[pl.ds(z.lent, z.rest)] = own[1][...]
    fill_borrowed(z, fw, fe, ext)


def aggregate(z, tiles, reads, first, adj, ext):
    rows = []
    for g in range(z.group):
        base = (first + g) * z.slots
        block = tiles[first + g] * z.slots
        picked = jnp.concatenate([ext[reads[base + k]] for k in range(z.slots)], axis=0)
        blocks = jnp.concatenate([adj[block + k] for k in range(z.slots)], axis=1)
        rows.append(dot(blocks, picked).astype(BF16))
    return jnp.concatenate(rows, axis=0)


def live_rows(z, value, first, live):
    parts = []
    for g in range(z.group):
        part = value[g * z.rows : (g + 1) * z.rows]
        parts.append(jnp.where(first + g < live, part, jnp.zeros_like(part)))
    return jnp.concatenate(parts, axis=0)


def first_lent(z, tiles, reads, ext, fw, fe, adj, w_self, w_nbr, bias, w_out):
    def kernel(tiles, reads, _ext, fw, fe, adj, ws, wn, bias, wo, west, east, agg, ext, acts):
        fill_borrowed(z, fw, fe, ext)

        def gather(s):
            agg[pl.ds(s * z.group, z.group)] = z.tiled(aggregate(z, tiles, reads, s * z.group, adj, ext))

        def middle(s):
            here = pl.ds(s * z.group, z.group)
            f = z.flat(ext[here])
            pre = dot(f, ws[0]) + dot(z.flat(agg[here]), wn[0]) + bias[0:1, :]
            acts[here] = z.tiled((pre * sigmoid(pre)).astype(BF16))

        def last(s):
            here = pl.ds(s * z.group, z.group)
            out = z.flat(ext[here]).astype(F32) + dot(z.flat(acts[here]), wo[0])
            half = z.edge // z.group
            target = west if s < half else east
            target[pl.ds(s % half * z.group, z.group)] = z.tiled(out.astype(BF16))

        staged(z.lent // z.group, gather, middle, last)

    return call(
        kernel,
        "first_lent",
        [SMEM] * 2 + [VMEM] * 8,
        [VMEM] * 4,
        [z.nodes(z.edge), z.nodes(z.edge), z.nodes(z.lent), z.nodes(z.ext)],
        [z.held(z.lent)],
        12,
        (tiles, reads, ext, fw, fe, adj, w_self, w_nbr, bias, w_out),
        {2: 3},
    )


def first_rest(z, tiles, reads, bound, live, f0, fw, fe, adj, w_self, w_nbr, bias, w_out, west, east):
    def kernel(tiles, reads, bound, live, f_lent, f_rest, fw, fe, adj, ws, wn, bias, wo, west, east,
               f1_lent, f1_rest, out, agg, ext, sems):
        copies = []
        for i in range(z.edge):
            for side, source in ((0, west), (1, east)):
                copy = pltpu.make_async_copy(
                    source.at[i], out.at[0, bound[0, side, i]], sems.at[side * z.edge + i]
                )
                copy.start()
                copies.append(copy)
        fill_extended(z, (f_lent, f_rest), fw, fe, ext)
        f1_lent[pl.ds(0, z.edge)] = west[...]
        f1_lent[pl.ds(z.edge, z.edge)] = east[...]

        def work(part, first):
            f = z.flat(ext[pl.ds(first, z.group)])
            aggs = aggregate(z, tiles, reads, first, adj, ext)
            here = pl.ds(first - z.lent, z.group)
            agg[here] = z.tiled(aggs)
            pre = dot(f, ws[0]) + dot(aggs, wn[0]) + bias[0:1, :]
            act = (pre * sigmoid(pre)).astype(BF16)
            res = live_rows(z, f.astype(F32) + dot(act, wo[0]), first, live[0])
            f1_rest[here] = z.tiled(res.astype(BF16))

        each_group(z, work, (1,))
        copy = pltpu.make_async_copy(f1_rest, out.at[0, pl.ds(z.lent, z.rest)], sems.at[z.lent])
        copy.start()
        for other in copies:
            other.wait()
        copy.wait()

    return call(
        kernel,
        "first_rest",
        [SMEM] * 4 + [VMEM] * 11,
        [VMEM, VMEM, ANY, VMEM],
        [
            z.nodes(z.lent),
            z.nodes(z.rest),
            jax.ShapeDtypeStruct((2, z.tiles, z.rows, z.cols), BF16),
            z.nodes(z.rest),
        ],
        [z.held(z.ext), pltpu.SemaphoreType.DMA((1 + z.lent,))],
        10,
        (tiles, reads, bound, live, *f0, fw, fe, adj, w_self, w_nbr, bias, w_out, west, east),
    )


def second_own(z, f1, m1, w_self, bias, wt):
    def kernel(f_lent, f_rest, m_lent, m_rest, ws, bias, wt, own, hidden, ext):
        ext[pl.ds(0, z.lent)] = f_lent[...]
        ext[pl.ds(z.lent, z.rest)] = f_rest[...]

        def work(part, first):
            f = z.flat(group_of(z, (f_lent, f_rest), part, first)[...])
            m = z.flat(group_of(z, (m_lent, m_rest), part, first)[...])
            here = pl.ds(first, z.group)
            own[here] = z.tiled(dot(f, ws[1]) + bias[1:2, :])
            hidden[here] = z.tiled(dot(m, wt[1, 2]))

        each_group(z, work)

    return call(
        kernel,
        "second_own",
        [VMEM] * 7,
        [VMEM] * 3,
        [z.nodes(z.tiles, F32)] * 2 + [z.nodes(z.ext)],
        [],
        12,
        (*f1, *m1, w_self, bias, wt),
    )


def saved(z, f0, agg0, w_self, w_nbr, bias):
    def kernel(f_lent, f_rest, a_lent, a_rest, ws, wn, bias, act, slope, token):
        token[...] = jnp.zeros_like(token)

        def work(part, first):
            f = z.flat(group_of(z, (f_lent, f_rest), part, first)[...])
            aggs = z.flat(group_of(z, (a_lent, a_rest), part, first)[...])
            pre = dot(f, ws[0]) + dot(aggs, wn[0]) + bias[0:1, :]
            sig = sigmoid(pre)
            here = pl.ds(first, z.group)
            act[here] = z.tiled((pre * sig).astype(BF16))
            slope[here] = z.tiled(sig * (1.0 + pre * (1.0 - sig)))

        each_group(z, work)

    return call(
        kernel,
        "saved",
        [VMEM] * 7,
        [VMEM] * 3,
        [z.nodes(z.tiles), z.nodes(z.tiles, F32), TOKEN],
        [],
        10,
        (*f0, *agg0, w_self, w_nbr, bias),
    )


def spread(z, tables, table, count, at, source, acc, add):
    blocks, sources, targets, counts = tables
    x = z.index

    @pl.loop(0, count, unroll=4)
    def _(target):
        base = (x.first[table] + target) * x.QUAD
        lefts, rights = [], []
        for k in range(x.QUAD):
            block = blocks[base + k]
            left = at[jnp.maximum(block, 0)]
            lefts.append(jnp.where(block >= 0, left, jnp.zeros_like(left)))
            rights.append(source(sources[base + k]))
        value = dot(jnp.concatenate(lefts, axis=1), jnp.concatenate(rights, axis=0))
        if add:
            acc[target] += value
        else:
            acc[target] = value

    @pl.loop(0, counts[table])
    def _(i):
        place = x.more[table] + i
        acc[targets[place]] += dot(at[blocks[place]], source(sources[place]))


def second(z, tiles, reads, tables, ext, fw, fe, adj, at, own, hidden, w_nbr, wt, after):
    groups = z.tiles // z.group

    def kernel(tiles, reads, blocks, sources, targets, counts, _ext, fw, fe, adj, at, own, hidden, wn,
               wt, _after, agg, act, dpre, dagg, to_west, to_east, ext, acc):
        fill_borrowed(z, fw, fe, ext)

        def gather(s):
            agg[pl.ds(s * z.group, z.group)] = z.tiled(aggregate(z, tiles, reads, s * z.group, adj, ext))

        def middle(s):
            here = pl.ds(s * z.group, z.group)
            pre = z.flat(own[here]) + dot(z.flat(agg[here]), wn[1])
            sig = sigmoid(pre)
            act[here] = z.tiled((pre * sig).astype(BF16))
            slope = sig * (1.0 + pre * (1.0 - sig))
            dpre[here] = z.tiled((z.flat(hidden[here]) * slope).astype(BF16))

        def last(s):
            here = pl.ds(s * z.group, z.group)
            dagg[here] = z.tiled(dot(z.flat(dpre[here]), wt[1, 1]).astype(BF16))

        staged(groups, gather, middle, last)
        spread(z, (blocks, sources, targets, counts), 1, z.lent, at, lambda q: dagg[q], acc, False)
        to_west[...] = acc[pl.ds(0, z.edge)].astype(BF16)
        to_east[...] = acc[pl.ds(z.edge, z.edge)].astype(BF16)

    return call(
        kernel,
        "second",
        [SMEM] * 6 + [VMEM] * 10,
        [VMEM] * 7,
        [z.nodes(z.tiles)] * 4 + [z.nodes(z.edge)] * 2 + [z.nodes(z.ext)],
        [z.held(z.lent, F32)],
        12,
        (tiles, reads, *tables, ext, fw, fe, adj, at, own, hidden, w_nbr, wt, after),
        {6: 6},
    )


class Plane:
    def __init__(self):
        dom, phase = lax.axis_size("dom"), lax.axis_size("phase")
        core = 2 if dom % 2 == 0 else 1
        self.sizes = (core, dom // core, phase)
        self.count = dom * phase
        place = lax.axis_index("dom")
        place = [lax.rem(place, core), place // core, lax.axis_index("phase")]
        self.place = jnp.stack(place + [jnp.zeros_like(place[0])] * 5).astype(jnp.int32)
        self.me = None

    def piece_of(self, me, steps):
        at = [lax.rem(me[i] + (steps[i] + n) % n, n) for i, n in enumerate(self.sizes)]
        return (at[0] * self.sizes[1] + at[1]) * self.sizes[2] + at[2]

    def passed(self, value, dim, steps):
        return self.passed_by(value, [steps if i == dim else 0 for i in range(3)])

    def passed_by(self, value, steps):
        pairs = []
        for c in range(self.sizes[0]):
            for d in range(self.sizes[1]):
                for p in range(self.sizes[2]):
                    to = [(at + by) % n for at, by, n in zip((c, d, p), steps, self.sizes)]
                    source = (d * self.sizes[0] + c) * self.sizes[2] + p
                    target = (to[1] * self.sizes[0] + to[0]) * self.sizes[2] + to[2]
                    pairs.append((source, target))
        return lax.ppermute(value, PLANE, pairs)

    def received(self, parts, dim):
        return [parts[0]] + [self.passed(parts[i], dim, i) for i in range(1, self.sizes[dim])]


def weight_grads(z, plane, f, agg, act, m, dpre, name, place=()):
    c = z.cols
    piece = -(-(3 * c + 1) // (plane.count * 16)) * 16
    core, ahead, side = plane.sizes
    arrays = (f, agg, act, m, dpre)
    flat_args = [x for a in arrays for x in (a if isinstance(a, tuple) else (a,))]

    def kernel(me, *refs):
        refs = list(refs)
        f, agg, act, m, dpre = [
            (refs.pop(0), refs.pop(0)) if isinstance(a, tuple) else refs.pop(0) for a in arrays
        ]
        copies = []
        if place:
            bound, _, *refs = refs
            *outs, grads, acc, sums, sems = refs
            for i in range(z.lent):
                target = grads.at[1, bound[0, i // z.edge, i % z.edge]]
                copies.append(pltpu.make_async_copy(m[0].at[i], target, sems.at[i]))
                copies[-1].start()
        else:
            *outs, acc, sums = refs
        acc[...] = jnp.zeros_like(acc)
        sums[...] = jnp.zeros_like(sums)

        def work(part, first):
            def rows(array):
                return z.flat(group_of(z, array, part, first)[...])

            grad = rows(dpre)
            turned = grad.T
            sums[0] += dot(turned, rows(f))
            sums[1] += dot(turned, rows(agg))
            sums[2] += dot(rows(m).T, rows(act))
            acc[pl.ds(3 * c, 1), :] += jnp.sum(grad.astype(F32), axis=0, keepdims=True)

        each_group(z, work)
        for i in range(3):
            acc[pl.ds(i * c, c), :] = sums[i].T
        for i, out in enumerate(outs):
            for j in range(ahead):
                for k in range(side):
                    owner = pl.multiple_of(plane.piece_of(me, (i, j, k)) * piece, 16)
                    out[j, k] = acc[pl.ds(owner, piece), :].astype(BF16)
        for copy in copies:
            copy.wait()

    return call(
        kernel,
        name,
        [SMEM] + [VMEM] * len(flat_args) + ([SMEM, ANY] if place else []),
        [VMEM] * core + ([ANY] if place else []),
        [jax.ShapeDtypeStruct((ahead, side, piece, c), BF16)] * core
        + ([jax.ShapeDtypeStruct(place[1].shape, BF16)] if place else []),
        [pltpu.VMEM((piece * plane.count, c), F32), pltpu.VMEM((3, c, c), F32)]
        + ([pltpu.SemaphoreType.DMA((z.lent,))] if place else []),
        14,
        (plane.me, *flat_args, *place),
        {2 + len(flat_args): core} if place else None,
    )


def added(values, split=False, after=()):
    shape = values[0].shape
    count = shape[0] if split else 1

    def kernel(*refs):
        outs = refs[-count:]
        for i, out in enumerate(outs):
            parts = [(ref[i] if split else ref[...]).astype(F32) for ref in refs[: len(values)]]
            total = parts[0]
            for part in parts[1:]:
                total = total + part
            out[...] = total.astype(BF16)

    args = [*values, *after]
    outs = call(
        kernel,
        "added",
        [VMEM] * len(values) + [ANY] * len(after),
        [VMEM] * count,
        [jax.ShapeDtypeStruct(shape[1:] if split else shape, BF16)] * count,
        [],
        8,
        args,
    )
    return outs if split else outs[0]


def plane_parts(plane, pieces, after=((), ())):
    parts = added(plane.received(pieces, 0), split=True, after=after[0])
    parts = added(plane.received(parts, 1), split=True, after=after[1])
    return plane.received(parts, 2)


def from_line(value, step):
    lines = lax.axis_size("feat")
    return lax.ppermute(value, "feat", [(i, i ^ step) for i in range(lines)])


def joined(early, late):
    def kernel(early, late, out):
        out[0] = early[...]
        out[1] = late[...]

    out = jax.ShapeDtypeStruct((2,) + late.shape, BF16)
    return call(kernel, "joined", [VMEM] * 2, VMEM, out, [], 4, (early, late))


def line_sum_of_four(both, near, early, late, after):
    def kernel(both, near, early0, early1, late0, late1, *rest):
        out = rest[-1]
        for layer, (first, second) in enumerate(((early0, early1), (late0, late1))):
            pair = both[layer].astype(F32) + near[layer].astype(F32)
            out[layer] = (pair + (first[...].astype(F32) + second[...].astype(F32))).astype(BF16)

    return call(
        kernel,
        "line_sum",
        [VMEM] * 6 + [ANY] * len(after),
        VMEM,
        jax.ShapeDtypeStruct(both.shape, BF16),
        [],
        6,
        (both, near, *early, *late, *after),
    )


def line_sum(share):
    lines = lax.axis_size("feat")
    if lines & (lines - 1) != 0:
        return lax.psum(share.astype(F32), "feat").astype(BF16)
    step = 1
    while step < lines:
        share = added([share, from_line(share, step)])
        step *= 2
    return share


def stacked(values):
    def kernel(*refs):
        for i, ref in enumerate(refs[:-1]):
            refs[-1][i] = ref[...]

    shape = (len(values),) + values[0].shape
    out = jax.ShapeDtypeStruct(shape, values[0].dtype)
    return call(kernel, "stacked", [VMEM] * len(values), VMEM, out, [], 4, values)


def plane_gathered(plane, share):
    core, ahead, side = plane.sizes
    steps = [(0, j, k) for j in range(ahead) for k in range(side)]
    share = stacked([share] + [plane.passed_by(share, by) for by in steps[1:]])
    share = share.reshape(ahead, side, *share.shape[-3:])
    return [share] + [plane.passed(share, 0, i) for i in range(1, core)]


def second_out(z, bound, live, f1, act, w_out, out):
    def kernel(bound, live, f_lent, f_rest, act, wo, _out, out, token, keep, sems):
        copies = []
        token[...] = jnp.zeros_like(token)

        def work(part, first):
            f = z.flat(group_of(z, (f_lent, f_rest), part, first)[...])
            res = f.astype(F32) + dot(z.flat(act[pl.ds(first, z.group)]), wo[1])
            keep[pl.ds(first, z.group)] = z.tiled(live_rows(z, res, first, live[0]).astype(BF16))

        each_group(z, work, (0,))
        for i in range(z.lent):
            copy = pltpu.make_async_copy(
                keep.at[i], out.at[1, bound[0, i // z.edge, i % z.edge]], sems.at[i]
            )
            copy.start()
            copies.append(copy)
        each_group(z, work, (1,))
        tail = pl.ds(z.lent, z.rest)
        copy = pltpu.make_async_copy(keep.at[tail], out.at[1, tail], sems.at[z.lent])
        copy.start()
        copies.append(copy)
        for copy in copies:
            copy.wait()

    return call(
        kernel,
        "second_out",
        [SMEM] * 2 + [VMEM] * 4 + [ANY],
        [ANY, VMEM],
        [jax.ShapeDtypeStruct(out.shape, BF16), TOKEN],
        [z.held(z.tiles), pltpu.SemaphoreType.DMA((z.lent + 1,))],
        12,
        (bound, live, *f1, act, w_out, out),
        {6: 0},
    )


def input_grad(z, layer, tables, m, dpre, dagg, at, wt):
    arrays = (m, dpre, dagg)
    flat_args = [x for a in arrays for x in (a if isinstance(a, tuple) else (a,))]

    def kernel(blocks, sources, targets, counts, *refs):
        refs = list(refs)
        m, dpre, dagg = [
            (refs.pop(0), refs.pop(0)) if isinstance(a, tuple) else refs.pop(0) for a in arrays
        ]
        at, wt, part_out, rest_out, token, acc = refs
        token[...] = jnp.zeros_like(token)
        x = z.index

        def source(q):
            if not isinstance(dagg, tuple):
                return dagg[q]
            lent = dagg[0][jnp.minimum(q, z.lent - 1)]
            rest = dagg[1][jnp.maximum(q - z.lent, 0)]
            return jnp.where(q < z.lent, lent, rest)

        def tile_of(array, part, base, i):
            return array[part][i] if isinstance(array, tuple) else array[base + i]

        for part, base, count in z.parts:

            @pl.loop(0, count, unroll=4)
            def _(i):
                lefts, rights = [tile_of(dpre, part, base, i)], [wt[layer, 0]]
                for k in range(x.QUAD):
                    block = blocks[(base + i) * x.QUAD + k]
                    left = at[jnp.maximum(block, 0)]
                    lefts.append(jnp.where(block >= 0, left, jnp.zeros_like(left)))
                    rights.append(source(sources[(base + i) * x.QUAD + k]))
                value = dot(jnp.concatenate(lefts, axis=1), jnp.concatenate(rights, axis=0))
                acc[base + i] = value + tile_of(m, part, base, i).astype(F32)

        @pl.loop(0, counts[0])
        def _(i):
            place = x.more[0] + i
            acc[targets[place]] += dot(at[blocks[place]], source(sources[place]))

        part_out[...] = acc[pl.ds(0, z.lent)]
        rest_out[...] = acc[pl.ds(z.lent, z.rest)].astype(BF16)

    return call(
        kernel,
        "input_grad%d" % layer,
        [SMEM] * 4 + [VMEM] * (len(flat_args) + 2),
        [VMEM] * 3,
        [z.nodes(z.lent, F32), z.nodes(z.rest), TOKEN],
        [z.held(z.tiles, F32)],
        20,
        [*tables, *flat_args, at, wt],
    )


def early_rest(z, tables, live, upstream, slope, at, wt):
    def kernel(blocks, sources, targets, counts, live, g, slope, at, wt, grads, m, dpre, dagg, outer, sem):
        copy = pltpu.make_async_copy(g, grads.at[1, pl.ds(z.lent, z.rest)], sem)
        copy.start()

        def work(part, first):
            here = pl.ds(first - z.lent, z.group)
            masked = live_rows(z, z.flat(g[here]), first, live[0])
            m[here] = z.tiled(masked)
            grad = dot(masked, wt[0, 2]) * z.flat(slope[pl.ds(first, z.group)])
            grad = grad.astype(BF16)
            dpre[here] = z.tiled(grad)
            dagg[here] = z.tiled(dot(grad, wt[0, 1]).astype(BF16))

        each_group(z, work, (1,))

        def source(q):
            return dagg[jnp.maximum(q - z.lent, 0)]

        spread(z, (blocks, sources, targets, counts), 3, z.lent, at, source, outer, False)
        copy.wait()

    return call(
        kernel,
        "early_rest",
        [SMEM] * 5 + [VMEM] * 4,
        [ANY] + [VMEM] * 4,
        [jax.ShapeDtypeStruct((2, z.tiles, z.rows, z.cols), BF16)]
        + [z.nodes(z.rest)] * 3
        + [z.nodes(z.lent, F32)],
        [pltpu.SemaphoreType.DMA],
        14,
        (*tables, live, upstream, slope, at, wt),
    )


def early_lent(z, tables, part, fw, fe, slope, outer, at, wt, after):
    def kernel(blocks, sources, targets, counts, part, fw, fe, slope, outer, at, wt, _ready, _late,
               m, dpre, dagg, to_west, to_east, acc):
        half = z.edge // z.group

        def collect(s):
            here = pl.ds(s * z.group, z.group)
            got = (fw if s < half else fe)[pl.ds(s % half * z.group, z.group)]
            m[here] = (part[here] + got.astype(F32)).astype(BF16)

        def middle(s):
            here = pl.ds(s * z.group, z.group)
            grad = dot(z.flat(m[here]), wt[0, 2]) * z.flat(slope[here])
            dpre[here] = z.tiled(grad.astype(BF16))

        def last(s):
            here = pl.ds(s * z.group, z.group)
            dagg[here] = z.tiled(dot(z.flat(dpre[here]), wt[0, 1]).astype(BF16))

        staged(2 * half, collect, middle, last)
        acc[...] = outer[...]

        def source(q):
            return dagg[jnp.minimum(q, z.lent - 1)]

        spread(z, (blocks, sources, targets, counts), 2, z.lent, at, source, acc, True)
        to_west[...] = acc[pl.ds(0, z.edge)].astype(BF16)
        to_east[...] = acc[pl.ds(z.edge, z.edge)].astype(BF16)

    return call(
        kernel,
        "early_lent",
        [SMEM] * 4 + [VMEM] * 9,
        [VMEM] * 5,
        [z.nodes(z.lent)] * 3 + [z.nodes(z.edge)] * 2,
        [z.held(z.lent, F32)],
        16,
        (*tables, part, fw, fe, slope, outer, at, wt, *after),
    )


def finish(z, bound, part, rest, fw, fe, grads):
    def kernel(bound, part, rest, fw, fe, _g, grads, keep, sems):
        copies = [pltpu.make_async_copy(rest, grads.at[0, pl.ds(z.lent, z.rest)], sems.at[z.lent])]
        copies[0].start()
        for i in range(z.lent):
            got = fw[i] if i < z.edge else fe[i - z.edge]
            keep[i] = (part[i] + got.astype(F32)).astype(BF16)
            copy = pltpu.make_async_copy(
                keep.at[i], grads.at[0, bound[0, i // z.edge, i % z.edge]], sems.at[i]
            )
            copy.start()
            copies.append(copy)
        for copy in copies:
            copy.wait()

    return call(
        kernel,
        "finish",
        [SMEM] + [VMEM] * 4 + [ANY],
        ANY,
        jax.ShapeDtypeStruct(grads.shape, BF16),
        [z.held(z.lent), pltpu.SemaphoreType.DMA((z.lent + 1,))],
        14,
        (bound, part, rest, fw, fe, grads),
        {5: 0},
    )


def unpack(z, plane, pieces):
    c = z.cols
    piece = pieces[0].shape[3]
    core, ahead, side = plane.sizes

    def kernel(me, *refs):
        pieces = refs[:core]
        *outs, bias, buf, sems = refs[core:]
        copies = []
        for layer in range(2):
            for i in range(core):
                for j in range(ahead):
                    for k in range(side):
                        start = pl.multiple_of(plane.piece_of(me, (-i, -j, -k)) * piece, 16)
                        buf[layer, pl.ds(start, piece), :] = pieces[i][j, k, layer].astype(F32)
            for i, out in enumerate(outs):
                copy = pltpu.make_async_copy(
                    buf.at[layer, pl.ds(i * c, c)], out.at[layer], sems.at[3 * layer + i]
                )
                copy.start()
                copies.append(copy)
            bias[layer : layer + 1, :] = buf[layer, pl.ds(3 * c, 1), :]
        for copy in copies:
            copy.wait()

    square = jax.ShapeDtypeStruct((2, c, c), F32)
    return call(
        kernel,
        "unpack",
        [SMEM] + [VMEM] * core,
        [ANY] * 3 + [VMEM],
        [square, square, square, jax.ShapeDtypeStruct((2, c), F32)],
        [pltpu.VMEM((2, piece * plane.count, c), F32), pltpu.SemaphoreType.DMA((6,))],
        10,
        (plane.me, *pieces),
    )


def per_device(
    node_in, out_cot, adjacency, tile_nbrs, bound_tiles, live_tiles, w_self, w_nbr, pre_bias, w_out
):
    z = Sizes(adjacency, node_in, bound_tiles)
    t, r, c = z.tiles, z.rows, z.cols
    features = node_in.reshape(t, r, c)
    cot = out_cot.reshape(t, r, c)
    plane = Plane()

    west, east = lend(z, bound_tiles, features)
    from_west = passed_along(east, 1)
    from_east = passed_along(west, -1)
    *nodes, adj, ext, tiles, reads, blocks, sources, targets, counts, plane.me = arrange(
        z, bound_tiles, tile_nbrs, live_tiles, plane.place, features, cot, adjacency.reshape(z.pairs, r, r)
    )
    f0, m1 = tuple(nodes[:2]), tuple(nodes[2:])
    tables = (blocks, sources, targets, counts)
    at, wt = turn(z, adj, w_self, w_nbr, w_out)

    west, east, agg_lent, _ = first_lent(
        z, tiles, reads, ext, from_west, from_east, adj, w_self, w_nbr, pre_bias, w_out
    )
    next_west = passed_along(east, 1)
    next_east = passed_along(west, -1)
    f1_lent, f1_rest, section_out, agg_rest = first_rest(
        z, tiles, reads, bound_tiles, live_tiles, f0, from_west, from_east, adj, w_self, w_nbr, pre_bias, w_out,
        west, east,
    )
    f1, agg0 = (f1_lent, f1_rest), (agg_lent, agg_rest)
    own, hidden, ext = second_own(z, f1, m1, w_self, pre_bias, wt)
    act0, slope, ready = saved(z, f0, agg0, w_self, w_nbr, pre_bias)

    agg1, act1, dpre1, dagg1, to_west, to_east, _ = second(
        z, tiles, reads, tables, ext, next_west, next_east, adj, at, own, hidden, w_nbr, wt, ready
    )
    back_west = passed_along(to_east, 1)
    back_east = passed_along(to_west, -1)
    late = weight_grads(z, plane, f1, agg1, act1, m1, dpre1, "weight_grads1")
    section_out, ready = second_out(z, bound_tiles, live_tiles, f1, act1, w_out, section_out)
    part, upstream, done = input_grad(z, 1, tables, m1, dpre1, dagg1, at, wt)
    late = plane_parts(plane, late, ((ready,), (done,)))
    grads, m0_rest, dpre_rest, dagg_rest, outer = early_rest(
        z, tables, live_tiles, upstream, slope, at, wt
    )
    late = added(late, after=(outer,))

    m0_lent, dpre_lent, dagg_lent, to_west, to_east = early_lent(
        z, tables, part, back_west, back_east, slope, outer, at, wt, (ready, late)
    )
    back_west = passed_along(to_east, 1)
    back_east = passed_along(to_west, -1)
    m0, dpre0, dagg0 = (m0_lent, m0_rest), (dpre_lent, dpre_rest), (dagg_lent, dagg_rest)
    *early, grads = weight_grads(z, plane, f0, agg0, act0, m0, dpre0, "weight_grads0", (bound_tiles, grads))


    late_far = [from_line(late, step) for step in (2, 3)] if lax.axis_size("feat") == 4 else []

    def meanwhile(early, tables, m0, dpre0, dagg0, at, wt):
        part, rest, _ = input_grad(z, 0, tables, m0, dpre0, dagg0, at, wt)
        return added(plane_parts(plane, early)), part, rest

    args = (early, tables, m0, dpre0, dagg0, at, wt)
    shapes = jax.eval_shape(meanwhile, *args)
    early, part, rest = lax.cond(
        live_tiles[0] > 0,
        meanwhile,
        lambda *_: jax.tree.map(lambda a: jnp.zeros(a.shape, a.dtype), shapes),
        *args,
    )
    both = joined(early, late)
    if lax.axis_size("feat") == 4:
        near = from_line(both, 1)
        far = [from_line(early, step) for step in (2, 3)]
        shares = line_sum_of_four(both, near, far, late_far, (back_west, back_east))
    else:
        shares = line_sum(both)
    pieces = plane_gathered(plane, shares)
    grads = finish(z, bound_tiles, part, rest, back_west, back_east, grads)
    grad_self, grad_nbr, grad_out, grad_bias = unpack(z, plane, pieces)
    return (
        section_out.reshape(2, t * r, c),
        grads.reshape(2, t * r, c),
        grad_self,
        grad_nbr,
        grad_bias,
        grad_out,
    )


def solution(mesh):
    rows = P(AXES)
    in_specs = (rows, rows, rows, rows, rows, rows, P(), P(), P(), P())
    out_specs = (P(None, AXES), P(None, AXES), P(), P(), P(), P())
    return jax.shard_map(
        per_device, mesh=mesh, in_specs=in_specs, out_specs=out_specs, check_vma=False
    )
```

```python
import jax
import jax.numpy as jnp
from jax import lax
from jax.experimental import pallas as pl
from jax.experimental.pallas import tpu as pltpu
from jax.sharding import PartitionSpec as P

AXES = ("dom", "phase", "feat")
PLANE = ("dom", "phase")
BF16 = jnp.bfloat16
F32 = jnp.float32
ANY = pl.BlockSpec(memory_space=pl.ANY)
SMEM = pl.BlockSpec(memory_space=pltpu.SMEM)
VMEM = pl.BlockSpec(memory_space=pltpu.VMEM)
MIB = 1024 * 1024
TOKEN = jax.ShapeDtypeStruct((8, 128), F32)


class Sizes:
    def __init__(self, adjacency, features, bound):
        self.tiles, self.slots, self.rows, _ = adjacency.shape
        self.cols = features.shape[-1]
        self.edge = bound.shape[-1]
        self.lent = 2 * self.edge
        self.rest = self.tiles - self.lent
        self.ext = self.tiles + self.lent
        self.pairs = self.tiles * self.slots
        self.group = next(g for g in (4, 2, 1) if self.edge % g == 0 and self.rest % g == 0)
        self.parts = ((0, 0, self.lent), (1, self.lent, self.rest))
        self.index = Index(self)

    def nodes(self, count, dtype=BF16):
        return jax.ShapeDtypeStruct((count, self.rows, self.cols), dtype)

    def held(self, count, dtype=BF16):
        return pltpu.VMEM((count, self.rows, self.cols), dtype)

    def flat(self, value):
        return value.reshape(self.group * self.rows, self.cols)

    def tiled(self, value):
        return value.reshape(self.group, self.rows, self.cols)


def group_of(z, array, part, first):
    if isinstance(array, tuple):
        base = z.lent if part else 0
        return array[part].at[pl.ds(first - base, z.group)]
    return array.at[pl.ds(first, z.group)]


def each_group(z, body, parts=(0, 1), unroll=1):
    for part, base, count in z.parts:
        if part in parts:

            @pl.loop(0, count // z.group, unroll=unroll)
            def _(s):
                body(part, base + s * z.group)


def staged(count, *stages):
    for s in range(count + len(stages) - 1):
        for i, stage in enumerate(stages):
            if 0 <= s - i < count:
                stage(s - i)


def passed_along(value, steps):
    count = lax.axis_size(AXES)
    return lax.ppermute(value, AXES, [(i, (i + steps) % count) for i in range(count)])


def dot(a, b):
    return jnp.dot(a, b, preferred_element_type=F32)


def dot_rows(a, b):
    return lax.dot_general(a, b, (((0,), (0,)), ((), ())), preferred_element_type=F32)


def call(kernel, name, in_specs, out_specs, out_shape, scratch, limit, args, aliases=None):
    return pl.pallas_call(
        kernel,
        in_specs=in_specs,
        out_specs=out_specs,
        out_shape=out_shape,
        scratch_shapes=scratch,
        input_output_aliases=aliases or {},
        compiler_params=pltpu.CompilerParams(vmem_limit_bytes=limit * MIB),
        cost_estimate=pl.CostEstimate(flops=1000, bytes_accessed=1000, transcendentals=0),
        name=name,
    )(*args)


def sigmoid(v):
    return 0.5 * jnp.tanh(0.5 * v) + 0.5


def lend(z, bound, features):
    def kernel(bound, feats, west, east, buf, index, sems):
        copies = [
            pltpu.make_async_copy(feats.at[pl.ds(0, z.lent)], buf, sems.at[0]),
            pltpu.make_async_copy(bound, index, sems.at[1]),
        ]
        for copy in copies:
            copy.start()
        for copy in copies:
            copy.wait()
        for i in range(z.edge):
            west[i] = buf[index[0, 0, i]]
            east[i] = buf[index[0, 1, i]]

    return call(
        kernel,
        "lend",
        [ANY, ANY],
        [VMEM, VMEM],
        [z.nodes(z.edge), z.nodes(z.edge)],
        [z.held(z.lent), pltpu.SMEM(bound.shape, jnp.int32), pltpu.SemaphoreType.DMA((2,))],
        56,
        (bound, features),
    )


class Index:
    QUAD = 4

    def __init__(self, z):
        self.first = (0, z.tiles, z.tiles + z.lent, z.tiles + 2 * z.lent, z.tiles + 3 * z.lent)
        self.targets = z.tiles + 3 * z.lent + 1
        self.more = tuple(self.QUAD * self.targets + i * z.pairs for i in range(5))
        self.size = self.QUAD * self.targets + 5 * z.pairs
        self.size = -(-self.size // 8) * 8


def arrange(z, bound, nbrs, live, place, features, cot, adjacency):
    s4 = z.slots
    x = z.index

    def kernel(bound, nbrs, live, place, feats, cot, adj, f_lent, f_rest, m_lent, m_rest, adj_out, ext,
               tiles, reads, blocks, sources, targets, counts, me, inverse, used, sems):
        copies = []
        for i in range(8):
            me[i] = place[i]

        def start(source, target):
            copy = pltpu.make_async_copy(source, target, sems.at[len(copies)])
            copy.start()
            copies.append(copy)

        tail = pl.ds(z.lent, z.rest)
        start(feats.at[tail], f_rest)
        start(feats.at[tail], ext.at[tail])
        start(cot.at[tail], m_rest)
        start(adj, adj_out)
        for i in range(z.lent):
            tile = bound[0, i // z.edge, i % z.edge]
            inverse[tile] = i
            start(feats.at[tile], f_lent.at[i])
            start(feats.at[tile], ext.at[i])
            start(cot.at[tile], m_lent.at[i])

        @pl.loop(0, x.targets)
        def _(i):
            used[i] = 0
            for k in range(x.QUAD):
                blocks[i * x.QUAD + k] = -1
                sources[i * x.QUAD + k] = 0

        for i in range(8):
            counts[i] = 0

        def put(table, target, block, position):
            place = used[target]
            used[target] = place + 1
            fits = place < x.QUAD
            listed = counts[table]
            counts[table] = listed + jnp.where(fits, 0, 1)
            at = jnp.where(fits, target * x.QUAD + place, x.more[0] + table * z.pairs + listed)
            blocks[at] = block
            sources[at] = position
            return at

        @pl.loop(0, z.tiles)
        def _(position):
            clipped = jnp.minimum(position, z.lent - 1)
            tile = jnp.where(position < z.lent, bound[0, clipped // z.edge, clipped % z.edge], position)
            tiles[position] = tile
            for k in range(s4):
                target = nbrs[tile, k]
                moved = jnp.where(target < z.lent, inverse[jnp.minimum(target, z.lent - 1)], target)
                reads[position * s4 + k] = moved
                block = tile * s4 + k
                own = moved < z.tiles
                at = put(jnp.where(own, 0, 1), moved, block, position)
                targets[at] = jnp.where(own, moved, moved - z.tiles)
                lent = position < z.lent
                table = jnp.where(own, 4, jnp.where(lent, 2, 3))
                shift = jnp.where(lent, z.lent, 2 * z.lent)
                at = put(table, jnp.where(own, x.first[4], moved + shift), block, position)
                targets[at] = moved - z.tiles

        for copy in copies:
            copy.wait()

        @pl.loop(0, z.rest)
        def _(i):
            @pl.when(z.lent + i >= live[0])
            def _():
                m_rest[i] = jnp.zeros((z.rows, z.cols), BF16)

    return call(
        kernel,
        "arrange",
        [SMEM] * 4 + [ANY] * 3,
        [VMEM] * 6 + [SMEM] * 7,
        [z.nodes(z.lent), z.nodes(z.rest), z.nodes(z.lent), z.nodes(z.rest)]
        + [jax.ShapeDtypeStruct(adjacency.shape, BF16), z.nodes(z.ext)]
        + [jax.ShapeDtypeStruct((n,), jnp.int32) for n in (z.tiles, z.pairs, x.size, x.size, x.size, 8, 8)],
        [
            pltpu.SMEM((z.lent,), jnp.int32),
            pltpu.SMEM((x.targets,), jnp.int32),
            pltpu.SemaphoreType.DMA((3 * z.lent + 4,)),
        ],
        14,
        (bound, nbrs, live, place, features, cot, adjacency),
    )


def turn(z, adj, w_self, w_nbr, w_out):
    def kernel(adj, ws, wn, wo, at, wt):
        for layer in range(2):
            wt[layer, 0] = ws[layer].T
            wt[layer, 1] = wn[layer].T
            wt[layer, 2] = wo[layer].T

        @pl.loop(0, z.pairs, unroll=4)
        def _(i):
            at[i] = adj[i].T

    return call(
        kernel,
        "turn",
        [VMEM] * 4,
        [VMEM, VMEM],
        [jax.ShapeDtypeStruct(adj.shape, BF16), jax.ShapeDtypeStruct((2, 3, z.cols, z.cols), BF16)],
        [],
        12,
        (adj, w_self, w_nbr, w_out),
    )


def fill_borrowed(z, fw, fe, ext):
    ext[pl.ds(z.tiles, z.edge)] = fw[...]
    ext[pl.ds(z.tiles + z.edge, z.edge)] = fe[...]


def fill_extended(z, own, fw, fe, ext):
    ext[pl.ds(0, z.lent)] = own[0][...]
    ext[pl.ds(z.lent, z.rest)] = own[1][...]
    fill_borrowed(z, fw, fe, ext)


def aggregate(z, tiles, reads, first, adj, ext):
    rows = []
    for g in range(z.group):
        base = (first + g) * z.slots
        block = tiles[first + g] * z.slots
        picked = jnp.concatenate([ext[reads[base + k]] for k in range(z.slots)], axis=0)
        blocks = jnp.concatenate([adj[block + k] for k in range(z.slots)], axis=1)
        rows.append(dot(blocks, picked).astype(BF16))
    return jnp.concatenate(rows, axis=0)


def live_rows(z, value, first, live):
    parts = []
    for g in range(z.group):
        part = value[g * z.rows : (g + 1) * z.rows]
        parts.append(jnp.where(first + g < live, part, jnp.zeros_like(part)))
    return jnp.concatenate(parts, axis=0)


def first_lent(z, tiles, reads, ext, fw, fe, adj, w_self, w_nbr, bias, w_out):
    def kernel(tiles, reads, _ext, fw, fe, adj, ws, wn, bias, wo, west, east, agg, ext, acts):
        fill_borrowed(z, fw, fe, ext)

        def gather(s):
            agg[pl.ds(s * z.group, z.group)] = z.tiled(aggregate(z, tiles, reads, s * z.group, adj, ext))

        def middle(s):
            here = pl.ds(s * z.group, z.group)
            f = z.flat(ext[here])
            pre = dot(f, ws[0]) + dot(z.flat(agg[here]), wn[0]) + bias[0:1, :]
            acts[here] = z.tiled((pre * sigmoid(pre)).astype(BF16))

        def last(s):
            here = pl.ds(s * z.group, z.group)
            out = z.flat(ext[here]).astype(F32) + dot(z.flat(acts[here]), wo[0])
            half = z.edge // z.group
            target = west if s < half else east
            target[pl.ds(s % half * z.group, z.group)] = z.tiled(out.astype(BF16))

        staged(z.lent // z.group, gather, middle, last)

    return call(
        kernel,
        "first_lent",
        [SMEM] * 2 + [VMEM] * 8,
        [VMEM] * 4,
        [z.nodes(z.edge), z.nodes(z.edge), z.nodes(z.lent), z.nodes(z.ext)],
        [z.held(z.lent)],
        12,
        (tiles, reads, ext, fw, fe, adj, w_self, w_nbr, bias, w_out),
        {2: 3},
    )


def first_rest(z, tiles, reads, bound, live, f0, fw, fe, adj, w_self, w_nbr, bias, w_out, west, east):
    def kernel(tiles, reads, bound, live, f_lent, f_rest, fw, fe, adj, ws, wn, bias, wo, west, east,
               f1_lent, f1_rest, out, agg, ext, sems):
        copies = []
        for i in range(z.edge):
            for side, source in ((0, west), (1, east)):
                copy = pltpu.make_async_copy(
                    source.at[i], out.at[0, bound[0, side, i]], sems.at[side * z.edge + i]
                )
                copy.start()
                copies.append(copy)
        fill_extended(z, (f_lent, f_rest), fw, fe, ext)
        f1_lent[pl.ds(0, z.edge)] = west[...]
        f1_lent[pl.ds(z.edge, z.edge)] = east[...]

        def work(part, first):
            f = z.flat(ext[pl.ds(first, z.group)])
            aggs = aggregate(z, tiles, reads, first, adj, ext)
            here = pl.ds(first - z.lent, z.group)
            agg[here] = z.tiled(aggs)
            pre = dot(f, ws[0]) + dot(aggs, wn[0]) + bias[0:1, :]
            act = (pre * sigmoid(pre)).astype(BF16)
            res = live_rows(z, f.astype(F32) + dot(act, wo[0]), first, live[0])
            f1_rest[here] = z.tiled(res.astype(BF16))

        each_group(z, work, (1,))
        copy = pltpu.make_async_copy(f1_rest, out.at[0, pl.ds(z.lent, z.rest)], sems.at[z.lent])
        copy.start()
        for other in copies:
            other.wait()
        copy.wait()

    return call(
        kernel,
        "first_rest",
        [SMEM] * 4 + [VMEM] * 11,
        [VMEM, VMEM, ANY, VMEM],
        [
            z.nodes(z.lent),
            z.nodes(z.rest),
            jax.ShapeDtypeStruct((2, z.tiles, z.rows, z.cols), BF16),
            z.nodes(z.rest),
        ],
        [z.held(z.ext), pltpu.SemaphoreType.DMA((1 + z.lent,))],
        10,
        (tiles, reads, bound, live, *f0, fw, fe, adj, w_self, w_nbr, bias, w_out, west, east),
    )


def second_own(z, f1, m1, w_self, bias, wt):
    def kernel(f_lent, f_rest, m_lent, m_rest, ws, bias, wt, own, hidden, ext):
        ext[pl.ds(0, z.lent)] = f_lent[...]
        ext[pl.ds(z.lent, z.rest)] = f_rest[...]

        def work(part, first):
            f = z.flat(group_of(z, (f_lent, f_rest), part, first)[...])
            m = z.flat(group_of(z, (m_lent, m_rest), part, first)[...])
            here = pl.ds(first, z.group)
            own[here] = z.tiled(dot(f, ws[1]) + bias[1:2, :])
            hidden[here] = z.tiled(dot(m, wt[1, 2]))

        each_group(z, work)

    return call(
        kernel,
        "second_own",
        [VMEM] * 7,
        [VMEM] * 3,
        [z.nodes(z.tiles, F32)] * 2 + [z.nodes(z.ext)],
        [],
        12,
        (*f1, *m1, w_self, bias, wt),
    )


def saved(z, f0, agg0, w_self, w_nbr, bias):
    def kernel(f_lent, f_rest, a_lent, a_rest, ws, wn, bias, act, slope, token):
        token[...] = jnp.zeros_like(token)

        def work(part, first):
            f = z.flat(group_of(z, (f_lent, f_rest), part, first)[...])
            aggs = z.flat(group_of(z, (a_lent, a_rest), part, first)[...])
            pre = dot(f, ws[0]) + dot(aggs, wn[0]) + bias[0:1, :]
            sig = sigmoid(pre)
            here = pl.ds(first, z.group)
            act[here] = z.tiled((pre * sig).astype(BF16))
            slope[here] = z.tiled(sig * (1.0 + pre * (1.0 - sig)))

        each_group(z, work)

    return call(
        kernel,
        "saved",
        [VMEM] * 7,
        [VMEM] * 3,
        [z.nodes(z.tiles), z.nodes(z.tiles, F32), TOKEN],
        [],
        10,
        (*f0, *agg0, w_self, w_nbr, bias),
    )


def spread(z, tables, table, count, at, source, acc, add):
    blocks, sources, targets, counts = tables
    x = z.index

    @pl.loop(0, count, unroll=4)
    def _(target):
        base = (x.first[table] + target) * x.QUAD
        lefts, rights = [], []
        for k in range(x.QUAD):
            block = blocks[base + k]
            left = at[jnp.maximum(block, 0)]
            lefts.append(jnp.where(block >= 0, left, jnp.zeros_like(left)))
            rights.append(source(sources[base + k]))
        value = dot(jnp.concatenate(lefts, axis=1), jnp.concatenate(rights, axis=0))
        if add:
            acc[target] += value
        else:
            acc[target] = value

    @pl.loop(0, counts[table])
    def _(i):
        place = x.more[table] + i
        acc[targets[place]] += dot(at[blocks[place]], source(sources[place]))


def second(z, tiles, reads, tables, ext, fw, fe, adj, at, own, hidden, w_nbr, wt, after):
    groups = z.tiles // z.group

    def kernel(tiles, reads, blocks, sources, targets, counts, _ext, fw, fe, adj, at, own, hidden, wn,
               wt, _after, agg, act, dpre, dagg, to_west, to_east, ext, acc):
        fill_borrowed(z, fw, fe, ext)

        def gather(s):
            agg[pl.ds(s * z.group, z.group)] = z.tiled(aggregate(z, tiles, reads, s * z.group, adj, ext))

        def middle(s):
            here = pl.ds(s * z.group, z.group)
            pre = z.flat(own[here]) + dot(z.flat(agg[here]), wn[1])
            sig = sigmoid(pre)
            act[here] = z.tiled((pre * sig).astype(BF16))
            slope = sig * (1.0 + pre * (1.0 - sig))
            dpre[here] = z.tiled((z.flat(hidden[here]) * slope).astype(BF16))

        def last(s):
            here = pl.ds(s * z.group, z.group)
            dagg[here] = z.tiled(dot(z.flat(dpre[here]), wt[1, 1]).astype(BF16))

        staged(groups, gather, middle, last)
        spread(z, (blocks, sources, targets, counts), 1, z.lent, at, lambda q: dagg[q], acc, False)
        to_west[...] = acc[pl.ds(0, z.edge)].astype(BF16)
        to_east[...] = acc[pl.ds(z.edge, z.edge)].astype(BF16)

    return call(
        kernel,
        "second",
        [SMEM] * 6 + [VMEM] * 10,
        [VMEM] * 7,
        [z.nodes(z.tiles)] * 4 + [z.nodes(z.edge)] * 2 + [z.nodes(z.ext)],
        [z.held(z.lent, F32)],
        12,
        (tiles, reads, *tables, ext, fw, fe, adj, at, own, hidden, w_nbr, wt, after),
        {6: 6},
    )


class Plane:
    def __init__(self):
        dom, phase = lax.axis_size("dom"), lax.axis_size("phase")
        core = 2 if dom % 2 == 0 else 1
        self.sizes = (core, dom // core, phase)
        self.count = dom * phase
        place = lax.axis_index("dom")
        place = [lax.rem(place, core), place // core, lax.axis_index("phase")]
        self.place = jnp.stack(place + [jnp.zeros_like(place[0])] * 5).astype(jnp.int32)
        self.me = None

    def piece_of(self, me, steps):
        at = [lax.rem(me[i] + (steps[i] + n) % n, n) for i, n in enumerate(self.sizes)]
        return (at[0] * self.sizes[1] + at[1]) * self.sizes[2] + at[2]

    def passed(self, value, dim, steps):
        return self.passed_by(value, [steps if i == dim else 0 for i in range(3)])

    def passed_by(self, value, steps):
        pairs = []
        for c in range(self.sizes[0]):
            for d in range(self.sizes[1]):
                for p in range(self.sizes[2]):
                    to = [(at + by) % n for at, by, n in zip((c, d, p), steps, self.sizes)]
                    source = (d * self.sizes[0] + c) * self.sizes[2] + p
                    target = (to[1] * self.sizes[0] + to[0]) * self.sizes[2] + to[2]
                    pairs.append((source, target))
        return lax.ppermute(value, PLANE, pairs)

    def received(self, parts, dim):
        return [parts[0]] + [self.passed(parts[i], dim, i) for i in range(1, self.sizes[dim])]


def weight_grads(z, plane, f, agg, act, m, dpre, name, place=()):
    c = z.cols
    piece = -(-(3 * c + 1) // (plane.count * 16)) * 16
    core, ahead, side = plane.sizes
    arrays = (f, agg, act, m, dpre)
    flat_args = [x for a in arrays for x in (a if isinstance(a, tuple) else (a,))]

    def kernel(me, *refs):
        refs = list(refs)
        f, agg, act, m, dpre = [
            (refs.pop(0), refs.pop(0)) if isinstance(a, tuple) else refs.pop(0) for a in arrays
        ]
        copies = []
        if place:
            bound, _, *refs = refs
            *outs, grads, acc, sums, sems = refs
            for i in range(z.lent):
                target = grads.at[1, bound[0, i // z.edge, i % z.edge]]
                copies.append(pltpu.make_async_copy(m[0].at[i], target, sems.at[i]))
                copies[-1].start()
        else:
            *outs, acc, sums = refs
        acc[...] = jnp.zeros_like(acc)
        sums[...] = jnp.zeros_like(sums)

        def work(part, first):
            def rows(array):
                return z.flat(group_of(z, array, part, first)[...])

            grad = rows(dpre)
            turned = grad.T
            sums[0] += dot(turned, rows(f))
            sums[1] += dot(turned, rows(agg))
            sums[2] += dot(rows(m).T, rows(act))
            acc[pl.ds(3 * c, 1), :] += jnp.sum(grad.astype(F32), axis=0, keepdims=True)

        each_group(z, work)
        for i in range(3):
            acc[pl.ds(i * c, c), :] = sums[i].T
        for i, out in enumerate(outs):
            for j in range(ahead):
                for k in range(side):
                    owner = pl.multiple_of(plane.piece_of(me, (i, j, k)) * piece, 16)
                    out[j, k] = acc[pl.ds(owner, piece), :].astype(BF16)
        for copy in copies:
            copy.wait()

    return call(
        kernel,
        name,
        [SMEM] + [VMEM] * len(flat_args) + ([SMEM, ANY] if place else []),
        [VMEM] * core + ([ANY] if place else []),
        [jax.ShapeDtypeStruct((ahead, side, piece, c), BF16)] * core
        + ([jax.ShapeDtypeStruct(place[1].shape, BF16)] if place else []),
        [pltpu.VMEM((piece * plane.count, c), F32), pltpu.VMEM((3, c, c), F32)]
        + ([pltpu.SemaphoreType.DMA((z.lent,))] if place else []),
        14,
        (plane.me, *flat_args, *place),
        {2 + len(flat_args): core} if place else None,
    )


def added(values, split=False, after=()):
    shape = values[0].shape
    count = shape[0] if split else 1

    def kernel(*refs):
        outs = refs[-count:]
        for i, out in enumerate(outs):
            parts = [(ref[i] if split else ref[...]).astype(F32) for ref in refs[: len(values)]]
            total = parts[0]
            for part in parts[1:]:
                total = total + part
            out[...] = total.astype(BF16)

    args = [*values, *after]
    outs = call(
        kernel,
        "added",
        [VMEM] * len(values) + [ANY] * len(after),
        [VMEM] * count,
        [jax.ShapeDtypeStruct(shape[1:] if split else shape, BF16)] * count,
        [],
        8,
        args,
    )
    return outs if split else outs[0]


def plane_parts(plane, pieces, after=((), ())):
    parts = added(plane.received(pieces, 0), split=True, after=after[0])
    parts = added(plane.received(parts, 1), split=True, after=after[1])
    return plane.received(parts, 2)


def from_line(value, step):
    lines = lax.axis_size("feat")
    return lax.ppermute(value, "feat", [(i, i ^ step) for i in range(lines)])


def joined(early, late):
    def kernel(early, late, out):
        out[0] = early[...]
        out[1] = late[...]

    out = jax.ShapeDtypeStruct((2,) + late.shape, BF16)
    return call(kernel, "joined", [VMEM] * 2, VMEM, out, [], 4, (early, late))


def line_sum_of_four(both, near, early, late, after):
    def kernel(both, near, early0, early1, late0, late1, *rest):
        out = rest[-1]
        for layer, (first, second) in enumerate(((early0, early1), (late0, late1))):
            pair = both[layer].astype(F32) + near[layer].astype(F32)
            out[layer] = (pair + (first[...].astype(F32) + second[...].astype(F32))).astype(BF16)

    return call(
        kernel,
        "line_sum",
        [VMEM] * 6 + [ANY] * len(after),
        VMEM,
        jax.ShapeDtypeStruct(both.shape, BF16),
        [],
        6,
        (both, near, *early, *late, *after),
    )


def line_sum(share):
    lines = lax.axis_size("feat")
    if lines & (lines - 1) != 0:
        return lax.psum(share.astype(F32), "feat").astype(BF16)
    step = 1
    while step < lines:
        share = added([share, from_line(share, step)])
        step *= 2
    return share


def stacked(values, after):
    def kernel(*refs):
        for i, ref in enumerate(refs[: len(values)]):
            refs[-1][i] = ref[...]

    shape = (len(values),) + values[0].shape
    out = jax.ShapeDtypeStruct(shape, values[0].dtype)
    args = (*values, *after)
    return call(kernel, "stacked", [VMEM] * len(args), VMEM, out, [], 4, args)


def plane_gathered(plane, share, after):
    core, ahead, side = plane.sizes
    steps = [(0, j, k) for j in range(ahead) for k in range(side)]
    share = stacked([share] + [plane.passed_by(share, by) for by in steps[1:]], after)
    share = share.reshape(ahead, side, *share.shape[-3:])
    return [share] + [plane.passed(share, 0, i) for i in range(1, core)]


def second_out(z, bound, live, f1, act, w_out, out):
    def kernel(bound, live, f_lent, f_rest, act, wo, _out, out, token, keep, sems):
        copies = []
        token[...] = jnp.zeros_like(token)

        def work(part, first):
            f = z.flat(group_of(z, (f_lent, f_rest), part, first)[...])
            res = f.astype(F32) + dot(z.flat(act[pl.ds(first, z.group)]), wo[1])
            keep[pl.ds(first, z.group)] = z.tiled(live_rows(z, res, first, live[0]).astype(BF16))

        each_group(z, work, (0,))
        for i in range(z.lent):
            copy = pltpu.make_async_copy(
                keep.at[i], out.at[1, bound[0, i // z.edge, i % z.edge]], sems.at[i]
            )
            copy.start()
            copies.append(copy)
        each_group(z, work, (1,))
        tail = pl.ds(z.lent, z.rest)
        copy = pltpu.make_async_copy(keep.at[tail], out.at[1, tail], sems.at[z.lent])
        copy.start()
        copies.append(copy)
        for copy in copies:
            copy.wait()

    return call(
        kernel,
        "second_out",
        [SMEM] * 2 + [VMEM] * 4 + [ANY],
        [ANY, VMEM],
        [jax.ShapeDtypeStruct(out.shape, BF16), TOKEN],
        [z.held(z.tiles), pltpu.SemaphoreType.DMA((z.lent + 1,))],
        12,
        (bound, live, *f1, act, w_out, out),
        {6: 0},
    )


def input_grad(z, layer, tables, m, dpre, dagg, at, wt):
    arrays = (m, dpre, dagg)
    flat_args = [x for a in arrays for x in (a if isinstance(a, tuple) else (a,))]

    def kernel(blocks, sources, targets, counts, *refs):
        refs = list(refs)
        m, dpre, dagg = [
            (refs.pop(0), refs.pop(0)) if isinstance(a, tuple) else refs.pop(0) for a in arrays
        ]
        at, wt, part_out, rest_out, token, acc = refs
        token[...] = jnp.zeros_like(token)
        x = z.index

        def source(q):
            if not isinstance(dagg, tuple):
                return dagg[q]
            lent = dagg[0][jnp.minimum(q, z.lent - 1)]
            rest = dagg[1][jnp.maximum(q - z.lent, 0)]
            return jnp.where(q < z.lent, lent, rest)

        def tile_of(array, part, base, i):
            return array[part][i] if isinstance(array, tuple) else array[base + i]

        for part, base, count in z.parts:

            @pl.loop(0, count, unroll=4)
            def _(i):
                lefts, rights = [tile_of(dpre, part, base, i)], [wt[layer, 0]]
                for k in range(x.QUAD):
                    block = blocks[(base + i) * x.QUAD + k]
                    left = at[jnp.maximum(block, 0)]
                    lefts.append(jnp.where(block >= 0, left, jnp.zeros_like(left)))
                    rights.append(source(sources[(base + i) * x.QUAD + k]))
                value = dot(jnp.concatenate(lefts, axis=1), jnp.concatenate(rights, axis=0))
                acc[base + i] = value + tile_of(m, part, base, i).astype(F32)

        @pl.loop(0, counts[0])
        def _(i):
            place = x.more[0] + i
            acc[targets[place]] += dot(at[blocks[place]], source(sources[place]))

        part_out[...] = acc[pl.ds(0, z.lent)]
        rest_out[...] = acc[pl.ds(z.lent, z.rest)].astype(BF16)

    return call(
        kernel,
        "input_grad%d" % layer,
        [SMEM] * 4 + [VMEM] * (len(flat_args) + 2),
        [VMEM] * 3,
        [z.nodes(z.lent, F32), z.nodes(z.rest), TOKEN],
        [z.held(z.tiles, F32)],
        20,
        [*tables, *flat_args, at, wt],
    )


def early_rest(z, tables, live, upstream, slope, at, wt):
    def kernel(blocks, sources, targets, counts, live, g, slope, at, wt, grads, m, dpre, dagg, outer, sem):
        copy = pltpu.make_async_copy(g, grads.at[1, pl.ds(z.lent, z.rest)], sem)
        copy.start()

        def work(part, first):
            here = pl.ds(first - z.lent, z.group)
            masked = live_rows(z, z.flat(g[here]), first, live[0])
            m[here] = z.tiled(masked)
            grad = dot(masked, wt[0, 2]) * z.flat(slope[pl.ds(first, z.group)])
            grad = grad.astype(BF16)
            dpre[here] = z.tiled(grad)
            dagg[here] = z.tiled(dot(grad, wt[0, 1]).astype(BF16))

        each_group(z, work, (1,))

        def source(q):
            return dagg[jnp.maximum(q - z.lent, 0)]

        spread(z, (blocks, sources, targets, counts), 3, z.lent, at, source, outer, False)
        copy.wait()

    return call(
        kernel,
        "early_rest",
        [SMEM] * 5 + [VMEM] * 4,
        [ANY] + [VMEM] * 4,
        [jax.ShapeDtypeStruct((2, z.tiles, z.rows, z.cols), BF16)]
        + [z.nodes(z.rest)] * 3
        + [z.nodes(z.lent, F32)],
        [pltpu.SemaphoreType.DMA],
        14,
        (*tables, live, upstream, slope, at, wt),
    )


def early_lent(z, tables, part, fw, fe, slope, outer, at, wt, after):
    def kernel(blocks, sources, targets, counts, part, fw, fe, slope, outer, at, wt, _ready, _late,
               m, dpre, dagg, to_west, to_east, acc):
        half = z.edge // z.group

        def collect(s):
            here = pl.ds(s * z.group, z.group)
            got = (fw if s < half else fe)[pl.ds(s % half * z.group, z.group)]
            m[here] = (part[here] + got.astype(F32)).astype(BF16)

        def middle(s):
            here = pl.ds(s * z.group, z.group)
            grad = dot(z.flat(m[here]), wt[0, 2]) * z.flat(slope[here])
            dpre[here] = z.tiled(grad.astype(BF16))

        def last(s):
            here = pl.ds(s * z.group, z.group)
            dagg[here] = z.tiled(dot(z.flat(dpre[here]), wt[0, 1]).astype(BF16))

        staged(2 * half, collect, middle, last)
        acc[...] = outer[...]

        def source(q):
            return dagg[jnp.minimum(q, z.lent - 1)]

        spread(z, (blocks, sources, targets, counts), 2, z.lent, at, source, acc, True)
        to_west[...] = acc[pl.ds(0, z.edge)].astype(BF16)
        to_east[...] = acc[pl.ds(z.edge, z.edge)].astype(BF16)

    return call(
        kernel,
        "early_lent",
        [SMEM] * 4 + [VMEM] * 9,
        [VMEM] * 5,
        [z.nodes(z.lent)] * 3 + [z.nodes(z.edge)] * 2,
        [z.held(z.lent, F32)],
        16,
        (*tables, part, fw, fe, slope, outer, at, wt, *after),
    )


def finish(z, bound, part, rest, fw, fe, grads):
    def kernel(bound, part, rest, fw, fe, _g, grads, token, keep, sems):
        token[...] = jnp.zeros_like(token)
        copies = [pltpu.make_async_copy(rest, grads.at[0, pl.ds(z.lent, z.rest)], sems.at[z.lent])]
        copies[0].start()
        for i in range(z.lent):
            got = fw[i] if i < z.edge else fe[i - z.edge]
            keep[i] = (part[i] + got.astype(F32)).astype(BF16)
            copy = pltpu.make_async_copy(
                keep.at[i], grads.at[0, bound[0, i // z.edge, i % z.edge]], sems.at[i]
            )
            copy.start()
            copies.append(copy)
        for copy in copies:
            copy.wait()

    return call(
        kernel,
        "finish",
        [SMEM] + [VMEM] * 4 + [ANY],
        [ANY, VMEM],
        [jax.ShapeDtypeStruct(grads.shape, BF16), TOKEN],
        [z.held(z.lent), pltpu.SemaphoreType.DMA((z.lent + 1,))],
        14,
        (bound, part, rest, fw, fe, grads),
        {5: 0},
    )


def unpack(z, plane, pieces):
    c = z.cols
    piece = pieces[0].shape[3]
    core, ahead, side = plane.sizes

    def kernel(me, *refs):
        pieces = refs[:core]
        *outs, bias, buf, sems = refs[core:]
        copies = []
        for layer in range(2):
            for i in range(core):
                for j in range(ahead):
                    for k in range(side):
                        start = pl.multiple_of(plane.piece_of(me, (-i, -j, -k)) * piece, 16)
                        buf[layer, pl.ds(start, piece), :] = pieces[i][j, k, layer].astype(F32)
            for i, out in enumerate(outs):
                copy = pltpu.make_async_copy(
                    buf.at[layer, pl.ds(i * c, c)], out.at[layer], sems.at[3 * layer + i]
                )
                copy.start()
                copies.append(copy)
            bias[layer : layer + 1, :] = buf[layer, pl.ds(3 * c, 1), :]
        for copy in copies:
            copy.wait()

    square = jax.ShapeDtypeStruct((2, c, c), F32)
    return call(
        kernel,
        "unpack",
        [SMEM] + [VMEM] * core,
        [ANY] * 3 + [VMEM],
        [square, square, square, jax.ShapeDtypeStruct((2, c), F32)],
        [pltpu.VMEM((2, piece * plane.count, c), F32), pltpu.SemaphoreType.DMA((6,))],
        10,
        (plane.me, *pieces),
    )


def per_device(
    node_in, out_cot, adjacency, tile_nbrs, bound_tiles, live_tiles, w_self, w_nbr, pre_bias, w_out
):
    z = Sizes(adjacency, node_in, bound_tiles)
    t, r, c = z.tiles, z.rows, z.cols
    features = node_in.reshape(t, r, c)
    cot = out_cot.reshape(t, r, c)
    plane = Plane()

    west, east = lend(z, bound_tiles, features)
    from_west = passed_along(east, 1)
    from_east = passed_along(west, -1)
    *nodes, adj, ext, tiles, reads, blocks, sources, targets, counts, plane.me = arrange(
        z, bound_tiles, tile_nbrs, live_tiles, plane.place, features, cot, adjacency.reshape(z.pairs, r, r)
    )
    f0, m1 = tuple(nodes[:2]), tuple(nodes[2:])
    tables = (blocks, sources, targets, counts)
    at, wt = turn(z, adj, w_self, w_nbr, w_out)

    west, east, agg_lent, _ = first_lent(
        z, tiles, reads, ext, from_west, from_east, adj, w_self, w_nbr, pre_bias, w_out
    )
    next_west = passed_along(east, 1)
    next_east = passed_along(west, -1)
    f1_lent, f1_rest, section_out, agg_rest = first_rest(
        z, tiles, reads, bound_tiles, live_tiles, f0, from_west, from_east, adj, w_self, w_nbr, pre_bias, w_out,
        west, east,
    )
    f1, agg0 = (f1_lent, f1_rest), (agg_lent, agg_rest)
    own, hidden, ext = second_own(z, f1, m1, w_self, pre_bias, wt)
    act0, slope, ready = saved(z, f0, agg0, w_self, w_nbr, pre_bias)

    agg1, act1, dpre1, dagg1, to_west, to_east, _ = second(
        z, tiles, reads, tables, ext, next_west, next_east, adj, at, own, hidden, w_nbr, wt, ready
    )
    back_west = passed_along(to_east, 1)
    back_east = passed_along(to_west, -1)
    late = weight_grads(z, plane, f1, agg1, act1, m1, dpre1, "weight_grads1")
    section_out, ready = second_out(z, bound_tiles, live_tiles, f1, act1, w_out, section_out)
    part, upstream, done = input_grad(z, 1, tables, m1, dpre1, dagg1, at, wt)
    late = plane_parts(plane, late, ((ready,), (done,)))
    grads, m0_rest, dpre_rest, dagg_rest, outer = early_rest(
        z, tables, live_tiles, upstream, slope, at, wt
    )
    late = added(late, after=(outer,))

    m0_lent, dpre_lent, dagg_lent, to_west, to_east = early_lent(
        z, tables, part, back_west, back_east, slope, outer, at, wt, (ready, late)
    )
    back_west = passed_along(to_east, 1)
    back_east = passed_along(to_west, -1)
    m0, dpre0, dagg0 = (m0_lent, m0_rest), (dpre_lent, dpre_rest), (dagg_lent, dagg_rest)
    *early, grads = weight_grads(z, plane, f0, agg0, act0, m0, dpre0, "weight_grads0", (bound_tiles, grads))


    late_far = [from_line(late, step) for step in (2, 3)] if lax.axis_size("feat") == 4 else []

    def meanwhile(early, tables, m0, dpre0, dagg0, at, wt):
        part, rest, _ = input_grad(z, 0, tables, m0, dpre0, dagg0, at, wt)
        return added(plane_parts(plane, early)), part, rest

    args = (early, tables, m0, dpre0, dagg0, at, wt)
    shapes = jax.eval_shape(meanwhile, *args)
    early, part, rest = lax.cond(
        live_tiles[0] > 0,
        meanwhile,
        lambda *_: jax.tree.map(lambda a: jnp.zeros(a.shape, a.dtype), shapes),
        *args,
    )
    both = joined(early, late)
    if lax.axis_size("feat") == 4:
        near = from_line(both, 1)
        far = [from_line(early, step) for step in (2, 3)]
        shares = line_sum_of_four(both, near, far, late_far, (back_west, back_east))
    else:
        shares = line_sum(both)
    grads, done = finish(z, bound_tiles, part, rest, back_west, back_east, grads)
    pieces = plane_gathered(plane, shares, (done,))
    grad_self, grad_nbr, grad_out, grad_bias = unpack(z, plane, pieces)
    return (
        section_out.reshape(2, t * r, c),
        grads.reshape(2, t * r, c),
        grad_self,
        grad_nbr,
        grad_bias,
        grad_out,
    )


def solution(mesh):
    rows = P(AXES)
    in_specs = (rows, rows, rows, rows, rows, rows, P(), P(), P(), P())
    out_specs = (P(None, AXES), P(None, AXES), P(), P(), P(), P())
    return jax.shard_map(
        per_device, mesh=mesh, in_specs=in_specs, out_specs=out_specs, check_vma=False
    )
```
